32 devices in a mesh: groups: 2 (over y), blk: 4 (over z), panel: 2 (over x), depth: 2 (over core).
Axes of the slice: x: 2, y: 2, z: 4, core: 2. Of those that a mesh axis runs over, the one named last changes fastest.
Arguments:
- x_blocks: float32 [16, 16, 128, 128], P(('groups', 'blk'), ('panel', 'depth')), parts along dimension 0, may hold values from -0.6 to 0.6
- columns: int32 [16, 16], P('groups'), parts along dimension 0, may hold values from 0 to 8, as said below
Outputs:
- purified: float32 [16, 16, 128, 128], P(('groups', 'blk'), ('panel', 'depth')), parts along dimension 0
The draws below stay inside these ranges and needn't reach their ends.
There are 2 independent parts, one for each index of `groups`. The reference program is written for one: setup_inputs(seed, part) draws one part's arguments, and reference() takes and returns one part's arrays. A program takes and returns all parts, laid end to end along the dimension named above; each array names one. Nothing has to cross between parts.
Inputs may be any that keep to these rules, and one draw needn't show every extreme that they name: `columns`: in each block row the present entries stand first and name distinct block rows, slot 0 names the row itself, empty slots hold 8; a row has between max(1, min(16, 8) // 2) and min(16, 8) present slots, the count differs from row to row, and some row has min(16, 8) present.
All inputs are finite; a program needn't handle non-finite values.
Results may differ from the reference program's by a relative error of at most 0.0003.
Values sent between devices are 32-bit elements; how exact they have to be, the bound alone decides.
No kernel may reach another device: no remote copies, remote signals or barrier semaphores. Data moves between devices by JAX's collectives and lax.ppermute only.
A program may use at most 64 MiB of HBM per device.

```python
import jax
import jax.numpy as jnp
from jax import lax

BS = 128
SLOTS = 16
NB = 8


def draw_columns(key, part):
    key = jax.random.fold_in(key, 11)
    key_order, key_count = jax.random.split(key)
    cap = min(SLOTS, NB)
    low = max(1, cap // 2)
    row_ids = jnp.arange(NB, dtype=jnp.int32)
    scores = jax.random.randint(key_order, (NB, NB), 0, 2 ** 16, dtype=jnp.int32) * NB + row_ids[None, :]
    scores = jnp.where(row_ids[:, None] == row_ids[None, :], -1, scores)
    ranking = jnp.argsort(scores, axis=1, stable=True)[:, :cap].astype(jnp.int32)
    if cap < SLOTS:
        ranking = jnp.concatenate([ranking, jnp.full((NB, SLOTS - cap), NB, dtype=jnp.int32)], axis=1)
    counts = jax.random.randint(key_count, (NB,), low, cap + 1, dtype=jnp.int32)
    counts = counts.at[0].set(cap).at[1].set(low)
    slot_ids = jnp.arange(SLOTS, dtype=jnp.int32)
    pattern = jnp.where(slot_ids[None, :] < counts[:, None], ranking, NB)
    return pattern.astype(jnp.int32)


def block_scale(stream_key, extent, cuts, least, high):
    level, own = 1.0, jax.random.fold_in(stream_key, 6)
    for position, shards_of in cuts:
        draws = jnp.exp(jax.random.uniform(jax.random.fold_in(own, position), (shards_of,), jnp.float32, least / len(cuts), high / len(cuts)))
        level = level * jnp.repeat(draws, extent[position] // shards_of).reshape([-1 if axis == position else 1 for axis in range(len(extent))])
    return level


def normal_values(own_key, shape, scale, limit, cuts=(), held_as=jnp.bfloat16):
    loudness = block_scale(own_key, shape, cuts, -0.22, 0.18) if cuts else 1.0
    array = jax.random.normal(own_key, shape, jnp.float32) * scale * loudness
    return jnp.minimum(jnp.maximum(array, -limit), limit).astype(held_as)


def setup_inputs(seed: int = 0, part: int = 0) -> dict:
    keys = jax.random.split(jax.random.key(seed), 3)
    part_splits = jax.random.split(jax.random.fold_in(keys[2], part), 3)
    x_blocks = normal_values(part_splits[0], (NB, SLOTS, BS, BS), 0.1, 0.6, ((0, 4), (1, 4)), jnp.float32)
    columns = draw_columns(jax.random.fold_in(jax.random.fold_in(keys[2], part), 71), part)
    return dict(x_blocks=x_blocks, columns=columns)


precise = lax.Precision.HIGHEST


def product(left_blocks, right_blocks, columns):
    order_rows = columns.shape[0]
    present = columns < order_rows
    safe_cols = jnp.where(present, columns, 0).astype(jnp.int32)

    def one_row(index_row):
        neighbors = safe_cols[index_row]
        their_rows = right_blocks[neighbors]
        their_cols = columns[neighbors]
        matches = (their_cols[None, :, :] == columns[index_row][:, None, None])
        matches = matches & present[index_row][None, :, None] & present[index_row][:, None, None]
        picked = jnp.einsum("stu,tuab->stab", matches.astype(jnp.float32), their_rows, precision=precise)
        return jnp.einsum("tab,stbc->sac", left_blocks[index_row], picked, precision=precise)

    return lax.map(one_row, jnp.arange(order_rows, dtype=jnp.int32))


def reference(x_blocks, columns):
    present = columns < columns.shape[0]
    masked = jnp.where(present[:, :, None, None], x_blocks, jnp.float32(0.0))
    squared = product(masked, masked, columns)
    cubed = product(squared, masked, columns)
    return 3.0 * squared - 2.0 * cubed
```

```python
import functools

import jax
import jax.numpy as jnp
from jax import lax
from jax.experimental import pallas as pl
from jax.experimental.pallas import tpu as pltpu
from jax.sharding import PartitionSpec as P

precise = lax.Precision.HIGHEST
AXES = ("blk", "panel", "depth")


def shifted(block, axis, distance):
    devices = range(lax.axis_size(axis))
    route = [((i - distance) % len(devices), i) for i in devices]
    return lax.ppermute(block, axis, route)


def slot_gather(blocks):
    return lax.all_gather(blocks, ("panel", "depth"), axis=1, tiled=True)


def slot_reduce(partial_value):
    return lax.psum_scatter(partial_value, ("panel", "depth"), scatter_dimension=1, tiled=True)


def rotate_one(incoming):
    return shifted(incoming, "blk", 1)


def ring_local(x_blocks, columns):
    slab_rows = x_blocks.shape[0]
    width_slots = x_blocks.shape[1]
    edge = x_blocks.shape[2]
    order_rows = columns.shape[0]
    all_slots = columns.shape[1]
    cycle_size = lax.axis_size("blk")
    cycle_place = lax.axis_index("blk")
    anchor = jnp.int32(0)
    first_own = cycle_place * slab_rows
    slot_first = lax.axis_index(("panel", "depth")) * width_slots
    my_cols = lax.dynamic_slice(columns, (first_own, anchor), (slab_rows, all_slots))
    own_cols = lax.dynamic_slice(my_cols, (anchor, slot_first), (slab_rows, width_slots))
    x_own = jnp.where((own_cols < order_rows)[:, :, None, None], x_blocks, jnp.float32(0.0))
    out_present = my_cols < order_rows
    empty = jnp.zeros((slab_rows, all_slots, edge, edge), jnp.float32)

    def contribute(partial_value, left_rows, incoming, source):
        group = incoming.shape[0]
        first_row = source * group
        their_cols = lax.dynamic_slice(columns, (first_row, slot_first), (group, width_slots))
        row_ids = first_row + jnp.arange(group, dtype=jnp.int32)
        selector = (my_cols[:, None, :] == row_ids[None, :, None]).astype(jnp.float32)
        picked = jnp.einsum("irs,isab->irab", selector, left_rows, precision=precise)
        products = jnp.einsum("irab,rubc->iruac", picked, incoming, precision=precise)
        targets = (their_cols[None, None, :, :] == my_cols[:, :, None, None]) & out_present[
            :, :, None, None
        ]
        placed = jnp.einsum(
            "isru,iruac->isac", targets.astype(jnp.float32), products, precision=precise
        )
        return partial_value + placed

    def one_way(left_rows, stored):

        def advance(offset, state):
            partial_value, incoming, stored = state
            source = (cycle_place - offset) % cycle_size
            partial_value = contribute(partial_value, left_rows, incoming, source)
            return (partial_value, rotate_one(incoming), stored)

        partial_value, incoming, stored = lax.fori_loop(
            0, cycle_size - 1, advance, (empty, x_own, stored)
        )
        source = (cycle_place + 1) % cycle_size
        return (contribute(partial_value, left_rows, incoming, source), stored)

    stored = jnp.zeros((1,), jnp.float32)
    left_first = slot_gather(x_own)
    partial_value, stored = one_way(left_first, stored)
    squared = slot_reduce(partial_value)
    left_second = slot_gather(squared)
    partial_value, stored = one_way(left_second, stored)
    cubed = slot_reduce(partial_value)
    return 3.0 * squared - 2.0 * cubed


def split(value):
    high = value.astype(jnp.bfloat16)
    low = (value - high.astype(jnp.float32)).astype(jnp.bfloat16)
    return high, low


def dot3(left, right):
    dot = functools.partial(jnp.dot, preferred_element_type=jnp.float32)
    return dot(left[0], right[0]) + (dot(left[0], right[1]) + dot(left[1], right[0]))


def purify_kernel(sizes, sources, cols_ref, place_ref, *refs):
    slab, width, edge, rows, chains, lanes = sizes
    pieces = refs[: len(sources)]
    out_ref, high, low, sq_ref, sq_high, sq_low, cu_ref = refs[len(sources) :]
    place, lane = place_ref[0], place_ref[1]

    high[...] = jnp.zeros_like(high)
    low[...] = jnp.zeros_like(low)
    for piece, (hop, swap) in zip(pieces, sources):
        plane = place + hop
        valid = (plane >= 0) & (plane < chains)
        core = (lane + swap) % lanes
        for r in range(slab):
            row = jnp.where(valid, plane * slab + r, 0)
            for w in range(width):
                col = cols_ref[row, core * width + w]

                @pl.when(valid & (col < rows))
                def _():
                    block_high, block_low = split(piece[r, w])
                    at = (
                        pl.ds(pl.multiple_of(row * edge, edge), edge),
                        pl.ds(pl.multiple_of(col * edge, edge), edge),
                    )
                    high[at] = block_high
                    low[at] = block_low

    mine = pl.ds(pl.multiple_of(place * (slab * edge), slab * edge), slab * edge)
    sq_ref[...] = dot3((high[mine, :], low[mine, :]), (high[...], low[...]))
    for r in range(slab):
        row = place * slab + r
        slots = [cols_ref[row, s] for s in range(cols_ref.shape[1])]
        for c in range(rows):
            there = functools.reduce(jnp.logical_or, [s == c for s in slots])
            at = (pl.ds(r * edge, edge), pl.ds(c * edge, edge))
            kept = jnp.where(there, sq_ref[at], 0.0)
            kept_high, kept_low = split(kept)
            sq_high[at] = kept_high
            sq_low[at] = kept_low
    cu_ref[...] = dot3((sq_high[...], sq_low[...]), (high[...], low[...]))
    for r in range(slab):
        for w in range(width):
            col = cols_ref[place * slab + r, place_ref[2] * width + w]
            there = col < rows
            at = (
                pl.ds(r * edge, edge),
                pl.ds(pl.multiple_of(jnp.where(there, col, 0) * edge, edge), edge),
            )
            out_ref[r, w] = jnp.where(there, 3.0 * sq_ref[at] - 2.0 * cu_ref[at], 0.0)


def gather_local(x_blocks, columns):
    slab, width, edge, _ = x_blocks.shape
    rows = columns.shape[0]
    chains, panels, lanes = (lax.axis_size(axis) for axis in AXES)

    def index(z, x, c):
        return (z * panels + x) * lanes + c

    def move(block, pairs):
        route = [
            (index(z, x, c), index(to_z, to_x, c))
            for (z, x), (to_z, to_x) in pairs
            for c in range(lanes)
        ]
        return lax.ppermute(block, AXES, route)

    def swap(block, planes):
        route = [
            (index(z, 0, c), index(z, 0, (c + 1) % lanes)) for z in planes for c in range(lanes)
        ]
        return lax.ppermute(block, AXES, route)

    last = chains - 1
    far = move(x_blocks, [((0, 0), (last, 1)), ((last, 0), (0, 1))])
    up, down = x_blocks, x_blocks
    held = [(x_blocks, 0, range(chains))]
    for hop in range(1, last):
        up = move(up, [((z, 0), (z + 1, 0)) for z in range(hop - 1, last)])
        down = move(down, [((z, 0), (z - 1, 0)) for z in range(1, chains - hop + 1)])
        held.append((up, -hop, range(hop, chains)))
        held.append((down, hop, range(chains - hop)))
    far = move(far, [((last, 1), (last, 0)), ((0, 1), (0, 0))])
    held.append((far, -last, [last]))
    held.append((far, last, [0]))

    sources, pieces = [], []
    swapped = None
    for block, hop, planes in held:
        if block is far:
            swapped = swap(far, [0, last]) if swapped is None else swapped
            other = swapped
        else:
            other = swap(block, planes)
        sources += [(hop, 0), (hop, 1)]
        pieces += [block, other]

    place = jnp.stack(
        [
            lax.axis_index("blk"),
            lax.axis_index("depth"),
            lax.axis_index("panel") * lanes + lax.axis_index("depth"),
        ]
    ).astype(jnp.int32)
    order = rows * edge
    sizes = (slab, width, edge, rows, chains, lanes)
    smem = pl.BlockSpec(memory_space=pltpu.SMEM)
    vmem = pl.BlockSpec(memory_space=pltpu.VMEM)
    return pl.pallas_call(
        functools.partial(purify_kernel, sizes, sources),
        out_shape=jax.ShapeDtypeStruct(x_blocks.shape, jnp.float32),
        in_specs=[smem, smem] + [vmem] * len(pieces),
        out_specs=vmem,
        scratch_shapes=[
            pltpu.VMEM((order, order), jnp.bfloat16),
            pltpu.VMEM((order, order), jnp.bfloat16),
            pltpu.VMEM((slab * edge, order), jnp.float32),
            pltpu.VMEM((slab * edge, order), jnp.bfloat16),
            pltpu.VMEM((slab * edge, order), jnp.bfloat16),
            pltpu.VMEM((slab * edge, order), jnp.float32),
        ],
        compiler_params=pltpu.CompilerParams(vmem_limit_bytes=48 * 2**20),
        name="purify",
    )(columns, place, *pieces)


def local(x_blocks, columns):
    slab, width, edge, _ = x_blocks.shape
    rows, slots = columns.shape
    chains, panels, lanes = (lax.axis_size(axis) for axis in AXES)
    present = min(slots, rows)
    small = rows * rows * edge * edge * 4 <= 4 * 2**20
    if small and panels >= 2 and lanes == 2 and chains >= 3 and present <= lanes * width:
        return gather_local(x_blocks, columns)
    return ring_local(x_blocks, columns)


def solution(mesh):
    placed = (P(("groups", "blk"), ("panel", "depth"), None, None), P("groups", None))
    return jax.shard_map(
        local,
        mesh=mesh,
        in_specs=placed,
        out_specs=P(("groups", "blk"), ("panel", "depth"), None, None),
        check_vma=False,
    )
```

```python
import functools

import jax
import jax.numpy as jnp
from jax import lax
from jax.experimental import pallas as pl
from jax.experimental.pallas import tpu as pltpu
from jax.sharding import PartitionSpec as P

precise = lax.Precision.HIGHEST
AXES = ("blk", "panel", "depth")


def shifted(block, axis, distance):
    devices = range(lax.axis_size(axis))
    route = [((i - distance) % len(devices), i) for i in devices]
    return lax.ppermute(block, axis, route)


def slot_gather(blocks):
    return lax.all_gather(blocks, ("panel", "depth"), axis=1, tiled=True)


def slot_reduce(partial_value):
    return lax.psum_scatter(partial_value, ("panel", "depth"), scatter_dimension=1, tiled=True)


def rotate_one(incoming):
    return shifted(incoming, "blk", 1)


def ring_local(x_blocks, columns):
    slab_rows = x_blocks.shape[0]
    width_slots = x_blocks.shape[1]
    edge = x_blocks.shape[2]
    order_rows = columns.shape[0]
    all_slots = columns.shape[1]
    cycle_size = lax.axis_size("blk")
    cycle_place = lax.axis_index("blk")
    anchor = jnp.int32(0)
    first_own = cycle_place * slab_rows
    slot_first = lax.axis_index(("panel", "depth")) * width_slots
    my_cols = lax.dynamic_slice(columns, (first_own, anchor), (slab_rows, all_slots))
    own_cols = lax.dynamic_slice(my_cols, (anchor, slot_first), (slab_rows, width_slots))
    x_own = jnp.where((own_cols < order_rows)[:, :, None, None], x_blocks, jnp.float32(0.0))
    out_present = my_cols < order_rows
    empty = jnp.zeros((slab_rows, all_slots, edge, edge), jnp.float32)

    def contribute(partial_value, left_rows, incoming, source):
        group = incoming.shape[0]
        first_row = source * group
        their_cols = lax.dynamic_slice(columns, (first_row, slot_first), (group, width_slots))
        row_ids = first_row + jnp.arange(group, dtype=jnp.int32)
        selector = (my_cols[:, None, :] == row_ids[None, :, None]).astype(jnp.float32)
        picked = jnp.einsum("irs,isab->irab", selector, left_rows, precision=precise)
        products = jnp.einsum("irab,rubc->iruac", picked, incoming, precision=precise)
        targets = (their_cols[None, None, :, :] == my_cols[:, :, None, None]) & out_present[
            :, :, None, None
        ]
        placed = jnp.einsum(
            "isru,iruac->isac", targets.astype(jnp.float32), products, precision=precise
        )
        return partial_value + placed

    def one_way(left_rows, stored):

        def advance(offset, state):
            partial_value, incoming, stored = state
            source = (cycle_place - offset) % cycle_size
            partial_value = contribute(partial_value, left_rows, incoming, source)
            return (partial_value, rotate_one(incoming), stored)

        partial_value, incoming, stored = lax.fori_loop(
            0, cycle_size - 1, advance, (empty, x_own, stored)
        )
        source = (cycle_place + 1) % cycle_size
        return (contribute(partial_value, left_rows, incoming, source), stored)

    stored = jnp.zeros((1,), jnp.float32)
    left_first = slot_gather(x_own)
    partial_value, stored = one_way(left_first, stored)
    squared = slot_reduce(partial_value)
    left_second = slot_gather(squared)
    partial_value, stored = one_way(left_second, stored)
    cubed = slot_reduce(partial_value)
    return 3.0 * squared - 2.0 * cubed


def split(value):
    high = value.astype(jnp.bfloat16)
    low = (value - high.astype(jnp.float32)).astype(jnp.bfloat16)
    return high, low


def dot3(left, right):
    dot = functools.partial(jnp.dot, preferred_element_type=jnp.float32)
    return dot(left[0], right[0]) + (dot(left[0], right[1]) + dot(left[1], right[0]))


def purify_kernel(sizes, sources, cols_ref, place_ref, *refs):
    slab, width, edge, rows, chains, lanes = sizes
    pieces = refs[: len(sources)]
    out_ref, high, low, sq_ref, sq_high, sq_low, cu_ref = refs[len(sources) :]
    place, lane = place_ref[0], place_ref[1]

    high[...] = jnp.zeros_like(high)
    low[...] = jnp.zeros_like(low)
    for piece, (origin, swap) in zip(pieces, sources):
        plane = jnp.int32(-1)
        for here, source in origin:
            plane = jnp.where(place == here, source, plane)
        valid = plane >= 0
        core = (lane + swap) % lanes
        for r in range(slab):
            row = jnp.where(valid, plane * slab + r, 0)
            for w in range(width):
                col = cols_ref[row, core * width + w]

                @pl.when(valid & (col < rows))
                def _():
                    block_high, block_low = split(piece[r, w])
                    at = (
                        pl.ds(pl.multiple_of(row * edge, edge), edge),
                        pl.ds(pl.multiple_of(col * edge, edge), edge),
                    )
                    high[at] = block_high
                    low[at] = block_low

    mine = pl.ds(pl.multiple_of(place * (slab * edge), slab * edge), slab * edge)
    sq_ref[...] = dot3((high[mine, :], low[mine, :]), (high[...], low[...]))
    for r in range(slab):
        row = place * slab + r
        slots = [cols_ref[row, s] for s in range(cols_ref.shape[1])]
        for c in range(rows):
            there = functools.reduce(jnp.logical_or, [s == c for s in slots])
            at = (pl.ds(r * edge, edge), pl.ds(c * edge, edge))
            kept = jnp.where(there, sq_ref[at], 0.0)
            kept_high, kept_low = split(kept)
            sq_high[at] = kept_high
            sq_low[at] = kept_low
    cu_ref[...] = dot3((sq_high[...], sq_low[...]), (high[...], low[...]))
    for r in range(slab):
        for w in range(width):
            col = cols_ref[place * slab + r, place_ref[2] * width + w]
            there = col < rows
            at = (
                pl.ds(r * edge, edge),
                pl.ds(pl.multiple_of(jnp.where(there, col, 0) * edge, edge), edge),
            )
            out_ref[r, w] = jnp.where(there, 3.0 * sq_ref[at] - 2.0 * cu_ref[at], 0.0)


def gather_local(x_blocks, columns):
    slab, width, edge, _ = x_blocks.shape
    rows = columns.shape[0]
    chains, panels, lanes = (lax.axis_size(axis) for axis in AXES)

    def index(z, x, c):
        return (z * panels + x) * lanes + c

    def move(block, pairs):
        route = [
            (index(z, x, c), index(to_z, to_x, c))
            for (z, x), (to_z, to_x) in pairs
            for c in range(lanes)
        ]
        return lax.ppermute(block, AXES, route)

    def swap(block, planes):
        route = [
            (index(z, 0, c), index(z, 0, (c + 1) % lanes)) for z in planes for c in range(lanes)
        ]
        return lax.ppermute(block, AXES, route)

    last = chains - 1
    up, down = x_blocks, x_blocks
    held = [(x_blocks, [(z, z) for z in range(chains)])]
    for hop in range(1, last):
        ups = [((z, 0), (z + 1, 0)) for z in range(hop - 1, last)]
        downs = [((z, 0), (z - 1, 0)) for z in range(1, chains - hop + 1)]
        from_up = [(z, z - hop) for z in range(hop, chains)]
        from_down = [(z, z + hop) for z in range(chains - hop)]
        if hop == 1:
            ups += [((last, 0), (last, 1))]
            downs += [((0, 0), (0, 1))]
        if hop == 2:
            ups += [((last, 1), (0, 0))]
            downs += [((0, 1), (last, 0))]
            from_up += [(0, last)]
            from_down += [(last, 0)]
        up, down = move(up, ups), move(down, downs)
        held += [(up, from_up), (down, from_down)]

    sources, pieces = [], []
    for block, origin in held:
        sources += [(origin, 0), (origin, 1)]
        pieces += [block, swap(block, [z for z, _ in origin])]

    place = jnp.stack(
        [
            lax.axis_index("blk"),
            lax.axis_index("depth"),
            lax.axis_index("panel") * lanes + lax.axis_index("depth"),
        ]
    ).astype(jnp.int32)
    order = rows * edge
    sizes = (slab, width, edge, rows, chains, lanes)
    smem = pl.BlockSpec(memory_space=pltpu.SMEM)
    vmem = pl.BlockSpec(memory_space=pltpu.VMEM)
    return pl.pallas_call(
        functools.partial(purify_kernel, sizes, sources),
        out_shape=jax.ShapeDtypeStruct(x_blocks.shape, jnp.float32),
        in_specs=[smem, smem] + [vmem] * len(pieces),
        out_specs=vmem,
        scratch_shapes=[
            pltpu.VMEM((order, order), jnp.bfloat16),
            pltpu.VMEM((order, order), jnp.bfloat16),
            pltpu.VMEM((slab * edge, order), jnp.float32),
            pltpu.VMEM((slab * edge, order), jnp.bfloat16),
            pltpu.VMEM((slab * edge, order), jnp.bfloat16),
            pltpu.VMEM((slab * edge, order), jnp.float32),
        ],
        compiler_params=pltpu.CompilerParams(vmem_limit_bytes=48 * 2**20),
        name="purify",
    )(columns, place, *pieces)


def local(x_blocks, columns):
    slab, width, edge, _ = x_blocks.shape
    rows, slots = columns.shape
    chains, panels, lanes = (lax.axis_size(axis) for axis in AXES)
    present = min(slots, rows)
    small = rows * rows * edge * edge * 4 <= 4 * 2**20
    if small and panels >= 2 and lanes == 2 and chains >= 4 and present <= lanes * width:
        return gather_local(x_blocks, columns)
    return ring_local(x_blocks, columns)


def solution(mesh):
    placed = (P(("groups", "blk"), ("panel", "depth"), None, None), P("groups", None))
    return jax.shard_map(
        local,
        mesh=mesh,
        in_specs=placed,
        out_specs=P(("groups", "blk"), ("panel", "depth"), None, None),
        check_vma=False,
    )
```

```python
import functools

import jax
import jax.numpy as jnp
from jax import lax
from jax.experimental import pallas as pl
from jax.experimental.pallas import tpu as pltpu
from jax.sharding import PartitionSpec as P

precise = lax.Precision.HIGHEST
AXES = ("blk", "panel", "depth")


def shifted(block, axis, distance):
    devices = range(lax.axis_size(axis))
    route = [((i - distance) % len(devices), i) for i in devices]
    return lax.ppermute(block, axis, route)


def slot_gather(blocks):
    return lax.all_gather(blocks, ("panel", "depth"), axis=1, tiled=True)


def slot_reduce(partial_value):
    return lax.psum_scatter(partial_value, ("panel", "depth"), scatter_dimension=1, tiled=True)


def rotate_one(incoming):
    return shifted(incoming, "blk", 1)


def ring_local(x_blocks, columns):
    slab_rows = x_blocks.shape[0]
    width_slots = x_blocks.shape[1]
    edge = x_blocks.shape[2]
    order_rows = columns.shape[0]
    all_slots = columns.shape[1]
    cycle_size = lax.axis_size("blk")
    cycle_place = lax.axis_index("blk")
    anchor = jnp.int32(0)
    first_own = cycle_place * slab_rows
    slot_first = lax.axis_index(("panel", "depth")) * width_slots
    my_cols = lax.dynamic_slice(columns, (first_own, anchor), (slab_rows, all_slots))
    own_cols = lax.dynamic_slice(my_cols, (anchor, slot_first), (slab_rows, width_slots))
    x_own = jnp.where((own_cols < order_rows)[:, :, None, None], x_blocks, jnp.float32(0.0))
    out_present = my_cols < order_rows
    empty = jnp.zeros((slab_rows, all_slots, edge, edge), jnp.float32)

    def contribute(partial_value, left_rows, incoming, source):
        group = incoming.shape[0]
        first_row = source * group
        their_cols = lax.dynamic_slice(columns, (first_row, slot_first), (group, width_slots))
        row_ids = first_row + jnp.arange(group, dtype=jnp.int32)
        selector = (my_cols[:, None, :] == row_ids[None, :, None]).astype(jnp.float32)
        picked = jnp.einsum("irs,isab->irab", selector, left_rows, precision=precise)
        products = jnp.einsum("irab,rubc->iruac", picked, incoming, precision=precise)
        targets = (their_cols[None, None, :, :] == my_cols[:, :, None, None]) & out_present[
            :, :, None, None
        ]
        placed = jnp.einsum(
            "isru,iruac->isac", targets.astype(jnp.float32), products, precision=precise
        )
        return partial_value + placed

    def one_way(left_rows, stored):

        def advance(offset, state):
            partial_value, incoming, stored = state
            source = (cycle_place - offset) % cycle_size
            partial_value = contribute(partial_value, left_rows, incoming, source)
            return (partial_value, rotate_one(incoming), stored)

        partial_value, incoming, stored = lax.fori_loop(
            0, cycle_size - 1, advance, (empty, x_own, stored)
        )
        source = (cycle_place + 1) % cycle_size
        return (contribute(partial_value, left_rows, incoming, source), stored)

    stored = jnp.zeros((1,), jnp.float32)
    left_first = slot_gather(x_own)
    partial_value, stored = one_way(left_first, stored)
    squared = slot_reduce(partial_value)
    left_second = slot_gather(squared)
    partial_value, stored = one_way(left_second, stored)
    cubed = slot_reduce(partial_value)
    return 3.0 * squared - 2.0 * cubed


def split(value):
    high = value.astype(jnp.bfloat16)
    low = (value - high.astype(jnp.float32)).astype(jnp.bfloat16)
    return high, low


def dot(left, right):
    return jnp.dot(left, right, preferred_element_type=jnp.float32)


def stacked_dot(left, high, low):
    half = left.shape[0] // 2
    both = dot(left, high)
    return both[:half] + (both[half:] + dot(left[:half], low))


def lookup(table, place, lane):
    found = jnp.int32(-1)
    for z, entries in enumerate(table):
        for c, entry in enumerate(entries):
            found = jnp.where((place == z) & (lane == c), entry, found)
    return found


def store_piece(piece, plane, group, table_ref, high, low, own=None):
    slab, width, edge, _ = piece.shape
    act = 2 * width

    @pl.when(plane >= 0)
    def _():
        for r in range(slab):
            row = plane * slab + r
            for w in range(width):
                slot = group * width + w
                col = pl.ds(pl.multiple_of(table_ref[row, slot] * edge, edge), edge)
                block = jnp.where(table_ref[row, act + slot] > 0, piece[r, w], 0.0)
                block_high, block_low = split(block)
                at = pl.ds(pl.multiple_of(row * edge, edge), edge)
                high[at, col] = block_high
                low[at, col] = block_low
                if own is not None:
                    own[pl.ds(r * edge, edge), col] = block_high
                    own[pl.ds((slab + r) * edge, edge), col] = block_low


def early_kernel(
    tables, table_ref, place_ref, own_ref, own_swap, r1, r2, t1, t2, high, low, left, part_ref
):
    place, lane = place_ref[0], place_ref[1]
    near = tables[0]
    store_piece(own_ref, place, lane, table_ref, high, low, left)
    store_piece(own_swap, place, 1 - lane, table_ref, high, low, left)
    here, there = lookup(near, place, lane), lookup(near, place, 1 - lane)
    store_piece(r1, here, lane, table_ref, high, low)
    store_piece(r2, here, 1 - lane, table_ref, high, low)
    store_piece(t1, there, 1 - lane, table_ref, high, low)
    store_piece(t2, there, lane, table_ref, high, low)
    order = high.shape[0]
    depth, tile = order // 2, 256
    rows = pl.ds(pl.multiple_of(place // 2 * depth, depth), depth)
    for n in range(order // tile):
        cols = pl.ds(n * tile, tile)
        part_ref[:, cols] = stacked_dot(left[:, rows], high[rows, cols], low[rows, cols])


def late_kernel(
    tables, table_ref, place_ref, r3, r4, t3, t4, high_in, low_in, left, part_ref,
    out_ref, high, low, square, square_parts, cube,
):
    place, lane, group = place_ref[0], place_ref[1], place_ref[2]
    far = tables[1]
    here, there = lookup(far, place, lane), lookup(far, place, 1 - lane)
    store_piece(r3, here, lane, table_ref, high, low)
    store_piece(r4, here, 1 - lane, table_ref, high, low)
    store_piece(t3, there, 1 - lane, table_ref, high, low)
    store_piece(t4, there, lane, table_ref, high, low)
    order = high.shape[0]
    depth, tile = order // 2, 256
    slab, width, edge, _ = out_ref.shape
    act = 2 * width
    rows = pl.ds(pl.multiple_of((1 - place // 2) * depth, depth), depth)
    for n in range(order // tile):
        cols = pl.ds(n * tile, tile)
        square[:, cols] = part_ref[:, cols] + stacked_dot(
            left[:, rows], high[rows, cols], low[rows, cols]
        )
        for r in range(slab):
            for c in range(n * tile // edge, (n + 1) * tile // edge):
                kept = table_ref[place * slab + r, 2 * act + c] > 0
                col = pl.ds(c * edge, edge)
                block = jnp.where(kept, square[pl.ds(r * edge, edge), col], 0.0)
                block_high, block_low = split(block)
                square_parts[pl.ds(r * edge, edge), col] = block_high
                square_parts[pl.ds((slab + r) * edge, edge), col] = block_low
    for n in range(order // tile):
        cols = pl.ds(n * tile, tile)
        cube[:, cols] = stacked_dot(square_parts[...], high[:, cols], low[:, cols])
    for r in range(slab):
        for w in range(width):
            slot = jnp.minimum(group * width + w, act - 1)
            row = place * slab + r
            there = (group * width + w < act) & (table_ref[row, act + slot] > 0)
            at = (
                pl.ds(r * edge, edge),
                pl.ds(pl.multiple_of(table_ref[row, slot] * edge, edge), edge),
            )
            out_ref[r, w] = jnp.where(there, 3.0 * square[at] - 2.0 * cube[at], 0.0)


def slot_table(columns, act):
    rows = columns.shape[0]
    slots = columns[:, :act]
    here = slots < rows
    ids = jnp.arange(rows, dtype=jnp.int32)
    taken = jnp.any(slots[:, :, None] == ids, axis=1)
    count = jnp.sum(here.astype(jnp.int32), axis=1, keepdims=True)
    before = jnp.sum(
        (~taken[:, None, :] & (ids[None, :] < ids[:, None])[None]).astype(jnp.int32), axis=2
    )
    at = jnp.where(taken, -1, count + before)
    filled = jnp.sum(
        jnp.where(at[:, None, :] == jnp.arange(act, dtype=jnp.int32)[None, :, None], ids, 0), axis=2
    )
    order = jnp.where(here, slots, filled)
    return jnp.concatenate([order, here.astype(jnp.int32), taken.astype(jnp.int32)], axis=1)


def gather_local(x_blocks, columns):
    slab, width, edge, _ = x_blocks.shape
    rows = columns.shape[0]
    chains, panels, lanes = (lax.axis_size(axis) for axis in AXES)
    last = chains - 1

    def index(z, x, c):
        return (z * panels + x) * lanes + c

    def move(block, pairs):
        return lax.ppermute(block, AXES, [(index(*a), index(*b)) for a, b in pairs])

    def swap(block):
        return move(
            block, [((z, 0, c), (z, 0, 1 - c)) for z in range(chains) for c in range(lanes)]
        )

    first = [((z, 0, 0), (z + 1, 0, 0)) for z in range(last)]
    first += [((z, 0, 1), (z - 1, 0, 1)) for z in range(1, chains)]
    first += [((last, 0, 0), (last, 1, 0)), ((0, 0, 1), (0, 1, 1))]
    second = [((z, 0, 0), (z + 1, 0, 0)) for z in range(1, last)]
    second += [((z, 0, 1), (z - 1, 0, 1)) for z in range(1, last)]
    second += [((last, 1, 0), (0, 0, 0)), ((0, 1, 1), (last, 0, 1))]
    near = [(z - 1, z + 1 if z < last else -1) for z in range(chains)]
    far = [(z - 2 if z >= 2 else -1, z + 2 if z + 2 < chains else -1) for z in range(chains)]
    far[0] = (last, far[0][1])
    far[last] = (far[last][0], 0)
    tables = (near, far)

    r1 = move(x_blocks, first)
    own_swap = swap(x_blocks)
    r2 = move(own_swap, first)
    r3 = move(r1, second)
    t1 = swap(r1)
    r4 = move(r2, second)
    t2 = swap(r2)
    table = slot_table(columns, lanes * width)
    place = jnp.stack(
        [
            lax.axis_index("blk"),
            lax.axis_index("depth"),
            lax.axis_index("panel") * lanes + lax.axis_index("depth"),
        ]
    ).astype(jnp.int32)
    order, own = rows * edge, slab * edge
    smem = pl.BlockSpec(memory_space=pltpu.SMEM)
    vmem = pl.BlockSpec(memory_space=pltpu.VMEM)
    params = pltpu.CompilerParams(vmem_limit_bytes=24 * 2**20)
    high, low, left, part = pl.pallas_call(
        functools.partial(early_kernel, tables),
        out_shape=[
            jax.ShapeDtypeStruct((order, order), jnp.bfloat16),
            jax.ShapeDtypeStruct((order, order), jnp.bfloat16),
            jax.ShapeDtypeStruct((2 * own, order), jnp.bfloat16),
            jax.ShapeDtypeStruct((own, order), jnp.float32),
        ],
        in_specs=[smem] * 2 + [vmem] * 6,
        out_specs=[vmem] * 4,
        compiler_params=params,
        name="early",
    )(table, place, x_blocks, own_swap, r1, r2, t1, t2)
    r3, part = lax.optimization_barrier((r3, part))
    t3 = swap(r3)
    r4, t3 = lax.optimization_barrier((r4, t3))
    t4 = swap(r4)
    out, _, _ = pl.pallas_call(
        functools.partial(late_kernel, tables),
        out_shape=[
            jax.ShapeDtypeStruct(x_blocks.shape, jnp.float32),
            jax.ShapeDtypeStruct((order, order), jnp.bfloat16),
            jax.ShapeDtypeStruct((order, order), jnp.bfloat16),
        ],
        in_specs=[smem] * 2 + [vmem] * 8,
        out_specs=[vmem] * 3,
        input_output_aliases={6: 1, 7: 2},
        scratch_shapes=[
            pltpu.VMEM((own, order), jnp.float32),
            pltpu.VMEM((2 * own, order), jnp.bfloat16),
            pltpu.VMEM((own, order), jnp.float32),
        ],
        compiler_params=params,
        name="late",
    )(table, place, r3, r4, t3, t4, high, low, left, part)
    return out


def local(x_blocks, columns):
    slab, width, edge, _ = x_blocks.shape
    rows, slots = columns.shape
    chains, panels, lanes = (lax.axis_size(axis) for axis in AXES)
    full = rows <= slots and rows == lanes * width
    if full and rows <= 8 and edge % 128 == 0 and panels >= 2 and lanes == 2 and chains == 4:
        return gather_local(x_blocks, columns)
    return ring_local(x_blocks, columns)


def solution(mesh):
    placed = (P(("groups", "blk"), ("panel", "depth"), None, None), P("groups", None))
    return jax.shard_map(
        local,
        mesh=mesh,
        in_specs=placed,
        out_specs=P(("groups", "blk"), ("panel", "depth"), None, None),
        check_vma=False,
    )
```

```python
import functools

import jax
import jax.numpy as jnp
from jax import lax
from jax.experimental import pallas as pl
from jax.experimental.pallas import tpu as pltpu
from jax.sharding import PartitionSpec as P

precise = lax.Precision.HIGHEST
AXES = ("blk", "panel", "depth")


def shifted(block, axis, distance):
    devices = range(lax.axis_size(axis))
    route = [((i - distance) % len(devices), i) for i in devices]
    return lax.ppermute(block, axis, route)


def slot_gather(blocks):
    return lax.all_gather(blocks, ("panel", "depth"), axis=1, tiled=True)


def slot_reduce(partial_value):
    return lax.psum_scatter(partial_value, ("panel", "depth"), scatter_dimension=1, tiled=True)


def rotate_one(incoming):
    return shifted(incoming, "blk", 1)


def ring_local(x_blocks, columns):
    slab_rows = x_blocks.shape[0]
    width_slots = x_blocks.shape[1]
    edge = x_blocks.shape[2]
    order_rows = columns.shape[0]
    all_slots = columns.shape[1]
    cycle_size = lax.axis_size("blk")
    cycle_place = lax.axis_index("blk")
    anchor = jnp.int32(0)
    first_own = cycle_place * slab_rows
    slot_first = lax.axis_index(("panel", "depth")) * width_slots
    my_cols = lax.dynamic_slice(columns, (first_own, anchor), (slab_rows, all_slots))
    own_cols = lax.dynamic_slice(my_cols, (anchor, slot_first), (slab_rows, width_slots))
    x_own = jnp.where((own_cols < order_rows)[:, :, None, None], x_blocks, jnp.float32(0.0))
    out_present = my_cols < order_rows
    empty = jnp.zeros((slab_rows, all_slots, edge, edge), jnp.float32)

    def contribute(partial_value, left_rows, incoming, source):
        group = incoming.shape[0]
        first_row = source * group
        their_cols = lax.dynamic_slice(columns, (first_row, slot_first), (group, width_slots))
        row_ids = first_row + jnp.arange(group, dtype=jnp.int32)
        selector = (my_cols[:, None, :] == row_ids[None, :, None]).astype(jnp.float32)
        picked = jnp.einsum("irs,isab->irab", selector, left_rows, precision=precise)
        products = jnp.einsum("irab,rubc->iruac", picked, incoming, precision=precise)
        targets = (their_cols[None, None, :, :] == my_cols[:, :, None, None]) & out_present[
            :, :, None, None
        ]
        placed = jnp.einsum(
            "isru,iruac->isac", targets.astype(jnp.float32), products, precision=precise
        )
        return partial_value + placed

    def one_way(left_rows, stored):

        def advance(offset, state):
            partial_value, incoming, stored = state
            source = (cycle_place - offset) % cycle_size
            partial_value = contribute(partial_value, left_rows, incoming, source)
            return (partial_value, rotate_one(incoming), stored)

        partial_value, incoming, stored = lax.fori_loop(
            0, cycle_size - 1, advance, (empty, x_own, stored)
        )
        source = (cycle_place + 1) % cycle_size
        return (contribute(partial_value, left_rows, incoming, source), stored)

    stored = jnp.zeros((1,), jnp.float32)
    left_first = slot_gather(x_own)
    partial_value, stored = one_way(left_first, stored)
    squared = slot_reduce(partial_value)
    left_second = slot_gather(squared)
    partial_value, stored = one_way(left_second, stored)
    cubed = slot_reduce(partial_value)
    return 3.0 * squared - 2.0 * cubed


def split(value):
    high = value.astype(jnp.bfloat16)
    low = (value - high.astype(jnp.float32)).astype(jnp.bfloat16)
    return high, low


def dot(left, right):
    return jnp.dot(left, right, preferred_element_type=jnp.float32)


def stacked_dot(left, high, low):
    half = left.shape[0] // 2
    both = dot(left, high)
    return both[:half] + (both[half:] + dot(left[:half], low))


def lookup(table, place, lane):
    found = jnp.int32(-1)
    for z, entries in enumerate(table):
        for c, entry in enumerate(entries):
            found = jnp.where((place == z) & (lane == c), entry, found)
    return found


def store_piece(piece, plane, group, table_ref, high, low, own=None):
    slab, width, edge, _ = piece.shape
    act = 2 * width

    @pl.when(plane >= 0)
    def _():
        for r in range(slab):
            row = plane * slab + r
            for w in range(width):
                slot = group * width + w
                col = pl.ds(pl.multiple_of(table_ref[row, slot] * edge, edge), edge)
                block = jnp.where(table_ref[row, act + slot] > 0, piece[r, w], 0.0)
                block_high, block_low = split(block)
                at = pl.ds(pl.multiple_of(row * edge, edge), edge)
                high[at, col] = block_high
                low[at, col] = block_low
                if own is not None:
                    own[pl.ds(r * edge, edge), col] = block_high
                    own[pl.ds((slab + r) * edge, edge), col] = block_low


def early_kernel(
    tables, table_ref, place_ref, own_ref, own_swap, r1, r2, t1, t2, high, low, left, part_ref
):
    place, lane = place_ref[0], place_ref[1]
    near = tables[0]
    store_piece(own_ref, place, lane, table_ref, high, low, left)
    store_piece(own_swap, place, 1 - lane, table_ref, high, low, left)
    here, there = lookup(near, place, lane), lookup(near, place, 1 - lane)
    store_piece(r1, here, lane, table_ref, high, low)
    store_piece(r2, here, 1 - lane, table_ref, high, low)
    store_piece(t1, there, 1 - lane, table_ref, high, low)
    store_piece(t2, there, lane, table_ref, high, low)
    order = high.shape[0]
    depth, tile = order // 2, 256
    rows = pl.ds(pl.multiple_of(place // 2 * depth, depth), depth)
    for n in range(order // tile):
        cols = pl.ds(n * tile, tile)
        part_ref[:, cols] = stacked_dot(left[:, rows], high[rows, cols], low[rows, cols])


def late_kernel(
    tables, table_ref, place_ref, r3, r4, t3, t4, high_in, low_in, left, part_ref,
    out_ref, high, low, square, square_parts, cube,
):
    place, lane, group = place_ref[0], place_ref[1], place_ref[2]
    far = tables[1]
    here, there = lookup(far, place, lane), lookup(far, place, 1 - lane)
    store_piece(r3, here, lane, table_ref, high, low)
    store_piece(r4, here, 1 - lane, table_ref, high, low)
    store_piece(t3, there, 1 - lane, table_ref, high, low)
    store_piece(t4, there, lane, table_ref, high, low)
    order = high.shape[0]
    depth, tile = order // 2, 256
    slab, width, edge, _ = out_ref.shape
    act = 2 * width
    rows = pl.ds(pl.multiple_of((1 - place // 2) * depth, depth), depth)
    for n in range(order // tile):
        cols = pl.ds(n * tile, tile)
        square[:, cols] = part_ref[:, cols] + stacked_dot(
            left[:, rows], high[rows, cols], low[rows, cols]
        )
        for r in range(slab):
            for c in range(n * tile // edge, (n + 1) * tile // edge):
                kept = table_ref[place * slab + r, 2 * act + c] > 0
                col = pl.ds(c * edge, edge)
                block = jnp.where(kept, square[pl.ds(r * edge, edge), col], 0.0)
                block_high, block_low = split(block)
                square_parts[pl.ds(r * edge, edge), col] = block_high
                square_parts[pl.ds((slab + r) * edge, edge), col] = block_low
    for n in range(order // tile):
        cols = pl.ds(n * tile, tile)
        cube[:, cols] = stacked_dot(square_parts[...], high[:, cols], low[:, cols])
    for r in range(slab):
        for w in range(width):
            slot = jnp.minimum(group * width + w, act - 1)
            row = place * slab + r
            there = (group * width + w < act) & (table_ref[row, act + slot] > 0)
            at = (
                pl.ds(r * edge, edge),
                pl.ds(pl.multiple_of(table_ref[row, slot] * edge, edge), edge),
            )
            out_ref[r, w] = jnp.where(there, 3.0 * square[at] - 2.0 * cube[at], 0.0)


def slot_table(columns, act):
    rows = columns.shape[0]
    slots = columns[:, :act]
    here = slots < rows
    ids = jnp.arange(rows, dtype=jnp.int32)
    taken = jnp.any(slots[:, :, None] == ids, axis=1)
    count = jnp.sum(here.astype(jnp.int32), axis=1, keepdims=True)
    before = jnp.sum(
        (~taken[:, None, :] & (ids[None, :] < ids[:, None])[None]).astype(jnp.int32), axis=2
    )
    at = jnp.where(taken, -1, count + before)
    filled = jnp.sum(
        jnp.where(at[:, None, :] == jnp.arange(act, dtype=jnp.int32)[None, :, None], ids, 0), axis=2
    )
    order = jnp.where(here, slots, filled)
    return jnp.concatenate([order, here.astype(jnp.int32), taken.astype(jnp.int32)], axis=1)


def gather_local(x_blocks, columns):
    slab, width, edge, _ = x_blocks.shape
    rows = columns.shape[0]
    chains, panels, lanes = (lax.axis_size(axis) for axis in AXES)
    last = chains - 1

    def index(z, x, c):
        return (z * panels + x) * lanes + c

    def move(block, pairs):
        return lax.ppermute(block, AXES, [(index(*a), index(*b)) for a, b in pairs])

    def swap(block):
        return move(
            block,
            [
                ((z, x, c), (z, x, 1 - c))
                for z in range(chains)
                for x in range(panels)
                for c in range(lanes)
            ],
        )

    cycles = [
        [(z, 0, 0) for z in range(chains)] + [(last, 1, 0)],
        [(z, 0, 1) for z in reversed(range(chains))] + [(0, 1, 1)],
    ]
    hop = [(cycle[i - 1], cycle[i]) for cycle in cycles for i in range(len(cycle))]
    busy = set(cycles[0] + cycles[1])
    hop += [
        ((z, x, c), (z, x, c))
        for z in range(chains)
        for x in range(panels)
        for c in range(lanes)
        if (z, x, c) not in busy
    ]
    near = [(z - 1, z + 1 if z < last else -1) for z in range(chains)]
    far = [(z - 2 if z >= 2 else -1, z + 2 if z + 2 < chains else -1) for z in range(chains)]
    far[0] = (last, far[0][1])
    far[last] = (far[last][0], 0)
    tables = (near, far)

    r1 = move(x_blocks, hop)
    own_swap = swap(x_blocks)
    r2 = move(own_swap, hop)
    r3 = move(r1, hop)
    t1 = swap(r1)
    r4 = move(r2, hop)
    t2 = swap(r2)
    table = slot_table(columns, lanes * width)
    place = jnp.stack(
        [
            lax.axis_index("blk"),
            lax.axis_index("depth"),
            lax.axis_index("panel") * lanes + lax.axis_index("depth"),
        ]
    ).astype(jnp.int32)
    order, own = rows * edge, slab * edge
    smem = pl.BlockSpec(memory_space=pltpu.SMEM)
    vmem = pl.BlockSpec(memory_space=pltpu.VMEM)
    params = pltpu.CompilerParams(vmem_limit_bytes=24 * 2**20)
    high, low, left, part = pl.pallas_call(
        functools.partial(early_kernel, tables),
        out_shape=[
            jax.ShapeDtypeStruct((order, order), jnp.bfloat16),
            jax.ShapeDtypeStruct((order, order), jnp.bfloat16),
            jax.ShapeDtypeStruct((2 * own, order), jnp.bfloat16),
            jax.ShapeDtypeStruct((own, order), jnp.float32),
        ],
        in_specs=[smem] * 2 + [vmem] * 6,
        out_specs=[vmem] * 4,
        compiler_params=params,
        name="early",
    )(table, place, x_blocks, own_swap, r1, r2, t1, t2)
    r3, part = lax.optimization_barrier((r3, part))
    t3 = swap(r3)
    r4, t3 = lax.optimization_barrier((r4, t3))
    t4 = swap(r4)
    out, _, _ = pl.pallas_call(
        functools.partial(late_kernel, tables),
        out_shape=[
            jax.ShapeDtypeStruct(x_blocks.shape, jnp.float32),
            jax.ShapeDtypeStruct((order, order), jnp.bfloat16),
            jax.ShapeDtypeStruct((order, order), jnp.bfloat16),
        ],
        in_specs=[smem] * 2 + [vmem] * 8,
        out_specs=[vmem] * 3,
        input_output_aliases={6: 1, 7: 2},
        scratch_shapes=[
            pltpu.VMEM((own, order), jnp.float32),
            pltpu.VMEM((2 * own, order), jnp.bfloat16),
            pltpu.VMEM((own, order), jnp.float32),
        ],
        compiler_params=params,
        name="late",
    )(table, place, r3, r4, t3, t4, high, low, left, part)
    return out


def local(x_blocks, columns):
    slab, width, edge, _ = x_blocks.shape
    rows, slots = columns.shape
    chains, panels, lanes = (lax.axis_size(axis) for axis in AXES)
    full = rows <= slots and rows == lanes * width
    if full and rows <= 8 and edge % 128 == 0 and panels >= 2 and lanes == 2 and chains == 4:
        return gather_local(x_blocks, columns)
    return ring_local(x_blocks, columns)


def solution(mesh):
    placed = (P(("groups", "blk"), ("panel", "depth"), None, None), P("groups", None))
    return jax.shard_map(
        local,
        mesh=mesh,
        in_specs=placed,
        out_specs=P(("groups", "blk"), ("panel", "depth"), None, None),
        check_vma=False,
    )
```

```python
import functools

import jax
import jax.numpy as jnp
from jax import lax
from jax.experimental import pallas as pl
from jax.experimental.pallas import tpu as pltpu
from jax.sharding import PartitionSpec as P

precise = lax.Precision.HIGHEST
AXES = ("groups", "blk", "panel", "depth")


def shifted(block, axis, distance):
    devices = range(lax.axis_size(axis))
    route = [((i - distance) % len(devices), i) for i in devices]
    return lax.ppermute(block, axis, route)


def slot_gather(blocks):
    return lax.all_gather(blocks, ("panel", "depth"), axis=1, tiled=True)


def slot_reduce(partial_value):
    return lax.psum_scatter(partial_value, ("panel", "depth"), scatter_dimension=1, tiled=True)


def rotate_one(incoming):
    return shifted(incoming, "blk", 1)


def ring_local(x_blocks, columns):
    slab_rows = x_blocks.shape[0]
    width_slots = x_blocks.shape[1]
    edge = x_blocks.shape[2]
    order_rows = columns.shape[0]
    all_slots = columns.shape[1]
    cycle_size = lax.axis_size("blk")
    cycle_place = lax.axis_index("blk")
    anchor = jnp.int32(0)
    first_own = cycle_place * slab_rows
    slot_first = lax.axis_index(("panel", "depth")) * width_slots
    my_cols = lax.dynamic_slice(columns, (first_own, anchor), (slab_rows, all_slots))
    own_cols = lax.dynamic_slice(my_cols, (anchor, slot_first), (slab_rows, width_slots))
    x_own = jnp.where((own_cols < order_rows)[:, :, None, None], x_blocks, jnp.float32(0.0))
    out_present = my_cols < order_rows
    empty = jnp.zeros((slab_rows, all_slots, edge, edge), jnp.float32)

    def contribute(partial_value, left_rows, incoming, source):
        group = incoming.shape[0]
        first_row = source * group
        their_cols = lax.dynamic_slice(columns, (first_row, slot_first), (group, width_slots))
        row_ids = first_row + jnp.arange(group, dtype=jnp.int32)
        selector = (my_cols[:, None, :] == row_ids[None, :, None]).astype(jnp.float32)
        picked = jnp.einsum("irs,isab->irab", selector, left_rows, precision=precise)
        products = jnp.einsum("irab,rubc->iruac", picked, incoming, precision=precise)
        targets = (their_cols[None, None, :, :] == my_cols[:, :, None, None]) & out_present[
            :, :, None, None
        ]
        placed = jnp.einsum(
            "isru,iruac->isac", targets.astype(jnp.float32), products, precision=precise
        )
        return partial_value + placed

    def one_way(left_rows, stored):

        def advance(offset, state):
            partial_value, incoming, stored = state
            source = (cycle_place - offset) % cycle_size
            partial_value = contribute(partial_value, left_rows, incoming, source)
            return (partial_value, rotate_one(incoming), stored)

        partial_value, incoming, stored = lax.fori_loop(
            0, cycle_size - 1, advance, (empty, x_own, stored)
        )
        source = (cycle_place + 1) % cycle_size
        return (contribute(partial_value, left_rows, incoming, source), stored)

    stored = jnp.zeros((1,), jnp.float32)
    left_first = slot_gather(x_own)
    partial_value, stored = one_way(left_first, stored)
    squared = slot_reduce(partial_value)
    left_second = slot_gather(squared)
    partial_value, stored = one_way(left_second, stored)
    cubed = slot_reduce(partial_value)
    return 3.0 * squared - 2.0 * cubed


def split(value):
    high = value.astype(jnp.bfloat16)
    low = (value - high.astype(jnp.float32)).astype(jnp.bfloat16)
    return high, low


def dot(left, right):
    return jnp.dot(left, right, preferred_element_type=jnp.float32)


def stacked_dot(left, high, low):
    half = left.shape[0] // 2
    both = dot(left, high)
    return both[:half] + (both[half:] + dot(left[:half], low))


def lookup(table, place, lane):
    found = jnp.int32(-1)
    for z, entries in enumerate(table):
        for c, entry in enumerate(entries):
            found = jnp.where((place == z) & (lane == c), entry, found)
    return found


def store_piece(piece, plane, group, table_ref, high, low, own=None):
    slab, width, edge, _ = piece.shape
    act = 2 * width

    @pl.when(plane >= 0)
    def _():
        for r in range(slab):
            row = plane * slab + r
            for w in range(width):
                slot = group * width + w
                col = pl.ds(pl.multiple_of(table_ref[row, slot] * edge, edge), edge)
                block = jnp.where(table_ref[row, act + slot] > 0, piece[r, w], 0.0)
                block_high, block_low = split(block)
                at = pl.ds(pl.multiple_of(row * edge, edge), edge)
                high[at, col] = block_high
                low[at, col] = block_low
                if own is not None:
                    own[pl.ds(r * edge, edge), col] = block_high
                    own[pl.ds((slab + r) * edge, edge), col] = block_low


def early_kernel(
    tables, table_ref, place_ref, own_ref, own_swap, r1, r2, t1, t2, high, low, left, part_ref
):
    place, lane = place_ref[0], place_ref[1]
    near = tables[0]
    store_piece(own_ref, place, lane, table_ref, high, low, left)
    store_piece(own_swap, place, 1 - lane, table_ref, high, low, left)
    here, there = lookup(near, place, lane), lookup(near, place, 1 - lane)
    store_piece(r1, here, lane, table_ref, high, low)
    store_piece(r2, here, 1 - lane, table_ref, high, low)
    store_piece(t1, there, 1 - lane, table_ref, high, low)
    store_piece(t2, there, lane, table_ref, high, low)
    order = high.shape[0]
    depth, tile = order // 2, 256
    rows = pl.ds(pl.multiple_of(place // 2 * depth, depth), depth)
    for n in range(order // tile):
        cols = pl.ds(n * tile, tile)
        part_ref[:, cols] = stacked_dot(left[:, rows], high[rows, cols], low[rows, cols])


def late_kernel(
    tables, table_ref, place_ref, r3, r4, t3, t4, high_in, low_in, left, part_ref,
    out_ref, high, low, square, square_parts, cube,
):
    place, lane, group = place_ref[0], place_ref[1], place_ref[2]
    far = tables[1]
    here, there = lookup(far, place, lane), lookup(far, place, 1 - lane)
    store_piece(r3, here, lane, table_ref, high, low)
    store_piece(r4, here, 1 - lane, table_ref, high, low)
    store_piece(t3, there, 1 - lane, table_ref, high, low)
    store_piece(t4, there, lane, table_ref, high, low)
    order = high.shape[0]
    depth, tile = order // 2, 256
    slab, width, edge, _ = out_ref.shape
    act = 2 * width
    rows = pl.ds(pl.multiple_of((1 - place // 2) * depth, depth), depth)
    for n in range(order // tile):
        cols = pl.ds(n * tile, tile)
        square[:, cols] = part_ref[:, cols] + stacked_dot(
            left[:, rows], high[rows, cols], low[rows, cols]
        )
        for r in range(slab):
            for c in range(n * tile // edge, (n + 1) * tile // edge):
                kept = table_ref[place * slab + r, 2 * act + c] > 0
                col = pl.ds(c * edge, edge)
                block = jnp.where(kept, square[pl.ds(r * edge, edge), col], 0.0)
                block_high, block_low = split(block)
                square_parts[pl.ds(r * edge, edge), col] = block_high
                square_parts[pl.ds((slab + r) * edge, edge), col] = block_low
    for n in range(order // tile):
        cols = pl.ds(n * tile, tile)
        cube[:, cols] = stacked_dot(square_parts[...], high[:, cols], low[:, cols])
    for r in range(slab):
        for w in range(width):
            slot = jnp.minimum(group * width + w, act - 1)
            row = place * slab + r
            there = (group * width + w < act) & (table_ref[row, act + slot] > 0)
            at = (
                pl.ds(r * edge, edge),
                pl.ds(pl.multiple_of(table_ref[row, slot] * edge, edge), edge),
            )
            out_ref[r, w] = jnp.where(there, 3.0 * square[at] - 2.0 * cube[at], 0.0)


def slot_table(columns, act):
    rows = columns.shape[0]
    slots = columns[:, :act]
    here = slots < rows
    ids = jnp.arange(rows, dtype=jnp.int32)
    taken = jnp.any(slots[:, :, None] == ids, axis=1)
    count = jnp.sum(here.astype(jnp.int32), axis=1, keepdims=True)
    before = jnp.sum(
        (~taken[:, None, :] & (ids[None, :] < ids[:, None])[None]).astype(jnp.int32), axis=2
    )
    at = jnp.where(taken, -1, count + before)
    filled = jnp.sum(
        jnp.where(at[:, None, :] == jnp.arange(act, dtype=jnp.int32)[None, :, None], ids, 0), axis=2
    )
    order = jnp.where(here, slots, filled)
    return jnp.concatenate([order, here.astype(jnp.int32), taken.astype(jnp.int32)], axis=1)


def gather_local(x_blocks, columns):
    slab, width, edge, _ = x_blocks.shape
    rows = columns.shape[0]
    groups, chains, panels, lanes = (lax.axis_size(axis) for axis in AXES)
    last = chains - 1

    def index(g, place):
        z, x, c = place
        return (((g % groups) * chains + z) * panels + x) * lanes + c

    def move(block, pairs, idle=()):
        route = [(index(g, a), index(g, b)) for g in range(groups) for a, b in pairs]
        route += [(index(g, a), index(g + 1, a)) for g in range(groups) for a in idle]
        return lax.ppermute(block, AXES, route)

    def swap(block):
        return move(
            block,
            [
                ((z, x, c), (z, x, 1 - c))
                for z in range(chains)
                for x in range(panels)
                for c in range(lanes)
            ],
        )

    cycles = [
        [(z, 0, 0) for z in range(chains)] + [(last, 1, 0)],
        [(z, 0, 1) for z in reversed(range(chains))] + [(0, 1, 1)],
    ]
    hop = [(cycle[i - 1], cycle[i]) for cycle in cycles for i in range(len(cycle))]
    busy = set(cycles[0] + cycles[1])
    idle = [
        (z, x, c)
        for z in range(chains)
        for x in range(panels)
        for c in range(lanes)
        if (z, x, c) not in busy
    ]
    near = [(z - 1, z + 1 if z < last else -1) for z in range(chains)]
    far = [(z - 2 if z >= 2 else -1, z + 2 if z + 2 < chains else -1) for z in range(chains)]
    far[0] = (last, far[0][1])
    far[last] = (far[last][0], 0)
    tables = (near, far)

    r1 = move(x_blocks, hop, idle)
    own_swap = swap(x_blocks)
    r2 = move(own_swap, hop, idle)
    r3 = move(r1, hop, idle)
    t1 = swap(r1)
    r4 = move(r2, hop, idle)
    t2 = swap(r2)
    table = slot_table(columns, lanes * width)
    place = jnp.stack(
        [
            lax.axis_index("blk"),
            lax.axis_index("depth"),
            lax.axis_index("panel") * lanes + lax.axis_index("depth"),
        ]
    ).astype(jnp.int32)
    order, own = rows * edge, slab * edge
    smem = pl.BlockSpec(memory_space=pltpu.SMEM)
    vmem = pl.BlockSpec(memory_space=pltpu.VMEM)
    params = pltpu.CompilerParams(vmem_limit_bytes=24 * 2**20)
    high, low, left, part = pl.pallas_call(
        functools.partial(early_kernel, tables),
        out_shape=[
            jax.ShapeDtypeStruct((order, order), jnp.bfloat16),
            jax.ShapeDtypeStruct((order, order), jnp.bfloat16),
            jax.ShapeDtypeStruct((2 * own, order), jnp.bfloat16),
            jax.ShapeDtypeStruct((own, order), jnp.float32),
        ],
        in_specs=[smem] * 2 + [vmem] * 6,
        out_specs=[vmem] * 4,
        compiler_params=params,
        name="early",
    )(table, place, x_blocks, own_swap, r1, r2, t1, t2)
    r3, part = lax.optimization_barrier((r3, part))
    t3 = swap(r3)
    r4, t3 = lax.optimization_barrier((r4, t3))
    t4 = swap(r4)
    out, _, _ = pl.pallas_call(
        functools.partial(late_kernel, tables),
        out_shape=[
            jax.ShapeDtypeStruct(x_blocks.shape, jnp.float32),
            jax.ShapeDtypeStruct((order, order), jnp.bfloat16),
            jax.ShapeDtypeStruct((order, order), jnp.bfloat16),
        ],
        in_specs=[smem] * 2 + [vmem] * 8,
        out_specs=[vmem] * 3,
        input_output_aliases={6: 1, 7: 2},
        scratch_shapes=[
            pltpu.VMEM((own, order), jnp.float32),
            pltpu.VMEM((2 * own, order), jnp.bfloat16),
            pltpu.VMEM((own, order), jnp.float32),
        ],
        compiler_params=params,
        name="late",
    )(table, place, r3, r4, t3, t4, high, low, left, part)
    return out


def local(x_blocks, columns):
    slab, width, edge, _ = x_blocks.shape
    rows, slots = columns.shape
    _, chains, panels, lanes = (lax.axis_size(axis) for axis in AXES)
    full = rows <= slots and rows == lanes * width
    if full and rows <= 8 and edge % 128 == 0 and panels >= 2 and lanes == 2 and chains == 4:
        return gather_local(x_blocks, columns)
    return ring_local(x_blocks, columns)


def solution(mesh):
    placed = (P(("groups", "blk"), ("panel", "depth"), None, None), P("groups", None))
    return jax.shard_map(
        local,
        mesh=mesh,
        in_specs=placed,
        out_specs=P(("groups", "blk"), ("panel", "depth"), None, None),
        check_vma=False,
    )
```

```python
import functools

import jax
import jax.numpy as jnp
from jax import lax
from jax.experimental import pallas as pl
from jax.experimental.pallas import tpu as pltpu
from jax.sharding import PartitionSpec as P

precise = lax.Precision.HIGHEST
AXES = ("groups", "blk", "panel", "depth")


def shifted(block, axis, distance):
    devices = range(lax.axis_size(axis))
    route = [((i - distance) % len(devices), i) for i in devices]
    return lax.ppermute(block, axis, route)


def slot_gather(blocks):
    return lax.all_gather(blocks, ("panel", "depth"), axis=1, tiled=True)


def slot_reduce(partial_value):
    return lax.psum_scatter(partial_value, ("panel", "depth"), scatter_dimension=1, tiled=True)


def rotate_one(incoming):
    return shifted(incoming, "blk", 1)


def ring_local(x_blocks, columns):
    slab_rows = x_blocks.shape[0]
    width_slots = x_blocks.shape[1]
    edge = x_blocks.shape[2]
    order_rows = columns.shape[0]
    all_slots = columns.shape[1]
    cycle_size = lax.axis_size("blk")
    cycle_place = lax.axis_index("blk")
    anchor = jnp.int32(0)
    first_own = cycle_place * slab_rows
    slot_first = lax.axis_index(("panel", "depth")) * width_slots
    my_cols = lax.dynamic_slice(columns, (first_own, anchor), (slab_rows, all_slots))
    own_cols = lax.dynamic_slice(my_cols, (anchor, slot_first), (slab_rows, width_slots))
    x_own = jnp.where((own_cols < order_rows)[:, :, None, None], x_blocks, jnp.float32(0.0))
    out_present = my_cols < order_rows
    empty = jnp.zeros((slab_rows, all_slots, edge, edge), jnp.float32)

    def contribute(partial_value, left_rows, incoming, source):
        group = incoming.shape[0]
        first_row = source * group
        their_cols = lax.dynamic_slice(columns, (first_row, slot_first), (group, width_slots))
        row_ids = first_row + jnp.arange(group, dtype=jnp.int32)
        selector = (my_cols[:, None, :] == row_ids[None, :, None]).astype(jnp.float32)
        picked = jnp.einsum("irs,isab->irab", selector, left_rows, precision=precise)
        products = jnp.einsum("irab,rubc->iruac", picked, incoming, precision=precise)
        targets = (their_cols[None, None, :, :] == my_cols[:, :, None, None]) & out_present[
            :, :, None, None
        ]
        placed = jnp.einsum(
            "isru,iruac->isac", targets.astype(jnp.float32), products, precision=precise
        )
        return partial_value + placed

    def one_way(left_rows, stored):

        def advance(offset, state):
            partial_value, incoming, stored = state
            source = (cycle_place - offset) % cycle_size
            partial_value = contribute(partial_value, left_rows, incoming, source)
            return (partial_value, rotate_one(incoming), stored)

        partial_value, incoming, stored = lax.fori_loop(
            0, cycle_size - 1, advance, (empty, x_own, stored)
        )
        source = (cycle_place + 1) % cycle_size
        return (contribute(partial_value, left_rows, incoming, source), stored)

    stored = jnp.zeros((1,), jnp.float32)
    left_first = slot_gather(x_own)
    partial_value, stored = one_way(left_first, stored)
    squared = slot_reduce(partial_value)
    left_second = slot_gather(squared)
    partial_value, stored = one_way(left_second, stored)
    cubed = slot_reduce(partial_value)
    return 3.0 * squared - 2.0 * cubed


def split(value):
    high = value.astype(jnp.bfloat16)
    low = (value - high.astype(jnp.float32)).astype(jnp.bfloat16)
    return high, low


def dot(left, right):
    return jnp.dot(left, right, preferred_element_type=jnp.float32)


def stacked_dot(left, high, low):
    half = left.shape[0] // 2
    both = dot(left, high)
    return both[:half] + (both[half:] + dot(left[:half], low))


def lookup(table, place, lane):
    found = jnp.int32(-1)
    for z, entries in enumerate(table):
        for c, entry in enumerate(entries):
            found = jnp.where((place == z) & (lane == c), entry, found)
    return found


def store_piece(piece, plane, group, table_ref, high, low, own=None):
    slab, width, edge, _ = piece.shape
    act = 2 * width

    @pl.when(plane >= 0)
    def _():
        for r in range(slab):
            row = plane * slab + r
            for w in range(width):
                slot = group * width + w
                col = pl.ds(pl.multiple_of(table_ref[row, slot] * edge, edge), edge)
                block = jnp.where(table_ref[row, act + slot] > 0, piece[r, w], 0.0)
                block_high, block_low = split(block)
                at = pl.ds(pl.multiple_of(row * edge, edge), edge)
                high[at, col] = block_high
                low[at, col] = block_low
                if own is not None:
                    own[pl.ds(r * edge, edge), col] = block_high
                    own[pl.ds((slab + r) * edge, edge), col] = block_low


def early_kernel(
    tables, table_ref, place_ref, own_ref, own_swap, r1, r2, t1, t2, high, low, left, part_ref
):
    place, lane = place_ref[0], place_ref[1]
    near = tables[0]
    store_piece(own_ref, place, lane, table_ref, high, low, left)
    store_piece(own_swap, place, 1 - lane, table_ref, high, low, left)
    here, there = lookup(near, place, lane), lookup(near, place, 1 - lane)
    store_piece(r1, here, lane, table_ref, high, low)
    store_piece(r2, here, 1 - lane, table_ref, high, low)
    store_piece(t1, there, 1 - lane, table_ref, high, low)
    store_piece(t2, there, lane, table_ref, high, low)
    order = high.shape[0]
    depth, tile = order // 2, 256
    rows = pl.ds(pl.multiple_of(place // 2 * depth, depth), depth)
    for n in range(order // tile):
        cols = pl.ds(n * tile, tile)
        part_ref[:, cols] = stacked_dot(left[:, rows], high[rows, cols], low[rows, cols])


def late_kernel(
    tables, table_ref, place_ref, r3, r4, t3, t4, high_in, low_in, left, part_ref,
    out_ref, high, low, square, square_parts, cube,
):
    place, lane, group = place_ref[0], place_ref[1], place_ref[2]
    far = tables[1]
    here, there = lookup(far, place, lane), lookup(far, place, 1 - lane)
    store_piece(r3, here, lane, table_ref, high, low)
    store_piece(r4, here, 1 - lane, table_ref, high, low)
    store_piece(t3, there, 1 - lane, table_ref, high, low)
    store_piece(t4, there, lane, table_ref, high, low)
    order = high.shape[0]
    depth, tile = order // 2, 256
    slab, width, edge, _ = out_ref.shape
    act = 2 * width
    rows = pl.ds(pl.multiple_of((1 - place // 2) * depth, depth), depth)
    for n in range(order // tile):
        cols = pl.ds(n * tile, tile)
        square[:, cols] = part_ref[:, cols] + stacked_dot(
            left[:, rows], high[rows, cols], low[rows, cols]
        )
        for r in range(slab):
            for c in range(n * tile // edge, (n + 1) * tile // edge):
                kept = table_ref[place * slab + r, 2 * act + c] > 0
                col = pl.ds(c * edge, edge)
                block = jnp.where(kept, square[pl.ds(r * edge, edge), col], 0.0)
                block_high, block_low = split(block)
                square_parts[pl.ds(r * edge, edge), col] = block_high
                square_parts[pl.ds((slab + r) * edge, edge), col] = block_low
    for n in range(order // tile):
        cols = pl.ds(n * tile, tile)
        cube[:, cols] = stacked_dot(square_parts[...], high[:, cols], low[:, cols])
    for r in range(slab):
        for w in range(width):
            slot = jnp.minimum(group * width + w, act - 1)
            row = place * slab + r
            there = (group * width + w < act) & (table_ref[row, act + slot] > 0)
            at = (
                pl.ds(r * edge, edge),
                pl.ds(pl.multiple_of(table_ref[row, slot] * edge, edge), edge),
            )
            out_ref[r, w] = jnp.where(there, 3.0 * square[at] - 2.0 * cube[at], 0.0)


def slot_table(columns, act):
    rows = columns.shape[0]
    slots = columns[:, :act]
    here = slots < rows
    ids = jnp.arange(rows, dtype=jnp.int32)
    taken = jnp.any(slots[:, :, None] == ids, axis=1)
    count = jnp.sum(here.astype(jnp.int32), axis=1, keepdims=True)
    before = jnp.sum(
        (~taken[:, None, :] & (ids[None, :] < ids[:, None])[None]).astype(jnp.int32), axis=2
    )
    at = jnp.where(taken, -1, count + before)
    filled = jnp.sum(
        jnp.where(at[:, None, :] == jnp.arange(act, dtype=jnp.int32)[None, :, None], ids, 0), axis=2
    )
    order = jnp.where(here, slots, filled)
    return jnp.concatenate([order, here.astype(jnp.int32), taken.astype(jnp.int32)], axis=1)


def gather_local(x_blocks, columns):
    slab, width, edge, _ = x_blocks.shape
    rows = columns.shape[0]
    groups, chains, panels, lanes = (lax.axis_size(axis) for axis in AXES)
    last = chains - 1

    def index(g, place):
        z, x, c = place
        return (((g % groups) * chains + z) * panels + x) * lanes + c

    def move(block, cycles):
        pairs = [(cycle[i - 1], cycle[i]) for cycle in cycles for i in range(len(cycle))]
        busy = {a for a, _ in pairs}
        route = [(index(g, a), index(g, b)) for g in range(groups) for a, b in pairs]
        for z in range(chains):
            for x in range(panels):
                idle = [(z, x, c) for c in range(lanes) if (z, x, c) not in busy]
                for g in range(groups):
                    if len(idle) == lanes:
                        route += [(index(g, idle[c - 1]), index(g, idle[c])) for c in range(lanes)]
                    else:
                        route += [(index(g, a), index(g + 1, a)) for a in idle]
        return lax.ppermute(block, AXES, route)

    def swap(block):
        return move(block, [])

    up = [(z, 0, 0) for z in range(chains)] + [(last, 1, 0)]
    down = [(z, 0, 1) for z in reversed(range(chains))] + [(0, 1, 1)]
    first = [up + [(last, 1, 1)] + down + [(0, 1, 0)]]
    second = [up, down]
    near = [(z - 1, z + 1 if z < last else -1) for z in range(chains)]
    far = [(z - 2 if z >= 2 else -1, z + 2 if z + 2 < chains else -1) for z in range(chains)]
    far[0] = (last, far[0][1])
    far[last] = (far[last][0], 0)
    tables = (near, far)

    table = slot_table(columns, lanes * width)
    r1 = move(x_blocks, first)
    own_swap = swap(x_blocks)
    r2 = move(own_swap, first)
    r1, table = lax.optimization_barrier((r1, table))
    r3 = move(r1, second)
    t1 = swap(r1)
    r4 = move(r2, second)
    t2 = swap(r2)

    place = jnp.stack(
        [
            lax.axis_index("blk"),
            lax.axis_index("depth"),
            lax.axis_index("panel") * lanes + lax.axis_index("depth"),
        ]
    ).astype(jnp.int32)
    order, own = rows * edge, slab * edge
    smem = pl.BlockSpec(memory_space=pltpu.SMEM)
    vmem = pl.BlockSpec(memory_space=pltpu.VMEM)
    params = pltpu.CompilerParams(vmem_limit_bytes=24 * 2**20)
    high, low, left, part = pl.pallas_call(
        functools.partial(early_kernel, tables),
        out_shape=[
            jax.ShapeDtypeStruct((order, order), jnp.bfloat16),
            jax.ShapeDtypeStruct((order, order), jnp.bfloat16),
            jax.ShapeDtypeStruct((2 * own, order), jnp.bfloat16),
            jax.ShapeDtypeStruct((own, order), jnp.float32),
        ],
        in_specs=[smem] * 2 + [vmem] * 6,
        out_specs=[vmem] * 4,
        compiler_params=params,
        name="early",
    )(table, place, x_blocks, own_swap, r1, r2, t1, t2)
    r3, part = lax.optimization_barrier((r3, part))
    t3 = swap(r3)
    r4, t3 = lax.optimization_barrier((r4, t3))
    t4 = swap(r4)
    out, _, _ = pl.pallas_call(
        functools.partial(late_kernel, tables),
        out_shape=[
            jax.ShapeDtypeStruct(x_blocks.shape, jnp.float32),
            jax.ShapeDtypeStruct((order, order), jnp.bfloat16),
            jax.ShapeDtypeStruct((order, order), jnp.bfloat16),
        ],
        in_specs=[smem] * 2 + [vmem] * 8,
        out_specs=[vmem] * 3,
        input_output_aliases={6: 1, 7: 2},
        scratch_shapes=[
            pltpu.VMEM((own, order), jnp.float32),
            pltpu.VMEM((2 * own, order), jnp.bfloat16),
            pltpu.VMEM((own, order), jnp.float32),
        ],
        compiler_params=params,
        name="late",
    )(table, place, r3, r4, t3, t4, high, low, left, part)
    return out


def local(x_blocks, columns):
    slab, width, edge, _ = x_blocks.shape
    rows, slots = columns.shape
    _, chains, panels, lanes = (lax.axis_size(axis) for axis in AXES)
    full = rows <= slots and rows == lanes * width
    if full and rows <= 8 and edge % 128 == 0 and panels >= 2 and lanes == 2 and chains == 4:
        return gather_local(x_blocks, columns)
    return ring_local(x_blocks, columns)


def solution(mesh):
    placed = (P(("groups", "blk"), ("panel", "depth"), None, None), P("groups", None))
    return jax.shard_map(
        local,
        mesh=mesh,
        in_specs=placed,
        out_specs=P(("groups", "blk"), ("panel", "depth"), None, None),
        check_vma=False,
    )
```

```python
import functools

import jax
import jax.numpy as jnp
from jax import lax
from jax.experimental import pallas as pl
from jax.experimental.pallas import tpu as pltpu
from jax.sharding import PartitionSpec as P

precise = lax.Precision.HIGHEST
AXES = ("groups", "blk", "panel", "depth")


def shifted(block, axis, distance):
    devices = range(lax.axis_size(axis))
    route = [((i - distance) % len(devices), i) for i in devices]
    return lax.ppermute(block, axis, route)


def slot_gather(blocks):
    return lax.all_gather(blocks, ("panel", "depth"), axis=1, tiled=True)


def slot_reduce(partial_value):
    return lax.psum_scatter(partial_value, ("panel", "depth"), scatter_dimension=1, tiled=True)


def rotate_one(incoming):
    return shifted(incoming, "blk", 1)


def ring_local(x_blocks, columns):
    slab_rows = x_blocks.shape[0]
    width_slots = x_blocks.shape[1]
    edge = x_blocks.shape[2]
    order_rows = columns.shape[0]
    all_slots = columns.shape[1]
    cycle_size = lax.axis_size("blk")
    cycle_place = lax.axis_index("blk")
    anchor = jnp.int32(0)
    first_own = cycle_place * slab_rows
    slot_first = lax.axis_index(("panel", "depth")) * width_slots
    my_cols = lax.dynamic_slice(columns, (first_own, anchor), (slab_rows, all_slots))
    own_cols = lax.dynamic_slice(my_cols, (anchor, slot_first), (slab_rows, width_slots))
    x_own = jnp.where((own_cols < order_rows)[:, :, None, None], x_blocks, jnp.float32(0.0))
    out_present = my_cols < order_rows
    empty = jnp.zeros((slab_rows, all_slots, edge, edge), jnp.float32)

    def contribute(partial_value, left_rows, incoming, source):
        group = incoming.shape[0]
        first_row = source * group
        their_cols = lax.dynamic_slice(columns, (first_row, slot_first), (group, width_slots))
        row_ids = first_row + jnp.arange(group, dtype=jnp.int32)
        selector = (my_cols[:, None, :] == row_ids[None, :, None]).astype(jnp.float32)
        picked = jnp.einsum("irs,isab->irab", selector, left_rows, precision=precise)
        products = jnp.einsum("irab,rubc->iruac", picked, incoming, precision=precise)
        targets = (their_cols[None, None, :, :] == my_cols[:, :, None, None]) & out_present[
            :, :, None, None
        ]
        placed = jnp.einsum(
            "isru,iruac->isac", targets.astype(jnp.float32), products, precision=precise
        )
        return partial_value + placed

    def one_way(left_rows, stored):

        def advance(offset, state):
            partial_value, incoming, stored = state
            source = (cycle_place - offset) % cycle_size
            partial_value = contribute(partial_value, left_rows, incoming, source)
            return (partial_value, rotate_one(incoming), stored)

        partial_value, incoming, stored = lax.fori_loop(
            0, cycle_size - 1, advance, (empty, x_own, stored)
        )
        source = (cycle_place + 1) % cycle_size
        return (contribute(partial_value, left_rows, incoming, source), stored)

    stored = jnp.zeros((1,), jnp.float32)
    left_first = slot_gather(x_own)
    partial_value, stored = one_way(left_first, stored)
    squared = slot_reduce(partial_value)
    left_second = slot_gather(squared)
    partial_value, stored = one_way(left_second, stored)
    cubed = slot_reduce(partial_value)
    return 3.0 * squared - 2.0 * cubed


def split(value):
    high = value.astype(jnp.bfloat16)
    low = (value - high.astype(jnp.float32)).astype(jnp.bfloat16)
    return high, low


def dot(left, right):
    return jnp.dot(left, right, preferred_element_type=jnp.float32)


def stacked_dot(left, high, low):
    half = left.shape[0] // 2
    both = dot(left, high)
    return both[:half] + (both[half:] + dot(left[:half], low))


def lookup(table, place, lane):
    found = jnp.int32(-1)
    for z, entries in enumerate(table):
        for c, entry in enumerate(entries):
            found = jnp.where((place == z) & (lane == c), entry, found)
    return found


def store_piece(piece, plane, group, table_ref, high, low, own=None):
    slab, width, edge, _ = piece.shape
    act = 2 * width

    @pl.when(plane >= 0)
    def _():
        for r in range(slab):
            row = plane * slab + r
            for w in range(width):
                slot = group * width + w
                col = pl.ds(pl.multiple_of(table_ref[row, slot] * edge, edge), edge)
                block = jnp.where(table_ref[row, act + slot] > 0, piece[r, w], 0.0)
                block_high, block_low = split(block)
                at = pl.ds(pl.multiple_of(row * edge, edge), edge)
                high[at, col] = block_high
                low[at, col] = block_low
                if own is not None:
                    own[pl.ds(r * edge, edge), col] = block_high
                    own[pl.ds((slab + r) * edge, edge), col] = block_low


def early_kernel(
    tables, table_ref, place_ref, own_hbm, own_swap, r1, r2, t1, t2, r3,
    high, low, left, part_ref, own_ref, own_sem,
):
    place, lane = place_ref[0], place_ref[1]
    near, far = tables
    own_copy = pltpu.make_async_copy(own_hbm, own_ref, own_sem)
    own_copy.start()
    here, there = lookup(near, place, lane), lookup(near, place, 1 - lane)
    store_piece(own_swap, place, 1 - lane, table_ref, high, low, left)
    store_piece(r1, here, lane, table_ref, high, low)
    store_piece(r2, here, 1 - lane, table_ref, high, low)
    store_piece(t1, there, 1 - lane, table_ref, high, low)
    store_piece(t2, there, lane, table_ref, high, low)
    store_piece(r3, lookup(far, place, lane), lane, table_ref, high, low)
    own_copy.wait()
    store_piece(own_ref, place, lane, table_ref, high, low, left)
    order = high.shape[0]
    depth, tile = order // 2, 256
    rows = pl.ds(pl.multiple_of(place // 2 * depth, depth), depth)
    for n in range(order // tile):
        cols = pl.ds(n * tile, tile)
        part_ref[:, cols] = stacked_dot(left[:, rows], high[rows, cols], low[rows, cols])


def late_kernel(
    tables, table_ref, place_ref, r4, t3, t4, high_in, low_in, left, part_ref,
    out_ref, high, low, square, square_parts,
):
    place, lane, group = place_ref[0], place_ref[1], place_ref[2]
    far = tables[1]
    here, there = lookup(far, place, lane), lookup(far, place, 1 - lane)
    store_piece(t3, there, 1 - lane, table_ref, high, low)
    store_piece(r4, here, 1 - lane, table_ref, high, low)
    store_piece(t4, there, lane, table_ref, high, low)
    order = high.shape[0]
    depth, tile = order // 2, 256
    slab, width, edge, _ = out_ref.shape
    act = 2 * width
    rows = pl.ds(pl.multiple_of((1 - place // 2) * depth, depth), depth)
    for n in range(order // tile):
        cols = pl.ds(n * tile, tile)
        square[:, cols] = part_ref[:, cols] + stacked_dot(
            left[:, rows], high[rows, cols], low[rows, cols]
        )
        for r in range(slab):
            for c in range(n * tile // edge, (n + 1) * tile // edge):
                kept = table_ref[place * slab + r, 2 * act + c] > 0
                col = pl.ds(c * edge, edge)
                block = jnp.where(kept, square[pl.ds(r * edge, edge), col], 0.0)
                block_high, block_low = split(block)
                square_parts[pl.ds(2 * r * edge, edge), col] = block_high
                square_parts[pl.ds((2 * r + 1) * edge, edge), col] = block_low
    for r in range(slab):
        row = place * slab + r
        left_parts = square_parts[pl.ds(2 * r * edge, 2 * edge), :]
        for w in range(0, width, 2):
            slots = [jnp.minimum(group * width + w + k, act - 1) for k in range(2)]
            cols = [
                pl.ds(pl.multiple_of(table_ref[row, slot] * edge, edge), edge) for slot in slots
            ]
            cube = stacked_dot(
                left_parts,
                jnp.concatenate([high[:, col] for col in cols], axis=1),
                jnp.concatenate([low[:, col] for col in cols], axis=1),
            )
            for k in range(2):
                there = (group * width + w + k < act) & (table_ref[row, act + slots[k]] > 0)
                value = 3.0 * square[pl.ds(r * edge, edge), cols[k]]
                value = value - 2.0 * cube[:, k * edge : (k + 1) * edge]
                out_ref[r, w + k] = jnp.where(there, value, 0.0)


def slot_table(columns, act):
    rows = columns.shape[0]
    slots = columns[:, :act]
    here = slots < rows
    ids = jnp.arange(rows, dtype=jnp.int32)
    taken = jnp.any(slots[:, :, None] == ids, axis=1)
    count = jnp.sum(here.astype(jnp.int32), axis=1, keepdims=True)
    before = jnp.sum(
        (~taken[:, None, :] & (ids[None, :] < ids[:, None])[None]).astype(jnp.int32), axis=2
    )
    at = jnp.where(taken, -1, count + before)
    filled = jnp.sum(
        jnp.where(at[:, None, :] == jnp.arange(act, dtype=jnp.int32)[None, :, None], ids, 0), axis=2
    )
    order = jnp.where(here, slots, filled)
    return jnp.concatenate([order, here.astype(jnp.int32), taken.astype(jnp.int32)], axis=1)


def gather_local(x_blocks, columns):
    slab, width, edge, _ = x_blocks.shape
    rows = columns.shape[0]
    groups, chains, panels, lanes = (lax.axis_size(axis) for axis in AXES)
    last = chains - 1

    def index(g, place):
        z, x, c = place
        return (((g % groups) * chains + z) * panels + x) * lanes + c

    def move(block, cycles):
        pairs = [(cycle[i - 1], cycle[i]) for cycle in cycles for i in range(len(cycle))]
        busy = {a for a, _ in pairs}
        route = [(index(g, a), index(g, b)) for g in range(groups) for a, b in pairs]
        for z in range(chains):
            for x in range(panels):
                idle = [(z, x, c) for c in range(lanes) if (z, x, c) not in busy]
                for g in range(groups):
                    if len(idle) == lanes:
                        route += [(index(g, idle[c - 1]), index(g, idle[c])) for c in range(lanes)]
                    else:
                        route += [(index(g, a), index(g + 1, a)) for a in idle]
        return lax.ppermute(block, AXES, route)

    def swap(block):
        return move(block, [])

    up = [(z, 0, 0) for z in range(chains)] + [(last, 1, 0)]
    down = [(z, 0, 1) for z in reversed(range(chains))] + [(0, 1, 1)]
    first = [up + [(last, 1, 1)] + down + [(0, 1, 0)]]
    second = [up, down]
    near = [(z - 1, z + 1 if z < last else -1) for z in range(chains)]
    far = [(z - 2 if z >= 2 else -1, z + 2 if z + 2 < chains else -1) for z in range(chains)]
    far[0] = (last, far[0][1])
    far[last] = (far[last][0], 0)
    tables = (near, far)

    table = slot_table(columns, lanes * width)
    r1 = move(x_blocks, first)
    own_swap = swap(x_blocks)
    r2 = move(own_swap, first)
    r1, table = lax.optimization_barrier((r1, table))
    r3 = move(r1, second)
    t1 = swap(r1)
    r4 = move(r2, second)
    t2 = swap(r2)

    place = jnp.stack(
        [
            lax.axis_index("blk"),
            lax.axis_index("depth"),
            lax.axis_index("panel") * lanes + lax.axis_index("depth"),
        ]
    ).astype(jnp.int32)
    order, own = rows * edge, slab * edge
    smem = pl.BlockSpec(memory_space=pltpu.SMEM)
    vmem = pl.BlockSpec(memory_space=pltpu.VMEM)
    params = pltpu.CompilerParams(vmem_limit_bytes=24 * 2**20)
    high, low, left, part = pl.pallas_call(
        functools.partial(early_kernel, tables),
        out_shape=[
            jax.ShapeDtypeStruct((order, order), jnp.bfloat16),
            jax.ShapeDtypeStruct((order, order), jnp.bfloat16),
            jax.ShapeDtypeStruct((2 * own, order), jnp.bfloat16),
            jax.ShapeDtypeStruct((own, order), jnp.float32),
        ],
        in_specs=[smem] * 2 + [pl.BlockSpec(memory_space=pltpu.HBM)] + [vmem] * 6,
        out_specs=[vmem] * 4,
        scratch_shapes=[pltpu.VMEM(x_blocks.shape, jnp.float32), pltpu.SemaphoreType.DMA],
        compiler_params=params,
        name="early",
    )(table, place, x_blocks, own_swap, r1, r2, t1, t2, r3)
    t3 = swap(r3)
    r4, part = lax.optimization_barrier((r4, part))
    t4 = swap(r4)
    out, _, _ = pl.pallas_call(
        functools.partial(late_kernel, tables),
        out_shape=[
            jax.ShapeDtypeStruct(x_blocks.shape, jnp.float32),
            jax.ShapeDtypeStruct((order, order), jnp.bfloat16),
            jax.ShapeDtypeStruct((order, order), jnp.bfloat16),
        ],
        in_specs=[smem] * 2 + [vmem] * 7,
        out_specs=[vmem] * 3,
        input_output_aliases={5: 1, 6: 2},
        scratch_shapes=[
            pltpu.VMEM((own, order), jnp.float32),
            pltpu.VMEM((2 * own, order), jnp.bfloat16),
        ],
        compiler_params=params,
        name="late",
    )(table, place, r4, t3, t4, high, low, left, part)
    return out


def local(x_blocks, columns):
    slab, width, edge, _ = x_blocks.shape
    rows, slots = columns.shape
    _, chains, panels, lanes = (lax.axis_size(axis) for axis in AXES)
    full = rows <= slots and rows == lanes * width and width % 2 == 0
    if full and rows <= 8 and edge % 128 == 0 and panels >= 2 and lanes == 2 and chains == 4:
        return gather_local(x_blocks, columns)
    return ring_local(x_blocks, columns)


def solution(mesh):
    placed = (P(("groups", "blk"), ("panel", "depth"), None, None), P("groups", None))
    return jax.shard_map(
        local,
        mesh=mesh,
        in_specs=placed,
        out_specs=P(("groups", "blk"), ("panel", "depth"), None, None),
        check_vma=False,
    )
```

```python
import functools

import jax
import jax.numpy as jnp
from jax import lax
from jax.experimental import pallas as pl
from jax.experimental.pallas import tpu as pltpu
from jax.sharding import PartitionSpec as P

precise = lax.Precision.HIGHEST
AXES = ("groups", "blk", "panel", "depth")


def shifted(block, axis, distance):
    devices = range(lax.axis_size(axis))
    route = [((i - distance) % len(devices), i) for i in devices]
    return lax.ppermute(block, axis, route)


def slot_gather(blocks):
    return lax.all_gather(blocks, ("panel", "depth"), axis=1, tiled=True)


def slot_reduce(partial_value):
    return lax.psum_scatter(partial_value, ("panel", "depth"), scatter_dimension=1, tiled=True)


def rotate_one(incoming):
    return shifted(incoming, "blk", 1)


def ring_local(x_blocks, columns):
    slab_rows = x_blocks.shape[0]
    width_slots = x_blocks.shape[1]
    edge = x_blocks.shape[2]
    order_rows = columns.shape[0]
    all_slots = columns.shape[1]
    cycle_size = lax.axis_size("blk")
    cycle_place = lax.axis_index("blk")
    anchor = jnp.int32(0)
    first_own = cycle_place * slab_rows
    slot_first = lax.axis_index(("panel", "depth")) * width_slots
    my_cols = lax.dynamic_slice(columns, (first_own, anchor), (slab_rows, all_slots))
    own_cols = lax.dynamic_slice(my_cols, (anchor, slot_first), (slab_rows, width_slots))
    x_own = jnp.where((own_cols < order_rows)[:, :, None, None], x_blocks, jnp.float32(0.0))
    out_present = my_cols < order_rows
    empty = jnp.zeros((slab_rows, all_slots, edge, edge), jnp.float32)

    def contribute(partial_value, left_rows, incoming, source):
        group = incoming.shape[0]
        first_row = source * group
        their_cols = lax.dynamic_slice(columns, (first_row, slot_first), (group, width_slots))
        row_ids = first_row + jnp.arange(group, dtype=jnp.int32)
        selector = (my_cols[:, None, :] == row_ids[None, :, None]).astype(jnp.float32)
        picked = jnp.einsum("irs,isab->irab", selector, left_rows, precision=precise)
        products = jnp.einsum("irab,rubc->iruac", picked, incoming, precision=precise)
        targets = (their_cols[None, None, :, :] == my_cols[:, :, None, None]) & out_present[
            :, :, None, None
        ]
        placed = jnp.einsum(
            "isru,iruac->isac", targets.astype(jnp.float32), products, precision=precise
        )
        return partial_value + placed

    def one_way(left_rows, stored):

        def advance(offset, state):
            partial_value, incoming, stored = state
            source = (cycle_place - offset) % cycle_size
            partial_value = contribute(partial_value, left_rows, incoming, source)
            return (partial_value, rotate_one(incoming), stored)

        partial_value, incoming, stored = lax.fori_loop(
            0, cycle_size - 1, advance, (empty, x_own, stored)
        )
        source = (cycle_place + 1) % cycle_size
        return (contribute(partial_value, left_rows, incoming, source), stored)

    stored = jnp.zeros((1,), jnp.float32)
    left_first = slot_gather(x_own)
    partial_value, stored = one_way(left_first, stored)
    squared = slot_reduce(partial_value)
    left_second = slot_gather(squared)
    partial_value, stored = one_way(left_second, stored)
    cubed = slot_reduce(partial_value)
    return 3.0 * squared - 2.0 * cubed


def split(value):
    high = value.astype(jnp.bfloat16)
    low = (value - high.astype(jnp.float32)).astype(jnp.bfloat16)
    return high, low


def dot(left, right):
    return jnp.dot(left, right, preferred_element_type=jnp.float32)


def stacked_dot(left, high, low):
    half = left.shape[0] // 2
    both = dot(left, high)
    return both[:half] + (both[half:] + dot(left[:half], low))


def lookup(table, place, lane):
    found = jnp.int32(-1)
    for z, entries in enumerate(table):
        for c, entry in enumerate(entries):
            found = jnp.where((place == z) & (lane == c), entry, found)
    return found


def store_piece(piece, plane, group, table_ref, high, low, own=None):
    slab, width, edge, _ = piece.shape
    act = 2 * width

    @pl.when(plane >= 0)
    def _():
        for r in range(slab):
            row = plane * slab + r
            for w in range(width):
                slot = group * width + w
                col = pl.ds(pl.multiple_of(table_ref[row, slot] * edge, edge), edge)
                block = jnp.where(table_ref[row, act + slot] > 0, piece[r, w], 0.0)
                block_high, block_low = split(block)
                at = pl.ds(pl.multiple_of(row * edge, edge), edge)
                high[at, col] = block_high
                low[at, col] = block_low
                if own is not None:
                    own[pl.ds(r * edge, edge), col] = block_high
                    own[pl.ds((slab + r) * edge, edge), col] = block_low


def early_kernel(
    tables, table_ref, place_ref, own_hbm, own_swap, r1, r2, t1, t2, r3,
    high, low, left, part_ref, own_ref, own_sem,
):
    place, lane = place_ref[0], place_ref[1]
    near, far = tables
    own_copy = pltpu.make_async_copy(own_hbm, own_ref, own_sem)
    own_copy.start()
    here, there = lookup(near, place, lane), lookup(near, place, 1 - lane)
    store_piece(own_swap, place, 1 - lane, table_ref, high, low, left)
    store_piece(r1, here, lane, table_ref, high, low)
    store_piece(r2, here, 1 - lane, table_ref, high, low)
    store_piece(t1, there, 1 - lane, table_ref, high, low)
    store_piece(t2, there, lane, table_ref, high, low)
    store_piece(r3, lookup(far, place, lane), lane, table_ref, high, low)
    own_copy.wait()
    store_piece(own_ref, place, lane, table_ref, high, low, left)
    order = high.shape[0]
    depth, tile = order // 2, 256
    rows = pl.ds(pl.multiple_of(place // 2 * depth, depth), depth)
    for n in range(order // tile):
        cols = pl.ds(n * tile, tile)
        part_ref[:, cols] = stacked_dot(left[:, rows], high[rows, cols], low[rows, cols])


def late_kernel(
    tables, table_ref, place_ref, r4, t3, t4, high_in, low_in, left, part_ref,
    out_ref, high, low, square, square_parts,
):
    place, lane, group = place_ref[0], place_ref[1], place_ref[2]
    far = tables[1]
    here, there = lookup(far, place, lane), lookup(far, place, 1 - lane)
    store_piece(t3, there, 1 - lane, table_ref, high, low)
    store_piece(r4, here, 1 - lane, table_ref, high, low)
    store_piece(t4, there, lane, table_ref, high, low)
    order = high.shape[0]
    depth, tile = order // 2, 256
    slab, width, edge, _ = out_ref.shape
    act = 2 * width
    rows = pl.ds(pl.multiple_of((1 - place // 2) * depth, depth), depth)
    for n in range(order // tile):
        cols = pl.ds(n * tile, tile)
        square[:, cols] = part_ref[:, cols] + stacked_dot(
            left[:, rows], high[rows, cols], low[rows, cols]
        )
        for r in range(slab):
            for c in range(n * tile // edge, (n + 1) * tile // edge):
                kept = table_ref[place * slab + r, 2 * act + c] > 0
                col = pl.ds(c * edge, edge)
                block = jnp.where(kept, square[pl.ds(r * edge, edge), col], 0.0)
                block_high, block_low = split(block)
                square_parts[pl.ds(2 * r * edge, edge), col] = block_high
                square_parts[pl.ds((2 * r + 1) * edge, edge), col] = block_low
    for r in range(slab):
        row = place * slab + r
        left_parts = square_parts[pl.ds(2 * r * edge, 2 * edge), :]
        for w in range(0, width, 2):
            slots = [jnp.minimum(group * width + w + k, act - 1) for k in range(2)]
            cols = [
                pl.ds(pl.multiple_of(table_ref[row, slot] * edge, edge), edge) for slot in slots
            ]
            cube = stacked_dot(
                left_parts,
                jnp.concatenate([high[:, col] for col in cols], axis=1),
                jnp.concatenate([low[:, col] for col in cols], axis=1),
            )
            for k in range(2):
                there = (group * width + w + k < act) & (table_ref[row, act + slots[k]] > 0)
                value = 3.0 * square[pl.ds(r * edge, edge), cols[k]]
                value = value - 2.0 * cube[:, k * edge : (k + 1) * edge]
                out_ref[r, w + k] = jnp.where(there, value, 0.0)


def slot_table(columns, act):
    rows = columns.shape[0]
    slots = columns[:, :act]
    here = slots < rows
    ids = jnp.arange(rows, dtype=jnp.int32)
    taken = jnp.any(slots[:, :, None] == ids, axis=1)
    count = jnp.sum(here.astype(jnp.int32), axis=1, keepdims=True)
    before = jnp.sum(
        (~taken[:, None, :] & (ids[None, :] < ids[:, None])[None]).astype(jnp.int32), axis=2
    )
    at = jnp.where(taken, -1, count + before)
    filled = jnp.sum(
        jnp.where(at[:, None, :] == jnp.arange(act, dtype=jnp.int32)[None, :, None], ids, 0), axis=2
    )
    order = jnp.where(here, slots, filled)
    return jnp.concatenate([order, here.astype(jnp.int32), taken.astype(jnp.int32)], axis=1)


def gather_local(x_blocks, columns):
    slab, width, edge, _ = x_blocks.shape
    rows = columns.shape[0]
    groups, chains, panels, lanes = (lax.axis_size(axis) for axis in AXES)
    last = chains - 1

    def index(g, place):
        z, x, c = place
        return (((g % groups) * chains + z) * panels + x) * lanes + c

    def move(block, cycles):
        pairs = [(cycle[i - 1], cycle[i]) for cycle in cycles for i in range(len(cycle))]
        busy = {a for a, _ in pairs}
        route = [(index(g, a), index(g, b)) for g in range(groups) for a, b in pairs]
        for z in range(chains):
            for x in range(panels):
                idle = [(z, x, c) for c in range(lanes) if (z, x, c) not in busy]
                for g in range(groups):
                    if len(idle) == lanes:
                        route += [(index(g, idle[c - 1]), index(g, idle[c])) for c in range(lanes)]
                    else:
                        route += [(index(g, a), index(g + 1, a)) for a in idle]
        return lax.ppermute(block, AXES, route)

    def swap(block):
        return move(block, [])

    def move_only(block, chains_of):
        pairs = [(chain[i], chain[i + 1]) for chain in chains_of for i in range(len(chain) - 1)]
        route = [(index(g, a), index(g, b)) for g in range(groups) for a, b in pairs]
        return lax.ppermute(block, AXES, route)

    up = [(z, 0, 0) for z in range(chains)] + [(last, 1, 0)]
    down = [(z, 0, 1) for z in reversed(range(chains))] + [(0, 1, 1)]
    first = [up + [(last, 1, 1)] + down + [(0, 1, 0)]]
    second = [up, down]
    near = [(z - 1, z + 1 if z < last else -1) for z in range(chains)]
    far = [(z - 2 if z >= 2 else -1, z + 2 if z + 2 < chains else -1) for z in range(chains)]
    far[0] = (last, far[0][1])
    far[last] = (far[last][0], 0)
    tables = (near, far)

    table = slot_table(columns, lanes * width)
    r1 = move(x_blocks, first)
    own_swap = swap(x_blocks)
    r2 = move_only(own_swap, [up, down])
    r1, table = lax.optimization_barrier((r1, table))
    r3 = move(r1, second)
    t1 = swap(r1)
    r4 = move(r2, second)
    t2 = swap(r2)

    place = jnp.stack(
        [
            lax.axis_index("blk"),
            lax.axis_index("depth"),
            lax.axis_index("panel") * lanes + lax.axis_index("depth"),
        ]
    ).astype(jnp.int32)
    order, own = rows * edge, slab * edge
    smem = pl.BlockSpec(memory_space=pltpu.SMEM)
    vmem = pl.BlockSpec(memory_space=pltpu.VMEM)
    params = pltpu.CompilerParams(vmem_limit_bytes=24 * 2**20)
    high, low, left, part = pl.pallas_call(
        functools.partial(early_kernel, tables),
        out_shape=[
            jax.ShapeDtypeStruct((order, order), jnp.bfloat16),
            jax.ShapeDtypeStruct((order, order), jnp.bfloat16),
            jax.ShapeDtypeStruct((2 * own, order), jnp.bfloat16),
            jax.ShapeDtypeStruct((own, order), jnp.float32),
        ],
        in_specs=[smem] * 2 + [pl.BlockSpec(memory_space=pltpu.HBM)] + [vmem] * 6,
        out_specs=[vmem] * 4,
        scratch_shapes=[pltpu.VMEM(x_blocks.shape, jnp.float32), pltpu.SemaphoreType.DMA],
        compiler_params=params,
        name="early",
    )(table, place, x_blocks, own_swap, r1, r2, t1, t2, r3)
    t3 = swap(r3)
    r4, part = lax.optimization_barrier((r4, part))
    t4 = swap(r4)
    out, _, _ = pl.pallas_call(
        functools.partial(late_kernel, tables),
        out_shape=[
            jax.ShapeDtypeStruct(x_blocks.shape, jnp.float32),
            jax.ShapeDtypeStruct((order, order), jnp.bfloat16),
            jax.ShapeDtypeStruct((order, order), jnp.bfloat16),
        ],
        in_specs=[smem] * 2 + [vmem] * 7,
        out_specs=[vmem] * 3,
        input_output_aliases={5: 1, 6: 2},
        scratch_shapes=[
            pltpu.VMEM((own, order), jnp.float32),
            pltpu.VMEM((2 * own, order), jnp.bfloat16),
        ],
        compiler_params=params,
        name="late",
    )(table, place, r4, t3, t4, high, low, left, part)
    return out


def local(x_blocks, columns):
    slab, width, edge, _ = x_blocks.shape
    rows, slots = columns.shape
    _, chains, panels, lanes = (lax.axis_size(axis) for axis in AXES)
    full = rows <= slots and rows == lanes * width and width % 2 == 0
    if full and rows <= 8 and edge % 128 == 0 and panels >= 2 and lanes == 2 and chains == 4:
        return gather_local(x_blocks, columns)
    return ring_local(x_blocks, columns)


def solution(mesh):
    placed = (P(("groups", "blk"), ("panel", "depth"), None, None), P("groups", None))
    return jax.shard_map(
        local,
        mesh=mesh,
        in_specs=placed,
        out_specs=P(("groups", "blk"), ("panel", "depth"), None, None),
        check_vma=False,
    )
```

```python
import functools

import jax
import jax.numpy as jnp
from jax import lax
from jax.experimental import pallas as pl
from jax.experimental.pallas import tpu as pltpu
from jax.sharding import PartitionSpec as P

precise = lax.Precision.HIGHEST
AXES = ("groups", "blk", "panel", "depth")


def shifted(block, axis, distance):
    devices = range(lax.axis_size(axis))
    route = [((i - distance) % len(devices), i) for i in devices]
    return lax.ppermute(block, axis, route)


def slot_gather(blocks):
    return lax.all_gather(blocks, ("panel", "depth"), axis=1, tiled=True)


def slot_reduce(partial_value):
    return lax.psum_scatter(partial_value, ("panel", "depth"), scatter_dimension=1, tiled=True)


def rotate_one(incoming):
    return shifted(incoming, "blk", 1)


def ring_local(x_blocks, columns):
    slab_rows = x_blocks.shape[0]
    width_slots = x_blocks.shape[1]
    edge = x_blocks.shape[2]
    order_rows = columns.shape[0]
    all_slots = columns.shape[1]
    cycle_size = lax.axis_size("blk")
    cycle_place = lax.axis_index("blk")
    anchor = jnp.int32(0)
    first_own = cycle_place * slab_rows
    slot_first = lax.axis_index(("panel", "depth")) * width_slots
    my_cols = lax.dynamic_slice(columns, (first_own, anchor), (slab_rows, all_slots))
    own_cols = lax.dynamic_slice(my_cols, (anchor, slot_first), (slab_rows, width_slots))
    x_own = jnp.where((own_cols < order_rows)[:, :, None, None], x_blocks, jnp.float32(0.0))
    out_present = my_cols < order_rows
    empty = jnp.zeros((slab_rows, all_slots, edge, edge), jnp.float32)

    def contribute(partial_value, left_rows, incoming, source):
        group = incoming.shape[0]
        first_row = source * group
        their_cols = lax.dynamic_slice(columns, (first_row, slot_first), (group, width_slots))
        row_ids = first_row + jnp.arange(group, dtype=jnp.int32)
        selector = (my_cols[:, None, :] == row_ids[None, :, None]).astype(jnp.float32)
        picked = jnp.einsum("irs,isab->irab", selector, left_rows, precision=precise)
        products = jnp.einsum("irab,rubc->iruac", picked, incoming, precision=precise)
        targets = (their_cols[None, None, :, :] == my_cols[:, :, None, None]) & out_present[
            :, :, None, None
        ]
        placed = jnp.einsum(
            "isru,iruac->isac", targets.astype(jnp.float32), products, precision=precise
        )
        return partial_value + placed

    def one_way(left_rows, stored):

        def advance(offset, state):
            partial_value, incoming, stored = state
            source = (cycle_place - offset) % cycle_size
            partial_value = contribute(partial_value, left_rows, incoming, source)
            return (partial_value, rotate_one(incoming), stored)

        partial_value, incoming, stored = lax.fori_loop(
            0, cycle_size - 1, advance, (empty, x_own, stored)
        )
        source = (cycle_place + 1) % cycle_size
        return (contribute(partial_value, left_rows, incoming, source), stored)

    stored = jnp.zeros((1,), jnp.float32)
    left_first = slot_gather(x_own)
    partial_value, stored = one_way(left_first, stored)
    squared = slot_reduce(partial_value)
    left_second = slot_gather(squared)
    partial_value, stored = one_way(left_second, stored)
    cubed = slot_reduce(partial_value)
    return 3.0 * squared - 2.0 * cubed


def split(value):
    high = value.astype(jnp.bfloat16)
    low = (value - high.astype(jnp.float32)).astype(jnp.bfloat16)
    return high, low


def dot(left, right):
    return jnp.dot(left, right, preferred_element_type=jnp.float32)


def stacked_dot(left, high, low):
    half = left.shape[0] // 2
    both = dot(left, high)
    return both[:half] + (both[half:] + dot(left[:half], low))


def lookup(table, place, lane):
    found = jnp.int32(-1)
    for z, entries in enumerate(table):
        for c, entry in enumerate(entries):
            found = jnp.where((place == z) & (lane == c), entry, found)
    return found


def store_piece(piece, plane, group, table_ref, high, low, own=None):
    slab, width, edge, _ = piece.shape
    act = 2 * width

    @pl.when(plane >= 0)
    def _():
        for r in range(slab):
            row = plane * slab + r
            for w in range(width):
                slot = group * width + w
                col = pl.ds(pl.multiple_of(table_ref[row, slot] * edge, edge), edge)
                block = jnp.where(table_ref[row, act + slot] > 0, piece[r, w], 0.0)
                block_high, block_low = split(block)
                at = pl.ds(pl.multiple_of(row * edge, edge), edge)
                high[at, col] = block_high
                low[at, col] = block_low
                if own is not None:
                    own[pl.ds(r * edge, edge), col] = block_high
                    own[pl.ds((slab + r) * edge, edge), col] = block_low


def add_plane(plane, left, high, low, part_ref):
    depth, tile = part_ref.shape[0], 256

    @pl.when(plane >= 0)
    def _():
        rows = pl.ds(pl.multiple_of(plane * depth, depth), depth)
        for n in range(part_ref.shape[1] // tile):
            cols = pl.ds(n * tile, tile)
            part_ref[:, cols] += stacked_dot(left[:, rows], high[rows, cols], low[rows, cols])


def early_kernel(
    tables, table_ref, place_ref, own_hbm, own_swap, r1, r2, t1, t2, r3,
    high, low, left, part_ref, own_ref, own_sem,
):
    place, lane = place_ref[0], place_ref[1]
    near, far = tables
    own_copy = pltpu.make_async_copy(own_hbm, own_ref, own_sem)
    own_copy.start()
    here, there = lookup(near, place, lane), lookup(near, place, 1 - lane)
    part_ref[...] = jnp.zeros_like(part_ref)
    store_piece(own_swap, place, 1 - lane, table_ref, high, low, left)
    store_piece(r1, here, lane, table_ref, high, low)
    store_piece(r2, here, 1 - lane, table_ref, high, low)
    store_piece(t1, there, 1 - lane, table_ref, high, low)
    store_piece(t2, there, lane, table_ref, high, low)
    store_piece(r3, lookup(far, place, lane), lane, table_ref, high, low)
    own_copy.wait()
    store_piece(own_ref, place, lane, table_ref, high, low, left)
    for plane in (place, here, there):
        add_plane(plane, left, high, low, part_ref)


def middle_kernel(
    tables, table_ref, place_ref, r4, t3, high_in, low_in, left, part_in, high, low, part_ref
):
    place, lane = place_ref[0], place_ref[1]
    far = tables[1]
    here, there = lookup(far, place, lane), lookup(far, place, 1 - lane)
    store_piece(t3, there, 1 - lane, table_ref, high, low)
    store_piece(r4, here, 1 - lane, table_ref, high, low)
    add_plane(here, left, high, low, part_ref)


def late_kernel(
    tables, table_ref, place_ref, t4, high_in, low_in, left, part_in,
    out_hbm, high, low, square, square_parts, out_ref, out_sem,
):
    place, lane, group = place_ref[0], place_ref[1], place_ref[2]
    there = lookup(tables[1], place, 1 - lane)
    store_piece(t4, there, lane, table_ref, high, low)
    add_plane(there, left, high, low, square)
    slab, width, edge, _ = out_ref.shape
    act = 2 * width
    for r in range(slab):
        for c in range(square.shape[1] // edge):
            kept = table_ref[place * slab + r, 2 * act + c] > 0
            col = pl.ds(c * edge, edge)
            block = jnp.where(kept, square[pl.ds(r * edge, edge), col], 0.0)
            block_high, block_low = split(block)
            square_parts[pl.ds(2 * r * edge, edge), col] = block_high
            square_parts[pl.ds((2 * r + 1) * edge, edge), col] = block_low
    copies = []
    for r in range(slab):
        row = place * slab + r
        left_parts = square_parts[pl.ds(2 * r * edge, 2 * edge), :]
        for w in range(0, width, 2):
            slots = [jnp.minimum(group * width + w + k, act - 1) for k in range(2)]
            cols = [
                pl.ds(pl.multiple_of(table_ref[row, slot] * edge, edge), edge) for slot in slots
            ]
            cube = stacked_dot(
                left_parts,
                jnp.concatenate([high[:, col] for col in cols], axis=1),
                jnp.concatenate([low[:, col] for col in cols], axis=1),
            )
            for k in range(2):
                there = (group * width + w + k < act) & (table_ref[row, act + slots[k]] > 0)
                value = 3.0 * square[pl.ds(r * edge, edge), cols[k]]
                value = value - 2.0 * cube[:, k * edge : (k + 1) * edge]
                out_ref[r, w + k] = jnp.where(there, value, 0.0)
            ready = (r, pl.ds(w, 2))
            copies.append(
                pltpu.make_async_copy(out_ref.at[ready], out_hbm.at[ready], out_sem.at[len(copies)])
            )
            copies[-1].start()
    for copy in copies:
        copy.wait()


def slot_table(columns, act):
    rows = columns.shape[0]
    slots = columns[:, :act]
    here = slots < rows
    ids = jnp.arange(rows, dtype=jnp.int32)
    taken = jnp.any(slots[:, :, None] == ids, axis=1)
    count = jnp.sum(here.astype(jnp.int32), axis=1, keepdims=True)
    before = jnp.sum(
        (~taken[:, None, :] & (ids[None, :] < ids[:, None])[None]).astype(jnp.int32), axis=2
    )
    at = jnp.where(taken, -1, count + before)
    filled = jnp.sum(
        jnp.where(at[:, None, :] == jnp.arange(act, dtype=jnp.int32)[None, :, None], ids, 0), axis=2
    )
    order = jnp.where(here, slots, filled)
    return jnp.concatenate([order, here.astype(jnp.int32), taken.astype(jnp.int32)], axis=1)


def gather_local(x_blocks, columns):
    slab, width, edge, _ = x_blocks.shape
    rows = columns.shape[0]
    groups, chains, panels, lanes = (lax.axis_size(axis) for axis in AXES)
    last = chains - 1

    def index(g, place):
        z, x, c = place
        return (((g % groups) * chains + z) * panels + x) * lanes + c

    def move(block, cycles):
        pairs = [(cycle[i - 1], cycle[i]) for cycle in cycles for i in range(len(cycle))]
        busy = {a for a, _ in pairs}
        route = [(index(g, a), index(g, b)) for g in range(groups) for a, b in pairs]
        for z in range(chains):
            for x in range(panels):
                idle = [(z, x, c) for c in range(lanes) if (z, x, c) not in busy]
                for g in range(groups):
                    if len(idle) == lanes:
                        route += [(index(g, idle[c - 1]), index(g, idle[c])) for c in range(lanes)]
                    else:
                        route += [(index(g, a), index(g + 1, a)) for a in idle]
        return lax.ppermute(block, AXES, route)

    def swap(block):
        return move(block, [])

    def move_only(block, chains_of):
        pairs = [(chain[i], chain[i + 1]) for chain in chains_of for i in range(len(chain) - 1)]
        route = [(index(g, a), index(g, b)) for g in range(groups) for a, b in pairs]
        return lax.ppermute(block, AXES, route)

    up = [(z, 0, 0) for z in range(chains)] + [(last, 1, 0)]
    down = [(z, 0, 1) for z in reversed(range(chains))] + [(0, 1, 1)]
    first = [up + [(last, 1, 1)] + down + [(0, 1, 0)]]
    second = [up, down]
    near = [(z - 1, z + 1 if z < last else -1) for z in range(chains)]
    far = [(z - 2 if z >= 2 else -1, z + 2 if z + 2 < chains else -1) for z in range(chains)]
    far[0] = (last, far[0][1])
    far[last] = (far[last][0], 0)
    tables = (near, far)

    table = slot_table(columns, lanes * width)
    r1 = move(x_blocks, first)
    own_swap = swap(x_blocks)
    r2 = move_only(own_swap, [up, down])
    r1, table = lax.optimization_barrier((r1, table))
    r3 = move(r1, second)
    t1 = swap(r1)
    r4 = move(r2, second)
    t2 = swap(r2)

    place = jnp.stack(
        [
            lax.axis_index("blk"),
            lax.axis_index("depth"),
            lax.axis_index("panel") * lanes + lax.axis_index("depth"),
        ]
    ).astype(jnp.int32)
    order, own = rows * edge, slab * edge
    smem = pl.BlockSpec(memory_space=pltpu.SMEM)
    vmem = pl.BlockSpec(memory_space=pltpu.VMEM)
    params = pltpu.CompilerParams(vmem_limit_bytes=24 * 2**20)
    high, low, left, part = pl.pallas_call(
        functools.partial(early_kernel, tables),
        out_shape=[
            jax.ShapeDtypeStruct((order, order), jnp.bfloat16),
            jax.ShapeDtypeStruct((order, order), jnp.bfloat16),
            jax.ShapeDtypeStruct((2 * own, order), jnp.bfloat16),
            jax.ShapeDtypeStruct((own, order), jnp.float32),
        ],
        in_specs=[smem] * 2 + [pl.BlockSpec(memory_space=pltpu.HBM)] + [vmem] * 6,
        out_specs=[vmem] * 4,
        scratch_shapes=[pltpu.VMEM(x_blocks.shape, jnp.float32), pltpu.SemaphoreType.DMA],
        compiler_params=params,
        name="early",
    )(table, place, x_blocks, own_swap, r1, r2, t1, t2, r3)
    t3 = swap(r3)
    r4, part = lax.optimization_barrier((r4, part))
    t4 = swap(r4)
    dense = [jax.ShapeDtypeStruct(a.shape, a.dtype) for a in (high, low, part)]
    high, low, part = pl.pallas_call(
        functools.partial(middle_kernel, tables),
        out_shape=dense,
        in_specs=[smem] * 2 + [vmem] * 6,
        out_specs=[vmem] * 3,
        input_output_aliases={4: 0, 5: 1, 7: 2},
        compiler_params=params,
        name="middle",
    )(table, place, r4, t3, high, low, left, part)
    out, _, _, _ = pl.pallas_call(
        functools.partial(late_kernel, tables),
        out_shape=[jax.ShapeDtypeStruct(x_blocks.shape, jnp.float32)] + dense,
        in_specs=[smem] * 2 + [vmem] * 5,
        out_specs=[pl.BlockSpec(memory_space=pltpu.HBM)] + [vmem] * 3,
        input_output_aliases={3: 1, 4: 2, 6: 3},
        scratch_shapes=[
            pltpu.VMEM((2 * own, order), jnp.bfloat16),
            pltpu.VMEM(x_blocks.shape, jnp.float32),
            pltpu.SemaphoreType.DMA((slab * width // 2,)),
        ],
        compiler_params=params,
        name="late",
    )(table, place, t4, high, low, left, part)
    return out


def local(x_blocks, columns):
    slab, width, edge, _ = x_blocks.shape
    rows, slots = columns.shape
    _, chains, panels, lanes = (lax.axis_size(axis) for axis in AXES)
    full = rows <= slots and rows == lanes * width and width % 2 == 0
    if full and rows <= 8 and edge % 128 == 0 and panels >= 2 and lanes == 2 and chains == 4:
        return gather_local(x_blocks, columns)
    return ring_local(x_blocks, columns)


def solution(mesh):
    placed = (P(("groups", "blk"), ("panel", "depth"), None, None), P("groups", None))
    return jax.shard_map(
        local,
        mesh=mesh,
        in_specs=placed,
        out_specs=P(("groups", "blk"), ("panel", "depth"), None, None),
        check_vma=False,
    )
```

```python
import functools

import jax
import jax.numpy as jnp
from jax import lax
from jax.experimental import pallas as pl
from jax.experimental.pallas import tpu as pltpu
from jax.sharding import PartitionSpec as P

precise = lax.Precision.HIGHEST
AXES = ("groups", "blk", "panel", "depth")


def shifted(block, axis, distance):
    devices = range(lax.axis_size(axis))
    route = [((i - distance) % len(devices), i) for i in devices]
    return lax.ppermute(block, axis, route)


def slot_gather(blocks):
    return lax.all_gather(blocks, ("panel", "depth"), axis=1, tiled=True)


def slot_reduce(partial_value):
    return lax.psum_scatter(partial_value, ("panel", "depth"), scatter_dimension=1, tiled=True)


def rotate_one(incoming):
    return shifted(incoming, "blk", 1)


def ring_local(x_blocks, columns):
    slab_rows = x_blocks.shape[0]
    width_slots = x_blocks.shape[1]
    edge = x_blocks.shape[2]
    order_rows = columns.shape[0]
    all_slots = columns.shape[1]
    cycle_size = lax.axis_size("blk")
    cycle_place = lax.axis_index("blk")
    anchor = jnp.int32(0)
    first_own = cycle_place * slab_rows
    slot_first = lax.axis_index(("panel", "depth")) * width_slots
    my_cols = lax.dynamic_slice(columns, (first_own, anchor), (slab_rows, all_slots))
    own_cols = lax.dynamic_slice(my_cols, (anchor, slot_first), (slab_rows, width_slots))
    x_own = jnp.where((own_cols < order_rows)[:, :, None, None], x_blocks, jnp.float32(0.0))
    out_present = my_cols < order_rows
    empty = jnp.zeros((slab_rows, all_slots, edge, edge), jnp.float32)

    def contribute(partial_value, left_rows, incoming, source):
        group = incoming.shape[0]
        first_row = source * group
        their_cols = lax.dynamic_slice(columns, (first_row, slot_first), (group, width_slots))
        row_ids = first_row + jnp.arange(group, dtype=jnp.int32)
        selector = (my_cols[:, None, :] == row_ids[None, :, None]).astype(jnp.float32)
        picked = jnp.einsum("irs,isab->irab", selector, left_rows, precision=precise)
        products = jnp.einsum("irab,rubc->iruac", picked, incoming, precision=precise)
        targets = (their_cols[None, None, :, :] == my_cols[:, :, None, None]) & out_present[
            :, :, None, None
        ]
        placed = jnp.einsum(
            "isru,iruac->isac", targets.astype(jnp.float32), products, precision=precise
        )
        return partial_value + placed

    def one_way(left_rows, stored):

        def advance(offset, state):
            partial_value, incoming, stored = state
            source = (cycle_place - offset) % cycle_size
            partial_value = contribute(partial_value, left_rows, incoming, source)
            return (partial_value, rotate_one(incoming), stored)

        partial_value, incoming, stored = lax.fori_loop(
            0, cycle_size - 1, advance, (empty, x_own, stored)
        )
        source = (cycle_place + 1) % cycle_size
        return (contribute(partial_value, left_rows, incoming, source), stored)

    stored = jnp.zeros((1,), jnp.float32)
    left_first = slot_gather(x_own)
    partial_value, stored = one_way(left_first, stored)
    squared = slot_reduce(partial_value)
    left_second = slot_gather(squared)
    partial_value, stored = one_way(left_second, stored)
    cubed = slot_reduce(partial_value)
    return 3.0 * squared - 2.0 * cubed


def split(value):
    high = value.astype(jnp.bfloat16)
    low = (value - high.astype(jnp.float32)).astype(jnp.bfloat16)
    return high, low


def dot(left, right):
    return jnp.dot(left, right, preferred_element_type=jnp.float32)


def stacked_dot(left, high, low):
    half = left.shape[0] // 2
    both = dot(left, high)
    return both[:half] + (both[half:] + dot(left[:half], low))


def lookup(table, place, lane):
    found = jnp.int32(-1)
    for z, entries in enumerate(table):
        for c, entry in enumerate(entries):
            found = jnp.where((place == z) & (lane == c), entry, found)
    return found


def store_piece(piece, plane, group, table_ref, high, low, own=None):
    slab, width, edge, _ = piece.shape
    act = 2 * width

    @pl.when(plane >= 0)
    def _():
        for r in range(slab):
            row = plane * slab + r
            for w in range(width):
                slot = group * width + w
                col = pl.ds(pl.multiple_of(table_ref[row, slot] * edge, edge), edge)
                block = jnp.where(table_ref[row, act + slot] > 0, piece[r, w], 0.0)
                block_high, block_low = split(block)
                at = pl.ds(pl.multiple_of(row * edge, edge), edge)
                high[at, col] = block_high
                low[at, col] = block_low
                if own is not None:
                    own[pl.ds(r * edge, edge), col] = block_high
                    own[pl.ds((slab + r) * edge, edge), col] = block_low


def add_plane(plane, left, high, low, part_ref):
    depth, tile = part_ref.shape[0], 256

    @pl.when(plane >= 0)
    def _():
        rows = pl.ds(pl.multiple_of(plane * depth, depth), depth)
        for n in range(part_ref.shape[1] // tile):
            cols = pl.ds(n * tile, tile)
            part_ref[:, cols] += stacked_dot(left[:, rows], high[rows, cols], low[rows, cols])


def early_kernel(
    tables, table_ref, own_hbm, own_swap, r1, r2, t1, t2, r3,
    high, low, left, part_ref, own_ref, own_sem,
):
    place, lane = lax.axis_index("blk"), lax.axis_index("depth")
    near, far = tables
    own_copy = pltpu.make_async_copy(own_hbm, own_ref, own_sem)
    own_copy.start()
    here, there = lookup(near, place, lane), lookup(near, place, 1 - lane)
    part_ref[...] = jnp.zeros_like(part_ref)
    store_piece(own_swap, place, 1 - lane, table_ref, high, low, left)
    store_piece(r1, here, lane, table_ref, high, low)
    store_piece(r2, here, 1 - lane, table_ref, high, low)
    store_piece(t1, there, 1 - lane, table_ref, high, low)
    store_piece(t2, there, lane, table_ref, high, low)
    store_piece(r3, lookup(far, place, lane), lane, table_ref, high, low)
    own_copy.wait()
    store_piece(own_ref, place, lane, table_ref, high, low, left)
    for plane in (place, here, there):
        add_plane(plane, left, high, low, part_ref)


def middle_kernel(
    tables, table_ref, r4, t3, high_in, low_in, left, part_in, high, low, part_ref
):
    place, lane = lax.axis_index("blk"), lax.axis_index("depth")
    far = tables[1]
    here, there = lookup(far, place, lane), lookup(far, place, 1 - lane)
    store_piece(t3, there, 1 - lane, table_ref, high, low)
    store_piece(r4, here, 1 - lane, table_ref, high, low)
    add_plane(here, left, high, low, part_ref)


def late_kernel(
    tables, table_ref, t4, high_in, low_in, left, part_in,
    out_hbm, high, low, square, square_parts, out_ref, out_sem,
):
    place, lane = lax.axis_index("blk"), lax.axis_index("depth")
    group = lax.axis_index("panel") * 2 + lane
    there = lookup(tables[1], place, 1 - lane)
    store_piece(t4, there, lane, table_ref, high, low)
    add_plane(there, left, high, low, square)
    slab, width, edge, _ = out_ref.shape
    act = 2 * width
    for r in range(slab):
        for c in range(square.shape[1] // edge):
            kept = table_ref[place * slab + r, 2 * act + c] > 0
            col = pl.ds(c * edge, edge)
            block = jnp.where(kept, square[pl.ds(r * edge, edge), col], 0.0)
            block_high, block_low = split(block)
            square_parts[pl.ds(2 * r * edge, edge), col] = block_high
            square_parts[pl.ds((2 * r + 1) * edge, edge), col] = block_low
    copies = []
    for r in range(slab):
        row = place * slab + r
        left_parts = square_parts[pl.ds(2 * r * edge, 2 * edge), :]
        for w in range(0, width, 2):
            slots = [jnp.minimum(group * width + w + k, act - 1) for k in range(2)]
            cols = [
                pl.ds(pl.multiple_of(table_ref[row, slot] * edge, edge), edge) for slot in slots
            ]
            cube = stacked_dot(
                left_parts,
                jnp.concatenate([high[:, col] for col in cols], axis=1),
                jnp.concatenate([low[:, col] for col in cols], axis=1),
            )
            for k in range(2):
                there = (group * width + w + k < act) & (table_ref[row, act + slots[k]] > 0)
                value = 3.0 * square[pl.ds(r * edge, edge), cols[k]]
                value = value - 2.0 * cube[:, k * edge : (k + 1) * edge]
                out_ref[r, w + k] = jnp.where(there, value, 0.0)
            ready = (r, pl.ds(w, 2))
            copies.append(
                pltpu.make_async_copy(out_ref.at[ready], out_hbm.at[ready], out_sem.at[len(copies)])
            )
            copies[-1].start()
    for copy in copies:
        copy.wait()


def slot_table(columns, act):
    rows = columns.shape[0]
    slots = columns[:, :act]
    here = slots < rows
    ids = jnp.arange(rows, dtype=jnp.int32)
    taken = jnp.any(slots[:, :, None] == ids, axis=1)
    count = jnp.sum(here.astype(jnp.int32), axis=1, keepdims=True)
    before = jnp.sum(
        (~taken[:, None, :] & (ids[None, :] < ids[:, None])[None]).astype(jnp.int32), axis=2
    )
    at = jnp.where(taken, -1, count + before)
    filled = jnp.sum(
        jnp.where(at[:, None, :] == jnp.arange(act, dtype=jnp.int32)[None, :, None], ids, 0), axis=2
    )
    order = jnp.where(here, slots, filled)
    return jnp.concatenate([order, here.astype(jnp.int32), taken.astype(jnp.int32)], axis=1)


def gather_local(x_blocks, columns):
    slab, width, edge, _ = x_blocks.shape
    rows = columns.shape[0]
    groups, chains, panels, lanes = (lax.axis_size(axis) for axis in AXES)
    last = chains - 1

    def index(g, place):
        z, x, c = place
        return (((g % groups) * chains + z) * panels + x) * lanes + c

    def move(block, cycles):
        pairs = [(cycle[i - 1], cycle[i]) for cycle in cycles for i in range(len(cycle))]
        busy = {a for a, _ in pairs}
        route = [(index(g, a), index(g, b)) for g in range(groups) for a, b in pairs]
        for z in range(chains):
            for x in range(panels):
                idle = [(z, x, c) for c in range(lanes) if (z, x, c) not in busy]
                for g in range(groups):
                    if len(idle) == lanes:
                        route += [(index(g, idle[c - 1]), index(g, idle[c])) for c in range(lanes)]
                    else:
                        route += [(index(g, a), index(g + 1, a)) for a in idle]
        return lax.ppermute(block, AXES, route)

    def swap(block):
        return move(block, [])

    def move_only(block, chains_of):
        pairs = [(chain[i], chain[i + 1]) for chain in chains_of for i in range(len(chain) - 1)]
        route = [(index(g, a), index(g, b)) for g in range(groups) for a, b in pairs]
        return lax.ppermute(block, AXES, route)

    up = [(z, 0, 0) for z in range(chains)] + [(last, 1, 0)]
    down = [(z, 0, 1) for z in reversed(range(chains))] + [(0, 1, 1)]
    first = [up + [(last, 1, 1)] + down + [(0, 1, 0)]]
    second = [up, down]
    near = [(z - 1, z + 1 if z < last else -1) for z in range(chains)]
    far = [(z - 2 if z >= 2 else -1, z + 2 if z + 2 < chains else -1) for z in range(chains)]
    far[0] = (last, far[0][1])
    far[last] = (far[last][0], 0)
    tables = (near, far)

    table = slot_table(columns, lanes * width)
    r1 = move(x_blocks, first)
    own_swap = swap(x_blocks)
    r2 = move_only(own_swap, [up, down])
    r1, table = lax.optimization_barrier((r1, table))
    r3 = move(r1, second)
    t1 = swap(r1)
    r4 = move(r2, second)
    t2 = swap(r2)

    order, own = rows * edge, slab * edge
    table = pltpu.with_memory_space_constraint(table, pltpu.SMEM)
    smem = pl.BlockSpec(memory_space=pltpu.SMEM)
    vmem = pl.BlockSpec(memory_space=pltpu.VMEM)
    params = pltpu.CompilerParams(vmem_limit_bytes=24 * 2**20)
    def held(*arrays):
        return [pltpu.with_memory_space_constraint(a, pltpu.VMEM) for a in arrays]

    high, low, left, part = pl.pallas_call(
        functools.partial(early_kernel, tables),
        out_shape=[
            jax.ShapeDtypeStruct((order, order), jnp.bfloat16),
            jax.ShapeDtypeStruct((order, order), jnp.bfloat16),
            jax.ShapeDtypeStruct((2 * own, order), jnp.bfloat16),
            jax.ShapeDtypeStruct((own, order), jnp.float32),
        ],
        in_specs=[smem] + [pl.BlockSpec(memory_space=pltpu.HBM)] + [vmem] * 6,
        out_specs=[vmem] * 4,
        scratch_shapes=[pltpu.VMEM(x_blocks.shape, jnp.float32), pltpu.SemaphoreType.DMA],
        compiler_params=params,
        name="early",
    )(table, pltpu.with_memory_space_constraint(x_blocks, pltpu.HBM), own_swap, r1, r2, t1, t2, r3)
    t3 = swap(r3)
    r4, part = lax.optimization_barrier((r4, part))
    t4 = swap(r4)
    dense = [jax.ShapeDtypeStruct(a.shape, a.dtype) for a in (high, low, part)]
    high, low, part = pl.pallas_call(
        functools.partial(middle_kernel, tables),
        out_shape=dense,
        in_specs=[smem] + [vmem] * 6,
        out_specs=[vmem] * 3,
        input_output_aliases={3: 0, 4: 1, 6: 2},
        compiler_params=params,
        name="middle",
    )(table, r4, t3, *held(high, low, left, part))
    out, _, _, _ = pl.pallas_call(
        functools.partial(late_kernel, tables),
        out_shape=[jax.ShapeDtypeStruct(x_blocks.shape, jnp.float32)] + dense,
        in_specs=[smem] + [vmem] * 5,
        out_specs=[pl.BlockSpec(memory_space=pltpu.HBM)] + [vmem] * 3,
        input_output_aliases={2: 1, 3: 2, 5: 3},
        scratch_shapes=[
            pltpu.VMEM((2 * own, order), jnp.bfloat16),
            pltpu.VMEM(x_blocks.shape, jnp.float32),
            pltpu.SemaphoreType.DMA((slab * width // 2,)),
        ],
        compiler_params=params,
        name="late",
    )(table, t4, *held(high, low, left, part))
    return out


def local(x_blocks, columns):
    slab, width, edge, _ = x_blocks.shape
    rows, slots = columns.shape
    _, chains, panels, lanes = (lax.axis_size(axis) for axis in AXES)
    full = rows <= slots and rows == lanes * width and width % 2 == 0
    if full and rows <= 8 and edge % 128 == 0 and panels >= 2 and lanes == 2 and chains == 4:
        return gather_local(x_blocks, columns)
    return ring_local(x_blocks, columns)


def solution(mesh):
    placed = (P(("groups", "blk"), ("panel", "depth"), None, None), P("groups", None))
    return jax.shard_map(
        local,
        mesh=mesh,
        in_specs=placed,
        out_specs=P(("groups", "blk"), ("panel", "depth"), None, None),
        check_vma=False,
    )
```

```python
import functools

import jax
import jax.numpy as jnp
from jax import lax
from jax.experimental import pallas as pl
from jax.experimental.pallas import tpu as pltpu
from jax.sharding import PartitionSpec as P

precise = lax.Precision.HIGHEST
AXES = ("groups", "blk", "panel", "depth")


def shifted(block, axis, distance):
    devices = range(lax.axis_size(axis))
    route = [((i - distance) % len(devices), i) for i in devices]
    return lax.ppermute(block, axis, route)


def slot_gather(blocks):
    return lax.all_gather(blocks, ("panel", "depth"), axis=1, tiled=True)


def slot_reduce(partial_value):
    return lax.psum_scatter(partial_value, ("panel", "depth"), scatter_dimension=1, tiled=True)


def rotate_one(incoming):
    return shifted(incoming, "blk", 1)


def ring_local(x_blocks, columns):
    slab_rows = x_blocks.shape[0]
    width_slots = x_blocks.shape[1]
    edge = x_blocks.shape[2]
    order_rows = columns.shape[0]
    all_slots = columns.shape[1]
    cycle_size = lax.axis_size("blk")
    cycle_place = lax.axis_index("blk")
    anchor = jnp.int32(0)
    first_own = cycle_place * slab_rows
    slot_first = lax.axis_index(("panel", "depth")) * width_slots
    my_cols = lax.dynamic_slice(columns, (first_own, anchor), (slab_rows, all_slots))
    own_cols = lax.dynamic_slice(my_cols, (anchor, slot_first), (slab_rows, width_slots))
    x_own = jnp.where((own_cols < order_rows)[:, :, None, None], x_blocks, jnp.float32(0.0))
    out_present = my_cols < order_rows
    empty = jnp.zeros((slab_rows, all_slots, edge, edge), jnp.float32)

    def contribute(partial_value, left_rows, incoming, source):
        group = incoming.shape[0]
        first_row = source * group
        their_cols = lax.dynamic_slice(columns, (first_row, slot_first), (group, width_slots))
        row_ids = first_row + jnp.arange(group, dtype=jnp.int32)
        selector = (my_cols[:, None, :] == row_ids[None, :, None]).astype(jnp.float32)
        picked = jnp.einsum("irs,isab->irab", selector, left_rows, precision=precise)
        products = jnp.einsum("irab,rubc->iruac", picked, incoming, precision=precise)
        targets = (their_cols[None, None, :, :] == my_cols[:, :, None, None]) & out_present[
            :, :, None, None
        ]
        placed = jnp.einsum(
            "isru,iruac->isac", targets.astype(jnp.float32), products, precision=precise
        )
        return partial_value + placed

    def one_way(left_rows, stored):

        def advance(offset, state):
            partial_value, incoming, stored = state
            source = (cycle_place - offset) % cycle_size
            partial_value = contribute(partial_value, left_rows, incoming, source)
            return (partial_value, rotate_one(incoming), stored)

        partial_value, incoming, stored = lax.fori_loop(
            0, cycle_size - 1, advance, (empty, x_own, stored)
        )
        source = (cycle_place + 1) % cycle_size
        return (contribute(partial_value, left_rows, incoming, source), stored)

    stored = jnp.zeros((1,), jnp.float32)
    left_first = slot_gather(x_own)
    partial_value, stored = one_way(left_first, stored)
    squared = slot_reduce(partial_value)
    left_second = slot_gather(squared)
    partial_value, stored = one_way(left_second, stored)
    cubed = slot_reduce(partial_value)
    return 3.0 * squared - 2.0 * cubed


def split(value):
    high = value.astype(jnp.bfloat16)
    low = (value - high.astype(jnp.float32)).astype(jnp.bfloat16)
    return high, low


def dot(left, right):
    return jnp.dot(left, right, preferred_element_type=jnp.float32)


def stacked_dot(left, high, low):
    half = left.shape[0] // 2
    both = dot(left, high)
    return both[:half] + (both[half:] + dot(left[:half], low))


def lookup(table, place, lane):
    found = jnp.int32(-1)
    for z, entries in enumerate(table):
        for c, entry in enumerate(entries):
            found = jnp.where((place == z) & (lane == c), entry, found)
    return found


def store_piece(piece, plane, group, table_ref, high, low, own=None):
    slab, width, edge, _ = piece.shape
    act = 2 * width

    @pl.when(plane >= 0)
    def _():
        for r in range(slab):
            row = plane * slab + r
            for w in range(width):
                slot = group * width + w
                col = pl.ds(pl.multiple_of(table_ref[row, slot] * edge, edge), edge)
                block = jnp.where(table_ref[row, act + slot] > 0, piece[r, w], 0.0)
                block_high, block_low = split(block)
                at = pl.ds(pl.multiple_of(row * edge, edge), edge)
                high[at, col] = block_high
                low[at, col] = block_low
                if own is not None:
                    own[pl.ds(r * edge, edge), col] = block_high
                    own[pl.ds((slab + r) * edge, edge), col] = block_low


def add_plane(plane, left, high, low, part_ref):
    depth, tile = part_ref.shape[0], 256

    @pl.when(plane >= 0)
    def _():
        rows = pl.ds(pl.multiple_of(plane * depth, depth), depth)

        @pl.loop(0, part_ref.shape[1] // tile)
        def _(n):
            cols = pl.ds(pl.multiple_of(n * tile, tile), tile)
            part_ref[:, cols] += stacked_dot(left[:, rows], high[rows, cols], low[rows, cols])


def early_kernel(
    tables, table_ref, own_hbm, own_swap, r1, r2, t1, t2, r3,
    high, low, left, part_ref, own_ref, own_sem,
):
    place, lane = lax.axis_index("blk"), lax.axis_index("depth")
    near, far = tables
    own_copy = pltpu.make_async_copy(own_hbm, own_ref, own_sem)
    own_copy.start()
    here, there = lookup(near, place, lane), lookup(near, place, 1 - lane)
    part_ref[...] = jnp.zeros_like(part_ref)
    store_piece(own_swap, place, 1 - lane, table_ref, high, low, left)
    store_piece(r1, here, lane, table_ref, high, low)
    store_piece(r2, here, 1 - lane, table_ref, high, low)
    store_piece(t1, there, 1 - lane, table_ref, high, low)
    store_piece(t2, there, lane, table_ref, high, low)
    store_piece(r3, lookup(far, place, lane), lane, table_ref, high, low)
    own_copy.wait()
    store_piece(own_ref, place, lane, table_ref, high, low, left)
    for plane in (place, here, there):
        add_plane(plane, left, high, low, part_ref)


def middle_kernel(
    tables, table_ref, r4, t3, high_in, low_in, left, part_in, high, low, part_ref
):
    place, lane = lax.axis_index("blk"), lax.axis_index("depth")
    far = tables[1]
    here, there = lookup(far, place, lane), lookup(far, place, 1 - lane)
    store_piece(t3, there, 1 - lane, table_ref, high, low)
    store_piece(r4, here, 1 - lane, table_ref, high, low)
    add_plane(here, left, high, low, part_ref)


def late_kernel(
    tables, table_ref, t4, high_in, low_in, left, part_in,
    out_hbm, high, low, square, square_parts, out_ref, out_sem,
):
    place, lane = lax.axis_index("blk"), lax.axis_index("depth")
    group = lax.axis_index("panel") * 2 + lane
    there = lookup(tables[1], place, 1 - lane)
    store_piece(t4, there, lane, table_ref, high, low)
    add_plane(there, left, high, low, square)
    slab, width, edge, _ = out_ref.shape
    act = 2 * width
    @pl.loop(0, square.shape[1] // edge)
    def _(c):
        col = pl.ds(pl.multiple_of(c * edge, edge), edge)
        for r in range(slab):
            kept = table_ref[place * slab + r, 2 * act + c] > 0
            block = jnp.where(kept, square[pl.ds(r * edge, edge), col], 0.0)
            block_high, block_low = split(block)
            square_parts[pl.ds(2 * r * edge, edge), col] = block_high
            square_parts[pl.ds((2 * r + 1) * edge, edge), col] = block_low

    def leave(r, w, number):
        ready = (r, pl.ds(w, 2))
        return pltpu.make_async_copy(out_ref.at[ready], out_hbm.at[ready], out_sem.at[number])

    @pl.loop(0, slab * width // 2)
    def _(number):
        r, w = number // (width // 2), number % (width // 2) * 2
        row = place * slab + r
        slots = [jnp.minimum(group * width + w + k, act - 1) for k in range(2)]
        cols = [pl.ds(pl.multiple_of(table_ref[row, slot] * edge, edge), edge) for slot in slots]
        cube = stacked_dot(
            square_parts[pl.ds(pl.multiple_of(2 * r * edge, edge), 2 * edge), :],
            jnp.concatenate([high[:, col] for col in cols], axis=1),
            jnp.concatenate([low[:, col] for col in cols], axis=1),
        )
        for k in range(2):
            there = (group * width + w + k < act) & (table_ref[row, act + slots[k]] > 0)
            value = 3.0 * square[pl.ds(pl.multiple_of(r * edge, edge), edge), cols[k]]
            value = value - 2.0 * cube[:, k * edge : (k + 1) * edge]
            out_ref[r, w + k] = jnp.where(there, value, 0.0)
        leave(r, w, number).start()

    for number in range(slab * width // 2):
        leave(number // (width // 2), number % (width // 2) * 2, number).wait()


def slot_table(columns, act):
    rows = columns.shape[0]
    slots = columns[:, :act]
    here = slots < rows
    ids = jnp.arange(rows, dtype=jnp.int32)
    taken = jnp.any(slots[:, :, None] == ids, axis=1)
    count = jnp.sum(here.astype(jnp.int32), axis=1, keepdims=True)
    before = jnp.sum(
        (~taken[:, None, :] & (ids[None, :] < ids[:, None])[None]).astype(jnp.int32), axis=2
    )
    at = jnp.where(taken, -1, count + before)
    filled = jnp.sum(
        jnp.where(at[:, None, :] == jnp.arange(act, dtype=jnp.int32)[None, :, None], ids, 0), axis=2
    )
    order = jnp.where(here, slots, filled)
    return jnp.concatenate([order, here.astype(jnp.int32), taken.astype(jnp.int32)], axis=1)


def gather_local(x_blocks, columns):
    slab, width, edge, _ = x_blocks.shape
    rows = columns.shape[0]
    groups, chains, panels, lanes = (lax.axis_size(axis) for axis in AXES)
    last = chains - 1

    def index(g, place):
        z, x, c = place
        return (((g % groups) * chains + z) * panels + x) * lanes + c

    def move(block, cycles):
        pairs = [(cycle[i - 1], cycle[i]) for cycle in cycles for i in range(len(cycle))]
        busy = {a for a, _ in pairs}
        route = [(index(g, a), index(g, b)) for g in range(groups) for a, b in pairs]
        for z in range(chains):
            for x in range(panels):
                idle = [(z, x, c) for c in range(lanes) if (z, x, c) not in busy]
                for g in range(groups):
                    if len(idle) == lanes:
                        route += [(index(g, idle[c - 1]), index(g, idle[c])) for c in range(lanes)]
                    else:
                        route += [(index(g, a), index(g + 1, a)) for a in idle]
        return lax.ppermute(block, AXES, route)

    def swap(block):
        return move(block, [])

    def move_only(block, chains_of):
        pairs = [(chain[i], chain[i + 1]) for chain in chains_of for i in range(len(chain) - 1)]
        route = [(index(g, a), index(g, b)) for g in range(groups) for a, b in pairs]
        return lax.ppermute(block, AXES, route)

    up = [(z, 0, 0) for z in range(chains)] + [(last, 1, 0)]
    down = [(z, 0, 1) for z in reversed(range(chains))] + [(0, 1, 1)]
    first = [up + [(last, 1, 1)] + down + [(0, 1, 0)]]
    second = [up, down]
    near = [(z - 1, z + 1 if z < last else -1) for z in range(chains)]
    far = [(z - 2 if z >= 2 else -1, z + 2 if z + 2 < chains else -1) for z in range(chains)]
    far[0] = (last, far[0][1])
    far[last] = (far[last][0], 0)
    tables = (near, far)

    table = slot_table(columns, lanes * width)
    r1 = move(x_blocks, first)
    own_swap = swap(x_blocks)
    r2 = move_only(own_swap, [up, down])
    r1, table = lax.optimization_barrier((r1, table))
    r3 = move(r1, second)
    t1 = swap(r1)
    r4 = move(r2, second)
    t2 = swap(r2)

    order, own = rows * edge, slab * edge
    table = pltpu.with_memory_space_constraint(table, pltpu.SMEM)
    smem = pl.BlockSpec(memory_space=pltpu.SMEM)
    vmem = pl.BlockSpec(memory_space=pltpu.VMEM)
    params = pltpu.CompilerParams(vmem_limit_bytes=24 * 2**20)
    def held(*arrays):
        return [pltpu.with_memory_space_constraint(a, pltpu.VMEM) for a in arrays]

    high, low, left, part = pl.pallas_call(
        functools.partial(early_kernel, tables),
        out_shape=[
            jax.ShapeDtypeStruct((order, order), jnp.bfloat16),
            jax.ShapeDtypeStruct((order, order), jnp.bfloat16),
            jax.ShapeDtypeStruct((2 * own, order), jnp.bfloat16),
            jax.ShapeDtypeStruct((own, order), jnp.float32),
        ],
        in_specs=[smem] + [pl.BlockSpec(memory_space=pltpu.HBM)] + [vmem] * 6,
        out_specs=[vmem] * 4,
        scratch_shapes=[pltpu.VMEM(x_blocks.shape, jnp.float32), pltpu.SemaphoreType.DMA],
        compiler_params=params,
        name="early",
    )(table, pltpu.with_memory_space_constraint(x_blocks, pltpu.HBM), own_swap, r1, r2, t1, t2, r3)
    t3 = swap(r3)
    r4, part = lax.optimization_barrier((r4, part))
    t4 = swap(r4)
    dense = [jax.ShapeDtypeStruct(a.shape, a.dtype) for a in (high, low, part)]
    high, low, part = pl.pallas_call(
        functools.partial(middle_kernel, tables),
        out_shape=dense,
        in_specs=[smem] + [vmem] * 6,
        out_specs=[vmem] * 3,
        input_output_aliases={3: 0, 4: 1, 6: 2},
        compiler_params=params,
        name="middle",
    )(table, r4, t3, *held(high, low, left, part))
    out, _, _, _ = pl.pallas_call(
        functools.partial(late_kernel, tables),
        out_shape=[jax.ShapeDtypeStruct(x_blocks.shape, jnp.float32)] + dense,
        in_specs=[smem] + [vmem] * 5,
        out_specs=[pl.BlockSpec(memory_space=pltpu.HBM)] + [vmem] * 3,
        input_output_aliases={2: 1, 3: 2, 5: 3},
        scratch_shapes=[
            pltpu.VMEM((2 * own, order), jnp.bfloat16),
            pltpu.VMEM(x_blocks.shape, jnp.float32),
            pltpu.SemaphoreType.DMA((slab * width // 2,)),
        ],
        compiler_params=params,
        name="late",
    )(table, t4, *held(high, low, left, part))
    return out


def local(x_blocks, columns):
    slab, width, edge, _ = x_blocks.shape
    rows, slots = columns.shape
    _, chains, panels, lanes = (lax.axis_size(axis) for axis in AXES)
    full = rows <= slots and rows == lanes * width and width % 2 == 0
    if full and rows <= 8 and edge % 128 == 0 and panels >= 2 and lanes == 2 and chains == 4:
        return gather_local(x_blocks, columns)
    return ring_local(x_blocks, columns)


def solution(mesh):
    placed = (P(("groups", "blk"), ("panel", "depth"), None, None), P("groups", None))
    return jax.shard_map(
        local,
        mesh=mesh,
        in_specs=placed,
        out_specs=P(("groups", "blk"), ("panel", "depth"), None, None),
        check_vma=False,
    )
```

```python
import functools

import jax
import jax.numpy as jnp
from jax import lax
from jax.experimental import pallas as pl
from jax.experimental.pallas import tpu as pltpu
from jax.sharding import PartitionSpec as P

precise = lax.Precision.HIGHEST
AXES = ("groups", "blk", "panel", "depth")


def shifted(block, axis, distance):
    devices = range(lax.axis_size(axis))
    route = [((i - distance) % len(devices), i) for i in devices]
    return lax.ppermute(block, axis, route)


def slot_gather(blocks):
    return lax.all_gather(blocks, ("panel", "depth"), axis=1, tiled=True)


def slot_reduce(partial_value):
    return lax.psum_scatter(partial_value, ("panel", "depth"), scatter_dimension=1, tiled=True)


def rotate_one(incoming):
    return shifted(incoming, "blk", 1)


def ring_local(x_blocks, columns):
    slab_rows = x_blocks.shape[0]
    width_slots = x_blocks.shape[1]
    edge = x_blocks.shape[2]
    order_rows = columns.shape[0]
    all_slots = columns.shape[1]
    cycle_size = lax.axis_size("blk")
    cycle_place = lax.axis_index("blk")
    anchor = jnp.int32(0)
    first_own = cycle_place * slab_rows
    slot_first = lax.axis_index(("panel", "depth")) * width_slots
    my_cols = lax.dynamic_slice(columns, (first_own, anchor), (slab_rows, all_slots))
    own_cols = lax.dynamic_slice(my_cols, (anchor, slot_first), (slab_rows, width_slots))
    x_own = jnp.where((own_cols < order_rows)[:, :, None, None], x_blocks, jnp.float32(0.0))
    out_present = my_cols < order_rows
    empty = jnp.zeros((slab_rows, all_slots, edge, edge), jnp.float32)

    def contribute(partial_value, left_rows, incoming, source):
        group = incoming.shape[0]
        first_row = source * group
        their_cols = lax.dynamic_slice(columns, (first_row, slot_first), (group, width_slots))
        row_ids = first_row + jnp.arange(group, dtype=jnp.int32)
        selector = (my_cols[:, None, :] == row_ids[None, :, None]).astype(jnp.float32)
        picked = jnp.einsum("irs,isab->irab", selector, left_rows, precision=precise)
        products = jnp.einsum("irab,rubc->iruac", picked, incoming, precision=precise)
        targets = (their_cols[None, None, :, :] == my_cols[:, :, None, None]) & out_present[
            :, :, None, None
        ]
        placed = jnp.einsum(
            "isru,iruac->isac", targets.astype(jnp.float32), products, precision=precise
        )
        return partial_value + placed

    def one_way(left_rows, stored):

        def advance(offset, state):
            partial_value, incoming, stored = state
            source = (cycle_place - offset) % cycle_size
            partial_value = contribute(partial_value, left_rows, incoming, source)
            return (partial_value, rotate_one(incoming), stored)

        partial_value, incoming, stored = lax.fori_loop(
            0, cycle_size - 1, advance, (empty, x_own, stored)
        )
        source = (cycle_place + 1) % cycle_size
        return (contribute(partial_value, left_rows, incoming, source), stored)

    stored = jnp.zeros((1,), jnp.float32)
    left_first = slot_gather(x_own)
    partial_value, stored = one_way(left_first, stored)
    squared = slot_reduce(partial_value)
    left_second = slot_gather(squared)
    partial_value, stored = one_way(left_second, stored)
    cubed = slot_reduce(partial_value)
    return 3.0 * squared - 2.0 * cubed


def split(value):
    high = value.astype(jnp.bfloat16)
    low = (value - high.astype(jnp.float32)).astype(jnp.bfloat16)
    return high, low


def dot(left, right):
    return jnp.dot(left, right, preferred_element_type=jnp.float32)


def stacked_dot(left, high, low):
    half = left.shape[0] // 2
    both = dot(left, high)
    return both[:half] + (both[half:] + dot(left[:half], low))


def lookup(table, place, lane):
    found = jnp.int32(-1)
    for z, entries in enumerate(table):
        for c, entry in enumerate(entries):
            found = jnp.where((place == z) & (lane == c), entry, found)
    return found


def store_row(blocks, row, group, table_ref, high, low, own=None, own_row=0):
    width, edge, _ = blocks.shape
    act = 2 * width
    at = pl.ds(pl.multiple_of(row * edge, edge), edge)
    for w in range(width):
        slot = group * width + w
        col = pl.ds(pl.multiple_of(table_ref[row, slot] * edge, edge), edge)
        block = jnp.where(table_ref[row, act + slot] > 0, blocks[w], 0.0)
        block_high, block_low = split(block)
        high[at, col] = block_high
        low[at, col] = block_low
        if own is not None:
            own[pl.ds(own_row * edge, edge), col] = block_high
            own[pl.ds((own_row + 2) * edge, edge), col] = block_low


def store_piece(piece, code, sender, table_ref, high, low):
    @pl.when(code >= 0)
    def _():
        part = code % 4
        row = code // 4 * 2 + part % 2
        group = jnp.where(part < 2, sender, 1 - sender)
        store_row(piece.at[0], row, group, table_ref, high, low)


def add_rows(first, depth, left, high, low, part_ref):
    rows = pl.ds(pl.multiple_of(first, depth), depth)
    tile = 256
    for n in range(part_ref.shape[1] // tile):
        cols = pl.ds(n * tile, tile)
        part_ref[:, cols] += stacked_dot(left[:, rows], high[rows, cols], low[rows, cols])


def add_plane(plane, left, high, low, part_ref):
    depth = part_ref.shape[0]

    @pl.when(plane >= 0)
    def _():
        add_rows(plane * depth, depth, left, high, low, part_ref)


def store_pieces(pieces, codes, place, lane, table_ref, high, low):
    for (received, swapped), table in zip(pieces, codes):
        store_piece(received, lookup(table, place, lane), lane, table_ref, high, low)
        store_piece(swapped, lookup(table, place, 1 - lane), 1 - lane, table_ref, high, low)


def early_kernel(tables, table_ref, own_hbm, s0, s1, *refs):
    near, _, _, codes = tables
    pieces, (high, low, left, part_ref, own_ref, own_sem) = refs[:-6], refs[-6:]
    place, lane = lax.axis_index("blk"), lax.axis_index("depth")
    own_copy = pltpu.make_async_copy(own_hbm, own_ref, own_sem)
    own_copy.start()
    part_ref[...] = jnp.zeros_like(part_ref)
    for r, swapped in enumerate((s0, s1)):
        store_row(swapped.at[0], place * 2 + r, 1 - lane, table_ref, high, low, left, r)
    pairs = list(zip(pieces[::2], pieces[1::2]))
    store_pieces(pairs, codes[: len(pairs)], place, lane, table_ref, high, low)
    own_copy.wait()
    for r in range(2):
        store_row(own_ref.at[r], place * 2 + r, lane, table_ref, high, low, left, r)
    for plane in (place, lookup(near, place, lane), lookup(near, place, 1 - lane)):
        add_plane(plane, left, high, low, part_ref)


def middle_kernel(tables, table_ref, *refs):
    _, far, helped, codes = tables
    pieces, (_, _, left, _, high, low, part_ref) = refs[:-7], refs[-7:]
    place, lane = lax.axis_index("blk"), lax.axis_index("depth")
    pairs = list(zip(pieces[::2], pieces[1::2]))
    store_pieces(pairs, codes[-1 - len(pairs) : -1], place, lane, table_ref, high, low)
    edge = part_ref.shape[0] // 2
    add_plane(lookup(helped, place, lane), left, high, low, part_ref)
    add_rows(lookup(far, place, lane) * 2 * edge, edge, left, high, low, part_ref)


def late_kernel(
    tables, table_ref, r8, t8, high_in, low_in, left, part_in,
    out_hbm, high, low, square, square_parts, out_ref, out_sem,
):
    _, far, _, codes = tables
    place, lane = lax.axis_index("blk"), lax.axis_index("depth")
    group = lax.axis_index("panel") * 2 + lane
    slab, width, edge, _ = out_ref.shape
    act = 2 * width
    received = lookup(codes[-1], place, lane) >= 0
    last_row = lookup(far, place, lane) * 2 + 1
    store_row(
        jnp.where(received, r8[0], t8[0]),
        last_row,
        jnp.where(received, 1 - lane, lane),
        table_ref,
        high,
        low,
    )
    add_rows(last_row * edge, edge, left, high, low, square)
    for r in range(slab):
        for c in range(square.shape[1] // edge):
            kept = table_ref[place * slab + r, 2 * act + c] > 0
            col = pl.ds(c * edge, edge)
            block = jnp.where(kept, square[pl.ds(r * edge, edge), col], 0.0)
            block_high, block_low = split(block)
            square_parts[pl.ds(2 * r * edge, edge), col] = block_high
            square_parts[pl.ds((2 * r + 1) * edge, edge), col] = block_low
    copies = []
    for r in range(slab):
        row = place * slab + r
        left_parts = square_parts[pl.ds(2 * r * edge, 2 * edge), :]
        for w in range(0, width, 2):
            slots = [jnp.minimum(group * width + w + k, act - 1) for k in range(2)]
            cols = [
                pl.ds(pl.multiple_of(table_ref[row, slot] * edge, edge), edge) for slot in slots
            ]
            cube = stacked_dot(
                left_parts,
                jnp.concatenate([high[:, col] for col in cols], axis=1),
                jnp.concatenate([low[:, col] for col in cols], axis=1),
            )
            for k in range(2):
                there = (group * width + w + k < act) & (table_ref[row, act + slots[k]] > 0)
                value = 3.0 * square[pl.ds(r * edge, edge), cols[k]]
                value = value - 2.0 * cube[:, k * edge : (k + 1) * edge]
                out_ref[r, w + k] = jnp.where(there, value, 0.0)
            ready = (r, pl.ds(w, 2))
            copies.append(
                pltpu.make_async_copy(out_ref.at[ready], out_hbm.at[ready], out_sem.at[len(copies)])
            )
            copies[-1].start()
    for copy in copies:
        copy.wait()


def slot_table(columns, act):
    rows = columns.shape[0]
    slots = columns[:, :act]
    here = slots < rows
    ids = jnp.arange(rows, dtype=jnp.int32)
    taken = jnp.any(slots[:, :, None] == ids, axis=1)
    count = jnp.sum(here.astype(jnp.int32), axis=1, keepdims=True)
    before = jnp.sum(
        (~taken[:, None, :] & (ids[None, :] < ids[:, None])[None]).astype(jnp.int32), axis=2
    )
    at = jnp.where(taken, -1, count + before)
    filled = jnp.sum(
        jnp.where(at[:, None, :] == jnp.arange(act, dtype=jnp.int32)[None, :, None], ids, 0), axis=2
    )
    order = jnp.where(here, slots, filled)
    return jnp.concatenate([order, here.astype(jnp.int32), taken.astype(jnp.int32)], axis=1)


def gather_local(x_blocks, columns):
    slab, width, edge, _ = x_blocks.shape
    rows = columns.shape[0]
    groups, chains, panels, lanes = (lax.axis_size(axis) for axis in AXES)
    last = chains - 1

    def index(g, place):
        z, x, c = place
        return (((g % groups) * chains + z) * panels + x) * lanes + c

    def move(block, cycles):
        pairs = [(cycle[i - 1], cycle[i]) for cycle in cycles for i in range(len(cycle))]
        busy = {a for a, _ in pairs}
        route = [(index(g, a), index(g, b)) for g in range(groups) for a, b in pairs]
        for z in range(chains):
            for x in range(panels):
                idle = [(z, x, c) for c in range(lanes) if (z, x, c) not in busy]
                for g in range(groups):
                    if len(idle) == lanes:
                        route += [(index(g, idle[c - 1]), index(g, idle[c])) for c in range(lanes)]
                    else:
                        route += [(index(g, a), index(g + 1, a)) for a in idle]
        return lax.ppermute(block, AXES, route)

    def swap(block):
        return move(block, [])

    up = [(z, 0, 0) for z in range(chains)]
    down = [(z, 0, 1) for z in reversed(range(chains))]
    up_helper, down_helper = (last, 1, 0), (0, 1, 1)
    crossing = [up + [up_helper, (last, 1, 1)] + down + [down_helper, (0, 1, 0)]]
    helping = [up + [up_helper], down + [down_helper]]
    inside = [up + down]
    here = tuple(lax.axis_index(axis) for axis in AXES[1:])
    helper = functools.reduce(
        jnp.logical_or,
        [
            functools.reduce(jnp.logical_and, [i == j for i, j in zip(here, place)])
            for place in (up_helper, down_helper)
        ],
    )

    def help_with(received, block):
        return jnp.where(helper, received, block)

    codes = []
    for hop in range(8):
        table = []
        for z in range(chains):
            below, above = z - 1 - hop // 4, z + 1 + hop // 4
            table.append(
                [
                    below * 4 + hop % 4 if below >= 0 else -1,
                    above * 4 + hop % 4 if above < chains else -1,
                ]
            )
        if 2 <= hop < 6:
            table[0][0] = last * 4 + hop - 2
            table[last][1] = hop - 2
        codes.append(table)
    near = [(z - 1, z + 1 if z < last else -1) for z in range(chains)]
    far = [((z + 2) % chains,) * 2 for z in range(chains)]
    helped = [(last if z == 0 else 0 if z == last else -1,) * 2 for z in range(chains)]
    tables = (near, far, helped, codes)

    table = slot_table(columns, lanes * width)
    x0, x1 = x_blocks[:1], x_blocks[1:]
    r1, r2 = move(x0, crossing), move(x1, crossing)
    s0, s1 = swap(x0), swap(x1)
    r3 = move(help_with(r1, s0), helping)
    r4 = move(help_with(r2, s1), helping)
    r5 = move(help_with(r3, r1), helping)
    r6 = move(help_with(r4, r2), helping)
    r7, r8 = move(r3, inside), move(r4, inside)
    t1, t2, t3, t4, t5, t6, t7 = [swap(r) for r in (r1, r2, r3, r4, r5, r6, r7)]

    order, own = rows * edge, slab * edge
    table = pltpu.with_memory_space_constraint(table, pltpu.SMEM)
    smem = pl.BlockSpec(memory_space=pltpu.SMEM)
    vmem = pl.BlockSpec(memory_space=pltpu.VMEM)
    params = pltpu.CompilerParams(vmem_limit_bytes=24 * 2**20)
    def held(*arrays):
        return [pltpu.with_memory_space_constraint(a, pltpu.VMEM) for a in arrays]

    near_pieces = (r1, t1, r2, t2, r3, t3, r4, t4)
    high, low, left, part = pl.pallas_call(
        functools.partial(early_kernel, tables),
        out_shape=[
            jax.ShapeDtypeStruct((order, order), jnp.bfloat16),
            jax.ShapeDtypeStruct((order, order), jnp.bfloat16),
            jax.ShapeDtypeStruct((2 * own, order), jnp.bfloat16),
            jax.ShapeDtypeStruct((own, order), jnp.float32),
        ],
        in_specs=[smem, pl.BlockSpec(memory_space=pltpu.HBM)] + [vmem] * (2 + len(near_pieces)),
        out_specs=[vmem] * 4,
        scratch_shapes=[pltpu.VMEM(x_blocks.shape, jnp.float32), pltpu.SemaphoreType.DMA],
        compiler_params=params,
        name="early",
    )(table, pltpu.with_memory_space_constraint(x_blocks, pltpu.HBM), s0, s1, *near_pieces)
    r8, part = lax.optimization_barrier((r8, part))
    t8 = swap(r8)
    far_pieces = (r5, t5, r6, t6, r7, t7)
    dense = [jax.ShapeDtypeStruct(a.shape, a.dtype) for a in (high, low, part)]
    first = 1 + len(far_pieces)
    high, low, part = pl.pallas_call(
        functools.partial(middle_kernel, tables),
        out_shape=dense,
        in_specs=[smem] + [vmem] * (4 + len(far_pieces)),
        out_specs=[vmem] * 3,
        input_output_aliases={first: 0, first + 1: 1, first + 3: 2},
        compiler_params=params,
        name="middle",
    )(table, *far_pieces, *held(high, low, left, part))
    out, _, _, _ = pl.pallas_call(
        functools.partial(late_kernel, tables),
        out_shape=[jax.ShapeDtypeStruct(x_blocks.shape, jnp.float32)] + dense,
        in_specs=[smem] + [vmem] * 6,
        out_specs=[pl.BlockSpec(memory_space=pltpu.HBM)] + [vmem] * 3,
        input_output_aliases={3: 1, 4: 2, 6: 3},
        scratch_shapes=[
            pltpu.VMEM((2 * own, order), jnp.bfloat16),
            pltpu.VMEM(x_blocks.shape, jnp.float32),
            pltpu.SemaphoreType.DMA((slab * width // 2,)),
        ],
        compiler_params=params,
        name="late",
    )(table, r8, t8, *held(high, low, left, part))
    return out


def local(x_blocks, columns):
    slab, width, edge, _ = x_blocks.shape
    rows, slots = columns.shape
    _, chains, panels, lanes = (lax.axis_size(axis) for axis in AXES)
    full = rows <= slots and rows == lanes * width and width % 2 == 0
    if full and rows <= 8 and slab == 2 and edge == 128 and panels >= 2 and lanes == 2 and chains == 4:
        return gather_local(x_blocks, columns)
    return ring_local(x_blocks, columns)


def solution(mesh):
    placed = (P(("groups", "blk"), ("panel", "depth"), None, None), P("groups", None))
    return jax.shard_map(
        local,
        mesh=mesh,
        in_specs=placed,
        out_specs=P(("groups", "blk"), ("panel", "depth"), None, None),
        check_vma=False,
    )
```

```python
import functools

import jax
import jax.numpy as jnp
from jax import lax
from jax.experimental import pallas as pl
from jax.experimental.pallas import tpu as pltpu
from jax.sharding import PartitionSpec as P

precise = lax.Precision.HIGHEST
AXES = ("groups", "blk", "panel", "depth")


def shifted(block, axis, distance):
    devices = range(lax.axis_size(axis))
    route = [((i - distance) % len(devices), i) for i in devices]
    return lax.ppermute(block, axis, route)


def slot_gather(blocks):
    return lax.all_gather(blocks, ("panel", "depth"), axis=1, tiled=True)


def slot_reduce(partial_value):
    return lax.psum_scatter(partial_value, ("panel", "depth"), scatter_dimension=1, tiled=True)


def rotate_one(incoming):
    return shifted(incoming, "blk", 1)


def ring_local(x_blocks, columns):
    slab_rows = x_blocks.shape[0]
    width_slots = x_blocks.shape[1]
    edge = x_blocks.shape[2]
    order_rows = columns.shape[0]
    all_slots = columns.shape[1]
    cycle_size = lax.axis_size("blk")
    cycle_place = lax.axis_index("blk")
    anchor = jnp.int32(0)
    first_own = cycle_place * slab_rows
    slot_first = lax.axis_index(("panel", "depth")) * width_slots
    my_cols = lax.dynamic_slice(columns, (first_own, anchor), (slab_rows, all_slots))
    own_cols = lax.dynamic_slice(my_cols, (anchor, slot_first), (slab_rows, width_slots))
    x_own = jnp.where((own_cols < order_rows)[:, :, None, None], x_blocks, jnp.float32(0.0))
    out_present = my_cols < order_rows
    empty = jnp.zeros((slab_rows, all_slots, edge, edge), jnp.float32)

    def contribute(partial_value, left_rows, incoming, source):
        group = incoming.shape[0]
        first_row = source * group
        their_cols = lax.dynamic_slice(columns, (first_row, slot_first), (group, width_slots))
        row_ids = first_row + jnp.arange(group, dtype=jnp.int32)
        selector = (my_cols[:, None, :] == row_ids[None, :, None]).astype(jnp.float32)
        picked = jnp.einsum("irs,isab->irab", selector, left_rows, precision=precise)
        products = jnp.einsum("irab,rubc->iruac", picked, incoming, precision=precise)
        targets = (their_cols[None, None, :, :] == my_cols[:, :, None, None]) & out_present[
            :, :, None, None
        ]
        placed = jnp.einsum(
            "isru,iruac->isac", targets.astype(jnp.float32), products, precision=precise
        )
        return partial_value + placed

    def one_way(left_rows, stored):

        def advance(offset, state):
            partial_value, incoming, stored = state
            source = (cycle_place - offset) % cycle_size
            partial_value = contribute(partial_value, left_rows, incoming, source)
            return (partial_value, rotate_one(incoming), stored)

        partial_value, incoming, stored = lax.fori_loop(
            0, cycle_size - 1, advance, (empty, x_own, stored)
        )
        source = (cycle_place + 1) % cycle_size
        return (contribute(partial_value, left_rows, incoming, source), stored)

    stored = jnp.zeros((1,), jnp.float32)
    left_first = slot_gather(x_own)
    partial_value, stored = one_way(left_first, stored)
    squared = slot_reduce(partial_value)
    left_second = slot_gather(squared)
    partial_value, stored = one_way(left_second, stored)
    cubed = slot_reduce(partial_value)
    return 3.0 * squared - 2.0 * cubed


def split(value):
    high = value.astype(jnp.bfloat16)
    low = (value - high.astype(jnp.float32)).astype(jnp.bfloat16)
    return high, low


def dot(left, right):
    return jnp.dot(left, right, preferred_element_type=jnp.float32)


def stacked_dot(left, high, low):
    half = left.shape[0] // 2
    both = dot(left, high)
    return both[:half] + (both[half:] + dot(left[:half], low))


def lookup(table, place, lane):
    found = jnp.int32(-1)
    for z, entries in enumerate(table):
        for c, entry in enumerate(entries):
            found = jnp.where((place == z) & (lane == c), entry, found)
    return found


def store_piece(piece, plane, group, table_ref, high, low, own=None, slab=2, first=0):
    count, width, edge, _ = piece.shape
    act = 2 * width

    @pl.when(plane >= 0)
    def _():
        for r in range(count):
            row = plane * slab + first + r
            for w in range(width):
                slot = group * width + w
                col = pl.ds(pl.multiple_of(table_ref[row, slot] * edge, edge), edge)
                block = jnp.where(table_ref[row, act + slot] > 0, piece[r, w], 0.0)
                block_high, block_low = split(block)
                at = pl.ds(pl.multiple_of(row * edge, edge), edge)
                high[at, col] = block_high
                low[at, col] = block_low
                if own is not None:
                    own[pl.ds(r * edge, edge), col] = block_high
                    own[pl.ds((slab + r) * edge, edge), col] = block_low


def add_plane(plane, left, high, low, part_ref):
    depth, tile = part_ref.shape[0], 256

    @pl.when(plane >= 0)
    def _():
        rows = pl.ds(pl.multiple_of(plane * depth, depth), depth)
        for n in range(part_ref.shape[1] // tile):
            cols = pl.ds(n * tile, tile)
            part_ref[:, cols] += stacked_dot(left[:, rows], high[rows, cols], low[rows, cols])


def early_kernel(
    tables, table_ref, own_hbm, own_swap, r1, r2, t1, t2, r3,
    high, low, left, part_ref, own_ref, own_sem,
):
    place, lane = lax.axis_index("blk"), lax.axis_index("depth")
    near, far = tables
    own_copy = pltpu.make_async_copy(own_hbm, own_ref, own_sem)
    own_copy.start()
    here, there = lookup(near, place, lane), lookup(near, place, 1 - lane)
    part_ref[...] = jnp.zeros_like(part_ref)
    store_piece(own_swap, place, 1 - lane, table_ref, high, low, left)
    store_piece(r1, here, lane, table_ref, high, low)
    store_piece(r2, here, 1 - lane, table_ref, high, low)
    store_piece(t1, there, 1 - lane, table_ref, high, low)
    store_piece(t2, there, lane, table_ref, high, low)
    store_piece(r3, lookup(far, place, lane), lane, table_ref, high, low)
    own_copy.wait()
    store_piece(own_ref, place, lane, table_ref, high, low, left)
    for plane in (place, here, there):
        add_plane(plane, left, high, low, part_ref)


def middle_kernel(
    tables, table_ref, r4a, r4b, t3, t4a, high_in, low_in, left, part_in, high, low, part_ref
):
    place, lane = lax.axis_index("blk"), lax.axis_index("depth")
    far = tables[1]
    here, there = lookup(far, place, lane), lookup(far, place, 1 - lane)
    store_piece(t3, there, 1 - lane, table_ref, high, low)
    store_piece(r4a, here, 1 - lane, table_ref, high, low)
    store_piece(t4a, there, lane, table_ref, high, low)
    store_piece(r4b, here, 1 - lane, table_ref, high, low, first=1)
    add_plane(here, left, high, low, part_ref)


def late_kernel(
    tables, table_ref, t4b, high_in, low_in, left, part_in,
    out_hbm, high, low, square, square_parts, out_ref, out_sem,
):
    place, lane = lax.axis_index("blk"), lax.axis_index("depth")
    group = lax.axis_index("panel") * 2 + lane
    there = lookup(tables[1], place, 1 - lane)
    store_piece(t4b, there, lane, table_ref, high, low, first=1)
    add_plane(there, left, high, low, square)
    slab, width, edge, _ = out_ref.shape
    act = 2 * width
    for r in range(slab):
        for c in range(square.shape[1] // edge):
            kept = table_ref[place * slab + r, 2 * act + c] > 0
            col = pl.ds(c * edge, edge)
            block = jnp.where(kept, square[pl.ds(r * edge, edge), col], 0.0)
            block_high, block_low = split(block)
            square_parts[pl.ds(2 * r * edge, edge), col] = block_high
            square_parts[pl.ds((2 * r + 1) * edge, edge), col] = block_low
    copies = []
    for r in range(slab):
        row = place * slab + r
        left_parts = square_parts[pl.ds(2 * r * edge, 2 * edge), :]
        for w in range(0, width, 2):
            slots = [jnp.minimum(group * width + w + k, act - 1) for k in range(2)]
            cols = [
                pl.ds(pl.multiple_of(table_ref[row, slot] * edge, edge), edge) for slot in slots
            ]
            cube = stacked_dot(
                left_parts,
                jnp.concatenate([high[:, col] for col in cols], axis=1),
                jnp.concatenate([low[:, col] for col in cols], axis=1),
            )
            for k in range(2):
                there = (group * width + w + k < act) & (table_ref[row, act + slots[k]] > 0)
                value = 3.0 * square[pl.ds(r * edge, edge), cols[k]]
                value = value - 2.0 * cube[:, k * edge : (k + 1) * edge]
                out_ref[r, w + k] = jnp.where(there, value, 0.0)
            ready = (r, pl.ds(w, 2))
            copies.append(
                pltpu.make_async_copy(out_ref.at[ready], out_hbm.at[ready], out_sem.at[len(copies)])
            )
            copies[-1].start()
    for copy in copies:
        copy.wait()


def slot_table(columns, act):
    rows = columns.shape[0]
    slots = columns[:, :act]
    here = slots < rows
    ids = jnp.arange(rows, dtype=jnp.int32)
    taken = jnp.any(slots[:, :, None] == ids, axis=1)
    count = jnp.sum(here.astype(jnp.int32), axis=1, keepdims=True)
    before = jnp.sum(
        (~taken[:, None, :] & (ids[None, :] < ids[:, None])[None]).astype(jnp.int32), axis=2
    )
    at = jnp.where(taken, -1, count + before)
    filled = jnp.sum(
        jnp.where(at[:, None, :] == jnp.arange(act, dtype=jnp.int32)[None, :, None], ids, 0), axis=2
    )
    order = jnp.where(here, slots, filled)
    return jnp.concatenate([order, here.astype(jnp.int32), taken.astype(jnp.int32)], axis=1)


def gather_local(x_blocks, columns):
    slab, width, edge, _ = x_blocks.shape
    rows = columns.shape[0]
    groups, chains, panels, lanes = (lax.axis_size(axis) for axis in AXES)
    last = chains - 1

    def index(g, place):
        z, x, c = place
        return (((g % groups) * chains + z) * panels + x) * lanes + c

    def move(block, cycles):
        pairs = [(cycle[i - 1], cycle[i]) for cycle in cycles for i in range(len(cycle))]
        busy = {a for a, _ in pairs}
        route = [(index(g, a), index(g, b)) for g in range(groups) for a, b in pairs]
        for z in range(chains):
            for x in range(panels):
                idle = [(z, x, c) for c in range(lanes) if (z, x, c) not in busy]
                for g in range(groups):
                    if len(idle) == lanes:
                        route += [(index(g, idle[c - 1]), index(g, idle[c])) for c in range(lanes)]
                    else:
                        route += [(index(g, a), index(g + 1, a)) for a in idle]
        return lax.ppermute(block, AXES, route)

    def swap(block):
        return move(block, [])

    def move_only(block, chains_of):
        pairs = [(chain[i], chain[i + 1]) for chain in chains_of for i in range(len(chain) - 1)]
        route = [(index(g, a), index(g, b)) for g in range(groups) for a, b in pairs]
        return lax.ppermute(block, AXES, route)

    up = [(z, 0, 0) for z in range(chains)] + [(last, 1, 0)]
    down = [(z, 0, 1) for z in reversed(range(chains))] + [(0, 1, 1)]
    first = [up + [(last, 1, 1)] + down + [(0, 1, 0)]]
    second = [up, down]
    near = [(z - 1, z + 1 if z < last else -1) for z in range(chains)]
    far = [(z - 2 if z >= 2 else -1, z + 2 if z + 2 < chains else -1) for z in range(chains)]
    far[0] = (last, far[0][1])
    far[last] = (far[last][0], 0)
    tables = (near, far)

    table = slot_table(columns, lanes * width)
    r1 = move(x_blocks, first)
    own_swap = swap(x_blocks)
    r2 = move_only(own_swap, [up, down])
    r1, table = lax.optimization_barrier((r1, table))
    r3 = move(r1, second)
    t1 = swap(r1)
    r4a, r4b = move(r2[:1], second), move(r2[1:], second)
    t2 = swap(r2)

    order, own = rows * edge, slab * edge
    table = pltpu.with_memory_space_constraint(table, pltpu.SMEM)
    smem = pl.BlockSpec(memory_space=pltpu.SMEM)
    vmem = pl.BlockSpec(memory_space=pltpu.VMEM)
    params = pltpu.CompilerParams(vmem_limit_bytes=24 * 2**20)
    def held(*arrays):
        return [pltpu.with_memory_space_constraint(a, pltpu.VMEM) for a in arrays]

    high, low, left, part = pl.pallas_call(
        functools.partial(early_kernel, tables),
        out_shape=[
            jax.ShapeDtypeStruct((order, order), jnp.bfloat16),
            jax.ShapeDtypeStruct((order, order), jnp.bfloat16),
            jax.ShapeDtypeStruct((2 * own, order), jnp.bfloat16),
            jax.ShapeDtypeStruct((own, order), jnp.float32),
        ],
        in_specs=[smem] + [pl.BlockSpec(memory_space=pltpu.HBM)] + [vmem] * 6,
        out_specs=[vmem] * 4,
        scratch_shapes=[pltpu.VMEM(x_blocks.shape, jnp.float32), pltpu.SemaphoreType.DMA],
        compiler_params=params,
        name="early",
    )(table, pltpu.with_memory_space_constraint(x_blocks, pltpu.HBM), own_swap, r1, r2, t1, t2, r3)
    t3 = swap(r3)
    r4a, part = lax.optimization_barrier((r4a, part))
    t4a = swap(r4a)
    r4b, t4a = lax.optimization_barrier((r4b, t4a))
    t4b = swap(r4b)
    dense = [jax.ShapeDtypeStruct(a.shape, a.dtype) for a in (high, low, part)]
    high, low, part = pl.pallas_call(
        functools.partial(middle_kernel, tables),
        out_shape=dense,
        in_specs=[smem] + [vmem] * 8,
        out_specs=[vmem] * 3,
        input_output_aliases={5: 0, 6: 1, 8: 2},
        compiler_params=params,
        name="middle",
    )(table, r4a, r4b, t3, t4a, *held(high, low, left, part))
    out, _, _, _ = pl.pallas_call(
        functools.partial(late_kernel, tables),
        out_shape=[jax.ShapeDtypeStruct(x_blocks.shape, jnp.float32)] + dense,
        in_specs=[smem] + [vmem] * 5,
        out_specs=[pl.BlockSpec(memory_space=pltpu.HBM)] + [vmem] * 3,
        input_output_aliases={2: 1, 3: 2, 5: 3},
        scratch_shapes=[
            pltpu.VMEM((2 * own, order), jnp.bfloat16),
            pltpu.VMEM(x_blocks.shape, jnp.float32),
            pltpu.SemaphoreType.DMA((slab * width // 2,)),
        ],
        compiler_params=params,
        name="late",
    )(table, t4b, *held(high, low, left, part))
    return out


def local(x_blocks, columns):
    slab, width, edge, _ = x_blocks.shape
    rows, slots = columns.shape
    _, chains, panels, lanes = (lax.axis_size(axis) for axis in AXES)
    full = rows <= slots and rows == lanes * width and width % 2 == 0
    if full and rows <= 8 and slab == 2 and edge == 128 and panels >= 2 and lanes == 2 and chains == 4:
        return gather_local(x_blocks, columns)
    return ring_local(x_blocks, columns)


def solution(mesh):
    placed = (P(("groups", "blk"), ("panel", "depth"), None, None), P("groups", None))
    return jax.shard_map(
        local,
        mesh=mesh,
        in_specs=placed,
        out_specs=P(("groups", "blk"), ("panel", "depth"), None, None),
        check_vma=False,
    )
```

```python
import functools

import jax
import jax.numpy as jnp
from jax import lax
from jax.experimental import pallas as pl
from jax.experimental.pallas import tpu as pltpu
from jax.sharding import PartitionSpec as P

precise = lax.Precision.HIGHEST
AXES = ("groups", "blk", "panel", "depth")


def shifted(block, axis, distance):
    devices = range(lax.axis_size(axis))
    route = [((i - distance) % len(devices), i) for i in devices]
    return lax.ppermute(block, axis, route)


def slot_gather(blocks):
    return lax.all_gather(blocks, ("panel", "depth"), axis=1, tiled=True)


def slot_reduce(partial_value):
    return lax.psum_scatter(partial_value, ("panel", "depth"), scatter_dimension=1, tiled=True)


def rotate_one(incoming):
    return shifted(incoming, "blk", 1)


def ring_local(x_blocks, columns):
    slab_rows = x_blocks.shape[0]
    width_slots = x_blocks.shape[1]
    edge = x_blocks.shape[2]
    order_rows = columns.shape[0]
    all_slots = columns.shape[1]
    cycle_size = lax.axis_size("blk")
    cycle_place = lax.axis_index("blk")
    anchor = jnp.int32(0)
    first_own = cycle_place * slab_rows
    slot_first = lax.axis_index(("panel", "depth")) * width_slots
    my_cols = lax.dynamic_slice(columns, (first_own, anchor), (slab_rows, all_slots))
    own_cols = lax.dynamic_slice(my_cols, (anchor, slot_first), (slab_rows, width_slots))
    x_own = jnp.where((own_cols < order_rows)[:, :, None, None], x_blocks, jnp.float32(0.0))
    out_present = my_cols < order_rows
    empty = jnp.zeros((slab_rows, all_slots, edge, edge), jnp.float32)

    def contribute(partial_value, left_rows, incoming, source):
        group = incoming.shape[0]
        first_row = source * group
        their_cols = lax.dynamic_slice(columns, (first_row, slot_first), (group, width_slots))
        row_ids = first_row + jnp.arange(group, dtype=jnp.int32)
        selector = (my_cols[:, None, :] == row_ids[None, :, None]).astype(jnp.float32)
        picked = jnp.einsum("irs,isab->irab", selector, left_rows, precision=precise)
        products = jnp.einsum("irab,rubc->iruac", picked, incoming, precision=precise)
        targets = (their_cols[None, None, :, :] == my_cols[:, :, None, None]) & out_present[
            :, :, None, None
        ]
        placed = jnp.einsum(
            "isru,iruac->isac", targets.astype(jnp.float32), products, precision=precise
        )
        return partial_value + placed

    def one_way(left_rows, stored):

        def advance(offset, state):
            partial_value, incoming, stored = state
            source = (cycle_place - offset) % cycle_size
            partial_value = contribute(partial_value, left_rows, incoming, source)
            return (partial_value, rotate_one(incoming), stored)

        partial_value, incoming, stored = lax.fori_loop(
            0, cycle_size - 1, advance, (empty, x_own, stored)
        )
        source = (cycle_place + 1) % cycle_size
        return (contribute(partial_value, left_rows, incoming, source), stored)

    stored = jnp.zeros((1,), jnp.float32)
    left_first = slot_gather(x_own)
    partial_value, stored = one_way(left_first, stored)
    squared = slot_reduce(partial_value)
    left_second = slot_gather(squared)
    partial_value, stored = one_way(left_second, stored)
    cubed = slot_reduce(partial_value)
    return 3.0 * squared - 2.0 * cubed


def split(value):
    high = value.astype(jnp.bfloat16)
    low = (value - high.astype(jnp.float32)).astype(jnp.bfloat16)
    return high, low


def dot(left, right):
    return jnp.dot(left, right, preferred_element_type=jnp.float32)


def stacked_dot(left, high, low):
    half = left.shape[0] // 2
    both = dot(left, high)
    return both[:half] + (both[half:] + dot(left[:half], low))


def lookup(table, place, lane):
    found = jnp.int32(-1)
    for z, entries in enumerate(table):
        for c, entry in enumerate(entries):
            found = jnp.where((place == z) & (lane == c), entry, found)
    return found


def store_piece(piece, plane, group, table_ref, high, low, own=None, slab=2, first=0):
    count, width, edge, _ = piece.shape
    act = 2 * width

    @pl.when(plane >= 0)
    def _():
        for r in range(count):
            row = plane * slab + first + r
            for w in range(width):
                slot = group * width + w
                col = pl.ds(pl.multiple_of(table_ref[row, slot] * edge, edge), edge)
                block = jnp.where(table_ref[row, act + slot] > 0, piece[r, w], 0.0)
                block_high, block_low = split(block)
                at = pl.ds(pl.multiple_of(row * edge, edge), edge)
                high[at, col] = block_high
                low[at, col] = block_low
                if own is not None:
                    own[pl.ds(r * edge, edge), col] = block_high
                    own[pl.ds((slab + r) * edge, edge), col] = block_low


def add_plane(plane, left, high, low, part_ref):
    depth, tile = part_ref.shape[0], 256

    @pl.when(plane >= 0)
    def _():
        rows = pl.ds(pl.multiple_of(plane * depth, depth), depth)
        for n in range(part_ref.shape[1] // tile):
            cols = pl.ds(n * tile, tile)
            part_ref[:, cols] += stacked_dot(left[:, rows], high[rows, cols], low[rows, cols])


def early_kernel(
    tables, table_ref, own_hbm, own_swap, r1, r2a, r2b, t1, t2a, t2b, r3,
    high, low, left, part_ref, own_ref, own_sem,
):
    place, lane = lax.axis_index("blk"), lax.axis_index("depth")
    near, far = tables
    own_copy = pltpu.make_async_copy(own_hbm, own_ref, own_sem)
    own_copy.start()
    here, there = lookup(near, place, lane), lookup(near, place, 1 - lane)
    part_ref[...] = jnp.zeros_like(part_ref)
    store_piece(own_swap, place, 1 - lane, table_ref, high, low, left)
    store_piece(r1, here, lane, table_ref, high, low)
    store_piece(t1, there, 1 - lane, table_ref, high, low)
    for r, (received, swapped) in enumerate(((r2a, t2a), (r2b, t2b))):
        store_piece(received, here, 1 - lane, table_ref, high, low, first=r)
        store_piece(swapped, there, lane, table_ref, high, low, first=r)
    store_piece(r3, lookup(far, place, lane), lane, table_ref, high, low)
    own_copy.wait()
    store_piece(own_ref, place, lane, table_ref, high, low, left)
    for plane in (place, here, there):
        add_plane(plane, left, high, low, part_ref)


def middle_kernel(
    tables, table_ref, r4a, r4b, t3, t4a, high_in, low_in, left, part_in, high, low, part_ref
):
    place, lane = lax.axis_index("blk"), lax.axis_index("depth")
    far = tables[1]
    here, there = lookup(far, place, lane), lookup(far, place, 1 - lane)
    store_piece(t3, there, 1 - lane, table_ref, high, low)
    store_piece(r4a, here, 1 - lane, table_ref, high, low)
    store_piece(t4a, there, lane, table_ref, high, low)
    store_piece(r4b, here, 1 - lane, table_ref, high, low, first=1)
    add_plane(here, left, high, low, part_ref)


def late_kernel(
    tables, table_ref, t4b, high_in, low_in, left, part_in,
    out_hbm, high, low, square, square_parts, out_ref, out_sem,
):
    place, lane = lax.axis_index("blk"), lax.axis_index("depth")
    group = lax.axis_index("panel") * 2 + lane
    there = lookup(tables[1], place, 1 - lane)
    store_piece(t4b, there, lane, table_ref, high, low, first=1)
    add_plane(there, left, high, low, square)
    slab, width, edge, _ = out_ref.shape
    act = 2 * width
    for r in range(slab):
        for c in range(square.shape[1] // edge):
            kept = table_ref[place * slab + r, 2 * act + c] > 0
            col = pl.ds(c * edge, edge)
            block = jnp.where(kept, square[pl.ds(r * edge, edge), col], 0.0)
            block_high, block_low = split(block)
            square_parts[pl.ds(2 * r * edge, edge), col] = block_high
            square_parts[pl.ds((2 * r + 1) * edge, edge), col] = block_low
    copies = []
    for r in range(slab):
        row = place * slab + r
        left_parts = square_parts[pl.ds(2 * r * edge, 2 * edge), :]
        for w in range(0, width, 2):
            slots = [jnp.minimum(group * width + w + k, act - 1) for k in range(2)]
            cols = [
                pl.ds(pl.multiple_of(table_ref[row, slot] * edge, edge), edge) for slot in slots
            ]
            cube = stacked_dot(
                left_parts,
                jnp.concatenate([high[:, col] for col in cols], axis=1),
                jnp.concatenate([low[:, col] for col in cols], axis=1),
            )
            for k in range(2):
                there = (group * width + w + k < act) & (table_ref[row, act + slots[k]] > 0)
                value = 3.0 * square[pl.ds(r * edge, edge), cols[k]]
                value = value - 2.0 * cube[:, k * edge : (k + 1) * edge]
                out_ref[r, w + k] = jnp.where(there, value, 0.0)
            ready = (r, pl.ds(w, 2))
            copies.append(
                pltpu.make_async_copy(out_ref.at[ready], out_hbm.at[ready], out_sem.at[len(copies)])
            )
            copies[-1].start()
    for copy in copies:
        copy.wait()


def slot_table(columns, act):
    rows = columns.shape[0]
    slots = columns[:, :act]
    here = slots < rows
    ids = jnp.arange(rows, dtype=jnp.int32)
    taken = jnp.any(slots[:, :, None] == ids, axis=1)
    count = jnp.sum(here.astype(jnp.int32), axis=1, keepdims=True)
    before = jnp.sum(
        (~taken[:, None, :] & (ids[None, :] < ids[:, None])[None]).astype(jnp.int32), axis=2
    )
    at = jnp.where(taken, -1, count + before)
    filled = jnp.sum(
        jnp.where(at[:, None, :] == jnp.arange(act, dtype=jnp.int32)[None, :, None], ids, 0), axis=2
    )
    order = jnp.where(here, slots, filled)
    return jnp.concatenate([order, here.astype(jnp.int32), taken.astype(jnp.int32)], axis=1)


def gather_local(x_blocks, columns):
    slab, width, edge, _ = x_blocks.shape
    rows = columns.shape[0]
    groups, chains, panels, lanes = (lax.axis_size(axis) for axis in AXES)
    last = chains - 1

    def index(g, place):
        z, x, c = place
        return (((g % groups) * chains + z) * panels + x) * lanes + c

    def move(block, cycles):
        pairs = [(cycle[i - 1], cycle[i]) for cycle in cycles for i in range(len(cycle))]
        busy = {a for a, _ in pairs}
        route = [(index(g, a), index(g, b)) for g in range(groups) for a, b in pairs]
        for z in range(chains):
            for x in range(panels):
                idle = [(z, x, c) for c in range(lanes) if (z, x, c) not in busy]
                for g in range(groups):
                    if len(idle) == lanes:
                        route += [(index(g, idle[c - 1]), index(g, idle[c])) for c in range(lanes)]
                    else:
                        route += [(index(g, a), index(g + 1, a)) for a in idle]
        return lax.ppermute(block, AXES, route)

    def swap(block):
        return move(block, [])

    def move_only(block, chains_of):
        pairs = [(chain[i], chain[i + 1]) for chain in chains_of for i in range(len(chain) - 1)]
        route = [(index(g, a), index(g, b)) for g in range(groups) for a, b in pairs]
        return lax.ppermute(block, AXES, route)

    up = [(z, 0, 0) for z in range(chains)] + [(last, 1, 0)]
    down = [(z, 0, 1) for z in reversed(range(chains))] + [(0, 1, 1)]
    first = [up + [(last, 1, 1)] + down + [(0, 1, 0)]]
    second = [up, down]
    near = [(z - 1, z + 1 if z < last else -1) for z in range(chains)]
    far = [(z - 2 if z >= 2 else -1, z + 2 if z + 2 < chains else -1) for z in range(chains)]
    far[0] = (last, far[0][1])
    far[last] = (far[last][0], 0)
    tables = (near, far)

    table = slot_table(columns, lanes * width)
    x_late, columns = lax.optimization_barrier((x_blocks, columns))
    r1 = move(x_blocks, first)
    own_swap = swap(x_late)
    r2a, r2b = [move_only(own_swap[r : r + 1], [up, down]) for r in range(2)]
    r3 = move(r1, second)
    t1 = swap(r1)
    r4a, r4b = move(r2a, second), move(r2b, second)
    t2a, t2b = swap(r2a), swap(r2b)

    order, own = rows * edge, slab * edge
    table = pltpu.with_memory_space_constraint(table, pltpu.SMEM)
    smem = pl.BlockSpec(memory_space=pltpu.SMEM)
    vmem = pl.BlockSpec(memory_space=pltpu.VMEM)
    params = pltpu.CompilerParams(vmem_limit_bytes=24 * 2**20)
    def held(*arrays):
        return [pltpu.with_memory_space_constraint(a, pltpu.VMEM) for a in arrays]

    high, low, left, part = pl.pallas_call(
        functools.partial(early_kernel, tables),
        out_shape=[
            jax.ShapeDtypeStruct((order, order), jnp.bfloat16),
            jax.ShapeDtypeStruct((order, order), jnp.bfloat16),
            jax.ShapeDtypeStruct((2 * own, order), jnp.bfloat16),
            jax.ShapeDtypeStruct((own, order), jnp.float32),
        ],
        in_specs=[smem] + [pl.BlockSpec(memory_space=pltpu.HBM)] + [vmem] * 8,
        out_specs=[vmem] * 4,
        scratch_shapes=[pltpu.VMEM(x_blocks.shape, jnp.float32), pltpu.SemaphoreType.DMA],
        compiler_params=params,
        name="early",
    )(table, pltpu.with_memory_space_constraint(x_blocks, pltpu.HBM), own_swap, r1, r2a, r2b, t1, t2a, t2b, r3)
    t3 = swap(r3)
    r4a, part = lax.optimization_barrier((r4a, part))
    t4a = swap(r4a)
    r4b, t4a = lax.optimization_barrier((r4b, t4a))
    t4b = swap(r4b)
    dense = [jax.ShapeDtypeStruct(a.shape, a.dtype) for a in (high, low, part)]
    high, low, part = pl.pallas_call(
        functools.partial(middle_kernel, tables),
        out_shape=dense,
        in_specs=[smem] + [vmem] * 8,
        out_specs=[vmem] * 3,
        input_output_aliases={5: 0, 6: 1, 8: 2},
        compiler_params=params,
        name="middle",
    )(table, r4a, r4b, t3, t4a, *held(high, low, left, part))
    out, _, _, _ = pl.pallas_call(
        functools.partial(late_kernel, tables),
        out_shape=[jax.ShapeDtypeStruct(x_blocks.shape, jnp.float32)] + dense,
        in_specs=[smem] + [vmem] * 5,
        out_specs=[pl.BlockSpec(memory_space=pltpu.HBM)] + [vmem] * 3,
        input_output_aliases={2: 1, 3: 2, 5: 3},
        scratch_shapes=[
            pltpu.VMEM((2 * own, order), jnp.bfloat16),
            pltpu.VMEM(x_blocks.shape, jnp.float32),
            pltpu.SemaphoreType.DMA((slab * width // 2,)),
        ],
        compiler_params=params,
        name="late",
    )(table, t4b, *held(high, low, left, part))
    return out


def local(x_blocks, columns):
    slab, width, edge, _ = x_blocks.shape
    rows, slots = columns.shape
    _, chains, panels, lanes = (lax.axis_size(axis) for axis in AXES)
    full = rows <= slots and rows == lanes * width and width % 2 == 0
    if full and rows <= 8 and slab == 2 and edge == 128 and panels >= 2 and lanes == 2 and chains == 4:
        return gather_local(x_blocks, columns)
    return ring_local(x_blocks, columns)


def solution(mesh):
    placed = (P(("groups", "blk"), ("panel", "depth"), None, None), P("groups", None))
    return jax.shard_map(
        local,
        mesh=mesh,
        in_specs=placed,
        out_specs=P(("groups", "blk"), ("panel", "depth"), None, None),
        check_vma=False,
    )
```

```python
import functools

import jax
import jax.numpy as jnp
from jax import lax
from jax.experimental import pallas as pl
from jax.experimental.pallas import tpu as pltpu
from jax.sharding import PartitionSpec as P

precise = lax.Precision.HIGHEST
AXES = ("groups", "blk", "panel", "depth")


def shifted(block, axis, distance):
    devices = range(lax.axis_size(axis))
    route = [((i - distance) % len(devices), i) for i in devices]
    return lax.ppermute(block, axis, route)


def slot_gather(blocks):
    return lax.all_gather(blocks, ("panel", "depth"), axis=1, tiled=True)


def slot_reduce(partial_value):
    return lax.psum_scatter(partial_value, ("panel", "depth"), scatter_dimension=1, tiled=True)


def rotate_one(incoming):
    return shifted(incoming, "blk", 1)


def ring_local(x_blocks, columns):
    slab_rows = x_blocks.shape[0]
    width_slots = x_blocks.shape[1]
    edge = x_blocks.shape[2]
    order_rows = columns.shape[0]
    all_slots = columns.shape[1]
    cycle_size = lax.axis_size("blk")
    cycle_place = lax.axis_index("blk")
    anchor = jnp.int32(0)
    first_own = cycle_place * slab_rows
    slot_first = lax.axis_index(("panel", "depth")) * width_slots
    my_cols = lax.dynamic_slice(columns, (first_own, anchor), (slab_rows, all_slots))
    own_cols = lax.dynamic_slice(my_cols, (anchor, slot_first), (slab_rows, width_slots))
    x_own = jnp.where((own_cols < order_rows)[:, :, None, None], x_blocks, jnp.float32(0.0))
    out_present = my_cols < order_rows
    empty = jnp.zeros((slab_rows, all_slots, edge, edge), jnp.float32)

    def contribute(partial_value, left_rows, incoming, source):
        group = incoming.shape[0]
        first_row = source * group
        their_cols = lax.dynamic_slice(columns, (first_row, slot_first), (group, width_slots))
        row_ids = first_row + jnp.arange(group, dtype=jnp.int32)
        selector = (my_cols[:, None, :] == row_ids[None, :, None]).astype(jnp.float32)
        picked = jnp.einsum("irs,isab->irab", selector, left_rows, precision=precise)
        products = jnp.einsum("irab,rubc->iruac", picked, incoming, precision=precise)
        targets = (their_cols[None, None, :, :] == my_cols[:, :, None, None]) & out_present[
            :, :, None, None
        ]
        placed = jnp.einsum(
            "isru,iruac->isac", targets.astype(jnp.float32), products, precision=precise
        )
        return partial_value + placed

    def one_way(left_rows, stored):

        def advance(offset, state):
            partial_value, incoming, stored = state
            source = (cycle_place - offset) % cycle_size
            partial_value = contribute(partial_value, left_rows, incoming, source)
            return (partial_value, rotate_one(incoming), stored)

        partial_value, incoming, stored = lax.fori_loop(
            0, cycle_size - 1, advance, (empty, x_own, stored)
        )
        source = (cycle_place + 1) % cycle_size
        return (contribute(partial_value, left_rows, incoming, source), stored)

    stored = jnp.zeros((1,), jnp.float32)
    left_first = slot_gather(x_own)
    partial_value, stored = one_way(left_first, stored)
    squared = slot_reduce(partial_value)
    left_second = slot_gather(squared)
    partial_value, stored = one_way(left_second, stored)
    cubed = slot_reduce(partial_value)
    return 3.0 * squared - 2.0 * cubed


def split(value):
    high = value.astype(jnp.bfloat16)
    low = (value - high.astype(jnp.float32)).astype(jnp.bfloat16)
    return high, low


def dot(left, right):
    return jnp.dot(left, right, preferred_element_type=jnp.float32)


def stacked_dot(left, high, low):
    half = left.shape[0] // 2
    both = dot(left, high)
    return both[:half] + (both[half:] + dot(left[:half], low))


def lookup(table, place, lane):
    found = jnp.int32(-1)
    for z, entries in enumerate(table):
        for c, entry in enumerate(entries):
            found = jnp.where((place == z) & (lane == c), entry, found)
    return found


def store_piece(piece, plane, group, table_ref, high, low, own=None, slab=2, first=0):
    count, width, edge, _ = piece.shape
    act = 2 * width

    @pl.when(plane >= 0)
    def _():
        for r in range(count):
            row = plane * slab + first + r
            for w in range(width):
                slot = group * width + w
                col = pl.ds(pl.multiple_of(table_ref[row, slot] * edge, edge), edge)
                block = jnp.where(table_ref[row, act + slot] > 0, piece[r, w], 0.0)
                block_high, block_low = split(block)
                at = pl.ds(pl.multiple_of(row * edge, edge), edge)
                high[at, col] = block_high
                low[at, col] = block_low
                if own is not None:
                    own[pl.ds(r * edge, edge), col] = block_high
                    own[pl.ds((slab + r) * edge, edge), col] = block_low


def add_rows(first, depth, left, high, low, part_ref):
    rows, tile = pl.ds(pl.multiple_of(first, depth), depth), 256
    for n in range(part_ref.shape[1] // tile):
        cols = pl.ds(n * tile, tile)
        part_ref[:, cols] += stacked_dot(left[:, rows], high[rows, cols], low[rows, cols])


def add_plane(plane, left, high, low, part_ref):
    depth = part_ref.shape[0]

    @pl.when(plane >= 0)
    def _():
        add_rows(plane * depth, depth, left, high, low, part_ref)


def add_row(plane, r, left, high, low, part_ref):
    depth = part_ref.shape[0] // 2

    @pl.when(plane >= 0)
    def _():
        add_rows((plane * 2 + r) * depth, depth, left, high, low, part_ref)


def early_kernel(
    tables, table_ref, own_hbm, own_swap, r1, r2, t1, t2, r3,
    high, low, left, part_ref, own_ref, own_sem,
):
    place, lane = lax.axis_index("blk"), lax.axis_index("depth")
    near, far = tables
    own_copy = pltpu.make_async_copy(own_hbm, own_ref, own_sem)
    own_copy.start()
    here, there = lookup(near, place, lane), lookup(near, place, 1 - lane)
    part_ref[...] = jnp.zeros_like(part_ref)
    store_piece(own_swap, place, 1 - lane, table_ref, high, low, left)
    store_piece(r1, here, lane, table_ref, high, low)
    store_piece(r2, here, 1 - lane, table_ref, high, low)
    store_piece(t1, there, 1 - lane, table_ref, high, low)
    store_piece(t2, there, lane, table_ref, high, low)
    store_piece(r3, lookup(far, place, lane), lane, table_ref, high, low)
    own_copy.wait()
    store_piece(own_ref, place, lane, table_ref, high, low, left)
    for plane in (place, here, there):
        add_plane(plane, left, high, low, part_ref)


def waiting_kernel(
    tables, table_ref, r4a, high_in, low_in, left, part_in, high, low, part_ref
):
    place, lane = lax.axis_index("blk"), lax.axis_index("depth")
    here = lookup(tables[1], place, lane)
    store_piece(r4a, here, 1 - lane, table_ref, high, low)
    add_row(here, 0, left, high, low, part_ref)


def middle_kernel(
    tables, table_ref, r4b, t3, t4a, high_in, low_in, left, part_in, high, low, part_ref
):
    place, lane = lax.axis_index("blk"), lax.axis_index("depth")
    far = tables[1]
    here, there = lookup(far, place, lane), lookup(far, place, 1 - lane)
    store_piece(t3, there, 1 - lane, table_ref, high, low)
    store_piece(t4a, there, lane, table_ref, high, low)
    store_piece(r4b, here, 1 - lane, table_ref, high, low, first=1)
    add_row(there, 0, left, high, low, part_ref)
    add_row(here, 1, left, high, low, part_ref)


def late_kernel(
    tables, table_ref, t4b, high_in, low_in, left, part_in,
    out_hbm, high, low, square, square_parts, out_ref, out_sem,
):
    place, lane = lax.axis_index("blk"), lax.axis_index("depth")
    group = lax.axis_index("panel") * 2 + lane
    slab, width, edge, _ = out_ref.shape
    act, tile = 2 * width, 256
    there = lookup(tables[1], place, 1 - lane)
    store_piece(t4b, there, lane, table_ref, high, low, first=1)
    rows = pl.ds(pl.multiple_of((jnp.maximum(there, 0) * 2 + 1) * edge, edge), edge)
    for n in range(square.shape[1] // tile):
        cols = pl.ds(n * tile, tile)
        more = stacked_dot(left[:, rows], high[rows, cols], low[rows, cols])
        total = square[:, cols] + jnp.where(there >= 0, more, 0.0)
        square[:, cols] = total
        for r in range(slab):
            for k in range(tile // edge):
                c = n * (tile // edge) + k
                kept = table_ref[place * slab + r, 2 * act + c] > 0
                block = total[r * edge : (r + 1) * edge, k * edge : (k + 1) * edge]
                block_high, block_low = split(jnp.where(kept, block, 0.0))
                col = pl.ds(c * edge, edge)
                square_parts[pl.ds(2 * r * edge, edge), col] = block_high
                square_parts[pl.ds((2 * r + 1) * edge, edge), col] = block_low
    copies = []
    for r in range(slab):
        row = place * slab + r
        left_parts = square_parts[pl.ds(2 * r * edge, 2 * edge), :]
        for w in range(0, width, 2):
            slots = [jnp.minimum(group * width + w + k, act - 1) for k in range(2)]
            cols = [
                pl.ds(pl.multiple_of(table_ref[row, slot] * edge, edge), edge) for slot in slots
            ]
            cube = stacked_dot(
                left_parts,
                jnp.concatenate([high[:, col] for col in cols], axis=1),
                jnp.concatenate([low[:, col] for col in cols], axis=1),
            )
            for k in range(2):
                there = (group * width + w + k < act) & (table_ref[row, act + slots[k]] > 0)
                value = 3.0 * square[pl.ds(r * edge, edge), cols[k]]
                value = value - 2.0 * cube[:, k * edge : (k + 1) * edge]
                out_ref[r, w + k] = jnp.where(there, value, 0.0)
            ready = (r, pl.ds(w, 2))
            copies.append(
                pltpu.make_async_copy(out_ref.at[ready], out_hbm.at[ready], out_sem.at[len(copies)])
            )
            copies[-1].start()
    for copy in copies:
        copy.wait()


def slot_table(columns, act):
    rows = columns.shape[0]
    slots = columns[:, :act]
    here = slots < rows
    ids = jnp.arange(rows, dtype=jnp.int32)
    taken = jnp.any(slots[:, :, None] == ids, axis=1)
    count = jnp.sum(here.astype(jnp.int32), axis=1, keepdims=True)
    before = jnp.sum(
        (~taken[:, None, :] & (ids[None, :] < ids[:, None])[None]).astype(jnp.int32), axis=2
    )
    at = jnp.where(taken, -1, count + before)
    filled = jnp.sum(
        jnp.where(at[:, None, :] == jnp.arange(act, dtype=jnp.int32)[None, :, None], ids, 0), axis=2
    )
    order = jnp.where(here, slots, filled)
    return jnp.concatenate([order, here.astype(jnp.int32), taken.astype(jnp.int32)], axis=1)


def gather_local(x_blocks, columns):
    slab, width, edge, _ = x_blocks.shape
    rows = columns.shape[0]
    groups, chains, panels, lanes = (lax.axis_size(axis) for axis in AXES)
    last = chains - 1

    def index(g, place):
        z, x, c = place
        return (((g % groups) * chains + z) * panels + x) * lanes + c

    def move(block, cycles):
        pairs = [(cycle[i - 1], cycle[i]) for cycle in cycles for i in range(len(cycle))]
        busy = {a for a, _ in pairs}
        route = [(index(g, a), index(g, b)) for g in range(groups) for a, b in pairs]
        for z in range(chains):
            for x in range(panels):
                idle = [(z, x, c) for c in range(lanes) if (z, x, c) not in busy]
                for g in range(groups):
                    if len(idle) == lanes:
                        route += [(index(g, idle[c - 1]), index(g, idle[c])) for c in range(lanes)]
                    else:
                        route += [(index(g, a), index(g + 1, a)) for a in idle]
        return lax.ppermute(block, AXES, route)

    def swap(block):
        return move(block, [])

    def move_only(block, chains_of):
        pairs = [(chain[i], chain[i + 1]) for chain in chains_of for i in range(len(chain) - 1)]
        route = [(index(g, a), index(g, b)) for g in range(groups) for a, b in pairs]
        return lax.ppermute(block, AXES, route)

    up = [(z, 0, 0) for z in range(chains)] + [(last, 1, 0)]
    down = [(z, 0, 1) for z in reversed(range(chains))] + [(0, 1, 1)]
    first = [up + [(last, 1, 1)] + down + [(0, 1, 0)]]
    second = [up, down]
    near = [(z - 1, z + 1 if z < last else -1) for z in range(chains)]
    far = [(z - 2 if z >= 2 else -1, z + 2 if z + 2 < chains else -1) for z in range(chains)]
    far[0] = (last, far[0][1])
    far[last] = (far[last][0], 0)
    tables = (near, far)

    table = slot_table(columns, lanes * width)
    r1 = move(x_blocks, first)
    own_swap = swap(x_blocks)
    r2 = move_only(own_swap, [up, down])
    r1, table = lax.optimization_barrier((r1, table))
    r3 = move(r1, second)
    t1 = swap(r1)
    r4a, r4b = move(r2[:1], second), move(r2[1:], second)
    t2 = swap(r2)

    order, own = rows * edge, slab * edge
    table = pltpu.with_memory_space_constraint(table, pltpu.SMEM)
    smem = pl.BlockSpec(memory_space=pltpu.SMEM)
    vmem = pl.BlockSpec(memory_space=pltpu.VMEM)
    params = pltpu.CompilerParams(vmem_limit_bytes=24 * 2**20)
    def held(*arrays):
        return [pltpu.with_memory_space_constraint(a, pltpu.VMEM) for a in arrays]

    high, low, left, part = pl.pallas_call(
        functools.partial(early_kernel, tables),
        out_shape=[
            jax.ShapeDtypeStruct((order, order), jnp.bfloat16),
            jax.ShapeDtypeStruct((order, order), jnp.bfloat16),
            jax.ShapeDtypeStruct((2 * own, order), jnp.bfloat16),
            jax.ShapeDtypeStruct((own, order), jnp.float32),
        ],
        in_specs=[smem] + [pl.BlockSpec(memory_space=pltpu.HBM)] + [vmem] * 6,
        out_specs=[vmem] * 4,
        scratch_shapes=[pltpu.VMEM(x_blocks.shape, jnp.float32), pltpu.SemaphoreType.DMA],
        compiler_params=params,
        name="early",
    )(table, pltpu.with_memory_space_constraint(x_blocks, pltpu.HBM), own_swap, r1, r2, t1, t2, r3)
    t3 = swap(r3)
    r4a, part = lax.optimization_barrier((r4a, part))
    t4a = swap(r4a)
    dense = [jax.ShapeDtypeStruct(a.shape, a.dtype) for a in (high, low, part)]

    def add_to_square(kernel, name, *pieces):
        first = 1 + len(pieces)
        return pl.pallas_call(
            functools.partial(kernel, tables),
            out_shape=dense,
            in_specs=[smem] + [vmem] * (4 + len(pieces)),
            out_specs=[vmem] * 3,
            input_output_aliases={first: 0, first + 1: 1, first + 3: 2},
            compiler_params=params,
            name=name,
        )(table, *pieces, *held(high, low, left, part))

    high, low, part = add_to_square(waiting_kernel, "waiting", r4a)
    r4b, t4a, part = lax.optimization_barrier((r4b, t4a, part))
    t4b = swap(r4b)
    high, low, part = add_to_square(middle_kernel, "middle", r4b, t3, t4a)
    out, _, _, _ = pl.pallas_call(
        functools.partial(late_kernel, tables),
        out_shape=[jax.ShapeDtypeStruct(x_blocks.shape, jnp.float32)] + dense,
        in_specs=[smem] + [vmem] * 5,
        out_specs=[pl.BlockSpec(memory_space=pltpu.HBM)] + [vmem] * 3,
        input_output_aliases={2: 1, 3: 2, 5: 3},
        scratch_shapes=[
            pltpu.VMEM((2 * own, order), jnp.bfloat16),
            pltpu.VMEM(x_blocks.shape, jnp.float32),
            pltpu.SemaphoreType.DMA((slab * width // 2,)),
        ],
        compiler_params=params,
        name="late",
    )(table, t4b, *held(high, low, left, part))
    return out


def local(x_blocks, columns):
    slab, width, edge, _ = x_blocks.shape
    rows, slots = columns.shape
    _, chains, panels, lanes = (lax.axis_size(axis) for axis in AXES)
    full = rows <= slots and rows == lanes * width and width % 2 == 0
    if full and rows <= 8 and slab == 2 and edge == 128 and panels >= 2 and lanes == 2 and chains == 4:
        return gather_local(x_blocks, columns)
    return ring_local(x_blocks, columns)


def solution(mesh):
    placed = (P(("groups", "blk"), ("panel", "depth"), None, None), P("groups", None))
    return jax.shard_map(
        local,
        mesh=mesh,
        in_specs=placed,
        out_specs=P(("groups", "blk"), ("panel", "depth"), None, None),
        check_vma=False,
    )
```

```python
import functools

import jax
import jax.numpy as jnp
from jax import lax
from jax.experimental import pallas as pl
from jax.experimental.pallas import tpu as pltpu
from jax.sharding import PartitionSpec as P

precise = lax.Precision.HIGHEST
AXES = ("groups", "blk", "panel", "depth")


def shifted(block, axis, distance):
    devices = range(lax.axis_size(axis))
    route = [((i - distance) % len(devices), i) for i in devices]
    return lax.ppermute(block, axis, route)


def slot_gather(blocks):
    return lax.all_gather(blocks, ("panel", "depth"), axis=1, tiled=True)


def slot_reduce(partial_value):
    return lax.psum_scatter(partial_value, ("panel", "depth"), scatter_dimension=1, tiled=True)


def rotate_one(incoming):
    return shifted(incoming, "blk", 1)


def ring_local(x_blocks, columns):
    slab_rows = x_blocks.shape[0]
    width_slots = x_blocks.shape[1]
    edge = x_blocks.shape[2]
    order_rows = columns.shape[0]
    all_slots = columns.shape[1]
    cycle_size = lax.axis_size("blk")
    cycle_place = lax.axis_index("blk")
    anchor = jnp.int32(0)
    first_own = cycle_place * slab_rows
    slot_first = lax.axis_index(("panel", "depth")) * width_slots
    my_cols = lax.dynamic_slice(columns, (first_own, anchor), (slab_rows, all_slots))
    own_cols = lax.dynamic_slice(my_cols, (anchor, slot_first), (slab_rows, width_slots))
    x_own = jnp.where((own_cols < order_rows)[:, :, None, None], x_blocks, jnp.float32(0.0))
    out_present = my_cols < order_rows
    empty = jnp.zeros((slab_rows, all_slots, edge, edge), jnp.float32)

    def contribute(partial_value, left_rows, incoming, source):
        group = incoming.shape[0]
        first_row = source * group
        their_cols = lax.dynamic_slice(columns, (first_row, slot_first), (group, width_slots))
        row_ids = first_row + jnp.arange(group, dtype=jnp.int32)
        selector = (my_cols[:, None, :] == row_ids[None, :, None]).astype(jnp.float32)
        picked = jnp.einsum("irs,isab->irab", selector, left_rows, precision=precise)
        products = jnp.einsum("irab,rubc->iruac", picked, incoming, precision=precise)
        targets = (their_cols[None, None, :, :] == my_cols[:, :, None, None]) & out_present[
            :, :, None, None
        ]
        placed = jnp.einsum(
            "isru,iruac->isac", targets.astype(jnp.float32), products, precision=precise
        )
        return partial_value + placed

    def one_way(left_rows, stored):

        def advance(offset, state):
            partial_value, incoming, stored = state
            source = (cycle_place - offset) % cycle_size
            partial_value = contribute(partial_value, left_rows, incoming, source)
            return (partial_value, rotate_one(incoming), stored)

        partial_value, incoming, stored = lax.fori_loop(
            0, cycle_size - 1, advance, (empty, x_own, stored)
        )
        source = (cycle_place + 1) % cycle_size
        return (contribute(partial_value, left_rows, incoming, source), stored)

    stored = jnp.zeros((1,), jnp.float32)
    left_first = slot_gather(x_own)
    partial_value, stored = one_way(left_first, stored)
    squared = slot_reduce(partial_value)
    left_second = slot_gather(squared)
    partial_value, stored = one_way(left_second, stored)
    cubed = slot_reduce(partial_value)
    return 3.0 * squared - 2.0 * cubed


def split(value):
    high = value.astype(jnp.bfloat16)
    low = (value - high.astype(jnp.float32)).astype(jnp.bfloat16)
    return high, low


def dot(left, right):
    return jnp.dot(left, right, preferred_element_type=jnp.float32)


def stacked_dot(left, high, low):
    half = left.shape[0] // 2
    both = dot(left, high)
    return both[:half] + (both[half:] + dot(left[:half], low))


def lookup(table, place, lane):
    found = jnp.int32(-1)
    for z, entries in enumerate(table):
        for c, entry in enumerate(entries):
            found = jnp.where((place == z) & (lane == c), entry, found)
    return found


def store_piece(piece, plane, group, table_ref, high, low, own=None, slab=2, first=0):
    count, width, edge, _ = piece.shape
    act = 2 * width

    @pl.when(plane >= 0)
    def _():
        for r in range(count):
            row = plane * slab + first + r
            for w in range(width):
                slot = group * width + w
                col = pl.ds(pl.multiple_of(table_ref[row, slot] * edge, edge), edge)
                block = jnp.where(table_ref[row, act + slot] > 0, piece[r, w], 0.0)
                block_high, block_low = split(block)
                at = pl.ds(pl.multiple_of(row * edge, edge), edge)
                high[at, col] = block_high
                low[at, col] = block_low
                if own is not None:
                    own[pl.ds(r * edge, edge), col] = block_high
                    own[pl.ds((slab + r) * edge, edge), col] = block_low


def add_plane(plane, left, high, low, part_ref):
    depth, tile = part_ref.shape[0], 256

    @pl.when(plane >= 0)
    def _():
        rows = pl.ds(pl.multiple_of(plane * depth, depth), depth)
        for n in range(part_ref.shape[1] // tile):
            cols = pl.ds(n * tile, tile)
            part_ref[:, cols] += stacked_dot(left[:, rows], high[rows, cols], low[rows, cols])


def early_kernel(
    tables, table_ref, own_hbm, own_swap, r1, r2, t1, t2, r3,
    high, low, left, part_ref, own_ref, own_sem,
):
    place, lane = lax.axis_index("blk"), lax.axis_index("depth")
    near, far = tables
    own_copy = pltpu.make_async_copy(own_hbm, own_ref, own_sem)
    own_copy.start()
    here, there = lookup(near, place, lane), lookup(near, place, 1 - lane)
    part_ref[...] = jnp.zeros_like(part_ref)
    store_piece(own_swap, place, 1 - lane, table_ref, high, low, left)
    store_piece(r1, here, lane, table_ref, high, low)
    store_piece(r2, here, 1 - lane, table_ref, high, low)
    store_piece(t1, there, 1 - lane, table_ref, high, low)
    store_piece(t2, there, lane, table_ref, high, low)
    store_piece(r3, lookup(far, place, lane), lane, table_ref, high, low)
    own_copy.wait()
    store_piece(own_ref, place, lane, table_ref, high, low, left)
    for plane in (place, here, there):
        add_plane(plane, left, high, low, part_ref)


def middle_kernel(
    tables, table_ref, r4a, r4b, t3, t4a, high_in, low_in, left, part_in, high, low, part_ref
):
    place, lane = lax.axis_index("blk"), lax.axis_index("depth")
    far = tables[1]
    here, there = lookup(far, place, lane), lookup(far, place, 1 - lane)
    store_piece(t3, there, 1 - lane, table_ref, high, low)
    store_piece(r4a, here, 1 - lane, table_ref, high, low)
    store_piece(t4a, there, lane, table_ref, high, low)
    store_piece(r4b, here, 1 - lane, table_ref, high, low, first=1)
    add_plane(here, left, high, low, part_ref)


def late_kernel(
    tables, table_ref, t4b, high_in, low_in, left, part_in,
    out_hbm, high, low, square, square_parts, out_ref, out_sem,
):
    place, lane = lax.axis_index("blk"), lax.axis_index("depth")
    group = lax.axis_index("panel") * 2 + lane
    there = lookup(tables[1], place, 1 - lane)
    store_piece(t4b, there, lane, table_ref, high, low, first=1)
    add_plane(there, left, high, low, square)
    slab, width, edge, _ = out_ref.shape
    act = 2 * width
    for r in range(slab):
        for c in range(square.shape[1] // edge):
            kept = table_ref[place * slab + r, 2 * act + c] > 0
            col = pl.ds(c * edge, edge)
            block = jnp.where(kept, square[pl.ds(r * edge, edge), col], 0.0)
            block_high, block_low = split(block)
            square_parts[pl.ds(2 * r * edge, edge), col] = block_high
            square_parts[pl.ds((2 * r + 1) * edge, edge), col] = block_low
    copies = []
    for r in range(slab):
        row = place * slab + r
        left_parts = square_parts[pl.ds(2 * r * edge, 2 * edge), :]
        for w in range(0, width, 2):
            slots = [jnp.minimum(group * width + w + k, act - 1) for k in range(2)]
            cols = [
                pl.ds(pl.multiple_of(table_ref[row, slot] * edge, edge), edge) for slot in slots
            ]
            cube = stacked_dot(
                left_parts,
                jnp.concatenate([high[:, col] for col in cols], axis=1),
                jnp.concatenate([low[:, col] for col in cols], axis=1),
            )
            for k in range(2):
                there = (group * width + w + k < act) & (table_ref[row, act + slots[k]] > 0)
                value = 3.0 * square[pl.ds(r * edge, edge), cols[k]]
                value = value - 2.0 * cube[:, k * edge : (k + 1) * edge]
                out_ref[r, w + k] = jnp.where(there, value, 0.0)
            ready = (r, pl.ds(w, 2))
            copies.append(
                pltpu.make_async_copy(out_ref.at[ready], out_hbm.at[ready], out_sem.at[len(copies)])
            )
            copies[-1].start()
    for copy in copies:
        copy.wait()


def slot_table(columns, act):
    rows = columns.shape[0]
    slots = columns[:, :act]
    here = slots < rows
    ids = jnp.arange(rows, dtype=jnp.int32)
    taken = jnp.any(slots[:, :, None] == ids, axis=1)
    count = jnp.sum(here.astype(jnp.int32), axis=1, keepdims=True)
    before = jnp.sum(
        (~taken[:, None, :] & (ids[None, :] < ids[:, None])[None]).astype(jnp.int32), axis=2
    )
    at = jnp.where(taken, -1, count + before)
    filled = jnp.sum(
        jnp.where(at[:, None, :] == jnp.arange(act, dtype=jnp.int32)[None, :, None], ids, 0), axis=2
    )
    order = jnp.where(here, slots, filled)
    return jnp.concatenate([order, here.astype(jnp.int32), taken.astype(jnp.int32)], axis=1)


def gather_local(x_blocks, columns):
    slab, width, edge, _ = x_blocks.shape
    rows = columns.shape[0]
    groups, chains, panels, lanes = (lax.axis_size(axis) for axis in AXES)
    last = chains - 1

    def index(g, place):
        z, x, c = place
        return (((g % groups) * chains + z) * panels + x) * lanes + c

    def move(block, cycles):
        pairs = [(cycle[i - 1], cycle[i]) for cycle in cycles for i in range(len(cycle))]
        busy = {a for a, _ in pairs}
        route = [(index(g, a), index(g, b)) for g in range(groups) for a, b in pairs]
        for z in range(chains):
            for x in range(panels):
                idle = [(z, x, c) for c in range(lanes) if (z, x, c) not in busy]
                for g in range(groups):
                    if len(idle) == lanes:
                        route += [(index(g, idle[c - 1]), index(g, idle[c])) for c in range(lanes)]
                    else:
                        route += [(index(g, a), index(g + 1, a)) for a in idle]
        return lax.ppermute(block, AXES, route)

    def swap(block):
        return move(block, [])

    def move_only(block, chains_of):
        pairs = [(chain[i], chain[i + 1]) for chain in chains_of for i in range(len(chain) - 1)]
        route = [(index(g, a), index(g, b)) for g in range(groups) for a, b in pairs]
        return lax.ppermute(block, AXES, route)

    up = [(z, 0, 1) for z in range(chains)] + [(last, 1, 1)]
    down = [(z, 0, 0) for z in reversed(range(chains))] + [(0, 1, 0)]
    first = [up + [(last, 1, 0)] + down + [(0, 1, 1)]]
    second = [up, down]
    near = [(z + 1 if z < last else -1, z - 1) for z in range(chains)]
    far = [(z + 2 if z + 2 < chains else -1, z - 2 if z >= 2 else -1) for z in range(chains)]
    far[0] = (far[0][0], last)
    far[last] = (0, far[last][1])
    tables = (near, far)

    table = slot_table(columns, lanes * width)
    r1 = move(x_blocks, first)
    own_swap = swap(x_blocks)
    r2 = move_only(own_swap, [up, down])
    r1, table = lax.optimization_barrier((r1, table))
    r3 = move(r1, second)
    t1 = swap(r1)
    r4a, r4b = move(r2[:1], second), move(r2[1:], second)
    t2 = swap(r2)

    order, own = rows * edge, slab * edge
    table = pltpu.with_memory_space_constraint(table, pltpu.SMEM)
    smem = pl.BlockSpec(memory_space=pltpu.SMEM)
    vmem = pl.BlockSpec(memory_space=pltpu.VMEM)
    params = pltpu.CompilerParams(vmem_limit_bytes=24 * 2**20)
    def held(*arrays):
        return [pltpu.with_memory_space_constraint(a, pltpu.VMEM) for a in arrays]

    high, low, left, part = pl.pallas_call(
        functools.partial(early_kernel, tables),
        out_shape=[
            jax.ShapeDtypeStruct((order, order), jnp.bfloat16),
            jax.ShapeDtypeStruct((order, order), jnp.bfloat16),
            jax.ShapeDtypeStruct((2 * own, order), jnp.bfloat16),
            jax.ShapeDtypeStruct((own, order), jnp.float32),
        ],
        in_specs=[smem] + [pl.BlockSpec(memory_space=pltpu.HBM)] + [vmem] * 6,
        out_specs=[vmem] * 4,
        scratch_shapes=[pltpu.VMEM(x_blocks.shape, jnp.float32), pltpu.SemaphoreType.DMA],
        compiler_params=params,
        name="early",
    )(table, pltpu.with_memory_space_constraint(x_blocks, pltpu.HBM), own_swap, r1, r2, t1, t2, r3)
    t3 = swap(r3)
    r4a, part = lax.optimization_barrier((r4a, part))
    t4a = swap(r4a)
    r4b, t4a = lax.optimization_barrier((r4b, t4a))
    t4b = swap(r4b)
    dense = [jax.ShapeDtypeStruct(a.shape, a.dtype) for a in (high, low, part)]
    high, low, part = pl.pallas_call(
        functools.partial(middle_kernel, tables),
        out_shape=dense,
        in_specs=[smem] + [vmem] * 8,
        out_specs=[vmem] * 3,
        input_output_aliases={5: 0, 6: 1, 8: 2},
        compiler_params=params,
        name="middle",
    )(table, r4a, r4b, t3, t4a, *held(high, low, left, part))
    out, _, _, _ = pl.pallas_call(
        functools.partial(late_kernel, tables),
        out_shape=[jax.ShapeDtypeStruct(x_blocks.shape, jnp.float32)] + dense,
        in_specs=[smem] + [vmem] * 5,
        out_specs=[pl.BlockSpec(memory_space=pltpu.HBM)] + [vmem] * 3,
        input_output_aliases={2: 1, 3: 2, 5: 3},
        scratch_shapes=[
            pltpu.VMEM((2 * own, order), jnp.bfloat16),
            pltpu.VMEM(x_blocks.shape, jnp.float32),
            pltpu.SemaphoreType.DMA((slab * width // 2,)),
        ],
        compiler_params=params,
        name="late",
    )(table, t4b, *held(high, low, left, part))
    return out


def local(x_blocks, columns):
    slab, width, edge, _ = x_blocks.shape
    rows, slots = columns.shape
    _, chains, panels, lanes = (lax.axis_size(axis) for axis in AXES)
    full = rows <= slots and rows == lanes * width and width % 2 == 0
    if full and rows <= 8 and slab == 2 and edge == 128 and panels >= 2 and lanes == 2 and chains == 4:
        return gather_local(x_blocks, columns)
    return ring_local(x_blocks, columns)


def solution(mesh):
    placed = (P(("groups", "blk"), ("panel", "depth"), None, None), P("groups", None))
    return jax.shard_map(
        local,
        mesh=mesh,
        in_specs=placed,
        out_specs=P(("groups", "blk"), ("panel", "depth"), None, None),
        check_vma=False,
    )
```

```python
import functools

import jax
import jax.numpy as jnp
from jax import lax
from jax.experimental import pallas as pl
from jax.experimental.pallas import tpu as pltpu
from jax.sharding import PartitionSpec as P

precise = lax.Precision.HIGHEST
AXES = ("groups", "blk", "panel", "depth")


def shifted(block, axis, distance):
    devices = range(lax.axis_size(axis))
    route = [((i - distance) % len(devices), i) for i in devices]
    return lax.ppermute(block, axis, route)


def slot_gather(blocks):
    return lax.all_gather(blocks, ("panel", "depth"), axis=1, tiled=True)


def slot_reduce(partial_value):
    return lax.psum_scatter(partial_value, ("panel", "depth"), scatter_dimension=1, tiled=True)


def rotate_one(incoming):
    return shifted(incoming, "blk", 1)


def ring_local(x_blocks, columns):
    slab_rows = x_blocks.shape[0]
    width_slots = x_blocks.shape[1]
    edge = x_blocks.shape[2]
    order_rows = columns.shape[0]
    all_slots = columns.shape[1]
    cycle_size = lax.axis_size("blk")
    cycle_place = lax.axis_index("blk")
    anchor = jnp.int32(0)
    first_own = cycle_place * slab_rows
    slot_first = lax.axis_index(("panel", "depth")) * width_slots
    my_cols = lax.dynamic_slice(columns, (first_own, anchor), (slab_rows, all_slots))
    own_cols = lax.dynamic_slice(my_cols, (anchor, slot_first), (slab_rows, width_slots))
    x_own = jnp.where((own_cols < order_rows)[:, :, None, None], x_blocks, jnp.float32(0.0))
    out_present = my_cols < order_rows
    empty = jnp.zeros((slab_rows, all_slots, edge, edge), jnp.float32)

    def contribute(partial_value, left_rows, incoming, source):
        group = incoming.shape[0]
        first_row = source * group
        their_cols = lax.dynamic_slice(columns, (first_row, slot_first), (group, width_slots))
        row_ids = first_row + jnp.arange(group, dtype=jnp.int32)
        selector = (my_cols[:, None, :] == row_ids[None, :, None]).astype(jnp.float32)
        picked = jnp.einsum("irs,isab->irab", selector, left_rows, precision=precise)
        products = jnp.einsum("irab,rubc->iruac", picked, incoming, precision=precise)
        targets = (their_cols[None, None, :, :] == my_cols[:, :, None, None]) & out_present[
            :, :, None, None
        ]
        placed = jnp.einsum(
            "isru,iruac->isac", targets.astype(jnp.float32), products, precision=precise
        )
        return partial_value + placed

    def one_way(left_rows, stored):

        def advance(offset, state):
            partial_value, incoming, stored = state
            source = (cycle_place - offset) % cycle_size
            partial_value = contribute(partial_value, left_rows, incoming, source)
            return (partial_value, rotate_one(incoming), stored)

        partial_value, incoming, stored = lax.fori_loop(
            0, cycle_size - 1, advance, (empty, x_own, stored)
        )
        source = (cycle_place + 1) % cycle_size
        return (contribute(partial_value, left_rows, incoming, source), stored)

    stored = jnp.zeros((1,), jnp.float32)
    left_first = slot_gather(x_own)
    partial_value, stored = one_way(left_first, stored)
    squared = slot_reduce(partial_value)
    left_second = slot_gather(squared)
    partial_value, stored = one_way(left_second, stored)
    cubed = slot_reduce(partial_value)
    return 3.0 * squared - 2.0 * cubed


def split(value):
    high = value.astype(jnp.bfloat16)
    low = (value - high.astype(jnp.float32)).astype(jnp.bfloat16)
    return high, low


def dot(left, right):
    return jnp.dot(left, right, preferred_element_type=jnp.float32)


def stacked_dot(left, high, low):
    half = left.shape[0] // 2
    both = dot(left, high)
    return both[:half] + (both[half:] + dot(left[:half], low))


def lookup(table, place, lane):
    found = jnp.int32(-1)
    for z, entries in enumerate(table):
        for c, entry in enumerate(entries):
            found = jnp.where((place == z) & (lane == c), entry, found)
    return found


def store_piece(piece, plane, group, table_ref, high, low, own=None, slab=2, first=0):
    count, width, edge, _ = piece.shape
    act = 2 * width

    @pl.when(plane >= 0)
    def _():
        for r in range(count):
            row = plane * slab + first + r
            for w in range(width):
                slot = group * width + w
                col = pl.ds(pl.multiple_of(table_ref[row, slot] * edge, edge), edge)
                block = jnp.where(table_ref[row, act + slot] > 0, piece[r, w], 0.0)
                block_high, block_low = split(block)
                at = pl.ds(pl.multiple_of(row * edge, edge), edge)
                high[at, col] = block_high
                low[at, col] = block_low
                if own is not None:
                    own[pl.ds(r * edge, edge), col] = block_high
                    own[pl.ds((slab + r) * edge, edge), col] = block_low


def add_plane(plane, left, high, low, part_ref):
    depth, tile = part_ref.shape[0], 256

    @pl.when(plane >= 0)
    def _():
        rows = pl.ds(pl.multiple_of(plane * depth, depth), depth)
        for n in range(part_ref.shape[1] // tile):
            cols = pl.ds(n * tile, tile)
            part_ref[:, cols] += stacked_dot(left[:, rows], high[rows, cols], low[rows, cols])


def early_kernel(
    tables, table_ref, own_hbm, own_swap, r1, r2, t1, t2, r3,
    high, low, left, part_ref, own_ref, own_sem,
):
    place, lane = lax.axis_index("blk"), lax.axis_index("depth")
    near, far = tables
    own_copy = pltpu.make_async_copy(own_hbm, own_ref, own_sem)
    own_copy.start()
    here, there = lookup(near, place, lane), lookup(near, place, 1 - lane)
    part_ref[...] = jnp.zeros_like(part_ref)
    store_piece(own_swap, place, 1 - lane, table_ref, high, low, left)
    store_piece(r1, here, lane, table_ref, high, low)
    store_piece(r2, here, 1 - lane, table_ref, high, low)
    store_piece(t1, there, 1 - lane, table_ref, high, low)
    store_piece(t2, there, lane, table_ref, high, low)
    store_piece(r3, lookup(far, place, lane), lane, table_ref, high, low)
    own_copy.wait()
    store_piece(own_ref, place, lane, table_ref, high, low, left)
    for plane in (place, here, there):
        add_plane(plane, left, high, low, part_ref)


def middle_kernel(
    tables, table_ref, r4a, r4b, t3, t4a, high_in, low_in, left, part_in, high, low, part_ref
):
    place, lane = lax.axis_index("blk"), lax.axis_index("depth")
    far = tables[1]
    here, there = lookup(far, place, lane), lookup(far, place, 1 - lane)
    store_piece(t3, there, 1 - lane, table_ref, high, low)
    store_piece(r4a, here, 1 - lane, table_ref, high, low)
    store_piece(t4a, there, lane, table_ref, high, low)
    store_piece(r4b, here, 1 - lane, table_ref, high, low, first=1)
    add_plane(here, left, high, low, part_ref)


def late_kernel(
    tables, table_ref, t4b, high_in, low_in, left, part_in,
    out_hbm, high, low, square, square_parts, out_ref, out_sem,
):
    place, lane = lax.axis_index("blk"), lax.axis_index("depth")
    group = lax.axis_index("panel") * 2 + lane
    there = lookup(tables[1], place, 1 - lane)
    store_piece(t4b, there, lane, table_ref, high, low, first=1)
    add_plane(there, left, high, low, square)
    slab, width, edge, _ = out_ref.shape
    act = 2 * width
    for r in range(slab):
        for c in range(square.shape[1] // edge):
            kept = table_ref[place * slab + r, 2 * act + c] > 0
            col = pl.ds(c * edge, edge)
            block = jnp.where(kept, square[pl.ds(r * edge, edge), col], 0.0)
            block_high, block_low = split(block)
            square_parts[pl.ds(2 * r * edge, edge), col] = block_high
            square_parts[pl.ds((2 * r + 1) * edge, edge), col] = block_low
    copies = []
    for r in range(slab):
        row = place * slab + r
        left_parts = square_parts[pl.ds(2 * r * edge, 2 * edge), :]
        for w in range(0, width, 2):
            slots = [jnp.minimum(group * width + w + k, act - 1) for k in range(2)]
            cols = [
                pl.ds(pl.multiple_of(table_ref[row, slot] * edge, edge), edge) for slot in slots
            ]
            cube = stacked_dot(
                left_parts,
                jnp.concatenate([high[:, col] for col in cols], axis=1),
                jnp.concatenate([low[:, col] for col in cols], axis=1),
            )
            for k in range(2):
                there = (group * width + w + k < act) & (table_ref[row, act + slots[k]] > 0)
                value = 3.0 * square[pl.ds(r * edge, edge), cols[k]]
                value = value - 2.0 * cube[:, k * edge : (k + 1) * edge]
                out_ref[r, w + k] = jnp.where(there, value, 0.0)
            ready = (r, pl.ds(w, 2))
            copies.append(
                pltpu.make_async_copy(out_ref.at[ready], out_hbm.at[ready], out_sem.at[len(copies)])
            )
            copies[-1].start()
    for copy in copies:
        copy.wait()


def slot_table(columns, act):
    rows = columns.shape[0]
    slots = columns[:, :act]
    here = slots < rows
    ids = jnp.arange(rows, dtype=jnp.int32)
    taken = jnp.any(slots[:, :, None] == ids, axis=1)
    count = jnp.sum(here.astype(jnp.int32), axis=1, keepdims=True)
    before = jnp.sum(
        (~taken[:, None, :] & (ids[None, :] < ids[:, None])[None]).astype(jnp.int32), axis=2
    )
    at = jnp.where(taken, -1, count + before)
    filled = jnp.sum(
        jnp.where(at[:, None, :] == jnp.arange(act, dtype=jnp.int32)[None, :, None], ids, 0), axis=2
    )
    order = jnp.where(here, slots, filled)
    return jnp.concatenate([order, here.astype(jnp.int32), taken.astype(jnp.int32)], axis=1)


def gather_local(x_blocks, columns):
    slab, width, edge, _ = x_blocks.shape
    rows = columns.shape[0]
    groups, chains, panels, lanes = (lax.axis_size(axis) for axis in AXES)
    last = chains - 1

    def index(g, place):
        z, x, c = place
        return (((g % groups) * chains + z) * panels + x) * lanes + c

    def move(block, cycles):
        pairs = [(cycle[i - 1], cycle[i]) for cycle in cycles for i in range(len(cycle))]
        busy = {a for a, _ in pairs}
        route = [(index(g, a), index(g, b)) for g in range(groups) for a, b in pairs]
        for z in range(chains):
            for x in range(panels):
                idle = [(z, x, c) for c in range(lanes) if (z, x, c) not in busy]
                for g in range(groups):
                    if len(idle) == lanes:
                        route += [(index(g, idle[c - 1]), index(g, idle[c])) for c in range(lanes)]
                    else:
                        route += [(index(g, a), index(g + 1, a)) for a in idle]
        return lax.ppermute(block, AXES, route)

    def swap(block):
        return move(block, [])

    def move_only(block, chains_of):
        pairs = [(chain[i], chain[i + 1]) for chain in chains_of for i in range(len(chain) - 1)]
        route = [(index(g, a), index(g, b)) for g in range(groups) for a, b in pairs]
        return lax.ppermute(block, AXES, route)

    up = [(z, 0, 1) for z in range(chains)] + [(last, 1, 1)]
    down = [(z, 0, 0) for z in reversed(range(chains))] + [(0, 1, 0)]
    first = [up + [(last, 1, 0)] + down + [(0, 1, 1)]]
    second = [up, down]
    inside = [up[:-1] + down[:-1]]
    near = [(z + 1 if z < last else -1, z - 1) for z in range(chains)]
    far = [(z + 2 if z + 2 < chains else -1, z - 2 if z >= 2 else -1) for z in range(chains)]
    far[0] = (far[0][0], last)
    far[last] = (0, far[last][1])
    tables = (near, far)

    helper = functools.reduce(
        jnp.logical_or,
        [
            (lax.axis_index("blk") == z) & (lax.axis_index("panel") == x) & (lane == c)
            for lane in (lax.axis_index("depth"),)
            for z, x, c in (up[-1], down[-1])
        ],
    )

    table = slot_table(columns, lanes * width)
    r1 = move(x_blocks, first)
    own_swap = swap(x_blocks)
    r2 = move(own_swap, inside)
    crossed = [move_only(own_swap[r : r + 1], [up[-2:], down[-2:]]) for r in range(2)]
    r1, table = lax.optimization_barrier((r1, table))
    r3 = move(r1, second)
    t1 = swap(r1)
    r4a, r4b = [move(jnp.where(helper, crossed[r], r2[r : r + 1]), second) for r in range(2)]
    t2 = swap(r2)

    order, own = rows * edge, slab * edge
    table = pltpu.with_memory_space_constraint(table, pltpu.SMEM)
    smem = pl.BlockSpec(memory_space=pltpu.SMEM)
    vmem = pl.BlockSpec(memory_space=pltpu.VMEM)
    params = pltpu.CompilerParams(vmem_limit_bytes=24 * 2**20)
    def held(*arrays):
        return [pltpu.with_memory_space_constraint(a, pltpu.VMEM) for a in arrays]

    high, low, left, part = pl.pallas_call(
        functools.partial(early_kernel, tables),
        out_shape=[
            jax.ShapeDtypeStruct((order, order), jnp.bfloat16),
            jax.ShapeDtypeStruct((order, order), jnp.bfloat16),
            jax.ShapeDtypeStruct((2 * own, order), jnp.bfloat16),
            jax.ShapeDtypeStruct((own, order), jnp.float32),
        ],
        in_specs=[smem] + [pl.BlockSpec(memory_space=pltpu.HBM)] + [vmem] * 6,
        out_specs=[vmem] * 4,
        scratch_shapes=[pltpu.VMEM(x_blocks.shape, jnp.float32), pltpu.SemaphoreType.DMA],
        compiler_params=params,
        name="early",
    )(table, pltpu.with_memory_space_constraint(x_blocks, pltpu.HBM), own_swap, r1, r2, t1, t2, r3)
    t3 = swap(r3)
    r4a, part = lax.optimization_barrier((r4a, part))
    t4a = swap(r4a)
    r4b, t4a = lax.optimization_barrier((r4b, t4a))
    t4b = swap(r4b)
    dense = [jax.ShapeDtypeStruct(a.shape, a.dtype) for a in (high, low, part)]
    high, low, part = pl.pallas_call(
        functools.partial(middle_kernel, tables),
        out_shape=dense,
        in_specs=[smem] + [vmem] * 8,
        out_specs=[vmem] * 3,
        input_output_aliases={5: 0, 6: 1, 8: 2},
        compiler_params=params,
        name="middle",
    )(table, r4a, r4b, t3, t4a, *held(high, low, left, part))
    out, _, _, _ = pl.pallas_call(
        functools.partial(late_kernel, tables),
        out_shape=[jax.ShapeDtypeStruct(x_blocks.shape, jnp.float32)] + dense,
        in_specs=[smem] + [vmem] * 5,
        out_specs=[pl.BlockSpec(memory_space=pltpu.HBM)] + [vmem] * 3,
        input_output_aliases={2: 1, 3: 2, 5: 3},
        scratch_shapes=[
            pltpu.VMEM((2 * own, order), jnp.bfloat16),
            pltpu.VMEM(x_blocks.shape, jnp.float32),
            pltpu.SemaphoreType.DMA((slab * width // 2,)),
        ],
        compiler_params=params,
        name="late",
    )(table, t4b, *held(high, low, left, part))
    return out


def local(x_blocks, columns):
    slab, width, edge, _ = x_blocks.shape
    rows, slots = columns.shape
    _, chains, panels, lanes = (lax.axis_size(axis) for axis in AXES)
    full = rows <= slots and rows == lanes * width and width % 2 == 0
    if full and rows <= 8 and slab == 2 and edge == 128 and panels >= 2 and lanes == 2 and chains == 4:
        return gather_local(x_blocks, columns)
    return ring_local(x_blocks, columns)


def solution(mesh):
    placed = (P(("groups", "blk"), ("panel", "depth"), None, None), P("groups", None))
    return jax.shard_map(
        local,
        mesh=mesh,
        in_specs=placed,
        out_specs=P(("groups", "blk"), ("panel", "depth"), None, None),
        check_vma=False,
    )
```

```python
import functools

import jax
import jax.numpy as jnp
from jax import lax
from jax.experimental import pallas as pl
from jax.experimental.pallas import tpu as pltpu
from jax.sharding import PartitionSpec as P

precise = lax.Precision.HIGHEST
AXES = ("groups", "blk", "panel", "depth")


def shifted(block, axis, distance):
    devices = range(lax.axis_size(axis))
    route = [((i - distance) % len(devices), i) for i in devices]
    return lax.ppermute(block, axis, route)


def slot_gather(blocks):
    return lax.all_gather(blocks, ("panel", "depth"), axis=1, tiled=True)


def slot_reduce(partial_value):
    return lax.psum_scatter(partial_value, ("panel", "depth"), scatter_dimension=1, tiled=True)


def rotate_one(incoming):
    return shifted(incoming, "blk", 1)


def ring_local(x_blocks, columns):
    slab_rows = x_blocks.shape[0]
    width_slots = x_blocks.shape[1]
    edge = x_blocks.shape[2]
    order_rows = columns.shape[0]
    all_slots = columns.shape[1]
    cycle_size = lax.axis_size("blk")
    cycle_place = lax.axis_index("blk")
    anchor = jnp.int32(0)
    first_own = cycle_place * slab_rows
    slot_first = lax.axis_index(("panel", "depth")) * width_slots
    my_cols = lax.dynamic_slice(columns, (first_own, anchor), (slab_rows, all_slots))
    own_cols = lax.dynamic_slice(my_cols, (anchor, slot_first), (slab_rows, width_slots))
    x_own = jnp.where((own_cols < order_rows)[:, :, None, None], x_blocks, jnp.float32(0.0))
    out_present = my_cols < order_rows
    empty = jnp.zeros((slab_rows, all_slots, edge, edge), jnp.float32)

    def contribute(partial_value, left_rows, incoming, source):
        group = incoming.shape[0]
        first_row = source * group
        their_cols = lax.dynamic_slice(columns, (first_row, slot_first), (group, width_slots))
        row_ids = first_row + jnp.arange(group, dtype=jnp.int32)
        selector = (my_cols[:, None, :] == row_ids[None, :, None]).astype(jnp.float32)
        picked = jnp.einsum("irs,isab->irab", selector, left_rows, precision=precise)
        products = jnp.einsum("irab,rubc->iruac", picked, incoming, precision=precise)
        targets = (their_cols[None, None, :, :] == my_cols[:, :, None, None]) & out_present[
            :, :, None, None
        ]
        placed = jnp.einsum(
            "isru,iruac->isac", targets.astype(jnp.float32), products, precision=precise
        )
        return partial_value + placed

    def one_way(left_rows, stored):

        def advance(offset, state):
            partial_value, incoming, stored = state
            source = (cycle_place - offset) % cycle_size
            partial_value = contribute(partial_value, left_rows, incoming, source)
            return (partial_value, rotate_one(incoming), stored)

        partial_value, incoming, stored = lax.fori_loop(
            0, cycle_size - 1, advance, (empty, x_own, stored)
        )
        source = (cycle_place + 1) % cycle_size
        return (contribute(partial_value, left_rows, incoming, source), stored)

    stored = jnp.zeros((1,), jnp.float32)
    left_first = slot_gather(x_own)
    partial_value, stored = one_way(left_first, stored)
    squared = slot_reduce(partial_value)
    left_second = slot_gather(squared)
    partial_value, stored = one_way(left_second, stored)
    cubed = slot_reduce(partial_value)
    return 3.0 * squared - 2.0 * cubed


def split(value):
    high = value.astype(jnp.bfloat16)
    low = (value - high.astype(jnp.float32)).astype(jnp.bfloat16)
    return high, low


def dot(left, right):
    return jnp.dot(left, right, preferred_element_type=jnp.float32)


def stacked_dot(left, high, low):
    half = left.shape[0] // 2
    both = dot(left, high)
    return both[:half] + (both[half:] + dot(left[:half], low))


def lookup(table, place, lane):
    found = jnp.int32(-1)
    for z, entries in enumerate(table):
        for c, entry in enumerate(entries):
            found = jnp.where((place == z) & (lane == c), entry, found)
    return found


def store_piece(piece, plane, group, table_ref, high, low, own=None):
    slab, width, edge, _ = piece.shape
    act = 2 * width

    @pl.when(plane >= 0)
    def _():
        for r in range(slab):
            row = plane * slab + r
            for w in range(width):
                slot = group * width + w
                col = pl.ds(pl.multiple_of(table_ref[row, slot] * edge, edge), edge)
                block = jnp.where(table_ref[row, act + slot] > 0, piece[r, w], 0.0)
                block_high, block_low = split(block)
                at = pl.ds(pl.multiple_of(row * edge, edge), edge)
                high[at, col] = block_high
                low[at, col] = block_low
                if own is not None:
                    own[pl.ds(r * edge, edge), col] = block_high
                    own[pl.ds((slab + r) * edge, edge), col] = block_low


def add_plane(plane, left, high, low, part_ref):
    depth, tile = part_ref.shape[0], 256

    @pl.when(plane >= 0)
    def _():
        rows = pl.ds(pl.multiple_of(plane * depth, depth), depth)
        for n in range(part_ref.shape[1] // tile):
            cols = pl.ds(n * tile, tile)
            part_ref[:, cols] += stacked_dot(left[:, rows], high[rows, cols], low[rows, cols])


def early_kernel(
    tables, table_ref, own_hbm, own_swap, r1, r2, t1, t2, r3,
    high, low, left, part_ref, own_ref, own_sem,
):
    place, lane = lax.axis_index("blk"), lax.axis_index("depth")
    near, far = tables
    own_copy = pltpu.make_async_copy(own_hbm, own_ref, own_sem)
    own_copy.start()
    here, there = lookup(near, place, lane), lookup(near, place, 1 - lane)
    part_ref[...] = jnp.zeros_like(part_ref)
    store_piece(own_swap, place, 1 - lane, table_ref, high, low, left)
    store_piece(r1, here, lane, table_ref, high, low)
    store_piece(r2, here, 1 - lane, table_ref, high, low)
    store_piece(t1, there, 1 - lane, table_ref, high, low)
    store_piece(t2, there, lane, table_ref, high, low)
    store_piece(r3, lookup(far, place, lane), lane, table_ref, high, low)
    own_copy.wait()
    store_piece(own_ref, place, lane, table_ref, high, low, left)
    for plane in (place, here, there):
        add_plane(plane, left, high, low, part_ref)


def middle_kernel(
    tables, table_ref, r4, t3, high_in, low_in, left, part_in, high, low, part_ref
):
    place, lane = lax.axis_index("blk"), lax.axis_index("depth")
    far = tables[1]
    here, there = lookup(far, place, lane), lookup(far, place, 1 - lane)
    store_piece(t3, there, 1 - lane, table_ref, high, low)
    store_piece(r4, here, 1 - lane, table_ref, high, low)
    add_plane(here, left, high, low, part_ref)


def late_kernel(
    tables, table_ref, t4, high_in, low_in, left, part_in,
    out_hbm, high, low, square, square_parts, out_ref, out_sem,
):
    place, lane = lax.axis_index("blk"), lax.axis_index("depth")
    group = lax.axis_index("panel") * 2 + lane
    there = lookup(tables[1], place, 1 - lane)
    store_piece(t4, there, lane, table_ref, high, low)
    add_plane(there, left, high, low, square)
    slab, width, edge, _ = out_ref.shape
    act = 2 * width
    for r in range(slab):
        for c in range(square.shape[1] // edge):
            kept = table_ref[place * slab + r, 2 * act + c] > 0
            col = pl.ds(c * edge, edge)
            block = jnp.where(kept, square[pl.ds(r * edge, edge), col], 0.0)
            block_high, block_low = split(block)
            square_parts[pl.ds(2 * r * edge, edge), col] = block_high
            square_parts[pl.ds((2 * r + 1) * edge, edge), col] = block_low
    copies = []
    for r in range(slab):
        row = place * slab + r
        left_parts = square_parts[pl.ds(2 * r * edge, 2 * edge), :]
        for w in range(0, width, 2):
            slots = [jnp.minimum(group * width + w + k, act - 1) for k in range(2)]
            cols = [
                pl.ds(pl.multiple_of(table_ref[row, slot] * edge, edge), edge) for slot in slots
            ]
            cube = stacked_dot(
                left_parts,
                jnp.concatenate([high[:, col] for col in cols], axis=1),
                jnp.concatenate([low[:, col] for col in cols], axis=1),
            )
            for k in range(2):
                there = (group * width + w + k < act) & (table_ref[row, act + slots[k]] > 0)
                value = 3.0 * square[pl.ds(r * edge, edge), cols[k]]
                value = value - 2.0 * cube[:, k * edge : (k + 1) * edge]
                out_ref[r, w + k] = jnp.where(there, value, 0.0)
            ready = (r, pl.ds(w, 2))
            copies.append(
                pltpu.make_async_copy(out_ref.at[ready], out_hbm.at[ready], out_sem.at[len(copies)])
            )
            copies[-1].start()
    for copy in copies:
        copy.wait()


def slot_table(columns, act):
    rows = columns.shape[0]
    slots = columns[:, :act]
    here = slots < rows
    ids = jnp.arange(rows, dtype=jnp.int32)
    taken = jnp.any(slots[:, :, None] == ids, axis=1)
    count = jnp.sum(here.astype(jnp.int32), axis=1, keepdims=True)
    before = jnp.sum(
        (~taken[:, None, :] & (ids[None, :] < ids[:, None])[None]).astype(jnp.int32), axis=2
    )
    at = jnp.where(taken, -1, count + before)
    filled = jnp.sum(
        jnp.where(at[:, None, :] == jnp.arange(act, dtype=jnp.int32)[None, :, None], ids, 0), axis=2
    )
    order = jnp.where(here, slots, filled)
    return jnp.concatenate([order, here.astype(jnp.int32), taken.astype(jnp.int32)], axis=1)


def gather_local(x_blocks, columns):
    slab, width, edge, _ = x_blocks.shape
    rows = columns.shape[0]
    groups, chains, panels, lanes = (lax.axis_size(axis) for axis in AXES)
    last = chains - 1

    def index(g, place):
        z, x, c = place
        return (((g % groups) * chains + z) * panels + x) * lanes + c

    def move(block, cycles):
        pairs = [(cycle[i - 1], cycle[i]) for cycle in cycles for i in range(len(cycle))]
        busy = {a for a, _ in pairs}
        route = [(index(g, a), index(g, b)) for g in range(groups) for a, b in pairs]
        for z in range(chains):
            for x in range(panels):
                idle = [(z, x, c) for c in range(lanes) if (z, x, c) not in busy]
                for g in range(groups):
                    if len(idle) == lanes:
                        route += [(index(g, idle[c - 1]), index(g, idle[c])) for c in range(lanes)]
                    else:
                        route += [(index(g, a), index(g + 1, a)) for a in idle]
        return lax.ppermute(block, AXES, route)

    def swap(block):
        return move(block, [])

    def move_only(block, chains_of):
        pairs = [(chain[i], chain[i + 1]) for chain in chains_of for i in range(len(chain) - 1)]
        route = [(index(g, a), index(g, b)) for g in range(groups) for a, b in pairs]
        return lax.ppermute(block, AXES, route)

    up = [(z, 0, 1) for z in range(chains)] + [(last, 1, 1)]
    down = [(z, 0, 0) for z in reversed(range(chains))] + [(0, 1, 0)]
    first = [up + [(last, 1, 0)] + down + [(0, 1, 1)]]
    second = [up, down]
    near = [(z + 1 if z < last else -1, z - 1) for z in range(chains)]
    far = [(z + 2 if z + 2 < chains else -1, z - 2 if z >= 2 else -1) for z in range(chains)]
    far[0] = (far[0][0], last)
    far[last] = (0, far[last][1])
    tables = (near, far)

    table = slot_table(columns, lanes * width)
    r1 = move(x_blocks, first)
    own_swap = swap(x_blocks)
    r2 = move_only(own_swap, [up, down])
    r1, table = lax.optimization_barrier((r1, table))
    r3 = move(r1, second)
    t1 = swap(r1)
    r4 = move(r2, second)
    t2 = swap(r2)

    order, own = rows * edge, slab * edge
    table = pltpu.with_memory_space_constraint(table, pltpu.SMEM)
    smem = pl.BlockSpec(memory_space=pltpu.SMEM)
    vmem = pl.BlockSpec(memory_space=pltpu.VMEM)
    params = pltpu.CompilerParams(vmem_limit_bytes=24 * 2**20)
    def held(*arrays):
        return [pltpu.with_memory_space_constraint(a, pltpu.VMEM) for a in arrays]

    high, low, left, part = pl.pallas_call(
        functools.partial(early_kernel, tables),
        out_shape=[
            jax.ShapeDtypeStruct((order, order), jnp.bfloat16),
            jax.ShapeDtypeStruct((order, order), jnp.bfloat16),
            jax.ShapeDtypeStruct((2 * own, order), jnp.bfloat16),
            jax.ShapeDtypeStruct((own, order), jnp.float32),
        ],
        in_specs=[smem] + [pl.BlockSpec(memory_space=pltpu.HBM)] + [vmem] * 6,
        out_specs=[vmem] * 4,
        scratch_shapes=[pltpu.VMEM(x_blocks.shape, jnp.float32), pltpu.SemaphoreType.DMA],
        compiler_params=params,
        name="early",
    )(table, pltpu.with_memory_space_constraint(x_blocks, pltpu.HBM), own_swap, r1, r2, t1, t2, r3)
    t3 = swap(r3)
    r4, part = lax.optimization_barrier((r4, part))
    t4 = swap(r4)
    dense = [jax.ShapeDtypeStruct(a.shape, a.dtype) for a in (high, low, part)]
    high, low, part = pl.pallas_call(
        functools.partial(middle_kernel, tables),
        out_shape=dense,
        in_specs=[smem] + [vmem] * 6,
        out_specs=[vmem] * 3,
        input_output_aliases={3: 0, 4: 1, 6: 2},
        compiler_params=params,
        name="middle",
    )(table, r4, t3, *held(high, low, left, part))
    out, _, _, _ = pl.pallas_call(
        functools.partial(late_kernel, tables),
        out_shape=[jax.ShapeDtypeStruct(x_blocks.shape, jnp.float32)] + dense,
        in_specs=[smem] + [vmem] * 5,
        out_specs=[pl.BlockSpec(memory_space=pltpu.HBM)] + [vmem] * 3,
        input_output_aliases={2: 1, 3: 2, 5: 3},
        scratch_shapes=[
            pltpu.VMEM((2 * own, order), jnp.bfloat16),
            pltpu.VMEM(x_blocks.shape, jnp.float32),
            pltpu.SemaphoreType.DMA((slab * width // 2,)),
        ],
        compiler_params=params,
        name="late",
    )(table, t4, *held(high, low, left, part))
    return out


def local(x_blocks, columns):
    slab, width, edge, _ = x_blocks.shape
    rows, slots = columns.shape
    _, chains, panels, lanes = (lax.axis_size(axis) for axis in AXES)
    full = rows <= slots and rows == lanes * width and width % 2 == 0
    if full and rows <= 8 and edge % 128 == 0 and panels >= 2 and lanes == 2 and chains == 4:
        return gather_local(x_blocks, columns)
    return ring_local(x_blocks, columns)


def solution(mesh):
    placed = (P(("groups", "blk"), ("panel", "depth"), None, None), P("groups", None))
    return jax.shard_map(
        local,
        mesh=mesh,
        in_specs=placed,
        out_specs=P(("groups", "blk"), ("panel", "depth"), None, None),
        check_vma=False,
    )
```

```python
import functools

import jax
import jax.numpy as jnp
from jax import lax
from jax.experimental import pallas as pl
from jax.experimental.pallas import tpu as pltpu
from jax.sharding import PartitionSpec as P

precise = lax.Precision.HIGHEST
AXES = ("groups", "blk", "panel", "depth")


def shifted(block, axis, distance):
    devices = range(lax.axis_size(axis))
    route = [((i - distance) % len(devices), i) for i in devices]
    return lax.ppermute(block, axis, route)


def slot_gather(blocks):
    return lax.all_gather(blocks, ("panel", "depth"), axis=1, tiled=True)


def slot_reduce(partial_value):
    return lax.psum_scatter(partial_value, ("panel", "depth"), scatter_dimension=1, tiled=True)


def rotate_one(incoming):
    return shifted(incoming, "blk", 1)


def ring_local(x_blocks, columns):
    slab_rows = x_blocks.shape[0]
    width_slots = x_blocks.shape[1]
    edge = x_blocks.shape[2]
    order_rows = columns.shape[0]
    all_slots = columns.shape[1]
    cycle_size = lax.axis_size("blk")
    cycle_place = lax.axis_index("blk")
    anchor = jnp.int32(0)
    first_own = cycle_place * slab_rows
    slot_first = lax.axis_index(("panel", "depth")) * width_slots
    my_cols = lax.dynamic_slice(columns, (first_own, anchor), (slab_rows, all_slots))
    own_cols = lax.dynamic_slice(my_cols, (anchor, slot_first), (slab_rows, width_slots))
    x_own = jnp.where((own_cols < order_rows)[:, :, None, None], x_blocks, jnp.float32(0.0))
    out_present = my_cols < order_rows
    empty = jnp.zeros((slab_rows, all_slots, edge, edge), jnp.float32)

    def contribute(partial_value, left_rows, incoming, source):
        group = incoming.shape[0]
        first_row = source * group
        their_cols = lax.dynamic_slice(columns, (first_row, slot_first), (group, width_slots))
        row_ids = first_row + jnp.arange(group, dtype=jnp.int32)
        selector = (my_cols[:, None, :] == row_ids[None, :, None]).astype(jnp.float32)
        picked = jnp.einsum("irs,isab->irab", selector, left_rows, precision=precise)
        products = jnp.einsum("irab,rubc->iruac", picked, incoming, precision=precise)
        targets = (their_cols[None, None, :, :] == my_cols[:, :, None, None]) & out_present[
            :, :, None, None
        ]
        placed = jnp.einsum(
            "isru,iruac->isac", targets.astype(jnp.float32), products, precision=precise
        )
        return partial_value + placed

    def one_way(left_rows, stored):

        def advance(offset, state):
            partial_value, incoming, stored = state
            source = (cycle_place - offset) % cycle_size
            partial_value = contribute(partial_value, left_rows, incoming, source)
            return (partial_value, rotate_one(incoming), stored)

        partial_value, incoming, stored = lax.fori_loop(
            0, cycle_size - 1, advance, (empty, x_own, stored)
        )
        source = (cycle_place + 1) % cycle_size
        return (contribute(partial_value, left_rows, incoming, source), stored)

    stored = jnp.zeros((1,), jnp.float32)
    left_first = slot_gather(x_own)
    partial_value, stored = one_way(left_first, stored)
    squared = slot_reduce(partial_value)
    left_second = slot_gather(squared)
    partial_value, stored = one_way(left_second, stored)
    cubed = slot_reduce(partial_value)
    return 3.0 * squared - 2.0 * cubed


def split(value):
    high = value.astype(jnp.bfloat16)
    low = (value - high.astype(jnp.float32)).astype(jnp.bfloat16)
    return high, low


def dot(left, right):
    return jnp.dot(left, right, preferred_element_type=jnp.float32)


def stacked_dot(left, high, low):
    half = left.shape[0] // 2
    both = dot(left, high)
    return both[:half] + (both[half:] + dot(left[:half], low))


def lookup(table, place, lane):
    found = jnp.int32(-1)
    for z, entries in enumerate(table):
        for c, entry in enumerate(entries):
            found = jnp.where((place == z) & (lane == c), entry, found)
    return found


def store_piece(piece, plane, code_of, high, low, own=None):
    slab, width, edge, _ = piece.shape
    act = 2 * width

    @pl.when(plane >= 0)
    def _():
        for r in range(slab):
            row = plane * slab + r
            for w in range(width):
                code = code_of(r, w)
                col = pl.ds(pl.multiple_of(code % act * edge, edge), edge)
                block = jnp.where(code < act, piece[r, w], 0.0)
                block_high, block_low = split(block)
                at = pl.ds(pl.multiple_of(row * edge, edge), edge)
                high[at, col] = block_high
                low[at, col] = block_low
                if own is not None:
                    own[pl.ds(r * edge, edge), col] = block_high
                    own[pl.ds((slab + r) * edge, edge), col] = block_low


def table_codes(table_ref, plane, group, slab, width):
    row = jnp.maximum(plane, 0) * slab
    return lambda r, w: table_ref[row + r, group * width + w]


T3, R4, T4, OWN, KEPT = 0, 1, 2, 3, 4


def noted_codes(notes, kind, slab, width):
    return lambda r, w: notes[0, (kind * slab + r) * width + w]


def add_plane(plane, left, high, low, part_ref):
    depth, tile = part_ref.shape[0], 256

    @pl.when(plane >= 0)
    def _():
        rows = pl.ds(pl.multiple_of(plane * depth, depth), depth)
        for n in range(part_ref.shape[1] // tile):
            cols = pl.ds(n * tile, tile)
            part_ref[:, cols] += stacked_dot(left[:, rows], high[rows, cols], low[rows, cols])


def early_kernel(
    tables, table_ref, own_hbm, own_swap, r1, r2, t1, t2, r3,
    high, low, left, part_ref, notes_ref, own_ref, own_sem,
):
    place, lane = lax.axis_index("blk"), lax.axis_index("depth")
    near, far = tables
    slab, width = own_swap.shape[:2]
    act = 2 * width
    own_copy = pltpu.make_async_copy(own_hbm, own_ref, own_sem)
    own_copy.start()
    here, there = lookup(near, place, lane), lookup(near, place, 1 - lane)
    far_here, far_there = lookup(far, place, lane), lookup(far, place, 1 - lane)
    part_ref[...] = jnp.zeros_like(part_ref)

    def codes(plane, group):
        return table_codes(table_ref, plane, group, slab, width)

    kinds = ((far_there, 1 - lane), (far_here, 1 - lane), (far_there, lane), (place, lane))
    notes = jnp.zeros(notes_ref.shape, jnp.int32)
    index = lax.broadcasted_iota(jnp.int32, notes.shape, 1)
    for kind, (plane, group) in enumerate(kinds):
        for r in range(slab):
            for w in range(width):
                at = (kind * slab + r) * width + w
                notes = jnp.where(index == at, codes(plane, group)(r, w), notes)
    for r in range(slab):
        notes = jnp.where(
            index == KEPT * slab * width + r, table_ref[place * slab + r, act], notes
        )
    notes_ref[...] = notes

    store_piece(own_swap, place, codes(place, 1 - lane), high, low, left)
    store_piece(r1, here, codes(here, lane), high, low)
    store_piece(r2, here, codes(here, 1 - lane), high, low)
    store_piece(t1, there, codes(there, 1 - lane), high, low)
    store_piece(t2, there, codes(there, lane), high, low)
    store_piece(r3, far_here, codes(far_here, lane), high, low)
    own_copy.wait()
    store_piece(own_ref, place, codes(place, lane), high, low, left)
    for plane in (place, here, there):
        add_plane(plane, left, high, low, part_ref)


def middle_kernel(
    tables, notes_ref, r4, t3, high_in, low_in, left, part_in, high, low, part_ref
):
    place, lane = lax.axis_index("blk"), lax.axis_index("depth")
    here, there = lookup(tables[1], place, lane), lookup(tables[1], place, 1 - lane)
    slab, width = r4.shape[:2]
    notes = notes_ref[...]
    store_piece(t3, there, noted_codes(notes, T3, slab, width), high, low)
    store_piece(r4, here, noted_codes(notes, R4, slab, width), high, low)
    add_plane(here, left, high, low, part_ref)


def late_kernel(
    tables, notes_ref, t4, high_in, low_in, left, part_in,
    out_hbm, high, low, square, square_parts, out_ref, out_sem,
):
    place, lane = lax.axis_index("blk"), lax.axis_index("depth")
    there = lookup(tables[1], place, 1 - lane)
    slab, width, edge, _ = out_ref.shape
    act = 2 * width
    holds = lax.axis_index("panel") == 0
    notes = notes_ref[...]
    own_codes = noted_codes(notes, OWN, slab, width)
    store_piece(t4, there, noted_codes(notes, T4, slab, width), high, low)
    add_plane(there, left, high, low, square)
    for r in range(slab):
        flags = notes[0, KEPT * slab * width + r]
        for c in range(square.shape[1] // edge):
            kept = (flags >> c) % 2 > 0
            col = pl.ds(c * edge, edge)
            block = jnp.where(kept, square[pl.ds(r * edge, edge), col], 0.0)
            block_high, block_low = split(block)
            square_parts[pl.ds(2 * r * edge, edge), col] = block_high
            square_parts[pl.ds((2 * r + 1) * edge, edge), col] = block_low
    copies = []
    for r in range(slab):
        left_parts = square_parts[pl.ds(2 * r * edge, 2 * edge), :]
        for w in range(0, width, 2):
            codes = [own_codes(r, w + k) for k in range(2)]
            cols = [pl.ds(pl.multiple_of(code % act * edge, edge), edge) for code in codes]
            cube = stacked_dot(
                left_parts,
                jnp.concatenate([high[:, col] for col in cols], axis=1),
                jnp.concatenate([low[:, col] for col in cols], axis=1),
            )
            for k in range(2):
                value = 3.0 * square[pl.ds(r * edge, edge), cols[k]]
                value = value - 2.0 * cube[:, k * edge : (k + 1) * edge]
                out_ref[r, w + k] = jnp.where(holds & (codes[k] < act), value, 0.0)
            ready = (r, pl.ds(w, 2))
            copies.append(
                pltpu.make_async_copy(out_ref.at[ready], out_hbm.at[ready], out_sem.at[len(copies)])
            )
            copies[-1].start()
    for copy in copies:
        copy.wait()


def slot_table(columns, act):
    rows = columns.shape[0]
    slots = columns[:, :act]
    here = slots < rows
    ids = jnp.arange(rows, dtype=jnp.int32)
    taken = jnp.any(slots[:, :, None] == ids, axis=1)
    count = jnp.sum(here.astype(jnp.int32), axis=1, keepdims=True)
    before = jnp.sum(
        (~taken[:, None, :] & (ids[None, :] < ids[:, None])[None]).astype(jnp.int32), axis=2
    )
    at = jnp.where(taken, -1, count + before)
    filled = jnp.sum(
        jnp.where(at[:, None, :] == jnp.arange(act, dtype=jnp.int32)[None, :, None], ids, 0), axis=2
    )
    codes = jnp.where(here, slots, filled + act)
    kept = jnp.sum(jnp.where(taken, 1 << ids, 0), axis=1, keepdims=True)
    return jnp.concatenate([codes, kept], axis=1).astype(jnp.int32)


def gather_local(x_blocks, columns):
    slab, width, edge, _ = x_blocks.shape
    rows = columns.shape[0]
    groups, chains, panels, lanes = (lax.axis_size(axis) for axis in AXES)
    last = chains - 1

    def index(g, place):
        z, x, c = place
        return (((g % groups) * chains + z) * panels + x) * lanes + c

    def move(block, cycles):
        pairs = [(cycle[i - 1], cycle[i]) for cycle in cycles for i in range(len(cycle))]
        busy = {a for a, _ in pairs}
        route = [(index(g, a), index(g, b)) for g in range(groups) for a, b in pairs]
        for z in range(chains):
            for x in range(panels):
                idle = [(z, x, c) for c in range(lanes) if (z, x, c) not in busy]
                for g in range(groups):
                    if len(idle) == lanes:
                        route += [(index(g, idle[c - 1]), index(g, idle[c])) for c in range(lanes)]
                    else:
                        route += [(index(g, a), index(g + 1, a)) for a in idle]
        return lax.ppermute(block, AXES, route)

    def swap(block):
        return move(block, [])

    def move_only(block, chains_of):
        pairs = [(chain[i], chain[i + 1]) for chain in chains_of for i in range(len(chain) - 1)]
        route = [(index(g, a), index(g, b)) for g in range(groups) for a, b in pairs]
        return lax.ppermute(block, AXES, route)

    up = [(z, 0, 1) for z in range(chains)] + [(last, 1, 1)]
    down = [(z, 0, 0) for z in reversed(range(chains))] + [(0, 1, 0)]
    first = [up + [(last, 1, 0)] + down + [(0, 1, 1)]]
    second = [up, down]
    near = [(z + 1 if z < last else -1, z - 1) for z in range(chains)]
    far = [(z + 2 if z + 2 < chains else -1, z - 2 if z >= 2 else -1) for z in range(chains)]
    far[0] = (far[0][0], last)
    far[last] = (0, far[last][1])
    tables = (near, far)

    table = slot_table(columns, lanes * width)
    r1 = move(x_blocks, first)
    own_swap = swap(x_blocks)
    r2 = move_only(own_swap, [up, down])
    r1, table = lax.optimization_barrier((r1, table))
    r3 = move(r1, second)
    t1 = swap(r1)
    r4 = move(r2, second)
    t2 = swap(r2)

    order, own = rows * edge, slab * edge
    table = pltpu.with_memory_space_constraint(table, pltpu.SMEM)
    smem = pl.BlockSpec(memory_space=pltpu.SMEM)
    vmem = pl.BlockSpec(memory_space=pltpu.VMEM)
    params = pltpu.CompilerParams(vmem_limit_bytes=24 * 2**20)
    def held(*arrays):
        return [pltpu.with_memory_space_constraint(a, pltpu.VMEM) for a in arrays]

    high, low, left, part, notes = pl.pallas_call(
        functools.partial(early_kernel, tables),
        out_shape=[
            jax.ShapeDtypeStruct((order, order), jnp.bfloat16),
            jax.ShapeDtypeStruct((order, order), jnp.bfloat16),
            jax.ShapeDtypeStruct((2 * own, order), jnp.bfloat16),
            jax.ShapeDtypeStruct((own, order), jnp.float32),
            jax.ShapeDtypeStruct((8, 128), jnp.int32),
        ],
        in_specs=[smem] + [pl.BlockSpec(memory_space=pltpu.HBM)] + [vmem] * 6,
        out_specs=[vmem] * 5,
        scratch_shapes=[pltpu.VMEM(x_blocks.shape, jnp.float32), pltpu.SemaphoreType.DMA],
        compiler_params=params,
        name="early",
    )(table, pltpu.with_memory_space_constraint(x_blocks, pltpu.HBM), own_swap, r1, r2, t1, t2, r3)
    t3 = swap(r3)
    r4, part = lax.optimization_barrier((r4, part))
    t4 = swap(r4)
    dense = [jax.ShapeDtypeStruct(a.shape, a.dtype) for a in (high, low, part)]
    high, low, part = pl.pallas_call(
        functools.partial(middle_kernel, tables),
        out_shape=dense,
        in_specs=[vmem] * 7,
        out_specs=[vmem] * 3,
        input_output_aliases={3: 0, 4: 1, 6: 2},
        compiler_params=params,
        name="middle",
    )(notes, r4, t3, *held(high, low, left, part))
    out, _, _, _ = pl.pallas_call(
        functools.partial(late_kernel, tables),
        out_shape=[jax.ShapeDtypeStruct(x_blocks.shape, jnp.float32)] + dense,
        in_specs=[vmem] * 6,
        out_specs=[pl.BlockSpec(memory_space=pltpu.HBM)] + [vmem] * 3,
        input_output_aliases={2: 1, 3: 2, 5: 3},
        scratch_shapes=[
            pltpu.VMEM((2 * own, order), jnp.bfloat16),
            pltpu.VMEM(x_blocks.shape, jnp.float32),
            pltpu.SemaphoreType.DMA((slab * width // 2,)),
        ],
        compiler_params=params,
        name="late",
    )(notes, t4, *held(high, low, left, part))
    return out


def local(x_blocks, columns):
    slab, width, edge, _ = x_blocks.shape
    rows, slots = columns.shape
    _, chains, panels, lanes = (lax.axis_size(axis) for axis in AXES)
    full = rows <= slots and rows == lanes * width and width % 2 == 0
    if full and rows <= 8 and slab == 2 and edge == 128 and panels >= 2 and lanes == 2 and chains == 4:
        return gather_local(x_blocks, columns)
    return ring_local(x_blocks, columns)


def solution(mesh):
    placed = (P(("groups", "blk"), ("panel", "depth"), None, None), P("groups", None))
    return jax.shard_map(
        local,
        mesh=mesh,
        in_specs=placed,
        out_specs=P(("groups", "blk"), ("panel", "depth"), None, None),
        check_vma=False,
    )
```

```python
import functools

import jax
import jax.numpy as jnp
from jax import lax
from jax.experimental import pallas as pl
from jax.experimental.pallas import tpu as pltpu
from jax.sharding import PartitionSpec as P

precise = lax.Precision.HIGHEST
AXES = ("groups", "blk", "panel", "depth")


def shifted(block, axis, distance):
    devices = range(lax.axis_size(axis))
    route = [((i - distance) % len(devices), i) for i in devices]
    return lax.ppermute(block, axis, route)


def slot_gather(blocks):
    return lax.all_gather(blocks, ("panel", "depth"), axis=1, tiled=True)


def slot_reduce(partial_value):
    return lax.psum_scatter(partial_value, ("panel", "depth"), scatter_dimension=1, tiled=True)


def rotate_one(incoming):
    return shifted(incoming, "blk", 1)


def ring_local(x_blocks, columns):
    slab_rows = x_blocks.shape[0]
    width_slots = x_blocks.shape[1]
    edge = x_blocks.shape[2]
    order_rows = columns.shape[0]
    all_slots = columns.shape[1]
    cycle_size = lax.axis_size("blk")
    cycle_place = lax.axis_index("blk")
    anchor = jnp.int32(0)
    first_own = cycle_place * slab_rows
    slot_first = lax.axis_index(("panel", "depth")) * width_slots
    my_cols = lax.dynamic_slice(columns, (first_own, anchor), (slab_rows, all_slots))
    own_cols = lax.dynamic_slice(my_cols, (anchor, slot_first), (slab_rows, width_slots))
    x_own = jnp.where((own_cols < order_rows)[:, :, None, None], x_blocks, jnp.float32(0.0))
    out_present = my_cols < order_rows
    empty = jnp.zeros((slab_rows, all_slots, edge, edge), jnp.float32)

    def contribute(partial_value, left_rows, incoming, source):
        group = incoming.shape[0]
        first_row = source * group
        their_cols = lax.dynamic_slice(columns, (first_row, slot_first), (group, width_slots))
        row_ids = first_row + jnp.arange(group, dtype=jnp.int32)
        selector = (my_cols[:, None, :] == row_ids[None, :, None]).astype(jnp.float32)
        picked = jnp.einsum("irs,isab->irab", selector, left_rows, precision=precise)
        products = jnp.einsum("irab,rubc->iruac", picked, incoming, precision=precise)
        targets = (their_cols[None, None, :, :] == my_cols[:, :, None, None]) & out_present[
            :, :, None, None
        ]
        placed = jnp.einsum(
            "isru,iruac->isac", targets.astype(jnp.float32), products, precision=precise
        )
        return partial_value + placed

    def one_way(left_rows, stored):

        def advance(offset, state):
            partial_value, incoming, stored = state
            source = (cycle_place - offset) % cycle_size
            partial_value = contribute(partial_value, left_rows, incoming, source)
            return (partial_value, rotate_one(incoming), stored)

        partial_value, incoming, stored = lax.fori_loop(
            0, cycle_size - 1, advance, (empty, x_own, stored)
        )
        source = (cycle_place + 1) % cycle_size
        return (contribute(partial_value, left_rows, incoming, source), stored)

    stored = jnp.zeros((1,), jnp.float32)
    left_first = slot_gather(x_own)
    partial_value, stored = one_way(left_first, stored)
    squared = slot_reduce(partial_value)
    left_second = slot_gather(squared)
    partial_value, stored = one_way(left_second, stored)
    cubed = slot_reduce(partial_value)
    return 3.0 * squared - 2.0 * cubed


def split(value):
    high = value.astype(jnp.bfloat16)
    low = (value - high.astype(jnp.float32)).astype(jnp.bfloat16)
    return high, low


def dot(left, right):
    return jnp.dot(left, right, preferred_element_type=jnp.float32)


def stacked_dot(left, high, low):
    half = left.shape[0] // 2
    both = dot(left, high)
    return both[:half] + (both[half:] + dot(left[:half], low))


def lookup(table, place, lane):
    found = jnp.int32(-1)
    for z, entries in enumerate(table):
        for c, entry in enumerate(entries):
            found = jnp.where((place == z) & (lane == c), entry, found)
    return found


def store_piece(piece, plane, code_of, high, low, own=None, slab=2, first=0):
    count, width, edge, _ = piece.shape
    act = 2 * width

    @pl.when(plane >= 0)
    def _():
        for r in range(count):
            row = plane * slab + first + r
            for w in range(width):
                code = code_of(first + r, w)
                col = pl.ds(pl.multiple_of(code % act * edge, edge), edge)
                block = jnp.where(code < act, piece[r, w], 0.0)
                block_high, block_low = split(block)
                at = pl.ds(pl.multiple_of(row * edge, edge), edge)
                high[at, col] = block_high
                low[at, col] = block_low
                if own is not None:
                    own[pl.ds(r * edge, edge), col] = block_high
                    own[pl.ds((slab + r) * edge, edge), col] = block_low


def table_codes(table_ref, plane, group, slab, width):
    row = jnp.maximum(plane, 0) * slab
    return lambda r, w: table_ref[row + r, group * width + w]


T3, R4, T4, OWN, KEPT = 0, 1, 2, 3, 4


def noted_codes(notes, kind, slab, width):
    return lambda r, w: notes[0, (kind * slab + r) * width + w]


def add_plane(plane, left, high, low, part_ref):
    depth, tile = part_ref.shape[0], 256

    @pl.when(plane >= 0)
    def _():
        rows = pl.ds(pl.multiple_of(plane * depth, depth), depth)
        for n in range(part_ref.shape[1] // tile):
            cols = pl.ds(n * tile, tile)
            part_ref[:, cols] += stacked_dot(left[:, rows], high[rows, cols], low[rows, cols])


def early_kernel(
    tables, table_ref, own_hbm, own_swap, r1, r2, t1, t2, r3,
    high, low, left, part_ref, notes_ref, own_ref, own_sem,
):
    place, lane = lax.axis_index("blk"), lax.axis_index("depth")
    near, far = tables
    slab, width = own_swap.shape[:2]
    act = 2 * width
    own_copy = pltpu.make_async_copy(own_hbm, own_ref, own_sem)
    own_copy.start()
    here, there = lookup(near, place, lane), lookup(near, place, 1 - lane)
    far_here, far_there = lookup(far, place, lane), lookup(far, place, 1 - lane)
    part_ref[...] = jnp.zeros_like(part_ref)

    def codes(plane, group):
        return table_codes(table_ref, plane, group, slab, width)

    kinds = ((far_there, 1 - lane), (far_here, 1 - lane), (far_there, lane), (place, lane))
    notes = jnp.zeros(notes_ref.shape, jnp.int32)
    index = lax.broadcasted_iota(jnp.int32, notes.shape, 1)
    for kind, (plane, group) in enumerate(kinds):
        for r in range(slab):
            for w in range(width):
                at = (kind * slab + r) * width + w
                notes = jnp.where(index == at, codes(plane, group)(r, w), notes)
    for r in range(slab):
        notes = jnp.where(
            index == KEPT * slab * width + r, table_ref[place * slab + r, act], notes
        )
    notes_ref[...] = notes

    store_piece(own_swap, place, codes(place, 1 - lane), high, low, left)
    store_piece(r1, here, codes(here, lane), high, low)
    store_piece(r2, here, codes(here, 1 - lane), high, low)
    store_piece(t1, there, codes(there, 1 - lane), high, low)
    store_piece(t2, there, codes(there, lane), high, low)
    store_piece(r3, far_here, codes(far_here, lane), high, low)
    own_copy.wait()
    store_piece(own_ref, place, codes(place, lane), high, low, left)
    for plane in (place, here, there):
        add_plane(plane, left, high, low, part_ref)


def middle_kernel(
    tables, notes_ref, r4a, r4b, t3, t4a, high_in, low_in, left, part_in, high, low, part_ref
):
    place, lane = lax.axis_index("blk"), lax.axis_index("depth")
    here, there = lookup(tables[1], place, lane), lookup(tables[1], place, 1 - lane)
    slab, width = t3.shape[:2]
    notes = notes_ref[...]
    store_piece(t3, there, noted_codes(notes, T3, slab, width), high, low)
    store_piece(r4a, here, noted_codes(notes, R4, slab, width), high, low)
    store_piece(t4a, there, noted_codes(notes, T4, slab, width), high, low)
    store_piece(r4b, here, noted_codes(notes, R4, slab, width), high, low, first=1)
    add_plane(here, left, high, low, part_ref)


def late_kernel(
    tables, notes_ref, t4b, high_in, low_in, left, part_in,
    out_hbm, high, low, square, square_parts, out_ref, out_sem,
):
    place, lane = lax.axis_index("blk"), lax.axis_index("depth")
    there = lookup(tables[1], place, 1 - lane)
    slab, width, edge, _ = out_ref.shape
    act = 2 * width
    holds = lax.axis_index("panel") == 0
    notes = notes_ref[...]
    own_codes = noted_codes(notes, OWN, slab, width)
    store_piece(t4b, there, noted_codes(notes, T4, slab, width), high, low, first=1)
    add_plane(there, left, high, low, square)
    for r in range(slab):
        flags = notes[0, KEPT * slab * width + r]
        for c in range(square.shape[1] // edge):
            kept = (flags >> c) % 2 > 0
            col = pl.ds(c * edge, edge)
            block = jnp.where(kept, square[pl.ds(r * edge, edge), col], 0.0)
            block_high, block_low = split(block)
            square_parts[pl.ds(2 * r * edge, edge), col] = block_high
            square_parts[pl.ds((2 * r + 1) * edge, edge), col] = block_low
    copies = []
    for r in range(slab):
        left_parts = square_parts[pl.ds(2 * r * edge, 2 * edge), :]
        for w in range(0, width, 2):
            codes = [own_codes(r, w + k) for k in range(2)]
            cols = [pl.ds(pl.multiple_of(code % act * edge, edge), edge) for code in codes]
            cube = stacked_dot(
                left_parts,
                jnp.concatenate([high[:, col] for col in cols], axis=1),
                jnp.concatenate([low[:, col] for col in cols], axis=1),
            )
            for k in range(2):
                value = 3.0 * square[pl.ds(r * edge, edge), cols[k]]
                value = value - 2.0 * cube[:, k * edge : (k + 1) * edge]
                out_ref[r, w + k] = jnp.where(holds & (codes[k] < act), value, 0.0)
            ready = (r, pl.ds(w, 2))
            copies.append(
                pltpu.make_async_copy(out_ref.at[ready], out_hbm.at[ready], out_sem.at[len(copies)])
            )
            copies[-1].start()
    for copy in copies:
        copy.wait()


def slot_table(columns, act):
    rows = columns.shape[0]
    slots = columns[:, :act]
    here = slots < rows
    ids = jnp.arange(rows, dtype=jnp.int32)
    taken = jnp.any(slots[:, :, None] == ids, axis=1)
    count = jnp.sum(here.astype(jnp.int32), axis=1, keepdims=True)
    before = jnp.sum(
        (~taken[:, None, :] & (ids[None, :] < ids[:, None])[None]).astype(jnp.int32), axis=2
    )
    at = jnp.where(taken, -1, count + before)
    filled = jnp.sum(
        jnp.where(at[:, None, :] == jnp.arange(act, dtype=jnp.int32)[None, :, None], ids, 0), axis=2
    )
    codes = jnp.where(here, slots, filled + act)
    kept = jnp.sum(jnp.where(taken, 1 << ids, 0), axis=1, keepdims=True)
    return jnp.concatenate([codes, kept], axis=1).astype(jnp.int32)


def gather_local(x_blocks, columns):
    slab, width, edge, _ = x_blocks.shape
    rows = columns.shape[0]
    groups, chains, panels, lanes = (lax.axis_size(axis) for axis in AXES)
    last = chains - 1

    def index(g, place):
        z, x, c = place
        return (((g % groups) * chains + z) * panels + x) * lanes + c

    def move(block, cycles):
        pairs = [(cycle[i - 1], cycle[i]) for cycle in cycles for i in range(len(cycle))]
        busy = {a for a, _ in pairs}
        route = [(index(g, a), index(g, b)) for g in range(groups) for a, b in pairs]
        for z in range(chains):
            for x in range(panels):
                idle = [(z, x, c) for c in range(lanes) if (z, x, c) not in busy]
                for g in range(groups):
                    if len(idle) == lanes:
                        route += [(index(g, idle[c - 1]), index(g, idle[c])) for c in range(lanes)]
                    else:
                        route += [(index(g, a), index(g + 1, a)) for a in idle]
        return lax.ppermute(block, AXES, route)

    def swap(block):
        return move(block, [])

    def move_only(block, chains_of):
        pairs = [(chain[i], chain[i + 1]) for chain in chains_of for i in range(len(chain) - 1)]
        route = [(index(g, a), index(g, b)) for g in range(groups) for a, b in pairs]
        return lax.ppermute(block, AXES, route)

    up = [(z, 0, 1) for z in range(chains)] + [(last, 1, 1)]
    down = [(z, 0, 0) for z in reversed(range(chains))] + [(0, 1, 0)]
    first = [up + [(last, 1, 0)] + down + [(0, 1, 1)]]
    second = [up, down]
    near = [(z + 1 if z < last else -1, z - 1) for z in range(chains)]
    far = [(z + 2 if z + 2 < chains else -1, z - 2 if z >= 2 else -1) for z in range(chains)]
    far[0] = (far[0][0], last)
    far[last] = (0, far[last][1])
    tables = (near, far)

    table = slot_table(columns, lanes * width)
    r1 = move(x_blocks, first)
    own_swap = swap(x_blocks)
    r2 = move_only(own_swap, [up, down])
    r1, table = lax.optimization_barrier((r1, table))
    r3 = move(r1, second)
    t1 = swap(r1)
    r4a, r4b = move(r2[:1], second), move(r2[1:], second)
    t2 = swap(r2)

    order, own = rows * edge, slab * edge
    table = pltpu.with_memory_space_constraint(table, pltpu.SMEM)
    smem = pl.BlockSpec(memory_space=pltpu.SMEM)
    vmem = pl.BlockSpec(memory_space=pltpu.VMEM)
    params = pltpu.CompilerParams(vmem_limit_bytes=24 * 2**20)
    def held(*arrays):
        return [pltpu.with_memory_space_constraint(a, pltpu.VMEM) for a in arrays]

    high, low, left, part, notes = pl.pallas_call(
        functools.partial(early_kernel, tables),
        out_shape=[
            jax.ShapeDtypeStruct((order, order), jnp.bfloat16),
            jax.ShapeDtypeStruct((order, order), jnp.bfloat16),
            jax.ShapeDtypeStruct((2 * own, order), jnp.bfloat16),
            jax.ShapeDtypeStruct((own, order), jnp.float32),
            jax.ShapeDtypeStruct((8, 128), jnp.int32),
        ],
        in_specs=[smem] + [pl.BlockSpec(memory_space=pltpu.HBM)] + [vmem] * 6,
        out_specs=[vmem] * 5,
        scratch_shapes=[pltpu.VMEM(x_blocks.shape, jnp.float32), pltpu.SemaphoreType.DMA],
        compiler_params=params,
        name="early",
    )(table, pltpu.with_memory_space_constraint(x_blocks, pltpu.HBM), own_swap, r1, r2, t1, t2, r3)
    t3 = swap(r3)
    r4a, part = lax.optimization_barrier((r4a, part))
    t4a = swap(r4a)
    r4b, t4a = lax.optimization_barrier((r4b, t4a))
    t4b = swap(r4b)
    dense = [jax.ShapeDtypeStruct(a.shape, a.dtype) for a in (high, low, part)]
    high, low, part = pl.pallas_call(
        functools.partial(middle_kernel, tables),
        out_shape=dense,
        in_specs=[vmem] * 9,
        out_specs=[vmem] * 3,
        input_output_aliases={5: 0, 6: 1, 8: 2},
        compiler_params=params,
        name="middle",
    )(notes, r4a, r4b, t3, t4a, *held(high, low, left, part))
    out, _, _, _ = pl.pallas_call(
        functools.partial(late_kernel, tables),
        out_shape=[jax.ShapeDtypeStruct(x_blocks.shape, jnp.float32)] + dense,
        in_specs=[vmem] * 6,
        out_specs=[pl.BlockSpec(memory_space=pltpu.HBM)] + [vmem] * 3,
        input_output_aliases={2: 1, 3: 2, 5: 3},
        scratch_shapes=[
            pltpu.VMEM((2 * own, order), jnp.bfloat16),
            pltpu.VMEM(x_blocks.shape, jnp.float32),
            pltpu.SemaphoreType.DMA((slab * width // 2,)),
        ],
        compiler_params=params,
        name="late",
    )(notes, t4b, *held(high, low, left, part))
    return out


def local(x_blocks, columns):
    slab, width, edge, _ = x_blocks.shape
    rows, slots = columns.shape
    _, chains, panels, lanes = (lax.axis_size(axis) for axis in AXES)
    full = rows <= slots and rows == lanes * width and width % 2 == 0
    if full and rows <= 8 and slab == 2 and edge == 128 and panels >= 2 and lanes == 2 and chains == 4:
        return gather_local(x_blocks, columns)
    return ring_local(x_blocks, columns)


def solution(mesh):
    placed = (P(("groups", "blk"), ("panel", "depth"), None, None), P("groups", None))
    return jax.shard_map(
        local,
        mesh=mesh,
        in_specs=placed,
        out_specs=P(("groups", "blk"), ("panel", "depth"), None, None),
        check_vma=False,
    )
```

```python
import functools

import jax
import jax.numpy as jnp
from jax import lax
from jax.experimental import pallas as pl
from jax.experimental.pallas import tpu as pltpu
from jax.sharding import PartitionSpec as P

precise = lax.Precision.HIGHEST
AXES = ("groups", "blk", "panel", "depth")


def shifted(block, axis, distance):
    devices = range(lax.axis_size(axis))
    route = [((i - distance) % len(devices), i) for i in devices]
    return lax.ppermute(block, axis, route)


def slot_gather(blocks):
    return lax.all_gather(blocks, ("panel", "depth"), axis=1, tiled=True)


def slot_reduce(partial_value):
    return lax.psum_scatter(partial_value, ("panel", "depth"), scatter_dimension=1, tiled=True)


def rotate_one(incoming):
    return shifted(incoming, "blk", 1)


def ring_local(x_blocks, columns):
    slab_rows = x_blocks.shape[0]
    width_slots = x_blocks.shape[1]
    edge = x_blocks.shape[2]
    order_rows = columns.shape[0]
    all_slots = columns.shape[1]
    cycle_size = lax.axis_size("blk")
    cycle_place = lax.axis_index("blk")
    anchor = jnp.int32(0)
    first_own = cycle_place * slab_rows
    slot_first = lax.axis_index(("panel", "depth")) * width_slots
    my_cols = lax.dynamic_slice(columns, (first_own, anchor), (slab_rows, all_slots))
    own_cols = lax.dynamic_slice(my_cols, (anchor, slot_first), (slab_rows, width_slots))
    x_own = jnp.where((own_cols < order_rows)[:, :, None, None], x_blocks, jnp.float32(0.0))
    out_present = my_cols < order_rows
    empty = jnp.zeros((slab_rows, all_slots, edge, edge), jnp.float32)

    def contribute(partial_value, left_rows, incoming, source):
        group = incoming.shape[0]
        first_row = source * group
        their_cols = lax.dynamic_slice(columns, (first_row, slot_first), (group, width_slots))
        row_ids = first_row + jnp.arange(group, dtype=jnp.int32)
        selector = (my_cols[:, None, :] == row_ids[None, :, None]).astype(jnp.float32)
        picked = jnp.einsum("irs,isab->irab", selector, left_rows, precision=precise)
        products = jnp.einsum("irab,rubc->iruac", picked, incoming, precision=precise)
        targets = (their_cols[None, None, :, :] == my_cols[:, :, None, None]) & out_present[
            :, :, None, None
        ]
        placed = jnp.einsum(
            "isru,iruac->isac", targets.astype(jnp.float32), products, precision=precise
        )
        return partial_value + placed

    def one_way(left_rows, stored):

        def advance(offset, state):
            partial_value, incoming, stored = state
            source = (cycle_place - offset) % cycle_size
            partial_value = contribute(partial_value, left_rows, incoming, source)
            return (partial_value, rotate_one(incoming), stored)

        partial_value, incoming, stored = lax.fori_loop(
            0, cycle_size - 1, advance, (empty, x_own, stored)
        )
        source = (cycle_place + 1) % cycle_size
        return (contribute(partial_value, left_rows, incoming, source), stored)

    stored = jnp.zeros((1,), jnp.float32)
    left_first = slot_gather(x_own)
    partial_value, stored = one_way(left_first, stored)
    squared = slot_reduce(partial_value)
    left_second = slot_gather(squared)
    partial_value, stored = one_way(left_second, stored)
    cubed = slot_reduce(partial_value)
    return 3.0 * squared - 2.0 * cubed


def split(value):
    high = value.astype(jnp.bfloat16)
    low = (value - high.astype(jnp.float32)).astype(jnp.bfloat16)
    return high, low


def dot(left, right):
    return jnp.dot(left, right, preferred_element_type=jnp.float32)


def stacked_dot(left, high, low):
    half = left.shape[0] // 2
    both = dot(left, high)
    return both[:half] + (both[half:] + dot(left[:half], low))


def lookup(table, place, lane):
    found = jnp.int32(-1)
    for z, entries in enumerate(table):
        for c, entry in enumerate(entries):
            found = jnp.where((place == z) & (lane == c), entry, found)
    return found


def store_piece(piece, plane, code_of, high, low, own=None, slab=2, first=0):
    count, width, edge, _ = piece.shape
    act = 2 * width

    @pl.when(plane >= 0)
    def _():
        for r in range(count):
            row = plane * slab + first + r
            for w in range(width):
                code = code_of(first + r, w)
                col = pl.ds(pl.multiple_of(code % act * edge, edge), edge)
                block = jnp.where(code < act, piece[r, w], 0.0)
                block_high, block_low = split(block)
                at = pl.ds(pl.multiple_of(row * edge, edge), edge)
                high[at, col] = block_high
                low[at, col] = block_low
                if own is not None:
                    own[pl.ds(r * edge, edge), col] = block_high
                    own[pl.ds((slab + r) * edge, edge), col] = block_low


def table_codes(table_ref, plane, group, slab, width):
    row = jnp.maximum(plane, 0) * slab
    return lambda r, w: table_ref[row + r, group * width + w]


T3, R4, T4, OWN, KEPT = 0, 1, 2, 3, 4


def noted_codes(notes, kind, slab, width):
    return lambda r, w: notes[0, (kind * slab + r) * width + w]


def add_plane(plane, left, high, low, part_ref):
    depth, tile = part_ref.shape[0], 256

    @pl.when(plane >= 0)
    def _():
        rows = pl.ds(pl.multiple_of(plane * depth, depth), depth)
        for n in range(part_ref.shape[1] // tile):
            cols = pl.ds(n * tile, tile)
            part_ref[:, cols] += stacked_dot(left[:, rows], high[rows, cols], low[rows, cols])


def early_kernel(
    tables, table_ref, own_hbm, own_swap, r1, r2, t1, t2, r3,
    high, low, left, part_ref, notes_ref, own_ref, own_sem,
):
    place, lane = lax.axis_index("blk"), lax.axis_index("depth")
    near, far = tables
    slab, width = own_swap.shape[:2]
    act = 2 * width
    own_copy = pltpu.make_async_copy(own_hbm, own_ref, own_sem)
    own_copy.start()
    here, there = lookup(near, place, lane), lookup(near, place, 1 - lane)
    far_here, far_there = lookup(far, place, lane), lookup(far, place, 1 - lane)
    part_ref[...] = jnp.zeros_like(part_ref)

    def codes(plane, group):
        return table_codes(table_ref, plane, group, slab, width)

    kinds = ((far_there, 1 - lane), (far_here, 1 - lane), (far_there, lane), (place, lane))
    notes = jnp.zeros(notes_ref.shape, jnp.int32)
    index = lax.broadcasted_iota(jnp.int32, notes.shape, 1)
    for kind, (plane, group) in enumerate(kinds):
        for r in range(slab):
            for w in range(width):
                at = (kind * slab + r) * width + w
                notes = jnp.where(index == at, codes(plane, group)(r, w), notes)
    for r in range(slab):
        notes = jnp.where(
            index == KEPT * slab * width + r, table_ref[place * slab + r, act], notes
        )
    notes_ref[...] = notes

    store_piece(own_swap, place, codes(place, 1 - lane), high, low, left)
    store_piece(r1, here, codes(here, lane), high, low)
    store_piece(r2, here, codes(here, 1 - lane), high, low)
    store_piece(t1, there, codes(there, 1 - lane), high, low)
    store_piece(t2, there, codes(there, lane), high, low)
    store_piece(r3, far_here, codes(far_here, lane), high, low)
    own_copy.wait()
    store_piece(own_ref, place, codes(place, lane), high, low, left)
    for plane in (place, here, there):
        add_plane(plane, left, high, low, part_ref)


def middle_kernel(
    tables, notes_ref, r4a, r4b, t3, t4a, high_in, low_in, left, part_in, high, low, part_ref
):
    place, lane = lax.axis_index("blk"), lax.axis_index("depth")
    here, there = lookup(tables[1], place, lane), lookup(tables[1], place, 1 - lane)
    slab, width = t3.shape[:2]
    notes = notes_ref[...]
    store_piece(t3, there, noted_codes(notes, T3, slab, width), high, low)
    store_piece(r4a, here, noted_codes(notes, R4, slab, width), high, low)
    store_piece(t4a, there, noted_codes(notes, T4, slab, width), high, low)
    store_piece(r4b, here, noted_codes(notes, R4, slab, width), high, low, first=1)
    add_plane(here, left, high, low, part_ref)


def late_kernel(
    tables, notes_ref, t4b, high_in, low_in, left, part_in,
    out_hbm, high, low, square, square_parts, out_ref, out_sem,
):
    place, lane = lax.axis_index("blk"), lax.axis_index("depth")
    there = lookup(tables[1], place, 1 - lane)
    slab, width, edge, _ = out_ref.shape
    act = 2 * width
    holds = lax.axis_index("panel") == 0
    notes = notes_ref[...]
    own_codes = noted_codes(notes, OWN, slab, width)
    store_piece(t4b, there, noted_codes(notes, T4, slab, width), high, low, first=1)
    add_plane(there, left, high, low, square)
    for r in range(slab):
        flags = notes[0, KEPT * slab * width + r]
        for c in range(square.shape[1] // edge):
            kept = (flags >> c) % 2 > 0
            col = pl.ds(c * edge, edge)
            block = jnp.where(kept, square[pl.ds(r * edge, edge), col], 0.0)
            block_high, block_low = split(block)
            square_parts[pl.ds(2 * r * edge, edge), col] = block_high
            square_parts[pl.ds((2 * r + 1) * edge, edge), col] = block_low
    copies = []
    for r in range(slab):
        left_parts = square_parts[pl.ds(2 * r * edge, 2 * edge), :]
        for w in range(0, width, 2):
            codes = [own_codes(r, w + k) for k in range(2)]
            cols = [pl.ds(pl.multiple_of(code % act * edge, edge), edge) for code in codes]
            cube = stacked_dot(
                left_parts,
                jnp.concatenate([high[:, col] for col in cols], axis=1),
                jnp.concatenate([low[:, col] for col in cols], axis=1),
            )
            for k in range(2):
                value = 3.0 * square[pl.ds(r * edge, edge), cols[k]]
                value = value - 2.0 * cube[:, k * edge : (k + 1) * edge]
                out_ref[r, w + k] = jnp.where(holds & (codes[k] < act), value, 0.0)
            ready = (r, pl.ds(w, 2))
            copies.append(
                pltpu.make_async_copy(out_ref.at[ready], out_hbm.at[ready], out_sem.at[len(copies)])
            )
            copies[-1].start()
    for copy in copies:
        copy.wait()


def slot_table(columns, act):
    rows = columns.shape[0]
    slots = columns[:, :act]
    here = slots < rows
    ids = jnp.arange(rows, dtype=jnp.int32)
    taken = jnp.any(slots[:, :, None] == ids, axis=1)
    count = jnp.sum(here.astype(jnp.int32), axis=1, keepdims=True)
    before = jnp.sum(
        (~taken[:, None, :] & (ids[None, :] < ids[:, None])[None]).astype(jnp.int32), axis=2
    )
    at = jnp.where(taken, -1, count + before)
    filled = jnp.sum(
        jnp.where(at[:, None, :] == jnp.arange(act, dtype=jnp.int32)[None, :, None], ids, 0), axis=2
    )
    codes = jnp.where(here, slots, filled + act)
    kept = jnp.sum(jnp.where(taken, 1 << ids, 0), axis=1, keepdims=True)
    return jnp.concatenate([codes, kept], axis=1).astype(jnp.int32)


def gather_local(x_blocks, columns):
    slab, width, edge, _ = x_blocks.shape
    rows = columns.shape[0]
    groups, chains, panels, lanes = (lax.axis_size(axis) for axis in AXES)
    last = chains - 1

    def index(g, place):
        z, x, c = place
        return (((g % groups) * chains + z) * panels + x) * lanes + c

    def move(block, cycles):
        pairs = [(cycle[i - 1], cycle[i]) for cycle in cycles for i in range(len(cycle))]
        busy = {a for a, _ in pairs}
        route = [(index(g, a), index(g, b)) for g in range(groups) for a, b in pairs]
        for z in range(chains):
            for x in range(panels):
                idle = [(z, x, c) for c in range(lanes) if (z, x, c) not in busy]
                for g in range(groups):
                    if len(idle) == lanes:
                        route += [(index(g, idle[c - 1]), index(g, idle[c])) for c in range(lanes)]
                    else:
                        route += [(index(g, a), index(g + 1, a)) for a in idle]
        return lax.ppermute(block, AXES, route)

    def swap(block):
        return move(block, [])

    def move_only(block, chains_of):
        pairs = [(chain[i], chain[i + 1]) for chain in chains_of for i in range(len(chain) - 1)]
        route = [(index(g, a), index(g, b)) for g in range(groups) for a, b in pairs]
        return lax.ppermute(block, AXES, route)

    up = [(z, 0, 1) for z in range(chains)] + [(last, 1, 1)]
    down = [(z, 0, 0) for z in reversed(range(chains))] + [(0, 1, 0)]
    first = [up + down]
    second = [up, down]
    near = [(z + 1 if z < last else -1, z - 1) for z in range(chains)]
    far = [(z + 2 if z + 2 < chains else -1, z - 2 if z >= 2 else -1) for z in range(chains)]
    far[0] = (far[0][0], last)
    far[last] = (0, far[last][1])
    tables = (near, far)

    table = slot_table(columns, lanes * width)
    r1 = move(x_blocks, first)
    own_swap = swap(x_blocks)
    r2 = move_only(own_swap, [up, down])
    r1, table = lax.optimization_barrier((r1, table))
    r3 = move(r1, second)
    t1 = swap(r1)
    r4a, r4b = move(r2[:1], second), move(r2[1:], second)
    t2 = swap(r2)

    order, own = rows * edge, slab * edge
    table = pltpu.with_memory_space_constraint(table, pltpu.SMEM)
    smem = pl.BlockSpec(memory_space=pltpu.SMEM)
    vmem = pl.BlockSpec(memory_space=pltpu.VMEM)
    params = pltpu.CompilerParams(vmem_limit_bytes=24 * 2**20)
    def held(*arrays):
        return [pltpu.with_memory_space_constraint(a, pltpu.VMEM) for a in arrays]

    high, low, left, part, notes = pl.pallas_call(
        functools.partial(early_kernel, tables),
        out_shape=[
            jax.ShapeDtypeStruct((order, order), jnp.bfloat16),
            jax.ShapeDtypeStruct((order, order), jnp.bfloat16),
            jax.ShapeDtypeStruct((2 * own, order), jnp.bfloat16),
            jax.ShapeDtypeStruct((own, order), jnp.float32),
            jax.ShapeDtypeStruct((8, 128), jnp.int32),
        ],
        in_specs=[smem] + [pl.BlockSpec(memory_space=pltpu.HBM)] + [vmem] * 6,
        out_specs=[vmem] * 5,
        scratch_shapes=[pltpu.VMEM(x_blocks.shape, jnp.float32), pltpu.SemaphoreType.DMA],
        compiler_params=params,
        name="early",
    )(table, pltpu.with_memory_space_constraint(x_blocks, pltpu.HBM), own_swap, r1, r2, t1, t2, r3)
    t3 = swap(r3)
    r4a, part = lax.optimization_barrier((r4a, part))
    t4a = swap(r4a)
    r4b, t4a = lax.optimization_barrier((r4b, t4a))
    t4b = swap(r4b)
    dense = [jax.ShapeDtypeStruct(a.shape, a.dtype) for a in (high, low, part)]
    high, low, part = pl.pallas_call(
        functools.partial(middle_kernel, tables),
        out_shape=dense,
        in_specs=[vmem] * 9,
        out_specs=[vmem] * 3,
        input_output_aliases={5: 0, 6: 1, 8: 2},
        compiler_params=params,
        name="middle",
    )(notes, r4a, r4b, t3, t4a, *held(high, low, left, part))
    out, _, _, _ = pl.pallas_call(
        functools.partial(late_kernel, tables),
        out_shape=[jax.ShapeDtypeStruct(x_blocks.shape, jnp.float32)] + dense,
        in_specs=[vmem] * 6,
        out_specs=[pl.BlockSpec(memory_space=pltpu.HBM)] + [vmem] * 3,
        input_output_aliases={2: 1, 3: 2, 5: 3},
        scratch_shapes=[
            pltpu.VMEM((2 * own, order), jnp.bfloat16),
            pltpu.VMEM(x_blocks.shape, jnp.float32),
            pltpu.SemaphoreType.DMA((slab * width // 2,)),
        ],
        compiler_params=params,
        name="late",
    )(notes, t4b, *held(high, low, left, part))
    return out


def local(x_blocks, columns):
    slab, width, edge, _ = x_blocks.shape
    rows, slots = columns.shape
    _, chains, panels, lanes = (lax.axis_size(axis) for axis in AXES)
    full = rows <= slots and rows == lanes * width and width % 2 == 0
    if full and rows <= 8 and slab == 2 and edge == 128 and panels >= 2 and lanes == 2 and chains == 4:
        return gather_local(x_blocks, columns)
    return ring_local(x_blocks, columns)


def solution(mesh):
    placed = (P(("groups", "blk"), ("panel", "depth"), None, None), P("groups", None))
    return jax.shard_map(
        local,
        mesh=mesh,
        in_specs=placed,
        out_specs=P(("groups", "blk"), ("panel", "depth"), None, None),
        check_vma=False,
    )
```

```python
import functools

import jax
import jax.numpy as jnp
from jax import lax
from jax.experimental import pallas as pl
from jax.experimental.pallas import tpu as pltpu
from jax.sharding import PartitionSpec as P

precise = lax.Precision.HIGHEST
AXES = ("groups", "blk", "panel", "depth")


def shifted(block, axis, distance):
    devices = range(lax.axis_size(axis))
    route = [((i - distance) % len(devices), i) for i in devices]
    return lax.ppermute(block, axis, route)


def slot_gather(blocks):
    return lax.all_gather(blocks, ("panel", "depth"), axis=1, tiled=True)


def slot_reduce(partial_value):
    return lax.psum_scatter(partial_value, ("panel", "depth"), scatter_dimension=1, tiled=True)


def rotate_one(incoming):
    return shifted(incoming, "blk", 1)


def ring_local(x_blocks, columns):
    slab_rows = x_blocks.shape[0]
    width_slots = x_blocks.shape[1]
    edge = x_blocks.shape[2]
    order_rows = columns.shape[0]
    all_slots = columns.shape[1]
    cycle_size = lax.axis_size("blk")
    cycle_place = lax.axis_index("blk")
    anchor = jnp.int32(0)
    first_own = cycle_place * slab_rows
    slot_first = lax.axis_index(("panel", "depth")) * width_slots
    my_cols = lax.dynamic_slice(columns, (first_own, anchor), (slab_rows, all_slots))
    own_cols = lax.dynamic_slice(my_cols, (anchor, slot_first), (slab_rows, width_slots))
    x_own = jnp.where((own_cols < order_rows)[:, :, None, None], x_blocks, jnp.float32(0.0))
    out_present = my_cols < order_rows
    empty = jnp.zeros((slab_rows, all_slots, edge, edge), jnp.float32)

    def contribute(partial_value, left_rows, incoming, source):
        group = incoming.shape[0]
        first_row = source * group
        their_cols = lax.dynamic_slice(columns, (first_row, slot_first), (group, width_slots))
        row_ids = first_row + jnp.arange(group, dtype=jnp.int32)
        selector = (my_cols[:, None, :] == row_ids[None, :, None]).astype(jnp.float32)
        picked = jnp.einsum("irs,isab->irab", selector, left_rows, precision=precise)
        products = jnp.einsum("irab,rubc->iruac", picked, incoming, precision=precise)
        targets = (their_cols[None, None, :, :] == my_cols[:, :, None, None]) & out_present[
            :, :, None, None
        ]
        placed = jnp.einsum(
            "isru,iruac->isac", targets.astype(jnp.float32), products, precision=precise
        )
        return partial_value + placed

    def one_way(left_rows, stored):

        def advance(offset, state):
            partial_value, incoming, stored = state
            source = (cycle_place - offset) % cycle_size
            partial_value = contribute(partial_value, left_rows, incoming, source)
            return (partial_value, rotate_one(incoming), stored)

        partial_value, incoming, stored = lax.fori_loop(
            0, cycle_size - 1, advance, (empty, x_own, stored)
        )
        source = (cycle_place + 1) % cycle_size
        return (contribute(partial_value, left_rows, incoming, source), stored)

    stored = jnp.zeros((1,), jnp.float32)
    left_first = slot_gather(x_own)
    partial_value, stored = one_way(left_first, stored)
    squared = slot_reduce(partial_value)
    left_second = slot_gather(squared)
    partial_value, stored = one_way(left_second, stored)
    cubed = slot_reduce(partial_value)
    return 3.0 * squared - 2.0 * cubed


def split(value):
    high = value.astype(jnp.bfloat16)
    low = (value - high.astype(jnp.float32)).astype(jnp.bfloat16)
    return high, low


def dot(left, right):
    return jnp.dot(left, right, preferred_element_type=jnp.float32)


def stacked_dot(left, high, low):
    half = left.shape[0] // 2
    both = dot(left, high)
    return both[:half] + (both[half:] + dot(left[:half], low))


def lookup(table, place, lane):
    found = jnp.int32(-1)
    for z, entries in enumerate(table):
        for c, entry in enumerate(entries):
            found = jnp.where((place == z) & (lane == c), entry, found)
    return found


def store_piece(piece, plane, code_of, high, low, own=None, slab=2, first=0):
    count, width, edge, _ = piece.shape
    act = 2 * width

    @pl.when(plane >= 0)
    def _():
        for r in range(count):
            row = plane * slab + first + r
            for w in range(width):
                code = code_of(first + r, w)
                col = pl.ds(pl.multiple_of(code % act * edge, edge), edge)
                block = jnp.where(code < act, piece[r, w], 0.0)
                block_high, block_low = split(block)
                at = pl.ds(pl.multiple_of(row * edge, edge), edge)
                high[at, col] = block_high
                low[at, col] = block_low
                if own is not None:
                    own[pl.ds(r * edge, edge), col] = block_high
                    own[pl.ds((slab + r) * edge, edge), col] = block_low


def table_codes(table_ref, plane, group, slab, width):
    row = jnp.maximum(plane, 0) * slab
    return lambda r, w: table_ref[row + r, group * width + w]


T3, R4, T4, OWN, KEPT = 0, 1, 2, 3, 4


def noted_codes(notes, kind, slab, width):
    return lambda r, w: notes[0, (kind * slab + r) * width + w]


def add_plane(plane, left, high, low, part_ref):
    depth, tile = part_ref.shape[0], 512

    @pl.when(plane >= 0)
    def _():
        rows = pl.ds(pl.multiple_of(plane * depth, depth), depth)
        for n in range(part_ref.shape[1] // tile):
            cols = pl.ds(n * tile, tile)
            part_ref[:, cols] += stacked_dot(left[:, rows], high[rows, cols], low[rows, cols])


def early_kernel(
    tables, table_ref, own_hbm, own_swap, r1, r2, t1, t2, r3,
    high, low, left, part_ref, notes_ref, own_ref, own_sem,
):
    place, lane = lax.axis_index("blk"), lax.axis_index("depth")
    near, far = tables
    slab, width = own_swap.shape[:2]
    act = 2 * width
    own_copy = pltpu.make_async_copy(own_hbm, own_ref, own_sem)
    own_copy.start()
    here, there = lookup(near, place, lane), lookup(near, place, 1 - lane)
    far_here, far_there = lookup(far, place, lane), lookup(far, place, 1 - lane)
    part_ref[...] = jnp.zeros_like(part_ref)

    def codes(plane, group):
        return table_codes(table_ref, plane, group, slab, width)

    kinds = ((far_there, 1 - lane), (far_here, 1 - lane), (far_there, lane), (place, lane))
    notes = jnp.zeros(notes_ref.shape, jnp.int32)
    index = lax.broadcasted_iota(jnp.int32, notes.shape, 1)
    for kind, (plane, group) in enumerate(kinds):
        for r in range(slab):
            for w in range(width):
                at = (kind * slab + r) * width + w
                notes = jnp.where(index == at, codes(plane, group)(r, w), notes)
    for r in range(slab):
        notes = jnp.where(
            index == KEPT * slab * width + r, table_ref[place * slab + r, act], notes
        )
    notes_ref[...] = notes

    store_piece(own_swap, place, codes(place, 1 - lane), high, low, left)
    store_piece(r1, here, codes(here, lane), high, low)
    store_piece(r2, here, codes(here, 1 - lane), high, low)
    store_piece(t1, there, codes(there, 1 - lane), high, low)
    store_piece(t2, there, codes(there, lane), high, low)
    store_piece(r3, far_here, codes(far_here, lane), high, low)
    own_copy.wait()
    store_piece(own_ref, place, codes(place, lane), high, low, left)
    for plane in (place, here, there):
        add_plane(plane, left, high, low, part_ref)


def middle_kernel(
    tables, notes_ref, r4a, r4b, t3, t4a, high_in, low_in, left, part_in, high, low, part_ref
):
    place, lane = lax.axis_index("blk"), lax.axis_index("depth")
    here, there = lookup(tables[1], place, lane), lookup(tables[1], place, 1 - lane)
    slab, width = t3.shape[:2]
    notes = notes_ref[...]
    store_piece(t3, there, noted_codes(notes, T3, slab, width), high, low)
    store_piece(r4a, here, noted_codes(notes, R4, slab, width), high, low)
    store_piece(t4a, there, noted_codes(notes, T4, slab, width), high, low)
    store_piece(r4b, here, noted_codes(notes, R4, slab, width), high, low, first=1)
    add_plane(here, left, high, low, part_ref)


def late_kernel(
    tables, notes_ref, t4b, high_in, low_in, left, part_in,
    out_hbm, high, low, square, square_parts, out_ref, out_sem,
):
    place, lane = lax.axis_index("blk"), lax.axis_index("depth")
    there = lookup(tables[1], place, 1 - lane)
    slab, width, edge, _ = out_ref.shape
    act = 2 * width
    holds = lax.axis_index("panel") == 0
    notes = notes_ref[...]
    own_codes = noted_codes(notes, OWN, slab, width)
    store_piece(t4b, there, noted_codes(notes, T4, slab, width), high, low, first=1)
    add_plane(there, left, high, low, square)
    for r in range(slab):
        flags = notes[0, KEPT * slab * width + r]
        for c in range(square.shape[1] // edge):
            kept = (flags >> c) % 2 > 0
            col = pl.ds(c * edge, edge)
            block = jnp.where(kept, square[pl.ds(r * edge, edge), col], 0.0)
            block_high, block_low = split(block)
            square_parts[pl.ds(2 * r * edge, edge), col] = block_high
            square_parts[pl.ds((2 * r + 1) * edge, edge), col] = block_low
    copies = []
    for r in range(slab):
        left_parts = square_parts[pl.ds(2 * r * edge, 2 * edge), :]
        codes = [own_codes(r, w) for w in range(width)]
        cols = [pl.ds(pl.multiple_of(code % act * edge, edge), edge) for code in codes]
        cube = stacked_dot(
            left_parts,
            jnp.concatenate([high[:, col] for col in cols], axis=1),
            jnp.concatenate([low[:, col] for col in cols], axis=1),
        )
        for w in range(width):
            value = 3.0 * square[pl.ds(r * edge, edge), cols[w]]
            value = value - 2.0 * cube[:, w * edge : (w + 1) * edge]
            out_ref[r, w] = jnp.where(holds & (codes[w] < act), value, 0.0)
        copies.append(pltpu.make_async_copy(out_ref.at[r], out_hbm.at[r], out_sem.at[r]))
        copies[-1].start()
    for copy in copies:
        copy.wait()


def slot_table(columns, act):
    rows = columns.shape[0]
    slots = columns[:, :act]
    here = slots < rows
    ids = jnp.arange(rows, dtype=jnp.int32)
    taken = jnp.any(slots[:, :, None] == ids, axis=1)
    count = jnp.sum(here.astype(jnp.int32), axis=1, keepdims=True)
    before = jnp.sum(
        (~taken[:, None, :] & (ids[None, :] < ids[:, None])[None]).astype(jnp.int32), axis=2
    )
    at = jnp.where(taken, -1, count + before)
    filled = jnp.sum(
        jnp.where(at[:, None, :] == jnp.arange(act, dtype=jnp.int32)[None, :, None], ids, 0), axis=2
    )
    codes = jnp.where(here, slots, filled + act)
    kept = jnp.sum(jnp.where(taken, 1 << ids, 0), axis=1, keepdims=True)
    return jnp.concatenate([codes, kept], axis=1).astype(jnp.int32)


def gather_local(x_blocks, columns):
    slab, width, edge, _ = x_blocks.shape
    rows = columns.shape[0]
    groups, chains, panels, lanes = (lax.axis_size(axis) for axis in AXES)
    last = chains - 1

    def index(g, place):
        z, x, c = place
        return (((g % groups) * chains + z) * panels + x) * lanes + c

    def move(block, cycles):
        pairs = [(cycle[i - 1], cycle[i]) for cycle in cycles for i in range(len(cycle))]
        busy = {a for a, _ in pairs}
        route = [(index(g, a), index(g, b)) for g in range(groups) for a, b in pairs]
        for z in range(chains):
            for x in range(panels):
                idle = [(z, x, c) for c in range(lanes) if (z, x, c) not in busy]
                for g in range(groups):
                    if len(idle) == lanes:
                        route += [(index(g, idle[c - 1]), index(g, idle[c])) for c in range(lanes)]
                    else:
                        route += [(index(g, a), index(g + 1, a)) for a in idle]
        return lax.ppermute(block, AXES, route)

    def swap(block):
        return move(block, [])

    def move_only(block, chains_of):
        pairs = [(chain[i], chain[i + 1]) for chain in chains_of for i in range(len(chain) - 1)]
        route = [(index(g, a), index(g, b)) for g in range(groups) for a, b in pairs]
        return lax.ppermute(block, AXES, route)

    up = [(z, 0, 1) for z in range(chains)] + [(last, 1, 1)]
    down = [(z, 0, 0) for z in reversed(range(chains))] + [(0, 1, 0)]
    first = [up + [(last, 1, 0)] + down + [(0, 1, 1)]]
    second = [up, down]
    near = [(z + 1 if z < last else -1, z - 1) for z in range(chains)]
    far = [(z + 2 if z + 2 < chains else -1, z - 2 if z >= 2 else -1) for z in range(chains)]
    far[0] = (far[0][0], last)
    far[last] = (0, far[last][1])
    tables = (near, far)

    table = slot_table(columns, lanes * width)
    r1 = move(x_blocks, first)
    own_swap = swap(x_blocks)
    r2 = move_only(own_swap, [up, down])
    r1, table = lax.optimization_barrier((r1, table))
    r3 = move(r1, second)
    t1 = swap(r1)
    r4a, r4b = move(r2[:1], second), move(r2[1:], second)
    t2 = swap(r2)

    order, own = rows * edge, slab * edge
    table = pltpu.with_memory_space_constraint(table, pltpu.SMEM)
    smem = pl.BlockSpec(memory_space=pltpu.SMEM)
    vmem = pl.BlockSpec(memory_space=pltpu.VMEM)
    params = pltpu.CompilerParams(vmem_limit_bytes=24 * 2**20)
    def held(*arrays):
        return [pltpu.with_memory_space_constraint(a, pltpu.VMEM) for a in arrays]

    high, low, left, part, notes = pl.pallas_call(
        functools.partial(early_kernel, tables),
        out_shape=[
            jax.ShapeDtypeStruct((order, order), jnp.bfloat16),
            jax.ShapeDtypeStruct((order, order), jnp.bfloat16),
            jax.ShapeDtypeStruct((2 * own, order), jnp.bfloat16),
            jax.ShapeDtypeStruct((own, order), jnp.float32),
            jax.ShapeDtypeStruct((8, 128), jnp.int32),
        ],
        in_specs=[smem] + [pl.BlockSpec(memory_space=pltpu.HBM)] + [vmem] * 6,
        out_specs=[vmem] * 5,
        scratch_shapes=[pltpu.VMEM(x_blocks.shape, jnp.float32), pltpu.SemaphoreType.DMA],
        compiler_params=params,
        name="early",
    )(table, pltpu.with_memory_space_constraint(x_blocks, pltpu.HBM), own_swap, r1, r2, t1, t2, r3)
    t3 = swap(r3)
    r4a, part = lax.optimization_barrier((r4a, part))
    t4a = swap(r4a)
    r4b, t4a = lax.optimization_barrier((r4b, t4a))
    t4b = swap(r4b)
    dense = [jax.ShapeDtypeStruct(a.shape, a.dtype) for a in (high, low, part)]
    high, low, part = pl.pallas_call(
        functools.partial(middle_kernel, tables),
        out_shape=dense,
        in_specs=[vmem] * 9,
        out_specs=[vmem] * 3,
        input_output_aliases={5: 0, 6: 1, 8: 2},
        compiler_params=params,
        name="middle",
    )(notes, r4a, r4b, t3, t4a, *held(high, low, left, part))
    out, _, _, _ = pl.pallas_call(
        functools.partial(late_kernel, tables),
        out_shape=[jax.ShapeDtypeStruct(x_blocks.shape, jnp.float32)] + dense,
        in_specs=[vmem] * 6,
        out_specs=[pl.BlockSpec(memory_space=pltpu.HBM)] + [vmem] * 3,
        input_output_aliases={2: 1, 3: 2, 5: 3},
        scratch_shapes=[
            pltpu.VMEM((2 * own, order), jnp.bfloat16),
            pltpu.VMEM(x_blocks.shape, jnp.float32),
            pltpu.SemaphoreType.DMA((slab,)),
        ],
        compiler_params=params,
        name="late",
    )(notes, t4b, *held(high, low, left, part))
    return out


def local(x_blocks, columns):
    slab, width, edge, _ = x_blocks.shape
    rows, slots = columns.shape
    _, chains, panels, lanes = (lax.axis_size(axis) for axis in AXES)
    full = rows <= slots and rows == lanes * width and width % 2 == 0
    if full and rows <= 8 and slab == 2 and edge == 128 and panels >= 2 and lanes == 2 and chains == 4:
        return gather_local(x_blocks, columns)
    return ring_local(x_blocks, columns)


def solution(mesh):
    placed = (P(("groups", "blk"), ("panel", "depth"), None, None), P("groups", None))
    return jax.shard_map(
        local,
        mesh=mesh,
        in_specs=placed,
        out_specs=P(("groups", "blk"), ("panel", "depth"), None, None),
        check_vma=False,
    )
```

```python
import functools

import jax
import jax.numpy as jnp
from jax import lax
from jax.experimental import pallas as pl
from jax.experimental.pallas import tpu as pltpu
from jax.sharding import PartitionSpec as P

precise = lax.Precision.HIGHEST
AXES = ("groups", "blk", "panel", "depth")


def shifted(block, axis, distance):
    devices = range(lax.axis_size(axis))
    route = [((i - distance) % len(devices), i) for i in devices]
    return lax.ppermute(block, axis, route)


def slot_gather(blocks):
    return lax.all_gather(blocks, ("panel", "depth"), axis=1, tiled=True)


def slot_reduce(partial_value):
    return lax.psum_scatter(partial_value, ("panel", "depth"), scatter_dimension=1, tiled=True)


def rotate_one(incoming):
    return shifted(incoming, "blk", 1)


def ring_local(x_blocks, columns):
    slab_rows = x_blocks.shape[0]
    width_slots = x_blocks.shape[1]
    edge = x_blocks.shape[2]
    order_rows = columns.shape[0]
    all_slots = columns.shape[1]
    cycle_size = lax.axis_size("blk")
    cycle_place = lax.axis_index("blk")
    anchor = jnp.int32(0)
    first_own = cycle_place * slab_rows
    slot_first = lax.axis_index(("panel", "depth")) * width_slots
    my_cols = lax.dynamic_slice(columns, (first_own, anchor), (slab_rows, all_slots))
    own_cols = lax.dynamic_slice(my_cols, (anchor, slot_first), (slab_rows, width_slots))
    x_own = jnp.where((own_cols < order_rows)[:, :, None, None], x_blocks, jnp.float32(0.0))
    out_present = my_cols < order_rows
    empty = jnp.zeros((slab_rows, all_slots, edge, edge), jnp.float32)

    def contribute(partial_value, left_rows, incoming, source):
        group = incoming.shape[0]
        first_row = source * group
        their_cols = lax.dynamic_slice(columns, (first_row, slot_first), (group, width_slots))
        row_ids = first_row + jnp.arange(group, dtype=jnp.int32)
        selector = (my_cols[:, None, :] == row_ids[None, :, None]).astype(jnp.float32)
        picked = jnp.einsum("irs,isab->irab", selector, left_rows, precision=precise)
        products = jnp.einsum("irab,rubc->iruac", picked, incoming, precision=precise)
        targets = (their_cols[None, None, :, :] == my_cols[:, :, None, None]) & out_present[
            :, :, None, None
        ]
        placed = jnp.einsum(
            "isru,iruac->isac", targets.astype(jnp.float32), products, precision=precise
        )
        return partial_value + placed

    def one_way(left_rows, stored):

        def advance(offset, state):
            partial_value, incoming, stored = state
            source = (cycle_place - offset) % cycle_size
            partial_value = contribute(partial_value, left_rows, incoming, source)
            return (partial_value, rotate_one(incoming), stored)

        partial_value, incoming, stored = lax.fori_loop(
            0, cycle_size - 1, advance, (empty, x_own, stored)
        )
        source = (cycle_place + 1) % cycle_size
        return (contribute(partial_value, left_rows, incoming, source), stored)

    stored = jnp.zeros((1,), jnp.float32)
    left_first = slot_gather(x_own)
    partial_value, stored = one_way(left_first, stored)
    squared = slot_reduce(partial_value)
    left_second = slot_gather(squared)
    partial_value, stored = one_way(left_second, stored)
    cubed = slot_reduce(partial_value)
    return 3.0 * squared - 2.0 * cubed


def split(value):
    high = value.astype(jnp.bfloat16)
    low = (value - high.astype(jnp.float32)).astype(jnp.bfloat16)
    return high, low


def dot(left, right):
    return jnp.dot(left, right, preferred_element_type=jnp.float32)


def stacked_dot(left, high, low):
    half = left.shape[0] // 2
    both = dot(left, high)
    return both[:half] + (both[half:] + dot(left[:half], low))


def lookup(table, place, lane):
    found = jnp.int32(-1)
    for z, entries in enumerate(table):
        for c, entry in enumerate(entries):
            found = jnp.where((place == z) & (lane == c), entry, found)
    return found


def store_piece(piece, plane, code_of, high, low, own=None, slab=2, first=0):
    count, width, edge, _ = piece.shape
    act = 2 * width

    @pl.when(plane >= 0)
    def _():
        for r in range(count):
            row = plane * slab + first + r
            for w in range(width):
                code = code_of(first + r, w)
                col = pl.ds(pl.multiple_of(code % act * edge, edge), edge)
                block = jnp.where(code < act, piece[r, w], 0.0)
                block_high, block_low = split(block)
                at = pl.ds(pl.multiple_of(row * edge, edge), edge)
                high[at, col] = block_high
                low[at, col] = block_low
                if own is not None:
                    own[pl.ds(r * edge, edge), col] = block_high
                    own[pl.ds((slab + r) * edge, edge), col] = block_low


def table_codes(table_ref, plane, group, slab, width):
    row = jnp.maximum(plane, 0) * slab
    return lambda r, w: table_ref[row + r, group * width + w]


T3, R4, T4, OWN, KEPT = 0, 1, 2, 3, 4


def noted_codes(notes, kind, slab, width):
    return lambda r, w: notes[0, (kind * slab + r) * width + w]


def add_plane(plane, left, high, low, part_ref):
    depth, tile = part_ref.shape[0], 256

    @pl.when(plane >= 0)
    def _():
        rows = pl.ds(pl.multiple_of(plane * depth, depth), depth)
        for n in range(part_ref.shape[1] // tile):
            cols = pl.ds(n * tile, tile)
            part_ref[:, cols] += stacked_dot(left[:, rows], high[rows, cols], low[rows, cols])


def early_kernel(
    tables, table_ref, own_hbm, own_swap, r1, r2, t1, t2, r3,
    high, low, left, part_ref, notes_ref, own_ref, own_sem,
):
    place, lane = lax.axis_index("blk"), lax.axis_index("depth")
    near, far = tables
    slab, width = own_swap.shape[:2]
    act = 2 * width
    own_copy = pltpu.make_async_copy(own_hbm, own_ref, own_sem)
    own_copy.start()
    here, there = lookup(near, place, lane), lookup(near, place, 1 - lane)
    far_here, far_there = lookup(far, place, lane), lookup(far, place, 1 - lane)
    part_ref[...] = jnp.zeros_like(part_ref)

    def codes(plane, group):
        return table_codes(table_ref, plane, group, slab, width)

    kinds = ((far_there, 1 - lane), (far_here, 1 - lane), (far_there, lane), (place, lane))
    notes = jnp.zeros(notes_ref.shape, jnp.int32)
    index = lax.broadcasted_iota(jnp.int32, notes.shape, 1)
    for kind, (plane, group) in enumerate(kinds):
        for r in range(slab):
            for w in range(width):
                at = (kind * slab + r) * width + w
                notes = jnp.where(index == at, codes(plane, group)(r, w), notes)
    for r in range(slab):
        notes = jnp.where(
            index == KEPT * slab * width + r, table_ref[place * slab + r, act], notes
        )
    notes_ref[...] = notes

    store_piece(own_swap, place, codes(place, 1 - lane), high, low, left)
    store_piece(r1, here, codes(here, lane), high, low)
    store_piece(r2, here, codes(here, 1 - lane), high, low)
    store_piece(t1, there, codes(there, 1 - lane), high, low)
    store_piece(t2, there, codes(there, lane), high, low)
    store_piece(r3, far_here, codes(far_here, lane), high, low)
    own_copy.wait()
    store_piece(own_ref, place, codes(place, lane), high, low, left)
    for plane in (place, here, there):
        add_plane(plane, left, high, low, part_ref)


def middle_kernel(
    tables, notes_ref, r4a, r4b, t3, t4a, high_in, low_in, left, part_in, high, low, part_ref
):
    place, lane = lax.axis_index("blk"), lax.axis_index("depth")
    here, there = lookup(tables[1], place, lane), lookup(tables[1], place, 1 - lane)
    slab, width = t3.shape[:2]
    notes = notes_ref[...]
    store_piece(t3, there, noted_codes(notes, T3, slab, width), high, low)
    store_piece(r4a, here, noted_codes(notes, R4, slab, width), high, low)
    store_piece(t4a, there, noted_codes(notes, T4, slab, width), high, low)
    store_piece(r4b, here, noted_codes(notes, R4, slab, width), high, low, first=1)
    add_plane(here, left, high, low, part_ref)


def late_kernel(
    tables, notes_ref, t4b, high_in, low_in, left, part_in,
    out_hbm, high, low, square, square_parts, out_ref, out_sem,
):
    place, lane = lax.axis_index("blk"), lax.axis_index("depth")
    there = lookup(tables[1], place, 1 - lane)
    slab, width, edge, _ = out_ref.shape
    act = 2 * width
    holds = lax.axis_index("panel") == 0
    notes = notes_ref[...]
    own_codes = noted_codes(notes, OWN, slab, width)
    store_piece(t4b, there, noted_codes(notes, T4, slab, width), high, low, first=1)
    add_plane(there, left, high, low, square)
    for r in range(slab):
        flags = notes[0, KEPT * slab * width + r]
        for c in range(square.shape[1] // edge):
            kept = (flags >> c) % 2 > 0
            col = pl.ds(c * edge, edge)
            block = jnp.where(kept, square[pl.ds(r * edge, edge), col], 0.0)
            block_high, block_low = split(block)
            square_parts[pl.ds(2 * r * edge, edge), col] = block_high
            square_parts[pl.ds((2 * r + 1) * edge, edge), col] = block_low
    copies = []
    for r in range(slab):
        left_parts = square_parts[pl.ds(2 * r * edge, 2 * edge), :]
        for w in range(0, width, 2):
            codes = [own_codes(r, w + k) for k in range(2)]
            cols = [pl.ds(pl.multiple_of(code % act * edge, edge), edge) for code in codes]
            cube = stacked_dot(
                left_parts,
                jnp.concatenate([high[:, col] for col in cols], axis=1),
                jnp.concatenate([low[:, col] for col in cols], axis=1),
            )
            for k in range(2):
                value = 3.0 * square[pl.ds(r * edge, edge), cols[k]]
                value = value - 2.0 * cube[:, k * edge : (k + 1) * edge]
                out_ref[r, w + k] = jnp.where(holds & (codes[k] < act), value, 0.0)
            ready = (r, pl.ds(w, 2))
            copies.append(
                pltpu.make_async_copy(out_ref.at[ready], out_hbm.at[ready], out_sem.at[len(copies)])
            )
            copies[-1].start()
    for copy in copies:
        copy.wait()


def slot_table(columns, act):
    rows = columns.shape[0]
    slots = columns[:, :act]
    here = slots < rows
    ids = jnp.arange(rows, dtype=jnp.int32)
    taken = jnp.any(slots[:, :, None] == ids, axis=1)
    count = jnp.sum(here.astype(jnp.int32), axis=1, keepdims=True)
    before = jnp.sum(
        (~taken[:, None, :] & (ids[None, :] < ids[:, None])[None]).astype(jnp.int32), axis=2
    )
    at = jnp.where(taken, -1, count + before)
    filled = jnp.sum(
        jnp.where(at[:, None, :] == jnp.arange(act, dtype=jnp.int32)[None, :, None], ids, 0), axis=2
    )
    codes = jnp.where(here, slots, filled + act)
    kept = jnp.sum(jnp.where(taken, 1 << ids, 0), axis=1, keepdims=True)
    return jnp.concatenate([codes, kept], axis=1).astype(jnp.int32)


def gather_local(x_blocks, columns):
    slab, width, edge, _ = x_blocks.shape
    rows = columns.shape[0]
    groups, chains, panels, lanes = (lax.axis_size(axis) for axis in AXES)
    last = chains - 1

    def index(g, place):
        z, x, c = place
        return (((g % groups) * chains + z) * panels + x) * lanes + c

    def move(block, cycles):
        pairs = [(cycle[i - 1], cycle[i]) for cycle in cycles for i in range(len(cycle))]
        busy = {a for a, _ in pairs}
        route = [(index(g, a), index(g, b)) for g in range(groups) for a, b in pairs]
        for z in range(chains):
            for x in range(panels):
                idle = [(z, x, c) for c in range(lanes) if (z, x, c) not in busy]
                for g in range(groups):
                    if len(idle) == lanes:
                        route += [(index(g, idle[c - 1]), index(g, idle[c])) for c in range(lanes)]
                    else:
                        route += [(index(g, a), index(g + 1, a)) for a in idle]
        return lax.ppermute(block, AXES, route)

    def swap(block):
        return move(block, [])

    def move_only(block, chains_of):
        pairs = [(chain[i], chain[i + 1]) for chain in chains_of for i in range(len(chain) - 1)]
        route = [(index(g, a), index(g, b)) for g in range(groups) for a, b in pairs]
        return lax.ppermute(block, AXES, route)

    up = [(z, 0, 1) for z in range(chains)] + [(last, 1, 1)]
    down = [(z, 0, 0) for z in reversed(range(chains))] + [(0, 1, 0)]
    first = [up + [(last, 1, 0)] + down + [(0, 1, 1)]]
    second = [
        up[:-1] + [(last, 1, 0), up[-1]],
        down[:-1] + [(0, 1, 1), down[-1]],
    ]
    near = [(z + 1 if z < last else -1, z - 1) for z in range(chains)]
    far = [(z + 2 if z + 2 < chains else -1, z - 2 if z >= 2 else -1) for z in range(chains)]
    far[0] = (far[0][0], last)
    far[last] = (0, far[last][1])
    tables = (near, far)

    table = slot_table(columns, lanes * width)
    r1 = move(x_blocks, first)
    own_swap = swap(x_blocks)
    r2 = move_only(own_swap, [up, down])
    r1, table = lax.optimization_barrier((r1, table))
    r3 = move(r1, second)
    t1 = swap(r1)
    r4a, r4b = move(r2[:1], second), move(r2[1:], second)
    t2 = swap(r2)

    order, own = rows * edge, slab * edge
    table = pltpu.with_memory_space_constraint(table, pltpu.SMEM)
    smem = pl.BlockSpec(memory_space=pltpu.SMEM)
    vmem = pl.BlockSpec(memory_space=pltpu.VMEM)
    params = pltpu.CompilerParams(vmem_limit_bytes=24 * 2**20)
    def held(*arrays):
        return [pltpu.with_memory_space_constraint(a, pltpu.VMEM) for a in arrays]

    high, low, left, part, notes = pl.pallas_call(
        functools.partial(early_kernel, tables),
        out_shape=[
            jax.ShapeDtypeStruct((order, order), jnp.bfloat16),
            jax.ShapeDtypeStruct((order, order), jnp.bfloat16),
            jax.ShapeDtypeStruct((2 * own, order), jnp.bfloat16),
            jax.ShapeDtypeStruct((own, order), jnp.float32),
            jax.ShapeDtypeStruct((8, 128), jnp.int32),
        ],
        in_specs=[smem] + [pl.BlockSpec(memory_space=pltpu.HBM)] + [vmem] * 6,
        out_specs=[vmem] * 5,
        scratch_shapes=[pltpu.VMEM(x_blocks.shape, jnp.float32), pltpu.SemaphoreType.DMA],
        compiler_params=params,
        name="early",
    )(table, pltpu.with_memory_space_constraint(x_blocks, pltpu.HBM), own_swap, r1, r2, t1, t2, r3)
    t3 = swap(r3)
    r4a, part = lax.optimization_barrier((r4a, part))
    t4a = swap(r4a)
    r4b, t4a = lax.optimization_barrier((r4b, t4a))
    t4b = swap(r4b)
    dense = [jax.ShapeDtypeStruct(a.shape, a.dtype) for a in (high, low, part)]
    high, low, part = pl.pallas_call(
        functools.partial(middle_kernel, tables),
        out_shape=dense,
        in_specs=[vmem] * 9,
        out_specs=[vmem] * 3,
        input_output_aliases={5: 0, 6: 1, 8: 2},
        compiler_params=params,
        name="middle",
    )(notes, r4a, r4b, t3, t4a, *held(high, low, left, part))
    out, _, _, _ = pl.pallas_call(
        functools.partial(late_kernel, tables),
        out_shape=[jax.ShapeDtypeStruct(x_blocks.shape, jnp.float32)] + dense,
        in_specs=[vmem] * 6,
        out_specs=[pl.BlockSpec(memory_space=pltpu.HBM)] + [vmem] * 3,
        input_output_aliases={2: 1, 3: 2, 5: 3},
        scratch_shapes=[
            pltpu.VMEM((2 * own, order), jnp.bfloat16),
            pltpu.VMEM(x_blocks.shape, jnp.float32),
            pltpu.SemaphoreType.DMA((slab * width // 2,)),
        ],
        compiler_params=params,
        name="late",
    )(notes, t4b, *held(high, low, left, part))
    return out


def local(x_blocks, columns):
    slab, width, edge, _ = x_blocks.shape
    rows, slots = columns.shape
    _, chains, panels, lanes = (lax.axis_size(axis) for axis in AXES)
    full = rows <= slots and rows == lanes * width and width % 2 == 0
    if full and rows <= 8 and slab == 2 and edge == 128 and panels >= 2 and lanes == 2 and chains == 4:
        return gather_local(x_blocks, columns)
    return ring_local(x_blocks, columns)


def solution(mesh):
    placed = (P(("groups", "blk"), ("panel", "depth"), None, None), P("groups", None))
    return jax.shard_map(
        local,
        mesh=mesh,
        in_specs=placed,
        out_specs=P(("groups", "blk"), ("panel", "depth"), None, None),
        check_vma=False,
    )
```

```python
import functools

import jax
import jax.numpy as jnp
from jax import lax
from jax.experimental import pallas as pl
from jax.experimental.pallas import tpu as pltpu
from jax.sharding import PartitionSpec as P

precise = lax.Precision.HIGHEST
AXES = ("groups", "blk", "panel", "depth")


def shifted(block, axis, distance):
    devices = range(lax.axis_size(axis))
    route = [((i - distance) % len(devices), i) for i in devices]
    return lax.ppermute(block, axis, route)


def slot_gather(blocks):
    return lax.all_gather(blocks, ("panel", "depth"), axis=1, tiled=True)


def slot_reduce(partial_value):
    return lax.psum_scatter(partial_value, ("panel", "depth"), scatter_dimension=1, tiled=True)


def rotate_one(incoming):
    return shifted(incoming, "blk", 1)


def ring_local(x_blocks, columns):
    slab_rows = x_blocks.shape[0]
    width_slots = x_blocks.shape[1]
    edge = x_blocks.shape[2]
    order_rows = columns.shape[0]
    all_slots = columns.shape[1]
    cycle_size = lax.axis_size("blk")
    cycle_place = lax.axis_index("blk")
    anchor = jnp.int32(0)
    first_own = cycle_place * slab_rows
    slot_first = lax.axis_index(("panel", "depth")) * width_slots
    my_cols = lax.dynamic_slice(columns, (first_own, anchor), (slab_rows, all_slots))
    own_cols = lax.dynamic_slice(my_cols, (anchor, slot_first), (slab_rows, width_slots))
    x_own = jnp.where((own_cols < order_rows)[:, :, None, None], x_blocks, jnp.float32(0.0))
    out_present = my_cols < order_rows
    empty = jnp.zeros((slab_rows, all_slots, edge, edge), jnp.float32)

    def contribute(partial_value, left_rows, incoming, source):
        group = incoming.shape[0]
        first_row = source * group
        their_cols = lax.dynamic_slice(columns, (first_row, slot_first), (group, width_slots))
        row_ids = first_row + jnp.arange(group, dtype=jnp.int32)
        selector = (my_cols[:, None, :] == row_ids[None, :, None]).astype(jnp.float32)
        picked = jnp.einsum("irs,isab->irab", selector, left_rows, precision=precise)
        products = jnp.einsum("irab,rubc->iruac", picked, incoming, precision=precise)
        targets = (their_cols[None, None, :, :] == my_cols[:, :, None, None]) & out_present[
            :, :, None, None
        ]
        placed = jnp.einsum(
            "isru,iruac->isac", targets.astype(jnp.float32), products, precision=precise
        )
        return partial_value + placed

    def one_way(left_rows, stored):

        def advance(offset, state):
            partial_value, incoming, stored = state
            source = (cycle_place - offset) % cycle_size
            partial_value = contribute(partial_value, left_rows, incoming, source)
            return (partial_value, rotate_one(incoming), stored)

        partial_value, incoming, stored = lax.fori_loop(
            0, cycle_size - 1, advance, (empty, x_own, stored)
        )
        source = (cycle_place + 1) % cycle_size
        return (contribute(partial_value, left_rows, incoming, source), stored)

    stored = jnp.zeros((1,), jnp.float32)
    left_first = slot_gather(x_own)
    partial_value, stored = one_way(left_first, stored)
    squared = slot_reduce(partial_value)
    left_second = slot_gather(squared)
    partial_value, stored = one_way(left_second, stored)
    cubed = slot_reduce(partial_value)
    return 3.0 * squared - 2.0 * cubed


def split(value):
    high = value.astype(jnp.bfloat16)
    low = (value - high.astype(jnp.float32)).astype(jnp.bfloat16)
    return high, low


def dot(left, right):
    return jnp.dot(left, right, preferred_element_type=jnp.float32)


def stacked_dot(left, high, low):
    half = left.shape[0] // 2
    both = dot(left, high)
    return both[:half] + (both[half:] + dot(left[:half], low))


def lookup(table, place, lane):
    found = jnp.int32(-1)
    for z, entries in enumerate(table):
        for c, entry in enumerate(entries):
            found = jnp.where((place == z) & (lane == c), entry, found)
    return found


def store_piece(piece, plane, code_of, high, low, own=None, slab=2, first=0):
    count, width, edge, _ = piece.shape
    act = 2 * width

    @pl.when(plane >= 0)
    def _():
        for r in range(count):
            row = plane * slab + first + r
            for w in range(width):
                code = code_of(first + r, w)
                col = pl.ds(pl.multiple_of(code % act * edge, edge), edge)
                block = jnp.where(code < act, piece[r, w], 0.0)
                block_high, block_low = split(block)
                at = pl.ds(pl.multiple_of(row * edge, edge), edge)
                high[at, col] = block_high
                low[at, col] = block_low
                if own is not None:
                    own[pl.ds(r * edge, edge), col] = block_high
                    own[pl.ds((slab + r) * edge, edge), col] = block_low


def table_codes(table_ref, plane, group, slab, width):
    row = jnp.maximum(plane, 0) * slab
    return lambda r, w: table_ref[row + r, group * width + w]


T3, R4, T4, OWN, KEPT = 0, 1, 2, 3, 4


def noted_codes(notes, kind, slab, width):
    return lambda r, w: notes[0, (kind * slab + r) * width + w]


def add_plane(plane, left, high, low, part_ref):
    depth, tile = part_ref.shape[0], 512

    @pl.when(plane >= 0)
    def _():
        rows = pl.ds(pl.multiple_of(plane * depth, depth), depth)
        for n in range(part_ref.shape[1] // tile):
            cols = pl.ds(n * tile, tile)
            part_ref[:, cols] += stacked_dot(left[:, rows], high[rows, cols], low[rows, cols])


def early_kernel(
    tables, table_ref, own_hbm, own_swap, r1, r2, t1, t2, r3,
    high, low, left, part_ref, notes_ref, own_ref, own_sem,
):
    place, lane = lax.axis_index("blk"), lax.axis_index("depth")
    (near, near_senders), (far, far_senders) = tables
    slab, width = own_swap.shape[:2]
    act = 2 * width
    own_copy = pltpu.make_async_copy(own_hbm, own_ref, own_sem)
    own_copy.start()
    here, there = lookup(near, place, lane), lookup(near, place, 1 - lane)
    far_here, far_there = lookup(far, place, lane), lookup(far, place, 1 - lane)
    sender, other_sender = [lookup(near_senders, place, c) for c in (lane, 1 - lane)]
    far_sender, far_other = [lookup(far_senders, place, c) for c in (lane, 1 - lane)]
    part_ref[...] = jnp.zeros_like(part_ref)

    def codes(plane, group):
        return table_codes(table_ref, plane, group, slab, width)

    kinds = (
        (far_there, far_other),
        (far_here, 1 - far_sender),
        (far_there, 1 - far_other),
        (place, lane),
    )
    notes = jnp.zeros(notes_ref.shape, jnp.int32)
    index = lax.broadcasted_iota(jnp.int32, notes.shape, 1)
    for kind, (plane, group) in enumerate(kinds):
        for r in range(slab):
            for w in range(width):
                at = (kind * slab + r) * width + w
                notes = jnp.where(index == at, codes(plane, group)(r, w), notes)
    for r in range(slab):
        notes = jnp.where(
            index == KEPT * slab * width + r, table_ref[place * slab + r, act], notes
        )
    notes_ref[...] = notes

    store_piece(own_swap, place, codes(place, 1 - lane), high, low, left)
    store_piece(r1, here, codes(here, sender), high, low)
    store_piece(r2, here, codes(here, 1 - sender), high, low)
    store_piece(t1, there, codes(there, other_sender), high, low)
    store_piece(t2, there, codes(there, 1 - other_sender), high, low)
    store_piece(r3, far_here, codes(far_here, far_sender), high, low)
    own_copy.wait()
    store_piece(own_ref, place, codes(place, lane), high, low, left)
    for plane in (place, here, there):
        add_plane(plane, left, high, low, part_ref)


def middle_kernel(
    tables, notes_ref, r4a, r4b, t3, t4a, high_in, low_in, left, part_in, high, low, part_ref
):
    place, lane = lax.axis_index("blk"), lax.axis_index("depth")
    here, there = [lookup(tables[1][0], place, c) for c in (lane, 1 - lane)]
    slab, width = t3.shape[:2]
    notes = notes_ref[...]
    store_piece(t3, there, noted_codes(notes, T3, slab, width), high, low)
    store_piece(r4a, here, noted_codes(notes, R4, slab, width), high, low)
    store_piece(t4a, there, noted_codes(notes, T4, slab, width), high, low)
    store_piece(r4b, here, noted_codes(notes, R4, slab, width), high, low, first=1)
    add_plane(here, left, high, low, part_ref)


def late_kernel(
    tables, notes_ref, t4b, high_in, low_in, left, part_in,
    out_hbm, high, low, square, square_parts, out_ref, out_sem,
):
    place, lane = lax.axis_index("blk"), lax.axis_index("depth")
    there = lookup(tables[1][0], place, 1 - lane)
    slab, width, edge, _ = out_ref.shape
    act = 2 * width
    holds = lax.axis_index("panel") == 0
    notes = notes_ref[...]
    own_codes = noted_codes(notes, OWN, slab, width)
    store_piece(t4b, there, noted_codes(notes, T4, slab, width), high, low, first=1)
    add_plane(there, left, high, low, square)
    for r in range(slab):
        flags = notes[0, KEPT * slab * width + r]
        for c in range(square.shape[1] // edge):
            kept = (flags >> c) % 2 > 0
            col = pl.ds(c * edge, edge)
            block = jnp.where(kept, square[pl.ds(r * edge, edge), col], 0.0)
            block_high, block_low = split(block)
            square_parts[pl.ds(2 * r * edge, edge), col] = block_high
            square_parts[pl.ds((2 * r + 1) * edge, edge), col] = block_low
    copies = []
    for r in range(slab):
        left_parts = square_parts[pl.ds(2 * r * edge, 2 * edge), :]
        codes = [own_codes(r, w) for w in range(width)]
        cols = [pl.ds(pl.multiple_of(code % act * edge, edge), edge) for code in codes]
        cube = stacked_dot(
            left_parts,
            jnp.concatenate([high[:, col] for col in cols], axis=1),
            jnp.concatenate([low[:, col] for col in cols], axis=1),
        )
        for w in range(width):
            value = 3.0 * square[pl.ds(r * edge, edge), cols[w]]
            value = value - 2.0 * cube[:, w * edge : (w + 1) * edge]
            out_ref[r, w] = jnp.where(holds & (codes[w] < act), value, 0.0)
        copies.append(pltpu.make_async_copy(out_ref.at[r], out_hbm.at[r], out_sem.at[r]))
        copies[-1].start()
    for copy in copies:
        copy.wait()


def slot_table(columns, act):
    rows = columns.shape[0]
    slots = columns[:, :act]
    here = slots < rows
    ids = jnp.arange(rows, dtype=jnp.int32)
    taken = jnp.any(slots[:, :, None] == ids, axis=1)
    count = jnp.sum(here.astype(jnp.int32), axis=1, keepdims=True)
    before = jnp.sum(
        (~taken[:, None, :] & (ids[None, :] < ids[:, None])[None]).astype(jnp.int32), axis=2
    )
    at = jnp.where(taken, -1, count + before)
    filled = jnp.sum(
        jnp.where(at[:, None, :] == jnp.arange(act, dtype=jnp.int32)[None, :, None], ids, 0), axis=2
    )
    codes = jnp.where(here, slots, filled + act)
    kept = jnp.sum(jnp.where(taken, 1 << ids, 0), axis=1, keepdims=True)
    return jnp.concatenate([codes, kept], axis=1).astype(jnp.int32)


def gather_local(x_blocks, columns):
    slab, width, edge, _ = x_blocks.shape
    rows = columns.shape[0]
    groups, chains, panels, lanes = (lax.axis_size(axis) for axis in AXES)
    last = chains - 1

    def index(g, place):
        z, x, c = place
        return (((g % groups) * chains + z) * panels + x) * lanes + c

    def move(block, cycles):
        pairs = [(cycle[i - 1], cycle[i]) for cycle in cycles for i in range(len(cycle))]
        busy = {a for a, _ in pairs}
        route = [(index(g, a), index(g, b)) for g in range(groups) for a, b in pairs]
        for z in range(chains):
            for x in range(panels):
                idle = [(z, x, c) for c in range(lanes) if (z, x, c) not in busy]
                for g in range(groups):
                    if len(idle) == lanes:
                        route += [(index(g, idle[c - 1]), index(g, idle[c])) for c in range(lanes)]
                    else:
                        route += [(index(g, a), index(g + 1, a)) for a in idle]
        return lax.ppermute(block, AXES, route)

    def swap(block):
        return move(block, [])

    def move_only(block, chains_of):
        pairs = [(chain[i], chain[i + 1]) for chain in chains_of for i in range(len(chain) - 1)]
        route = [(index(g, a), index(g, b)) for g in range(groups) for a, b in pairs]
        return lax.ppermute(block, AXES, route)

    down_lane = [1 if z == 1 else 0 for z in range(chains)]
    up_lane = [1 - c for c in down_lane]
    up = [(z, 0, up_lane[z]) for z in range(chains)] + [(last, 1, up_lane[last])]
    down = [(z, 0, down_lane[z]) for z in reversed(range(chains))] + [(0, 1, down_lane[0])]
    first = [up + [(last, 1, down_lane[last])] + down + [(0, 1, up_lane[0])]]
    second = [up, down]

    def received(hops):
        planes, senders = [], []
        for z in range(chains):
            below = z - hops if z >= hops else -1
            above = z + hops if z + hops < chains else -1
            if hops == 2:
                below, above = last if z == 0 else below, 0 if z == last else above
            row = [above, below] if down_lane[z] == 0 else [below, above]
            lane_of = [down_lane, up_lane] if down_lane[z] == 0 else [up_lane, down_lane]
            planes.append(row)
            senders.append([lanes_of[plane] for plane, lanes_of in zip(row, lane_of)])
        return planes, senders

    tables = received(1), received(2)

    table = slot_table(columns, lanes * width)
    r1 = move(x_blocks, first)
    own_swap = swap(x_blocks)
    r2 = move_only(own_swap, [up, down])
    r1, table = lax.optimization_barrier((r1, table))
    r3 = move(r1, second)
    t1 = swap(r1)
    r4a, r4b = move(r2[:1], second), move(r2[1:], second)
    t2 = swap(r2)

    order, own = rows * edge, slab * edge
    table = pltpu.with_memory_space_constraint(table, pltpu.SMEM)
    smem = pl.BlockSpec(memory_space=pltpu.SMEM)
    vmem = pl.BlockSpec(memory_space=pltpu.VMEM)
    params = pltpu.CompilerParams(vmem_limit_bytes=24 * 2**20)
    def held(*arrays):
        return [pltpu.with_memory_space_constraint(a, pltpu.VMEM) for a in arrays]

    high, low, left, part, notes = pl.pallas_call(
        functools.partial(early_kernel, tables),
        out_shape=[
            jax.ShapeDtypeStruct((order, order), jnp.bfloat16),
            jax.ShapeDtypeStruct((order, order), jnp.bfloat16),
            jax.ShapeDtypeStruct((2 * own, order), jnp.bfloat16),
            jax.ShapeDtypeStruct((own, order), jnp.float32),
            jax.ShapeDtypeStruct((8, 128), jnp.int32),
        ],
        in_specs=[smem] + [pl.BlockSpec(memory_space=pltpu.HBM)] + [vmem] * 6,
        out_specs=[vmem] * 5,
        scratch_shapes=[pltpu.VMEM(x_blocks.shape, jnp.float32), pltpu.SemaphoreType.DMA],
        compiler_params=params,
        name="early",
    )(table, pltpu.with_memory_space_constraint(x_blocks, pltpu.HBM), own_swap, r1, r2, t1, t2, r3)
    t3 = swap(r3)
    r4a, part = lax.optimization_barrier((r4a, part))
    t4a = swap(r4a)
    r4b, t4a = lax.optimization_barrier((r4b, t4a))
    t4b = swap(r4b)
    dense = [jax.ShapeDtypeStruct(a.shape, a.dtype) for a in (high, low, part)]
    high, low, part = pl.pallas_call(
        functools.partial(middle_kernel, tables),
        out_shape=dense,
        in_specs=[vmem] * 9,
        out_specs=[vmem] * 3,
        input_output_aliases={5: 0, 6: 1, 8: 2},
        compiler_params=params,
        name="middle",
    )(notes, r4a, r4b, t3, t4a, *held(high, low, left, part))
    out, _, _, _ = pl.pallas_call(
        functools.partial(late_kernel, tables),
        out_shape=[jax.ShapeDtypeStruct(x_blocks.shape, jnp.float32)] + dense,
        in_specs=[vmem] * 6,
        out_specs=[pl.BlockSpec(memory_space=pltpu.HBM)] + [vmem] * 3,
        input_output_aliases={2: 1, 3: 2, 5: 3},
        scratch_shapes=[
            pltpu.VMEM((2 * own, order), jnp.bfloat16),
            pltpu.VMEM(x_blocks.shape, jnp.float32),
            pltpu.SemaphoreType.DMA((slab,)),
        ],
        compiler_params=params,
        name="late",
    )(notes, t4b, *held(high, low, left, part))
    return out


def local(x_blocks, columns):
    slab, width, edge, _ = x_blocks.shape
    rows, slots = columns.shape
    _, chains, panels, lanes = (lax.axis_size(axis) for axis in AXES)
    full = rows <= slots and rows == lanes * width and width % 2 == 0
    if full and rows <= 8 and slab == 2 and edge == 128 and panels >= 2 and lanes == 2 and chains == 4:
        return gather_local(x_blocks, columns)
    return ring_local(x_blocks, columns)


def solution(mesh):
    placed = (P(("groups", "blk"), ("panel", "depth"), None, None), P("groups", None))
    return jax.shard_map(
        local,
        mesh=mesh,
        in_specs=placed,
        out_specs=P(("groups", "blk"), ("panel", "depth"), None, None),
        check_vma=False,
    )
```

```python
import functools

import jax
import jax.numpy as jnp
from jax import lax
from jax.experimental import pallas as pl
from jax.experimental.pallas import tpu as pltpu
from jax.sharding import PartitionSpec as P

precise = lax.Precision.HIGHEST
AXES = ("groups", "blk", "panel", "depth")


def shifted(block, axis, distance):
    devices = range(lax.axis_size(axis))
    route = [((i - distance) % len(devices), i) for i in devices]
    return lax.ppermute(block, axis, route)


def slot_gather(blocks):
    return lax.all_gather(blocks, ("panel", "depth"), axis=1, tiled=True)


def slot_reduce(partial_value):
    return lax.psum_scatter(partial_value, ("panel", "depth"), scatter_dimension=1, tiled=True)


def rotate_one(incoming):
    return shifted(incoming, "blk", 1)


def ring_local(x_blocks, columns):
    slab_rows = x_blocks.shape[0]
    width_slots = x_blocks.shape[1]
    edge = x_blocks.shape[2]
    order_rows = columns.shape[0]
    all_slots = columns.shape[1]
    cycle_size = lax.axis_size("blk")
    cycle_place = lax.axis_index("blk")
    anchor = jnp.int32(0)
    first_own = cycle_place * slab_rows
    slot_first = lax.axis_index(("panel", "depth")) * width_slots
    my_cols = lax.dynamic_slice(columns, (first_own, anchor), (slab_rows, all_slots))
    own_cols = lax.dynamic_slice(my_cols, (anchor, slot_first), (slab_rows, width_slots))
    x_own = jnp.where((own_cols < order_rows)[:, :, None, None], x_blocks, jnp.float32(0.0))
    out_present = my_cols < order_rows
    empty = jnp.zeros((slab_rows, all_slots, edge, edge), jnp.float32)

    def contribute(partial_value, left_rows, incoming, source):
        group = incoming.shape[0]
        first_row = source * group
        their_cols = lax.dynamic_slice(columns, (first_row, slot_first), (group, width_slots))
        row_ids = first_row + jnp.arange(group, dtype=jnp.int32)
        selector = (my_cols[:, None, :] == row_ids[None, :, None]).astype(jnp.float32)
        picked = jnp.einsum("irs,isab->irab", selector, left_rows, precision=precise)
        products = jnp.einsum("irab,rubc->iruac", picked, incoming, precision=precise)
        targets = (their_cols[None, None, :, :] == my_cols[:, :, None, None]) & out_present[
            :, :, None, None
        ]
        placed = jnp.einsum(
            "isru,iruac->isac", targets.astype(jnp.float32), products, precision=precise
        )
        return partial_value + placed

    def one_way(left_rows, stored):

        def advance(offset, state):
            partial_value, incoming, stored = state
            source = (cycle_place - offset) % cycle_size
            partial_value = contribute(partial_value, left_rows, incoming, source)
            return (partial_value, rotate_one(incoming), stored)

        partial_value, incoming, stored = lax.fori_loop(
            0, cycle_size - 1, advance, (empty, x_own, stored)
        )
        source = (cycle_place + 1) % cycle_size
        return (contribute(partial_value, left_rows, incoming, source), stored)

    stored = jnp.zeros((1,), jnp.float32)
    left_first = slot_gather(x_own)
    partial_value, stored = one_way(left_first, stored)
    squared = slot_reduce(partial_value)
    left_second = slot_gather(squared)
    partial_value, stored = one_way(left_second, stored)
    cubed = slot_reduce(partial_value)
    return 3.0 * squared - 2.0 * cubed


def split(value):
    high = value.astype(jnp.bfloat16)
    low = (value - high.astype(jnp.float32)).astype(jnp.bfloat16)
    return high, low


def dot(left, right):
    return jnp.dot(left, right, preferred_element_type=jnp.float32)


def stacked_dot(left, high, low):
    half = left.shape[0] // 2
    both = dot(left, high)
    return both[:half] + (both[half:] + dot(left[:half], low))


def lookup(table, place, lane):
    found = jnp.int32(-1)
    for z, entries in enumerate(table):
        for c, entry in enumerate(entries):
            found = jnp.where((place == z) & (lane == c), entry, found)
    return found


def store_piece(piece, plane, code_of, high, low, own=None, slab=2, first=0):
    count, width, edge, _ = piece.shape
    act = 2 * width

    @pl.when(plane >= 0)
    def _():
        for r in range(count):
            row = plane * slab + first + r
            for w in range(width):
                code = code_of(first + r, w)
                col = pl.ds(pl.multiple_of(code % act * edge, edge), edge)
                block = jnp.where(code < act, piece[r, w], 0.0)
                block_high, block_low = split(block)
                at = pl.ds(pl.multiple_of(row * edge, edge), edge)
                high[at, col] = block_high
                low[at, col] = block_low
                if own is not None:
                    own[pl.ds(r * edge, edge), col] = block_high
                    own[pl.ds((slab + r) * edge, edge), col] = block_low


def table_codes(table_ref, plane, group, slab, width):
    row = jnp.maximum(plane, 0) * slab
    return lambda r, w: table_ref[row + r, group * width + w]


T3, R4, T4, OWN, KEPT = 0, 1, 2, 3, 4


def noted_codes(notes, kind, slab, width):
    return lambda r, w: notes[0, (kind * slab + r) * width + w]


def add_plane(plane, left, high, low, part_ref):
    depth, tile = part_ref.shape[0], 512

    @pl.when(plane >= 0)
    def _():
        rows = pl.ds(pl.multiple_of(plane * depth, depth), depth)
        for n in range(part_ref.shape[1] // tile):
            cols = pl.ds(n * tile, tile)
            part_ref[:, cols] += stacked_dot(left[:, rows], high[rows, cols], low[rows, cols])


def early_kernel(
    tables, table_ref, own_hbm, own_swap, r1, r2, t1, t2, r3,
    high, low, left, part_ref, notes_ref, own_ref, own_sem,
):
    place, lane = lax.axis_index("blk"), lax.axis_index("depth")
    (hop1, hop1_senders), (near, near_senders), (far, far_senders) = tables
    slab, width = own_swap.shape[:2]
    act = 2 * width
    own_copy = pltpu.make_async_copy(own_hbm, own_ref, own_sem)
    own_copy.start()
    here, there = lookup(near, place, lane), lookup(near, place, 1 - lane)
    far_here, far_there = lookup(far, place, lane), lookup(far, place, 1 - lane)
    first_here, first_there = [lookup(hop1, place, c) for c in (lane, 1 - lane)]
    first_sender, first_other = [lookup(hop1_senders, place, c) for c in (lane, 1 - lane)]
    sender, other_sender = [lookup(near_senders, place, c) for c in (lane, 1 - lane)]
    far_sender, far_other = [lookup(far_senders, place, c) for c in (lane, 1 - lane)]
    part_ref[...] = jnp.zeros_like(part_ref)

    def codes(plane, group):
        return table_codes(table_ref, plane, group, slab, width)

    kinds = (
        (far_there, far_other),
        (far_here, 1 - far_sender),
        (far_there, 1 - far_other),
        (place, lane),
    )
    notes = jnp.zeros(notes_ref.shape, jnp.int32)
    index = lax.broadcasted_iota(jnp.int32, notes.shape, 1)
    for kind, (plane, group) in enumerate(kinds):
        for r in range(slab):
            for w in range(width):
                at = (kind * slab + r) * width + w
                notes = jnp.where(index == at, codes(plane, group)(r, w), notes)
    for r in range(slab):
        notes = jnp.where(
            index == KEPT * slab * width + r, table_ref[place * slab + r, act], notes
        )
    notes_ref[...] = notes

    store_piece(own_swap, place, codes(place, 1 - lane), high, low, left)
    store_piece(r1, first_here, codes(first_here, first_sender), high, low)
    store_piece(r2, here, codes(here, 1 - sender), high, low)
    store_piece(t1, first_there, codes(first_there, first_other), high, low)
    store_piece(t2, there, codes(there, 1 - other_sender), high, low)
    store_piece(r3, far_here, codes(far_here, far_sender), high, low)
    own_copy.wait()
    store_piece(own_ref, place, codes(place, lane), high, low, left)
    for plane in (place, here, there):
        add_plane(plane, left, high, low, part_ref)


def middle_kernel(
    tables, notes_ref, r4a, r4b, t3, t4a, high_in, low_in, left, part_in, high, low, part_ref
):
    place, lane = lax.axis_index("blk"), lax.axis_index("depth")
    here, there = [lookup(tables[-1][0], place, c) for c in (lane, 1 - lane)]
    slab, width = t3.shape[:2]
    notes = notes_ref[...]
    store_piece(t3, there, noted_codes(notes, T3, slab, width), high, low)
    store_piece(r4a, here, noted_codes(notes, R4, slab, width), high, low)
    store_piece(t4a, there, noted_codes(notes, T4, slab, width), high, low)
    store_piece(r4b, here, noted_codes(notes, R4, slab, width), high, low, first=1)
    add_plane(here, left, high, low, part_ref)


def late_kernel(
    tables, notes_ref, t4b, high_in, low_in, left, part_in,
    out_hbm, high, low, square, square_parts, out_ref, out_sem,
):
    place, lane = lax.axis_index("blk"), lax.axis_index("depth")
    there = lookup(tables[-1][0], place, 1 - lane)
    slab, width, edge, _ = out_ref.shape
    act = 2 * width
    holds = lax.axis_index("panel") == 0
    notes = notes_ref[...]
    own_codes = noted_codes(notes, OWN, slab, width)
    store_piece(t4b, there, noted_codes(notes, T4, slab, width), high, low, first=1)
    add_plane(there, left, high, low, square)
    for r in range(slab):
        flags = notes[0, KEPT * slab * width + r]
        for c in range(square.shape[1] // edge):
            kept = (flags >> c) % 2 > 0
            col = pl.ds(c * edge, edge)
            block = jnp.where(kept, square[pl.ds(r * edge, edge), col], 0.0)
            block_high, block_low = split(block)
            square_parts[pl.ds(2 * r * edge, edge), col] = block_high
            square_parts[pl.ds((2 * r + 1) * edge, edge), col] = block_low
    copies = []
    for r in range(slab):
        left_parts = square_parts[pl.ds(2 * r * edge, 2 * edge), :]
        codes = [own_codes(r, w) for w in range(width)]
        cols = [pl.ds(pl.multiple_of(code % act * edge, edge), edge) for code in codes]
        cube = stacked_dot(
            left_parts,
            jnp.concatenate([high[:, col] for col in cols], axis=1),
            jnp.concatenate([low[:, col] for col in cols], axis=1),
        )
        for w in range(width):
            value = 3.0 * square[pl.ds(r * edge, edge), cols[w]]
            value = value - 2.0 * cube[:, w * edge : (w + 1) * edge]
            out_ref[r, w] = jnp.where(holds & (codes[w] < act), value, 0.0)
        copies.append(pltpu.make_async_copy(out_ref.at[r], out_hbm.at[r], out_sem.at[r]))
        copies[-1].start()
    for copy in copies:
        copy.wait()


def slot_table(columns, act):
    rows = columns.shape[0]
    slots = columns[:, :act]
    here = slots < rows
    ids = jnp.arange(rows, dtype=jnp.int32)
    taken = jnp.any(slots[:, :, None] == ids, axis=1)
    count = jnp.sum(here.astype(jnp.int32), axis=1, keepdims=True)
    before = jnp.sum(
        (~taken[:, None, :] & (ids[None, :] < ids[:, None])[None]).astype(jnp.int32), axis=2
    )
    at = jnp.where(taken, -1, count + before)
    filled = jnp.sum(
        jnp.where(at[:, None, :] == jnp.arange(act, dtype=jnp.int32)[None, :, None], ids, 0), axis=2
    )
    codes = jnp.where(here, slots, filled + act)
    kept = jnp.sum(jnp.where(taken, 1 << ids, 0), axis=1, keepdims=True)
    return jnp.concatenate([codes, kept], axis=1).astype(jnp.int32)


def gather_local(x_blocks, columns):
    slab, width, edge, _ = x_blocks.shape
    rows = columns.shape[0]
    groups, chains, panels, lanes = (lax.axis_size(axis) for axis in AXES)
    last = chains - 1

    def index(g, place):
        z, x, c = place
        return (((g % groups) * chains + z) * panels + x) * lanes + c

    def move(block, cycles):
        pairs = [(cycle[i - 1], cycle[i]) for cycle in cycles for i in range(len(cycle))]
        busy = {a for a, _ in pairs}
        route = [(index(g, a), index(g, b)) for g in range(groups) for a, b in pairs]
        for z in range(chains):
            for x in range(panels):
                idle = [(z, x, c) for c in range(lanes) if (z, x, c) not in busy]
                for g in range(groups):
                    if len(idle) == lanes:
                        route += [(index(g, idle[c - 1]), index(g, idle[c])) for c in range(lanes)]
                    else:
                        route += [(index(g, a), index(g + 1, a)) for a in idle]
        return lax.ppermute(block, AXES, route)

    def swap(block):
        return move(block, [])

    def move_only(block, chains_of):
        pairs = [(chain[i], chain[i + 1]) for chain in chains_of for i in range(len(chain) - 1)]
        route = [(index(g, a), index(g, b)) for g in range(groups) for a, b in pairs]
        return lax.ppermute(block, AXES, route)

    down_lane = [1 if z == 1 else 0 for z in range(chains)]
    up_lane = [1 - c for c in down_lane]
    up = [(z, 0, up_lane[z]) for z in range(chains)] + [(last, 1, up_lane[last])]
    down = [(z, 0, down_lane[z]) for z in reversed(range(chains))] + [(0, 1, down_lane[0])]
    first = [
        up[:last] + down + [(0, 1, up_lane[0])],
        [up[last], up[-1], (last, 1, down_lane[last])],
    ]
    second = [up, down]

    def received(hops):
        planes, senders = [], []
        for z in range(chains):
            below = z - hops if z >= hops else -1
            above = z + hops if z + hops < chains else -1
            if hops == 2:
                below, above = last if z == 0 else below, 0 if z == last else above
            row = [above, below] if down_lane[z] == 0 else [below, above]
            lane_of = [down_lane, up_lane] if down_lane[z] == 0 else [up_lane, down_lane]
            planes.append(row)
            senders.append([lanes_of[plane] for plane, lanes_of in zip(row, lane_of)])
        return planes, senders

    near, far = received(1), received(2)
    hop1 = [rows[:last] + [rows[last][::-1]] for rows in near]
    tables = hop1, near, far

    table = slot_table(columns, lanes * width)
    r1 = move(x_blocks, first)
    own_swap = swap(x_blocks)
    r2 = move_only(own_swap, [up, down])
    r1, table = lax.optimization_barrier((r1, table))
    r3 = move(r1, second)
    t1 = swap(r1)
    r4a, r4b = move(r2[:1], second), move(r2[1:], second)
    t2 = swap(r2)

    order, own = rows * edge, slab * edge
    table = pltpu.with_memory_space_constraint(table, pltpu.SMEM)
    smem = pl.BlockSpec(memory_space=pltpu.SMEM)
    vmem = pl.BlockSpec(memory_space=pltpu.VMEM)
    params = pltpu.CompilerParams(vmem_limit_bytes=24 * 2**20)
    def held(*arrays):
        return [pltpu.with_memory_space_constraint(a, pltpu.VMEM) for a in arrays]

    high, low, left, part, notes = pl.pallas_call(
        functools.partial(early_kernel, tables),
        out_shape=[
            jax.ShapeDtypeStruct((order, order), jnp.bfloat16),
            jax.ShapeDtypeStruct((order, order), jnp.bfloat16),
            jax.ShapeDtypeStruct((2 * own, order), jnp.bfloat16),
            jax.ShapeDtypeStruct((own, order), jnp.float32),
            jax.ShapeDtypeStruct((8, 128), jnp.int32),
        ],
        in_specs=[smem] + [pl.BlockSpec(memory_space=pltpu.HBM)] + [vmem] * 6,
        out_specs=[vmem] * 5,
        scratch_shapes=[pltpu.VMEM(x_blocks.shape, jnp.float32), pltpu.SemaphoreType.DMA],
        compiler_params=params,
        name="early",
    )(table, pltpu.with_memory_space_constraint(x_blocks, pltpu.HBM), own_swap, r1, r2, t1, t2, r3)
    t3 = swap(r3)
    r4a, part = lax.optimization_barrier((r4a, part))
    t4a = swap(r4a)
    r4b, t4a = lax.optimization_barrier((r4b, t4a))
    t4b = swap(r4b)
    dense = [jax.ShapeDtypeStruct(a.shape, a.dtype) for a in (high, low, part)]
    high, low, part = pl.pallas_call(
        functools.partial(middle_kernel, tables),
        out_shape=dense,
        in_specs=[vmem] * 9,
        out_specs=[vmem] * 3,
        input_output_aliases={5: 0, 6: 1, 8: 2},
        compiler_params=params,
        name="middle",
    )(notes, r4a, r4b, t3, t4a, *held(high, low, left, part))
    out, _, _, _ = pl.pallas_call(
        functools.partial(late_kernel, tables),
        out_shape=[jax.ShapeDtypeStruct(x_blocks.shape, jnp.float32)] + dense,
        in_specs=[vmem] * 6,
        out_specs=[pl.BlockSpec(memory_space=pltpu.HBM)] + [vmem] * 3,
        input_output_aliases={2: 1, 3: 2, 5: 3},
        scratch_shapes=[
            pltpu.VMEM((2 * own, order), jnp.bfloat16),
            pltpu.VMEM(x_blocks.shape, jnp.float32),
            pltpu.SemaphoreType.DMA((slab,)),
        ],
        compiler_params=params,
        name="late",
    )(notes, t4b, *held(high, low, left, part))
    return out


def local(x_blocks, columns):
    slab, width, edge, _ = x_blocks.shape
    rows, slots = columns.shape
    _, chains, panels, lanes = (lax.axis_size(axis) for axis in AXES)
    full = rows <= slots and rows == lanes * width and width % 2 == 0
    if full and rows <= 8 and slab == 2 and edge == 128 and panels >= 2 and lanes == 2 and chains == 4:
        return gather_local(x_blocks, columns)
    return ring_local(x_blocks, columns)


def solution(mesh):
    placed = (P(("groups", "blk"), ("panel", "depth"), None, None), P("groups", None))
    return jax.shard_map(
        local,
        mesh=mesh,
        in_specs=placed,
        out_specs=P(("groups", "blk"), ("panel", "depth"), None, None),
        check_vma=False,
    )
```

```python
import functools

import jax
import jax.numpy as jnp
from jax import lax
from jax.experimental import pallas as pl
from jax.experimental.pallas import tpu as pltpu
from jax.sharding import PartitionSpec as P

precise = lax.Precision.HIGHEST
AXES = ("groups", "blk", "panel", "depth")


def shifted(block, axis, distance):
    devices = range(lax.axis_size(axis))
    route = [((i - distance) % len(devices), i) for i in devices]
    return lax.ppermute(block, axis, route)


def slot_gather(blocks):
    return lax.all_gather(blocks, ("panel", "depth"), axis=1, tiled=True)


def slot_reduce(partial_value):
    return lax.psum_scatter(partial_value, ("panel", "depth"), scatter_dimension=1, tiled=True)


def rotate_one(incoming):
    return shifted(incoming, "blk", 1)


def ring_local(x_blocks, columns):
    slab_rows = x_blocks.shape[0]
    width_slots = x_blocks.shape[1]
    edge = x_blocks.shape[2]
    order_rows = columns.shape[0]
    all_slots = columns.shape[1]
    cycle_size = lax.axis_size("blk")
    cycle_place = lax.axis_index("blk")
    anchor = jnp.int32(0)
    first_own = cycle_place * slab_rows
    slot_first = lax.axis_index(("panel", "depth")) * width_slots
    my_cols = lax.dynamic_slice(columns, (first_own, anchor), (slab_rows, all_slots))
    own_cols = lax.dynamic_slice(my_cols, (anchor, slot_first), (slab_rows, width_slots))
    x_own = jnp.where((own_cols < order_rows)[:, :, None, None], x_blocks, jnp.float32(0.0))
    out_present = my_cols < order_rows
    empty = jnp.zeros((slab_rows, all_slots, edge, edge), jnp.float32)

    def contribute(partial_value, left_rows, incoming, source):
        group = incoming.shape[0]
        first_row = source * group
        their_cols = lax.dynamic_slice(columns, (first_row, slot_first), (group, width_slots))
        row_ids = first_row + jnp.arange(group, dtype=jnp.int32)
        selector = (my_cols[:, None, :] == row_ids[None, :, None]).astype(jnp.float32)
        picked = jnp.einsum("irs,isab->irab", selector, left_rows, precision=precise)
        products = jnp.einsum("irab,rubc->iruac", picked, incoming, precision=precise)
        targets = (their_cols[None, None, :, :] == my_cols[:, :, None, None]) & out_present[
            :, :, None, None
        ]
        placed = jnp.einsum(
            "isru,iruac->isac", targets.astype(jnp.float32), products, precision=precise
        )
        return partial_value + placed

    def one_way(left_rows, stored):

        def advance(offset, state):
            partial_value, incoming, stored = state
            source = (cycle_place - offset) % cycle_size
            partial_value = contribute(partial_value, left_rows, incoming, source)
            return (partial_value, rotate_one(incoming), stored)

        partial_value, incoming, stored = lax.fori_loop(
            0, cycle_size - 1, advance, (empty, x_own, stored)
        )
        source = (cycle_place + 1) % cycle_size
        return (contribute(partial_value, left_rows, incoming, source), stored)

    stored = jnp.zeros((1,), jnp.float32)
    left_first = slot_gather(x_own)
    partial_value, stored = one_way(left_first, stored)
    squared = slot_reduce(partial_value)
    left_second = slot_gather(squared)
    partial_value, stored = one_way(left_second, stored)
    cubed = slot_reduce(partial_value)
    return 3.0 * squared - 2.0 * cubed


def split(value):
    high = value.astype(jnp.bfloat16)
    low = (value - high.astype(jnp.float32)).astype(jnp.bfloat16)
    return high, low


def dot(left, right):
    return jnp.dot(left, right, preferred_element_type=jnp.float32)


def stacked_dot(left, high, low):
    half = left.shape[0] // 2
    both = dot(left, high)
    return both[:half] + (both[half:] + dot(left[:half], low))


def lookup(table, place, lane):
    found = jnp.int32(-1)
    for z, entries in enumerate(table):
        for c, entry in enumerate(entries):
            found = jnp.where((place == z) & (lane == c), entry, found)
    return found


def store_piece(piece, plane, code_of, high, low, own=None, slab=2, first=0):
    count, width, edge, _ = piece.shape
    act = 2 * width

    @pl.when(plane >= 0)
    def _():
        for r in range(count):
            row = plane * slab + first + r
            for w in range(width):
                code = code_of(first + r, w)
                col = pl.ds(pl.multiple_of(code % act * edge, edge), edge)
                block = jnp.where(code < act, piece[r, w], 0.0)
                block_high, block_low = split(block)
                at = pl.ds(pl.multiple_of(row * edge, edge), edge)
                high[at, col] = block_high
                low[at, col] = block_low
                if own is not None:
                    own[pl.ds(r * edge, edge), col] = block_high
                    own[pl.ds((slab + r) * edge, edge), col] = block_low


def table_codes(table_ref, plane, group, slab, width):
    row = jnp.maximum(plane, 0) * slab
    return lambda r, w: table_ref[row + r, group * width + w]


T3, R4, T4, OWN, KEPT = 0, 1, 2, 3, 4


def noted_codes(notes, kind, slab, width):
    return lambda r, w: notes[0, (kind * slab + r) * width + w]


def add_plane(plane, left, high, low, part_ref):
    depth, tile = part_ref.shape[0], 512

    @pl.when(plane >= 0)
    def _():
        rows = pl.ds(pl.multiple_of(plane * depth, depth), depth)
        for n in range(part_ref.shape[1] // tile):
            cols = pl.ds(n * tile, tile)
            part_ref[:, cols] += stacked_dot(left[:, rows], high[rows, cols], low[rows, cols])


def clear_row(plane, r, code_of, width, high, low):
    edge = high.shape[0] // (2 * width)

    @pl.when(plane >= 0)
    def _():
        at = pl.ds(pl.multiple_of((plane * 2 + r) * edge, edge), edge)
        for w in range(width):
            col = pl.ds(pl.multiple_of(code_of(r, w) % (2 * width) * edge, edge), edge)
            high[at, col] = jnp.zeros((edge, edge), jnp.bfloat16)
            low[at, col] = jnp.zeros((edge, edge), jnp.bfloat16)


def add_row_blocks(piece, plane, r, code_of, left, high, low, part_ref):
    _, width, edge, _ = piece.shape
    act = 2 * width

    @pl.when(plane >= 0)
    def _():
        at = pl.ds(pl.multiple_of((plane * 2 + r) * edge, edge), edge)
        for w in range(0, width, 2):
            codes = [code_of(r, w + k) for k in range(2)]
            cols = [pl.ds(pl.multiple_of(code % act * edge, edge), edge) for code in codes]
            parts = [
                split(jnp.where(code < act, piece[0, w + k], 0.0)) for k, code in enumerate(codes)
            ]
            for col, (block_high, block_low) in zip(cols, parts):
                high[at, col] = block_high
                low[at, col] = block_low
            more = stacked_dot(
                left[:, at],
                jnp.concatenate([block_high for block_high, _ in parts], axis=1),
                jnp.concatenate([block_low for _, block_low in parts], axis=1),
            )
            for k, col in enumerate(cols):
                part_ref[:, col] += more[:, k * edge : (k + 1) * edge]


def early_kernel(
    tables, table_ref, own_hbm, own_swap, r1, r2, t1, t2, r3,
    high, low, left, part_ref, notes_ref, own_ref, own_sem,
):
    place, lane = lax.axis_index("blk"), lax.axis_index("depth")
    (hop1, hop1_senders), (near, near_senders), (far, far_senders) = tables
    slab, width = own_swap.shape[:2]
    act = 2 * width
    own_copy = pltpu.make_async_copy(own_hbm, own_ref, own_sem)
    own_copy.start()
    here, there = lookup(near, place, lane), lookup(near, place, 1 - lane)
    far_here, far_there = lookup(far, place, lane), lookup(far, place, 1 - lane)
    first_here, first_there = [lookup(hop1, place, c) for c in (lane, 1 - lane)]
    first_sender, first_other = [lookup(hop1_senders, place, c) for c in (lane, 1 - lane)]
    sender, other_sender = [lookup(near_senders, place, c) for c in (lane, 1 - lane)]
    far_sender, far_other = [lookup(far_senders, place, c) for c in (lane, 1 - lane)]
    part_ref[...] = jnp.zeros_like(part_ref)

    def codes(plane, group):
        return table_codes(table_ref, plane, group, slab, width)

    kinds = (
        (far_there, far_other),
        (far_here, 1 - far_sender),
        (far_there, 1 - far_other),
        (place, lane),
    )
    notes = jnp.zeros(notes_ref.shape, jnp.int32)
    index = lax.broadcasted_iota(jnp.int32, notes.shape, 1)
    for kind, (plane, group) in enumerate(kinds):
        for r in range(slab):
            for w in range(width):
                at = (kind * slab + r) * width + w
                notes = jnp.where(index == at, codes(plane, group)(r, w), notes)
    for r in range(slab):
        notes = jnp.where(
            index == KEPT * slab * width + r, table_ref[place * slab + r, act], notes
        )
    notes_ref[...] = notes

    store_piece(own_swap, place, codes(place, 1 - lane), high, low, left)
    store_piece(r1, first_here, codes(first_here, first_sender), high, low)
    store_piece(r2, here, codes(here, 1 - sender), high, low)
    store_piece(t1, first_there, codes(first_there, first_other), high, low)
    store_piece(t2, there, codes(there, 1 - other_sender), high, low)
    store_piece(r3, far_here, codes(far_here, far_sender), high, low)
    own_copy.wait()
    store_piece(own_ref, place, codes(place, lane), high, low, left)
    for plane in (place, here, there):
        add_plane(plane, left, high, low, part_ref)


def waiting_kernel(tables, notes_ref, r4a, high_in, low_in, left, part_in, high, low, part_ref):
    place, lane = lax.axis_index("blk"), lax.axis_index("depth")
    here = lookup(tables[-1][0], place, lane)
    width = r4a.shape[1]
    codes = noted_codes(notes_ref[...], R4, 2, width)
    store_piece(r4a, here, codes, high, low)
    clear_row(here, 1, codes, width, high, low)
    add_plane(here, left, high, low, part_ref)


def middle_kernel(
    tables, notes_ref, r4b, t3, t4a, high_in, low_in, left, part_in, high, low, part_ref
):
    place, lane = lax.axis_index("blk"), lax.axis_index("depth")
    here, there = [lookup(tables[-1][0], place, c) for c in (lane, 1 - lane)]
    slab, width = t3.shape[:2]
    notes = notes_ref[...]
    codes = noted_codes(notes, T4, slab, width)
    store_piece(t3, there, noted_codes(notes, T3, slab, width), high, low)
    store_piece(t4a, there, codes, high, low)
    clear_row(there, 1, codes, width, high, low)
    add_plane(there, left, high, low, part_ref)
    add_row_blocks(
        r4b, here, 1, noted_codes(notes, R4, slab, width), left, high, low, part_ref
    )


def late_kernel(
    tables, notes_ref, t4b, high_in, low_in, left, part_in,
    out_hbm, high, low, square, square_parts, out_ref, out_sem,
):
    place, lane = lax.axis_index("blk"), lax.axis_index("depth")
    there = lookup(tables[-1][0], place, 1 - lane)
    slab, width, edge, _ = out_ref.shape
    act = 2 * width
    holds = lax.axis_index("panel") == 0
    notes = notes_ref[...]
    own_codes = noted_codes(notes, OWN, slab, width)
    add_row_blocks(
        t4b, there, 1, noted_codes(notes, T4, slab, width), left, high, low, square
    )
    for r in range(slab):
        flags = notes[0, KEPT * slab * width + r]
        for c in range(square.shape[1] // edge):
            kept = (flags >> c) % 2 > 0
            col = pl.ds(c * edge, edge)
            block = jnp.where(kept, square[pl.ds(r * edge, edge), col], 0.0)
            block_high, block_low = split(block)
            square_parts[pl.ds(2 * r * edge, edge), col] = block_high
            square_parts[pl.ds((2 * r + 1) * edge, edge), col] = block_low
    copies = []
    for r in range(slab):
        left_parts = square_parts[pl.ds(2 * r * edge, 2 * edge), :]
        codes = [own_codes(r, w) for w in range(width)]
        cols = [pl.ds(pl.multiple_of(code % act * edge, edge), edge) for code in codes]
        cube = stacked_dot(
            left_parts,
            jnp.concatenate([high[:, col] for col in cols], axis=1),
            jnp.concatenate([low[:, col] for col in cols], axis=1),
        )
        for w in range(width):
            value = 3.0 * square[pl.ds(r * edge, edge), cols[w]]
            value = value - 2.0 * cube[:, w * edge : (w + 1) * edge]
            out_ref[r, w] = jnp.where(holds & (codes[w] < act), value, 0.0)
        copies.append(pltpu.make_async_copy(out_ref.at[r], out_hbm.at[r], out_sem.at[r]))
        copies[-1].start()
    for copy in copies:
        copy.wait()


def slot_table(columns, act):
    rows = columns.shape[0]
    slots = columns[:, :act]
    here = slots < rows
    ids = jnp.arange(rows, dtype=jnp.int32)
    taken = jnp.any(slots[:, :, None] == ids, axis=1)
    count = jnp.sum(here.astype(jnp.int32), axis=1, keepdims=True)
    before = jnp.sum(
        (~taken[:, None, :] & (ids[None, :] < ids[:, None])[None]).astype(jnp.int32), axis=2
    )
    at = jnp.where(taken, -1, count + before)
    filled = jnp.sum(
        jnp.where(at[:, None, :] == jnp.arange(act, dtype=jnp.int32)[None, :, None], ids, 0), axis=2
    )
    codes = jnp.where(here, slots, filled + act)
    kept = jnp.sum(jnp.where(taken, 1 << ids, 0), axis=1, keepdims=True)
    return jnp.concatenate([codes, kept], axis=1).astype(jnp.int32)


def gather_local(x_blocks, columns):
    slab, width, edge, _ = x_blocks.shape
    rows = columns.shape[0]
    groups, chains, panels, lanes = (lax.axis_size(axis) for axis in AXES)
    last = chains - 1

    def index(g, place):
        z, x, c = place
        return (((g % groups) * chains + z) * panels + x) * lanes + c

    def move(block, cycles):
        pairs = [(cycle[i - 1], cycle[i]) for cycle in cycles for i in range(len(cycle))]
        busy = {a for a, _ in pairs}
        route = [(index(g, a), index(g, b)) for g in range(groups) for a, b in pairs]
        for z in range(chains):
            for x in range(panels):
                idle = [(z, x, c) for c in range(lanes) if (z, x, c) not in busy]
                for g in range(groups):
                    if len(idle) == lanes:
                        route += [(index(g, idle[c - 1]), index(g, idle[c])) for c in range(lanes)]
                    else:
                        route += [(index(g, a), index(g + 1, a)) for a in idle]
        return lax.ppermute(block, AXES, route)

    def swap(block):
        return move(block, [])

    def move_only(block, chains_of):
        pairs = [(chain[i], chain[i + 1]) for chain in chains_of for i in range(len(chain) - 1)]
        route = [(index(g, a), index(g, b)) for g in range(groups) for a, b in pairs]
        return lax.ppermute(block, AXES, route)

    down_lane = [1 if z == 1 else 0 for z in range(chains)]
    up_lane = [1 - c for c in down_lane]
    up = [(z, 0, up_lane[z]) for z in range(chains)] + [(last, 1, up_lane[last])]
    down = [(z, 0, down_lane[z]) for z in reversed(range(chains))] + [(0, 1, down_lane[0])]
    first = [
        up[:last] + down + [(0, 1, up_lane[0])],
        [up[last], up[-1], (last, 1, down_lane[last])],
    ]
    second = [up, down]

    def received(hops):
        planes, senders = [], []
        for z in range(chains):
            below = z - hops if z >= hops else -1
            above = z + hops if z + hops < chains else -1
            if hops == 2:
                below, above = last if z == 0 else below, 0 if z == last else above
            row = [above, below] if down_lane[z] == 0 else [below, above]
            lane_of = [down_lane, up_lane] if down_lane[z] == 0 else [up_lane, down_lane]
            planes.append(row)
            senders.append([lanes_of[plane] for plane, lanes_of in zip(row, lane_of)])
        return planes, senders

    near, far = received(1), received(2)
    hop1 = [rows[:last] + [rows[last][::-1]] for rows in near]
    tables = hop1, near, far

    table = slot_table(columns, lanes * width)
    r1 = move(x_blocks, first)
    own_swap = swap(x_blocks)
    r2 = move_only(own_swap, [up, down])
    r1, table = lax.optimization_barrier((r1, table))
    r3 = move(r1, second)
    t1 = swap(r1)
    r4a, r4b = move(r2[:1], second), move(r2[1:], second)
    t2 = swap(r2)

    order, own = rows * edge, slab * edge
    table = pltpu.with_memory_space_constraint(table, pltpu.SMEM)
    smem = pl.BlockSpec(memory_space=pltpu.SMEM)
    vmem = pl.BlockSpec(memory_space=pltpu.VMEM)
    params = pltpu.CompilerParams(vmem_limit_bytes=24 * 2**20)
    def held(*arrays):
        return [pltpu.with_memory_space_constraint(a, pltpu.VMEM) for a in arrays]

    high, low, left, part, notes = pl.pallas_call(
        functools.partial(early_kernel, tables),
        out_shape=[
            jax.ShapeDtypeStruct((order, order), jnp.bfloat16),
            jax.ShapeDtypeStruct((order, order), jnp.bfloat16),
            jax.ShapeDtypeStruct((2 * own, order), jnp.bfloat16),
            jax.ShapeDtypeStruct((own, order), jnp.float32),
            jax.ShapeDtypeStruct((8, 128), jnp.int32),
        ],
        in_specs=[smem] + [pl.BlockSpec(memory_space=pltpu.HBM)] + [vmem] * 6,
        out_specs=[vmem] * 5,
        scratch_shapes=[pltpu.VMEM(x_blocks.shape, jnp.float32), pltpu.SemaphoreType.DMA],
        compiler_params=params,
        name="early",
    )(table, pltpu.with_memory_space_constraint(x_blocks, pltpu.HBM), own_swap, r1, r2, t1, t2, r3)
    t3 = swap(r3)
    r4a, part = lax.optimization_barrier((r4a, part))
    t4a = swap(r4a)
    dense = [jax.ShapeDtypeStruct(a.shape, a.dtype) for a in (high, low, part)]

    def add_to_square(kernel, name, *pieces):
        at = 1 + len(pieces)
        return pl.pallas_call(
            functools.partial(kernel, tables),
            out_shape=dense,
            in_specs=[vmem] * (at + 4),
            out_specs=[vmem] * 3,
            input_output_aliases={at: 0, at + 1: 1, at + 3: 2},
            compiler_params=params,
            name=name,
        )(notes, *pieces, *held(high, low, left, part))

    high, low, part = add_to_square(waiting_kernel, "waiting", r4a)
    r4b, t4a, part = lax.optimization_barrier((r4b, t4a, part))
    t4b = swap(r4b)
    high, low, part = add_to_square(middle_kernel, "middle", r4b, t3, t4a)
    out, _, _, _ = pl.pallas_call(
        functools.partial(late_kernel, tables),
        out_shape=[jax.ShapeDtypeStruct(x_blocks.shape, jnp.float32)] + dense,
        in_specs=[vmem] * 6,
        out_specs=[pl.BlockSpec(memory_space=pltpu.HBM)] + [vmem] * 3,
        input_output_aliases={2: 1, 3: 2, 5: 3},
        scratch_shapes=[
            pltpu.VMEM((2 * own, order), jnp.bfloat16),
            pltpu.VMEM(x_blocks.shape, jnp.float32),
            pltpu.SemaphoreType.DMA((slab,)),
        ],
        compiler_params=params,
        name="late",
    )(notes, t4b, *held(high, low, left, part))
    return out


def local(x_blocks, columns):
    slab, width, edge, _ = x_blocks.shape
    rows, slots = columns.shape
    _, chains, panels, lanes = (lax.axis_size(axis) for axis in AXES)
    full = rows <= slots and rows == lanes * width and width % 2 == 0
    if full and rows <= 8 and slab == 2 and edge == 128 and panels >= 2 and lanes == 2 and chains == 4:
        return gather_local(x_blocks, columns)
    return ring_local(x_blocks, columns)


def solution(mesh):
    placed = (P(("groups", "blk"), ("panel", "depth"), None, None), P("groups", None))
    return jax.shard_map(
        local,
        mesh=mesh,
        in_specs=placed,
        out_specs=P(("groups", "blk"), ("panel", "depth"), None, None),
        check_vma=False,
    )
```

```python
import functools

import jax
import jax.numpy as jnp
from jax import lax
from jax.experimental import pallas as pl
from jax.experimental.pallas import tpu as pltpu
from jax.sharding import PartitionSpec as P

precise = lax.Precision.HIGHEST
AXES = ("groups", "blk", "panel", "depth")


def shifted(block, axis, distance):
    devices = range(lax.axis_size(axis))
    route = [((i - distance) % len(devices), i) for i in devices]
    return lax.ppermute(block, axis, route)


def slot_gather(blocks):
    return lax.all_gather(blocks, ("panel", "depth"), axis=1, tiled=True)


def slot_reduce(partial_value):
    return lax.psum_scatter(partial_value, ("panel", "depth"), scatter_dimension=1, tiled=True)


def rotate_one(incoming):
    return shifted(incoming, "blk", 1)


def ring_local(x_blocks, columns):
    slab_rows = x_blocks.shape[0]
    width_slots = x_blocks.shape[1]
    edge = x_blocks.shape[2]
    order_rows = columns.shape[0]
    all_slots = columns.shape[1]
    cycle_size = lax.axis_size("blk")
    cycle_place = lax.axis_index("blk")
    anchor = jnp.int32(0)
    first_own = cycle_place * slab_rows
    slot_first = lax.axis_index(("panel", "depth")) * width_slots
    my_cols = lax.dynamic_slice(columns, (first_own, anchor), (slab_rows, all_slots))
    own_cols = lax.dynamic_slice(my_cols, (anchor, slot_first), (slab_rows, width_slots))
    x_own = jnp.where((own_cols < order_rows)[:, :, None, None], x_blocks, jnp.float32(0.0))
    out_present = my_cols < order_rows
    empty = jnp.zeros((slab_rows, all_slots, edge, edge), jnp.float32)

    def contribute(partial_value, left_rows, incoming, source):
        group = incoming.shape[0]
        first_row = source * group
        their_cols = lax.dynamic_slice(columns, (first_row, slot_first), (group, width_slots))
        row_ids = first_row + jnp.arange(group, dtype=jnp.int32)
        selector = (my_cols[:, None, :] == row_ids[None, :, None]).astype(jnp.float32)
        picked = jnp.einsum("irs,isab->irab", selector, left_rows, precision=precise)
        products = jnp.einsum("irab,rubc->iruac", picked, incoming, precision=precise)
        targets = (their_cols[None, None, :, :] == my_cols[:, :, None, None]) & out_present[
            :, :, None, None
        ]
        placed = jnp.einsum(
            "isru,iruac->isac", targets.astype(jnp.float32), products, precision=precise
        )
        return partial_value + placed

    def one_way(left_rows, stored):

        def advance(offset, state):
            partial_value, incoming, stored = state
            source = (cycle_place - offset) % cycle_size
            partial_value = contribute(partial_value, left_rows, incoming, source)
            return (partial_value, rotate_one(incoming), stored)

        partial_value, incoming, stored = lax.fori_loop(
            0, cycle_size - 1, advance, (empty, x_own, stored)
        )
        source = (cycle_place + 1) % cycle_size
        return (contribute(partial_value, left_rows, incoming, source), stored)

    stored = jnp.zeros((1,), jnp.float32)
    left_first = slot_gather(x_own)
    partial_value, stored = one_way(left_first, stored)
    squared = slot_reduce(partial_value)
    left_second = slot_gather(squared)
    partial_value, stored = one_way(left_second, stored)
    cubed = slot_reduce(partial_value)
    return 3.0 * squared - 2.0 * cubed


def split(value):
    high = value.astype(jnp.bfloat16)
    low = (value - high.astype(jnp.float32)).astype(jnp.bfloat16)
    return high, low


def dot(left, right):
    return jnp.dot(left, right, preferred_element_type=jnp.float32)


def stacked_dot(left, high, low):
    half = left.shape[0] // 2
    both = dot(left, high)
    return both[:half] + (both[half:] + dot(left[:half], low))


def joined_dot(left, high, low):
    half = left.shape[0] // 2
    left_high, left_low = left[:half], left[half:]
    return dot(
        jnp.concatenate([left_high, left_low, left_high], axis=1),
        jnp.concatenate([high, high, low], axis=0),
    )


def lookup(table, place, lane):
    found = jnp.int32(-1)
    for z, entries in enumerate(table):
        for c, entry in enumerate(entries):
            found = jnp.where((place == z) & (lane == c), entry, found)
    return found


def store_piece(piece, plane, code_of, high, low, own=None, slab=2, first=0):
    count, width, edge, _ = piece.shape
    act = 2 * width

    @pl.when(plane >= 0)
    def _():
        for r in range(count):
            row = plane * slab + first + r
            for w in range(width):
                code = code_of(first + r, w)
                col = pl.ds(pl.multiple_of(code % act * edge, edge), edge)
                block = jnp.where(code < act, piece[r, w], 0.0)
                block_high, block_low = split(block)
                at = pl.ds(pl.multiple_of(row * edge, edge), edge)
                high[at, col] = block_high
                low[at, col] = block_low
                if own is not None:
                    own[pl.ds(r * edge, edge), col] = block_high
                    own[pl.ds((slab + r) * edge, edge), col] = block_low


def table_codes(table_ref, plane, group, slab, width):
    row = jnp.maximum(plane, 0) * slab
    return lambda r, w: table_ref[row + r, group * width + w]


T3, R4, T4, OWN, KEPT = 0, 1, 2, 3, 4


def noted_codes(notes, kind, slab, width):
    return lambda r, w: notes[0, (kind * slab + r) * width + w]


def add_plane(plane, left, high, low, part_ref):
    depth, tile = part_ref.shape[0], 512

    @pl.when(plane >= 0)
    def _():
        rows = pl.ds(pl.multiple_of(plane * depth, depth), depth)
        for n in range(part_ref.shape[1] // tile):
            cols = pl.ds(n * tile, tile)
            part_ref[:, cols] += joined_dot(left[:, rows], high[rows, cols], low[rows, cols])


def early_kernel(
    tables, table_ref, own_hbm, own_swap, r1, r2, t1, t2, r3,
    high, low, left, part_ref, notes_ref, own_ref, own_sem,
):
    place, lane = lax.axis_index("blk"), lax.axis_index("depth")
    (hop1, hop1_senders), (near, near_senders), (far, far_senders) = tables
    slab, width = own_swap.shape[:2]
    act = 2 * width
    own_copy = pltpu.make_async_copy(own_hbm, own_ref, own_sem)
    own_copy.start()
    here, there = lookup(near, place, lane), lookup(near, place, 1 - lane)
    far_here, far_there = lookup(far, place, lane), lookup(far, place, 1 - lane)
    first_here, first_there = [lookup(hop1, place, c) for c in (lane, 1 - lane)]
    first_sender, first_other = [lookup(hop1_senders, place, c) for c in (lane, 1 - lane)]
    sender, other_sender = [lookup(near_senders, place, c) for c in (lane, 1 - lane)]
    far_sender, far_other = [lookup(far_senders, place, c) for c in (lane, 1 - lane)]
    part_ref[...] = jnp.zeros_like(part_ref)

    def codes(plane, group):
        return table_codes(table_ref, plane, group, slab, width)

    kinds = (
        (far_there, far_other),
        (far_here, 1 - far_sender),
        (far_there, 1 - far_other),
        (place, lane),
    )
    notes = jnp.zeros(notes_ref.shape, jnp.int32)
    index = lax.broadcasted_iota(jnp.int32, notes.shape, 1)
    for kind, (plane, group) in enumerate(kinds):
        for r in range(slab):
            for w in range(width):
                at = (kind * slab + r) * width + w
                notes = jnp.where(index == at, codes(plane, group)(r, w), notes)
    for r in range(slab):
        notes = jnp.where(
            index == KEPT * slab * width + r, table_ref[place * slab + r, act], notes
        )
    notes_ref[...] = notes

    store_piece(own_swap, place, codes(place, 1 - lane), high, low, left)
    store_piece(r1, first_here, codes(first_here, first_sender), high, low)
    store_piece(r2, here, codes(here, 1 - sender), high, low)
    store_piece(t1, first_there, codes(first_there, first_other), high, low)
    store_piece(t2, there, codes(there, 1 - other_sender), high, low)
    store_piece(r3, far_here, codes(far_here, far_sender), high, low)
    own_copy.wait()
    store_piece(own_ref, place, codes(place, lane), high, low, left)
    for plane in (place, here, there):
        add_plane(plane, left, high, low, part_ref)


def middle_kernel(
    tables, notes_ref, r4a, r4b, t3, t4a, high_in, low_in, left, part_in, high, low, part_ref
):
    place, lane = lax.axis_index("blk"), lax.axis_index("depth")
    here, there = [lookup(tables[-1][0], place, c) for c in (lane, 1 - lane)]
    slab, width = t3.shape[:2]
    notes = notes_ref[...]
    store_piece(t3, there, noted_codes(notes, T3, slab, width), high, low)
    store_piece(r4a, here, noted_codes(notes, R4, slab, width), high, low)
    store_piece(t4a, there, noted_codes(notes, T4, slab, width), high, low)
    store_piece(r4b, here, noted_codes(notes, R4, slab, width), high, low, first=1)
    add_plane(here, left, high, low, part_ref)


def late_kernel(
    tables, notes_ref, t4b, high_in, low_in, left, part_in,
    out_hbm, high, low, square, square_parts, out_ref, out_sem,
):
    place, lane = lax.axis_index("blk"), lax.axis_index("depth")
    there = lookup(tables[-1][0], place, 1 - lane)
    slab, width, edge, _ = out_ref.shape
    act = 2 * width
    holds = lax.axis_index("panel") == 0
    notes = notes_ref[...]
    own_codes = noted_codes(notes, OWN, slab, width)
    store_piece(t4b, there, noted_codes(notes, T4, slab, width), high, low, first=1)
    add_plane(there, left, high, low, square)
    for r in range(slab):
        flags = notes[0, KEPT * slab * width + r]
        for c in range(square.shape[1] // edge):
            kept = (flags >> c) % 2 > 0
            col = pl.ds(c * edge, edge)
            block = jnp.where(kept, square[pl.ds(r * edge, edge), col], 0.0)
            block_high, block_low = split(block)
            square_parts[pl.ds(2 * r * edge, edge), col] = block_high
            square_parts[pl.ds((2 * r + 1) * edge, edge), col] = block_low
    copies = []
    for r in range(slab):
        left_parts = square_parts[pl.ds(2 * r * edge, 2 * edge), :]
        codes = [own_codes(r, w) for w in range(width)]
        cols = [pl.ds(pl.multiple_of(code % act * edge, edge), edge) for code in codes]
        cube = stacked_dot(
            left_parts,
            jnp.concatenate([high[:, col] for col in cols], axis=1),
            jnp.concatenate([low[:, col] for col in cols], axis=1),
        )
        for w in range(width):
            value = 3.0 * square[pl.ds(r * edge, edge), cols[w]]
            value = value - 2.0 * cube[:, w * edge : (w + 1) * edge]
            out_ref[r, w] = jnp.where(holds & (codes[w] < act), value, 0.0)
        copies.append(pltpu.make_async_copy(out_ref.at[r], out_hbm.at[r], out_sem.at[r]))
        copies[-1].start()
    for copy in copies:
        copy.wait()


def slot_table(columns, act):
    rows = columns.shape[0]
    slots = columns[:, :act]
    here = slots < rows
    ids = jnp.arange(rows, dtype=jnp.int32)
    taken = jnp.any(slots[:, :, None] == ids, axis=1)
    count = jnp.sum(here.astype(jnp.int32), axis=1, keepdims=True)
    before = jnp.sum(
        (~taken[:, None, :] & (ids[None, :] < ids[:, None])[None]).astype(jnp.int32), axis=2
    )
    at = jnp.where(taken, -1, count + before)
    filled = jnp.sum(
        jnp.where(at[:, None, :] == jnp.arange(act, dtype=jnp.int32)[None, :, None], ids, 0), axis=2
    )
    codes = jnp.where(here, slots, filled + act)
    kept = jnp.sum(jnp.where(taken, 1 << ids, 0), axis=1, keepdims=True)
    return jnp.concatenate([codes, kept], axis=1).astype(jnp.int32)


def gather_local(x_blocks, columns):
    slab, width, edge, _ = x_blocks.shape
    rows = columns.shape[0]
    groups, chains, panels, lanes = (lax.axis_size(axis) for axis in AXES)
    last = chains - 1

    def index(g, place):
        z, x, c = place
        return (((g % groups) * chains + z) * panels + x) * lanes + c

    def move(block, cycles):
        pairs = [(cycle[i - 1], cycle[i]) for cycle in cycles for i in range(len(cycle))]
        busy = {a for a, _ in pairs}
        route = [(index(g, a), index(g, b)) for g in range(groups) for a, b in pairs]
        for z in range(chains):
            for x in range(panels):
                idle = [(z, x, c) for c in range(lanes) if (z, x, c) not in busy]
                for g in range(groups):
                    if len(idle) == lanes:
                        route += [(index(g, idle[c - 1]), index(g, idle[c])) for c in range(lanes)]
                    else:
                        route += [(index(g, a), index(g + 1, a)) for a in idle]
        return lax.ppermute(block, AXES, route)

    def swap(block):
        return move(block, [])

    def move_only(block, chains_of):
        pairs = [(chain[i], chain[i + 1]) for chain in chains_of for i in range(len(chain) - 1)]
        route = [(index(g, a), index(g, b)) for g in range(groups) for a, b in pairs]
        return lax.ppermute(block, AXES, route)

    down_lane = [1 if z == 1 else 0 for z in range(chains)]
    up_lane = [1 - c for c in down_lane]
    up = [(z, 0, up_lane[z]) for z in range(chains)] + [(last, 1, up_lane[last])]
    down = [(z, 0, down_lane[z]) for z in reversed(range(chains))] + [(0, 1, down_lane[0])]
    first = [
        up[:last] + down + [(0, 1, up_lane[0])],
        [up[last], up[-1], (last, 1, down_lane[last])],
    ]
    second = [up, down]

    def received(hops):
        planes, senders = [], []
        for z in range(chains):
            below = z - hops if z >= hops else -1
            above = z + hops if z + hops < chains else -1
            if hops == 2:
                below, above = last if z == 0 else below, 0 if z == last else above
            row = [above, below] if down_lane[z] == 0 else [below, above]
            lane_of = [down_lane, up_lane] if down_lane[z] == 0 else [up_lane, down_lane]
            planes.append(row)
            senders.append([lanes_of[plane] for plane, lanes_of in zip(row, lane_of)])
        return planes, senders

    near, far = received(1), received(2)
    hop1 = [rows[:last] + [rows[last][::-1]] for rows in near]
    tables = hop1, near, far

    table = slot_table(columns, lanes * width)
    r1 = move(x_blocks, first)
    own_swap = swap(x_blocks)
    r2 = move_only(own_swap, [up, down])
    r1, table = lax.optimization_barrier((r1, table))
    r3 = move(r1, second)
    t1 = swap(r1)
    r4a, r4b = move(r2[:1], second), move(r2[1:], second)
    t2 = swap(r2)

    order, own = rows * edge, slab * edge
    table = pltpu.with_memory_space_constraint(table, pltpu.SMEM)
    smem = pl.BlockSpec(memory_space=pltpu.SMEM)
    vmem = pl.BlockSpec(memory_space=pltpu.VMEM)
    params = pltpu.CompilerParams(vmem_limit_bytes=24 * 2**20)
    def held(*arrays):
        return [pltpu.with_memory_space_constraint(a, pltpu.VMEM) for a in arrays]

    high, low, left, part, notes = pl.pallas_call(
        functools.partial(early_kernel, tables),
        out_shape=[
            jax.ShapeDtypeStruct((order, order), jnp.bfloat16),
            jax.ShapeDtypeStruct((order, order), jnp.bfloat16),
            jax.ShapeDtypeStruct((2 * own, order), jnp.bfloat16),
            jax.ShapeDtypeStruct((own, order), jnp.float32),
            jax.ShapeDtypeStruct((8, 128), jnp.int32),
        ],
        in_specs=[smem] + [pl.BlockSpec(memory_space=pltpu.HBM)] + [vmem] * 6,
        out_specs=[vmem] * 5,
        scratch_shapes=[pltpu.VMEM(x_blocks.shape, jnp.float32), pltpu.SemaphoreType.DMA],
        compiler_params=params,
        name="early",
    )(table, pltpu.with_memory_space_constraint(x_blocks, pltpu.HBM), own_swap, r1, r2, t1, t2, r3)
    t3 = swap(r3)
    r4a, part = lax.optimization_barrier((r4a, part))
    t4a = swap(r4a)
    r4b, t4a = lax.optimization_barrier((r4b, t4a))
    t4b = swap(r4b)
    dense = [jax.ShapeDtypeStruct(a.shape, a.dtype) for a in (high, low, part)]
    high, low, part = pl.pallas_call(
        functools.partial(middle_kernel, tables),
        out_shape=dense,
        in_specs=[vmem] * 9,
        out_specs=[vmem] * 3,
        input_output_aliases={5: 0, 6: 1, 8: 2},
        compiler_params=params,
        name="middle",
    )(notes, r4a, r4b, t3, t4a, *held(high, low, left, part))
    out, _, _, _ = pl.pallas_call(
        functools.partial(late_kernel, tables),
        out_shape=[jax.ShapeDtypeStruct(x_blocks.shape, jnp.float32)] + dense,
        in_specs=[vmem] * 6,
        out_specs=[pl.BlockSpec(memory_space=pltpu.HBM)] + [vmem] * 3,
        input_output_aliases={2: 1, 3: 2, 5: 3},
        scratch_shapes=[
            pltpu.VMEM((2 * own, order), jnp.bfloat16),
            pltpu.VMEM(x_blocks.shape, jnp.float32),
            pltpu.SemaphoreType.DMA((slab,)),
        ],
        compiler_params=params,
        name="late",
    )(notes, t4b, *held(high, low, left, part))
    return out


def local(x_blocks, columns):
    slab, width, edge, _ = x_blocks.shape
    rows, slots = columns.shape
    _, chains, panels, lanes = (lax.axis_size(axis) for axis in AXES)
    full = rows <= slots and rows == lanes * width and width % 2 == 0
    if full and rows <= 8 and slab == 2 and edge == 128 and panels >= 2 and lanes == 2 and chains == 4:
        return gather_local(x_blocks, columns)
    return ring_local(x_blocks, columns)


def solution(mesh):
    placed = (P(("groups", "blk"), ("panel", "depth"), None, None), P("groups", None))
    return jax.shard_map(
        local,
        mesh=mesh,
        in_specs=placed,
        out_specs=P(("groups", "blk"), ("panel", "depth"), None, None),
        check_vma=False,
    )
```

```python
import functools

import jax
import jax.numpy as jnp
from jax import lax
from jax.experimental import pallas as pl
from jax.experimental.pallas import tpu as pltpu
from jax.sharding import PartitionSpec as P

precise = lax.Precision.HIGHEST
AXES = ("groups", "blk", "panel", "depth")


def shifted(block, axis, distance):
    devices = range(lax.axis_size(axis))
    route = [((i - distance) % len(devices), i) for i in devices]
    return lax.ppermute(block, axis, route)


def slot_gather(blocks):
    return lax.all_gather(blocks, ("panel", "depth"), axis=1, tiled=True)


def slot_reduce(partial_value):
    return lax.psum_scatter(partial_value, ("panel", "depth"), scatter_dimension=1, tiled=True)


def rotate_one(incoming):
    return shifted(incoming, "blk", 1)


def ring_local(x_blocks, columns):
    slab_rows = x_blocks.shape[0]
    width_slots = x_blocks.shape[1]
    edge = x_blocks.shape[2]
    order_rows = columns.shape[0]
    all_slots = columns.shape[1]
    cycle_size = lax.axis_size("blk")
    cycle_place = lax.axis_index("blk")
    anchor = jnp.int32(0)
    first_own = cycle_place * slab_rows
    slot_first = lax.axis_index(("panel", "depth")) * width_slots
    my_cols = lax.dynamic_slice(columns, (first_own, anchor), (slab_rows, all_slots))
    own_cols = lax.dynamic_slice(my_cols, (anchor, slot_first), (slab_rows, width_slots))
    x_own = jnp.where((own_cols < order_rows)[:, :, None, None], x_blocks, jnp.float32(0.0))
    out_present = my_cols < order_rows
    empty = jnp.zeros((slab_rows, all_slots, edge, edge), jnp.float32)

    def contribute(partial_value, left_rows, incoming, source):
        group = incoming.shape[0]
        first_row = source * group
        their_cols = lax.dynamic_slice(columns, (first_row, slot_first), (group, width_slots))
        row_ids = first_row + jnp.arange(group, dtype=jnp.int32)
        selector = (my_cols[:, None, :] == row_ids[None, :, None]).astype(jnp.float32)
        picked = jnp.einsum("irs,isab->irab", selector, left_rows, precision=precise)
        products = jnp.einsum("irab,rubc->iruac", picked, incoming, precision=precise)
        targets = (their_cols[None, None, :, :] == my_cols[:, :, None, None]) & out_present[
            :, :, None, None
        ]
        placed = jnp.einsum(
            "isru,iruac->isac", targets.astype(jnp.float32), products, precision=precise
        )
        return partial_value + placed

    def one_way(left_rows, stored):

        def advance(offset, state):
            partial_value, incoming, stored = state
            source = (cycle_place - offset) % cycle_size
            partial_value = contribute(partial_value, left_rows, incoming, source)
            return (partial_value, rotate_one(incoming), stored)

        partial_value, incoming, stored = lax.fori_loop(
            0, cycle_size - 1, advance, (empty, x_own, stored)
        )
        source = (cycle_place + 1) % cycle_size
        return (contribute(partial_value, left_rows, incoming, source), stored)

    stored = jnp.zeros((1,), jnp.float32)
    left_first = slot_gather(x_own)
    partial_value, stored = one_way(left_first, stored)
    squared = slot_reduce(partial_value)
    left_second = slot_gather(squared)
    partial_value, stored = one_way(left_second, stored)
    cubed = slot_reduce(partial_value)
    return 3.0 * squared - 2.0 * cubed


def split(value):
    high = value.astype(jnp.bfloat16)
    low = (value - high.astype(jnp.float32)).astype(jnp.bfloat16)
    return high, low


def dot(left, right):
    return jnp.dot(left, right, preferred_element_type=jnp.float32)


def stacked_dot(left, high, low):
    half = left.shape[0] // 2
    both = dot(left, high)
    return both[:half] + (both[half:] + dot(left[:half], low))


def lookup(table, place, lane):
    found = jnp.int32(-1)
    for z, entries in enumerate(table):
        for c, entry in enumerate(entries):
            found = jnp.where((place == z) & (lane == c), entry, found)
    return found


def store_piece(piece, plane, code_of, high, low, own=None, slab=2, first=0):
    count, width, edge, _ = piece.shape
    act = 2 * width

    @pl.when(plane >= 0)
    def _():
        for r in range(count):
            row = plane * slab + first + r
            for w in range(width):
                code = code_of(first + r, w)
                col = pl.ds(pl.multiple_of(code % act * edge, edge), edge)
                block = jnp.where(code < act, piece[r, w], 0.0)
                block_high, block_low = split(block)
                at = pl.ds(pl.multiple_of(row * edge, edge), edge)
                high[at, col] = block_high
                low[at, col] = block_low
                if own is not None:
                    own[pl.ds(r * edge, edge), col] = block_high
                    own[pl.ds((slab + r) * edge, edge), col] = block_low


def table_codes(table_ref, plane, group, slab, width):
    row = jnp.maximum(plane, 0) * slab
    return lambda r, w: table_ref[row + r, group * width + w]


T3, R4, T4, OWN, KEPT = 0, 1, 2, 3, 4


def noted_codes(notes, kind, slab, width):
    return lambda r, w: notes[0, (kind * slab + r) * width + w]


def add_plane(plane, left, high, low, part_ref):
    depth, tile = part_ref.shape[0], 512

    @pl.when(plane >= 0)
    def _():
        rows = pl.ds(pl.multiple_of(plane * depth, depth), depth)
        for n in range(part_ref.shape[1] // tile):
            cols = pl.ds(n * tile, tile)
            part_ref[:, cols] += stacked_dot(left[:, rows], high[rows, cols], low[rows, cols])


def clear_row(plane, r, code_of, width, high, low):
    edge = high.shape[0] // (2 * width)

    @pl.when(plane >= 0)
    def _():
        at = pl.ds(pl.multiple_of((plane * 2 + r) * edge, edge), edge)
        for w in range(width):
            col = pl.ds(pl.multiple_of(code_of(r, w) % (2 * width) * edge, edge), edge)
            high[at, col] = jnp.zeros((edge, edge), jnp.bfloat16)
            low[at, col] = jnp.zeros((edge, edge), jnp.bfloat16)


def add_row_blocks(piece, plane, r, code_of, left, high, low, part_ref):
    _, width, edge, _ = piece.shape
    act = 2 * width

    @pl.when(plane >= 0)
    def _():
        at = pl.ds(pl.multiple_of((plane * 2 + r) * edge, edge), edge)
        codes = [code_of(r, w) for w in range(width)]
        cols = [pl.ds(pl.multiple_of(code % act * edge, edge), edge) for code in codes]
        blocks = [jnp.where(code < act, piece[0, w], 0.0) for w, code in enumerate(codes)]
        block_high, block_low = split(jnp.concatenate(blocks, axis=1))
        more = stacked_dot(left[:, at], block_high, block_low)
        sums = [part_ref[:, col] + more[:, w * edge : (w + 1) * edge] for w, col in enumerate(cols)]
        for w, col in enumerate(cols):
            part_ref[:, col] = sums[w]
            high[at, col] = block_high[:, w * edge : (w + 1) * edge]
            low[at, col] = block_low[:, w * edge : (w + 1) * edge]


def early_kernel(
    tables, table_ref, own_hbm, own_swap, r1, r2, t1, t2, r3,
    high, low, left, part_ref, notes_ref, own_ref, own_sem,
):
    place, lane = lax.axis_index("blk"), lax.axis_index("depth")
    (hop1, hop1_senders), (near, near_senders), (far, far_senders) = tables
    slab, width = own_swap.shape[:2]
    act = 2 * width
    own_copy = pltpu.make_async_copy(own_hbm, own_ref, own_sem)
    own_copy.start()
    here, there = lookup(near, place, lane), lookup(near, place, 1 - lane)
    far_here, far_there = lookup(far, place, lane), lookup(far, place, 1 - lane)
    first_here, first_there = [lookup(hop1, place, c) for c in (lane, 1 - lane)]
    first_sender, first_other = [lookup(hop1_senders, place, c) for c in (lane, 1 - lane)]
    sender, other_sender = [lookup(near_senders, place, c) for c in (lane, 1 - lane)]
    far_sender, far_other = [lookup(far_senders, place, c) for c in (lane, 1 - lane)]
    part_ref[...] = jnp.zeros_like(part_ref)

    def codes(plane, group):
        return table_codes(table_ref, plane, group, slab, width)

    kinds = (
        (far_there, far_other),
        (far_here, 1 - far_sender),
        (far_there, 1 - far_other),
        (place, lane),
    )
    notes = jnp.zeros(notes_ref.shape, jnp.int32)
    index = lax.broadcasted_iota(jnp.int32, notes.shape, 1)
    for kind, (plane, group) in enumerate(kinds):
        for r in range(slab):
            for w in range(width):
                at = (kind * slab + r) * width + w
                notes = jnp.where(index == at, codes(plane, group)(r, w), notes)
    for r in range(slab):
        notes = jnp.where(
            index == KEPT * slab * width + r, table_ref[place * slab + r, act], notes
        )
    notes_ref[...] = notes

    store_piece(own_swap, place, codes(place, 1 - lane), high, low, left)
    store_piece(r1, first_here, codes(first_here, first_sender), high, low)
    store_piece(r2, here, codes(here, 1 - sender), high, low)
    store_piece(t1, first_there, codes(first_there, first_other), high, low)
    store_piece(t2, there, codes(there, 1 - other_sender), high, low)
    store_piece(r3, far_here, codes(far_here, far_sender), high, low)
    own_copy.wait()
    store_piece(own_ref, place, codes(place, lane), high, low, left)
    for plane in (place, here, there):
        add_plane(plane, left, high, low, part_ref)


def waiting_kernel(tables, notes_ref, r4a, high_in, low_in, left, part_in, high, low, part_ref):
    place, lane = lax.axis_index("blk"), lax.axis_index("depth")
    here = lookup(tables[-1][0], place, lane)
    width = r4a.shape[1]
    codes = noted_codes(notes_ref[...], R4, 2, width)
    store_piece(r4a, here, codes, high, low)
    clear_row(here, 1, codes, width, high, low)
    add_plane(here, left, high, low, part_ref)


def middle_kernel(
    tables, notes_ref, r4b, t3, t4a, high_in, low_in, left, part_in, high, low, part_ref
):
    place, lane = lax.axis_index("blk"), lax.axis_index("depth")
    here, there = [lookup(tables[-1][0], place, c) for c in (lane, 1 - lane)]
    slab, width = t3.shape[:2]
    notes = notes_ref[...]
    codes = noted_codes(notes, T4, slab, width)
    store_piece(t3, there, noted_codes(notes, T3, slab, width), high, low)
    store_piece(t4a, there, codes, high, low)
    clear_row(there, 1, codes, width, high, low)
    add_plane(there, left, high, low, part_ref)
    add_row_blocks(
        r4b, here, 1, noted_codes(notes, R4, slab, width), left, high, low, part_ref
    )


def late_kernel(
    tables, notes_ref, t4b, high_in, low_in, left, part_in,
    out_hbm, high, low, square, square_parts, out_ref, out_sem,
):
    place, lane = lax.axis_index("blk"), lax.axis_index("depth")
    there = lookup(tables[-1][0], place, 1 - lane)
    slab, width, edge, _ = out_ref.shape
    act = 2 * width
    holds = lax.axis_index("panel") == 0
    notes = notes_ref[...]
    own_codes = noted_codes(notes, OWN, slab, width)
    add_row_blocks(
        t4b, there, 1, noted_codes(notes, T4, slab, width), left, high, low, square
    )
    for r in range(slab):
        flags = notes[0, KEPT * slab * width + r]
        for c in range(square.shape[1] // edge):
            kept = (flags >> c) % 2 > 0
            col = pl.ds(c * edge, edge)
            block = jnp.where(kept, square[pl.ds(r * edge, edge), col], 0.0)
            block_high, block_low = split(block)
            square_parts[pl.ds(2 * r * edge, edge), col] = block_high
            square_parts[pl.ds((2 * r + 1) * edge, edge), col] = block_low
    copies = []
    for r in range(slab):
        left_parts = square_parts[pl.ds(2 * r * edge, 2 * edge), :]
        codes = [own_codes(r, w) for w in range(width)]
        cols = [pl.ds(pl.multiple_of(code % act * edge, edge), edge) for code in codes]
        cube = stacked_dot(
            left_parts,
            jnp.concatenate([high[:, col] for col in cols], axis=1),
            jnp.concatenate([low[:, col] for col in cols], axis=1),
        )
        for w in range(width):
            value = 3.0 * square[pl.ds(r * edge, edge), cols[w]]
            value = value - 2.0 * cube[:, w * edge : (w + 1) * edge]
            out_ref[r, w] = jnp.where(holds & (codes[w] < act), value, 0.0)
        copies.append(pltpu.make_async_copy(out_ref.at[r], out_hbm.at[r], out_sem.at[r]))
        copies[-1].start()
    for copy in copies:
        copy.wait()


def slot_table(columns, act):
    rows = columns.shape[0]
    slots = columns[:, :act]
    here = slots < rows
    ids = jnp.arange(rows, dtype=jnp.int32)
    taken = jnp.any(slots[:, :, None] == ids, axis=1)
    count = jnp.sum(here.astype(jnp.int32), axis=1, keepdims=True)
    before = jnp.sum(
        (~taken[:, None, :] & (ids[None, :] < ids[:, None])[None]).astype(jnp.int32), axis=2
    )
    at = jnp.where(taken, -1, count + before)
    filled = jnp.sum(
        jnp.where(at[:, None, :] == jnp.arange(act, dtype=jnp.int32)[None, :, None], ids, 0), axis=2
    )
    codes = jnp.where(here, slots, filled + act)
    kept = jnp.sum(jnp.where(taken, 1 << ids, 0), axis=1, keepdims=True)
    return jnp.concatenate([codes, kept], axis=1).astype(jnp.int32)


def gather_local(x_blocks, columns):
    slab, width, edge, _ = x_blocks.shape
    rows = columns.shape[0]
    groups, chains, panels, lanes = (lax.axis_size(axis) for axis in AXES)
    last = chains - 1

    def index(g, place):
        z, x, c = place
        return (((g % groups) * chains + z) * panels + x) * lanes + c

    def move(block, cycles):
        pairs = [(cycle[i - 1], cycle[i]) for cycle in cycles for i in range(len(cycle))]
        busy = {a for a, _ in pairs}
        route = [(index(g, a), index(g, b)) for g in range(groups) for a, b in pairs]
        for z in range(chains):
            for x in range(panels):
                idle = [(z, x, c) for c in range(lanes) if (z, x, c) not in busy]
                for g in range(groups):
                    if len(idle) == lanes:
                        route += [(index(g, idle[c - 1]), index(g, idle[c])) for c in range(lanes)]
                    else:
                        route += [(index(g, a), index(g + 1, a)) for a in idle]
        return lax.ppermute(block, AXES, route)

    def swap(block):
        return move(block, [])

    def move_only(block, chains_of):
        pairs = [(chain[i], chain[i + 1]) for chain in chains_of for i in range(len(chain) - 1)]
        route = [(index(g, a), index(g, b)) for g in range(groups) for a, b in pairs]
        return lax.ppermute(block, AXES, route)

    down_lane = [1 if z == 1 else 0 for z in range(chains)]
    up_lane = [1 - c for c in down_lane]
    up = [(z, 0, up_lane[z]) for z in range(chains)] + [(last, 1, up_lane[last])]
    down = [(z, 0, down_lane[z]) for z in reversed(range(chains))] + [(0, 1, down_lane[0])]
    first = [
        up[:last] + down + [(0, 1, up_lane[0])],
        [up[last], up[-1], (last, 1, down_lane[last])],
    ]
    second = [up, down]

    def received(hops):
        planes, senders = [], []
        for z in range(chains):
            below = z - hops if z >= hops else -1
            above = z + hops if z + hops < chains else -1
            if hops == 2:
                below, above = last if z == 0 else below, 0 if z == last else above
            row = [above, below] if down_lane[z] == 0 else [below, above]
            lane_of = [down_lane, up_lane] if down_lane[z] == 0 else [up_lane, down_lane]
            planes.append(row)
            senders.append([lanes_of[plane] for plane, lanes_of in zip(row, lane_of)])
        return planes, senders

    near, far = received(1), received(2)
    hop1 = [rows[:last] + [rows[last][::-1]] for rows in near]
    tables = hop1, near, far

    table = slot_table(columns, lanes * width)
    r1 = move(x_blocks, first)
    own_swap = swap(x_blocks)
    r2 = move_only(own_swap, [up, down])
    r1, table = lax.optimization_barrier((r1, table))
    r3 = move(r1, second)
    t1 = swap(r1)
    r4a, r4b = move(r2[:1], second), move(r2[1:], second)
    t2 = swap(r2)

    order, own = rows * edge, slab * edge
    table = pltpu.with_memory_space_constraint(table, pltpu.SMEM)
    smem = pl.BlockSpec(memory_space=pltpu.SMEM)
    vmem = pl.BlockSpec(memory_space=pltpu.VMEM)
    params = pltpu.CompilerParams(vmem_limit_bytes=24 * 2**20)
    def held(*arrays):
        return [pltpu.with_memory_space_constraint(a, pltpu.VMEM) for a in arrays]

    high, low, left, part, notes = pl.pallas_call(
        functools.partial(early_kernel, tables),
        out_shape=[
            jax.ShapeDtypeStruct((order, order), jnp.bfloat16),
            jax.ShapeDtypeStruct((order, order), jnp.bfloat16),
            jax.ShapeDtypeStruct((2 * own, order), jnp.bfloat16),
            jax.ShapeDtypeStruct((own, order), jnp.float32),
            jax.ShapeDtypeStruct((8, 128), jnp.int32),
        ],
        in_specs=[smem] + [pl.BlockSpec(memory_space=pltpu.HBM)] + [vmem] * 6,
        out_specs=[vmem] * 5,
        scratch_shapes=[pltpu.VMEM(x_blocks.shape, jnp.float32), pltpu.SemaphoreType.DMA],
        compiler_params=params,
        name="early",
    )(table, pltpu.with_memory_space_constraint(x_blocks, pltpu.HBM), own_swap, r1, r2, t1, t2, r3)
    t3 = swap(r3)
    r4a, part = lax.optimization_barrier((r4a, part))
    t4a = swap(r4a)
    dense = [jax.ShapeDtypeStruct(a.shape, a.dtype) for a in (high, low, part)]

    def add_to_square(kernel, name, *pieces):
        at = 1 + len(pieces)
        return pl.pallas_call(
            functools.partial(kernel, tables),
            out_shape=dense,
            in_specs=[vmem] * (at + 4),
            out_specs=[vmem] * 3,
            input_output_aliases={at: 0, at + 1: 1, at + 3: 2},
            compiler_params=params,
            name=name,
        )(notes, *pieces, *held(high, low, left, part))

    high, low, part = add_to_square(waiting_kernel, "waiting", r4a)
    r4b, t4a, part = lax.optimization_barrier((r4b, t4a, part))
    t4b = swap(r4b)
    high, low, part = add_to_square(middle_kernel, "middle", r4b, t3, t4a)
    out, _, _, _ = pl.pallas_call(
        functools.partial(late_kernel, tables),
        out_shape=[jax.ShapeDtypeStruct(x_blocks.shape, jnp.float32)] + dense,
        in_specs=[vmem] * 6,
        out_specs=[pl.BlockSpec(memory_space=pltpu.HBM)] + [vmem] * 3,
        input_output_aliases={2: 1, 3: 2, 5: 3},
        scratch_shapes=[
            pltpu.VMEM((2 * own, order), jnp.bfloat16),
            pltpu.VMEM(x_blocks.shape, jnp.float32),
            pltpu.SemaphoreType.DMA((slab,)),
        ],
        compiler_params=params,
        name="late",
    )(notes, t4b, *held(high, low, left, part))
    return out


def local(x_blocks, columns):
    slab, width, edge, _ = x_blocks.shape
    rows, slots = columns.shape
    _, chains, panels, lanes = (lax.axis_size(axis) for axis in AXES)
    full = rows <= slots and rows == lanes * width and width % 2 == 0
    if full and rows <= 8 and slab == 2 and edge == 128 and panels >= 2 and lanes == 2 and chains == 4:
        return gather_local(x_blocks, columns)
    return ring_local(x_blocks, columns)


def solution(mesh):
    placed = (P(("groups", "blk"), ("panel", "depth"), None, None), P("groups", None))
    return jax.shard_map(
        local,
        mesh=mesh,
        in_specs=placed,
        out_specs=P(("groups", "blk"), ("panel", "depth"), None, None),
        check_vma=False,
    )
```

```python
import functools

import jax
import jax.numpy as jnp
from jax import lax
from jax.experimental import pallas as pl
from jax.experimental.pallas import tpu as pltpu
from jax.sharding import PartitionSpec as P

precise = lax.Precision.HIGHEST
AXES = ("groups", "blk", "panel", "depth")


def shifted(block, axis, distance):
    devices = range(lax.axis_size(axis))
    route = [((i - distance) % len(devices), i) for i in devices]
    return lax.ppermute(block, axis, route)


def slot_gather(blocks):
    return lax.all_gather(blocks, ("panel", "depth"), axis=1, tiled=True)


def slot_reduce(partial_value):
    return lax.psum_scatter(partial_value, ("panel", "depth"), scatter_dimension=1, tiled=True)


def rotate_one(incoming):
    return shifted(incoming, "blk", 1)


def ring_local(x_blocks, columns):
    slab_rows = x_blocks.shape[0]
    width_slots = x_blocks.shape[1]
    edge = x_blocks.shape[2]
    order_rows = columns.shape[0]
    all_slots = columns.shape[1]
    cycle_size = lax.axis_size("blk")
    cycle_place = lax.axis_index("blk")
    anchor = jnp.int32(0)
    first_own = cycle_place * slab_rows
    slot_first = lax.axis_index(("panel", "depth")) * width_slots
    my_cols = lax.dynamic_slice(columns, (first_own, anchor), (slab_rows, all_slots))
    own_cols = lax.dynamic_slice(my_cols, (anchor, slot_first), (slab_rows, width_slots))
    x_own = jnp.where((own_cols < order_rows)[:, :, None, None], x_blocks, jnp.float32(0.0))
    out_present = my_cols < order_rows
    empty = jnp.zeros((slab_rows, all_slots, edge, edge), jnp.float32)

    def contribute(partial_value, left_rows, incoming, source):
        group = incoming.shape[0]
        first_row = source * group
        their_cols = lax.dynamic_slice(columns, (first_row, slot_first), (group, width_slots))
        row_ids = first_row + jnp.arange(group, dtype=jnp.int32)
        selector = (my_cols[:, None, :] == row_ids[None, :, None]).astype(jnp.float32)
        picked = jnp.einsum("irs,isab->irab", selector, left_rows, precision=precise)
        products = jnp.einsum("irab,rubc->iruac", picked, incoming, precision=precise)
        targets = (their_cols[None, None, :, :] == my_cols[:, :, None, None]) & out_present[
            :, :, None, None
        ]
        placed = jnp.einsum(
            "isru,iruac->isac", targets.astype(jnp.float32), products, precision=precise
        )
        return partial_value + placed

    def one_way(left_rows, stored):

        def advance(offset, state):
            partial_value, incoming, stored = state
            source = (cycle_place - offset) % cycle_size
            partial_value = contribute(partial_value, left_rows, incoming, source)
            return (partial_value, rotate_one(incoming), stored)

        partial_value, incoming, stored = lax.fori_loop(
            0, cycle_size - 1, advance, (empty, x_own, stored)
        )
        source = (cycle_place + 1) % cycle_size
        return (contribute(partial_value, left_rows, incoming, source), stored)

    stored = jnp.zeros((1,), jnp.float32)
    left_first = slot_gather(x_own)
    partial_value, stored = one_way(left_first, stored)
    squared = slot_reduce(partial_value)
    left_second = slot_gather(squared)
    partial_value, stored = one_way(left_second, stored)
    cubed = slot_reduce(partial_value)
    return 3.0 * squared - 2.0 * cubed


def split(value):
    high = value.astype(jnp.bfloat16)
    low = (value - high.astype(jnp.float32)).astype(jnp.bfloat16)
    return high, low


def dot(left, right):
    return jnp.dot(left, right, preferred_element_type=jnp.float32)


def stacked_dot(left, high, low):
    half = left.shape[0] // 2
    both = dot(left, high)
    return both[:half] + (both[half:] + dot(left[:half], low))


def lookup(table, place, lane):
    found = jnp.int32(-1)
    for z, entries in enumerate(table):
        for c, entry in enumerate(entries):
            found = jnp.where((place == z) & (lane == c), entry, found)
    return found


def store_piece(piece, plane, code_of, high, low, own=None, slab=2, first=0):
    count, width, edge, _ = piece.shape
    act = 2 * width

    @pl.when(plane >= 0)
    def _():
        for r in range(count):
            row = plane * slab + first + r
            for w in range(width):
                code = code_of(first + r, w)
                col = pl.ds(pl.multiple_of((code & (act - 1)) * edge, edge), edge)
                block = jnp.where(code < act, piece[r, w], 0.0)
                block_high, block_low = split(block)
                at = pl.ds(pl.multiple_of(row * edge, edge), edge)
                high[at, col] = block_high
                low[at, col] = block_low
                if own is not None:
                    own[pl.ds(r * edge, edge), col] = block_high
                    own[pl.ds((slab + r) * edge, edge), col] = block_low


def table_codes(table_ref, plane, group, slab, width):
    row = jnp.maximum(plane, 0) * slab
    return lambda r, w: table_ref[row + r, group * width + w]


T3, R4, T4, OWN, KEPT = 0, 1, 2, 3, 4


def packed(values, bits):
    return functools.reduce(jnp.bitwise_or, [v << (bits * k) for k, v in enumerate(values)])


def noted_codes(notes, kind, width):
    codes = notes[0, kind]
    return lambda r, w: (codes >> (4 * (r * width + w))) & 15


def add_plane(plane, left, high, low, part_ref):
    depth, tile = part_ref.shape[0], 512

    @pl.when(plane >= 0)
    def _():
        rows = pl.ds(pl.multiple_of(plane * depth, depth), depth)
        for n in range(part_ref.shape[1] // tile):
            cols = pl.ds(n * tile, tile)
            part_ref[:, cols] += stacked_dot(left[:, rows], high[rows, cols], low[rows, cols])


def clear_row(plane, r, code_of, width, high, low):
    edge = high.shape[0] // (2 * width)

    @pl.when(plane >= 0)
    def _():
        at = pl.ds(pl.multiple_of((plane * 2 + r) * edge, edge), edge)
        for w in range(width):
            col = pl.ds(pl.multiple_of((code_of(r, w) & (2 * width - 1)) * edge, edge), edge)
            high[at, col] = jnp.zeros((edge, edge), jnp.bfloat16)
            low[at, col] = jnp.zeros((edge, edge), jnp.bfloat16)


def add_row_blocks(piece, plane, r, code_of, left, high, low, part_ref):
    _, width, edge, _ = piece.shape
    act = 2 * width

    @pl.when(plane >= 0)
    def _():
        at = pl.ds(pl.multiple_of((plane * 2 + r) * edge, edge), edge)
        codes = [code_of(r, w) for w in range(width)]
        cols = [pl.ds(pl.multiple_of((code & (act - 1)) * edge, edge), edge) for code in codes]
        blocks = [jnp.where(code < act, piece[0, w], 0.0) for w, code in enumerate(codes)]
        block_high, block_low = split(jnp.concatenate(blocks, axis=1))
        more = stacked_dot(left[:, at], block_high, block_low)
        sums = [part_ref[:, col] + more[:, w * edge : (w + 1) * edge] for w, col in enumerate(cols)]
        for w, col in enumerate(cols):
            part_ref[:, col] = sums[w]
            high[at, col] = block_high[:, w * edge : (w + 1) * edge]
            low[at, col] = block_low[:, w * edge : (w + 1) * edge]


def early_kernel(
    tables, table_ref, own_hbm, own_swap, r1, r2, t1, t2, r3,
    high, low, left, part_ref, notes_ref, own_ref, own_sem,
):
    place, lane = lax.axis_index("blk"), lax.axis_index("depth")
    (hop1, hop1_senders), (near, near_senders), (far, far_senders) = tables
    slab, width = own_swap.shape[:2]
    act = 2 * width
    own_copy = pltpu.make_async_copy(own_hbm, own_ref, own_sem)
    own_copy.start()
    here, there = lookup(near, place, lane), lookup(near, place, 1 - lane)
    far_here, far_there = lookup(far, place, lane), lookup(far, place, 1 - lane)
    first_here, first_there = [lookup(hop1, place, c) for c in (lane, 1 - lane)]
    first_sender, first_other = [lookup(hop1_senders, place, c) for c in (lane, 1 - lane)]
    sender, other_sender = [lookup(near_senders, place, c) for c in (lane, 1 - lane)]
    far_sender, far_other = [lookup(far_senders, place, c) for c in (lane, 1 - lane)]
    part_ref[...] = jnp.zeros_like(part_ref)

    def codes(plane, group):
        return table_codes(table_ref, plane, group, slab, width)

    kinds = (
        (far_there, far_other),
        (far_here, 1 - far_sender),
        (far_there, 1 - far_other),
        (place, lane),
    )
    values = [
        packed([codes(plane, group)(r, w) for r in range(slab) for w in range(width)], 4)
        for plane, group in kinds
    ]
    values.append(packed([table_ref[place * slab + r, act] for r in range(slab)], act))
    notes = jnp.zeros(notes_ref.shape, jnp.int32)
    index = lax.broadcasted_iota(jnp.int32, notes.shape, 1)
    for at, value in enumerate(values):
        notes = jnp.where(index == at, value, notes)
    notes_ref[...] = notes

    store_piece(own_swap, place, codes(place, 1 - lane), high, low, left)
    store_piece(r1, first_here, codes(first_here, first_sender), high, low)
    store_piece(r2, here, codes(here, 1 - sender), high, low)
    store_piece(t1, first_there, codes(first_there, first_other), high, low)
    store_piece(t2, there, codes(there, 1 - other_sender), high, low)
    store_piece(r3, far_here, codes(far_here, far_sender), high, low)
    own_copy.wait()
    store_piece(own_ref, place, codes(place, lane), high, low, left)
    for plane in (place, here, there):
        add_plane(plane, left, high, low, part_ref)


def waiting_kernel(tables, notes_ref, r4a, high_in, low_in, left, part_in, high, low, part_ref):
    place, lane = lax.axis_index("blk"), lax.axis_index("depth")
    here = lookup(tables[-1][0], place, lane)
    width = r4a.shape[1]
    codes = noted_codes(notes_ref[...], R4, width)
    store_piece(r4a, here, codes, high, low)
    clear_row(here, 1, codes, width, high, low)
    add_plane(here, left, high, low, part_ref)


def middle_kernel(
    tables, notes_ref, r4b, t3, t4a, high_in, low_in, left, part_in, high, low, part_ref
):
    place, lane = lax.axis_index("blk"), lax.axis_index("depth")
    here, there = [lookup(tables[-1][0], place, c) for c in (lane, 1 - lane)]
    slab, width = t3.shape[:2]
    notes = notes_ref[...]
    codes = noted_codes(notes, T4, width)
    store_piece(t3, there, noted_codes(notes, T3, width), high, low)
    store_piece(t4a, there, codes, high, low)
    clear_row(there, 1, codes, width, high, low)
    add_plane(there, left, high, low, part_ref)
    add_row_blocks(
        r4b, here, 1, noted_codes(notes, R4, width), left, high, low, part_ref
    )


def late_kernel(
    tables, notes_ref, t4b, high_in, low_in, left, part_in,
    out_hbm, high, low, square, square_parts, out_ref, out_sem,
):
    place, lane = lax.axis_index("blk"), lax.axis_index("depth")
    there = lookup(tables[-1][0], place, 1 - lane)
    slab, width, edge, _ = out_ref.shape
    act = 2 * width
    holds = lax.axis_index("panel") == 0
    notes = notes_ref[...]
    own_codes = noted_codes(notes, OWN, width)
    add_row_blocks(
        t4b, there, 1, noted_codes(notes, T4, width), left, high, low, square
    )
    flags = notes[0, KEPT]
    for r in range(slab):
        for c in range(square.shape[1] // edge):
            kept = (flags >> (r * act + c)) & 1 > 0
            col = pl.ds(c * edge, edge)
            block = jnp.where(kept, square[pl.ds(r * edge, edge), col], 0.0)
            block_high, block_low = split(block)
            square_parts[pl.ds(2 * r * edge, edge), col] = block_high
            square_parts[pl.ds((2 * r + 1) * edge, edge), col] = block_low
    copies = []
    for r in range(slab):
        left_parts = square_parts[pl.ds(2 * r * edge, 2 * edge), :]
        codes = [own_codes(r, w) for w in range(width)]
        cols = [pl.ds(pl.multiple_of((code & (act - 1)) * edge, edge), edge) for code in codes]
        cube = stacked_dot(
            left_parts,
            jnp.concatenate([high[:, col] for col in cols], axis=1),
            jnp.concatenate([low[:, col] for col in cols], axis=1),
        )
        for w in range(width):
            value = 3.0 * square[pl.ds(r * edge, edge), cols[w]]
            value = value - 2.0 * cube[:, w * edge : (w + 1) * edge]
            out_ref[r, w] = jnp.where(holds & (codes[w] < act), value, 0.0)
        copies.append(pltpu.make_async_copy(out_ref.at[r], out_hbm.at[r], out_sem.at[r]))
        copies[-1].start()
    for copy in copies:
        copy.wait()


def slot_table(columns, act):
    rows = columns.shape[0]
    slots = columns[:, :act]
    here = slots < rows
    ids = jnp.arange(rows, dtype=jnp.int32)
    taken = jnp.any(slots[:, :, None] == ids, axis=1)
    count = jnp.sum(here.astype(jnp.int32), axis=1, keepdims=True)
    before = jnp.sum(
        (~taken[:, None, :] & (ids[None, :] < ids[:, None])[None]).astype(jnp.int32), axis=2
    )
    at = jnp.where(taken, -1, count + before)
    filled = jnp.sum(
        jnp.where(at[:, None, :] == jnp.arange(act, dtype=jnp.int32)[None, :, None], ids, 0), axis=2
    )
    codes = jnp.where(here, slots, filled + act)
    kept = jnp.sum(jnp.where(taken, 1 << ids, 0), axis=1, keepdims=True)
    return jnp.concatenate([codes, kept], axis=1).astype(jnp.int32)


def gather_local(x_blocks, columns):
    slab, width, edge, _ = x_blocks.shape
    rows = columns.shape[0]
    groups, chains, panels, lanes = (lax.axis_size(axis) for axis in AXES)
    last = chains - 1

    def index(g, place):
        z, x, c = place
        return (((g % groups) * chains + z) * panels + x) * lanes + c

    def move(block, cycles):
        pairs = [(cycle[i - 1], cycle[i]) for cycle in cycles for i in range(len(cycle))]
        busy = {a for a, _ in pairs}
        route = [(index(g, a), index(g, b)) for g in range(groups) for a, b in pairs]
        for z in range(chains):
            for x in range(panels):
                idle = [(z, x, c) for c in range(lanes) if (z, x, c) not in busy]
                for g in range(groups):
                    if len(idle) == lanes:
                        route += [(index(g, idle[c - 1]), index(g, idle[c])) for c in range(lanes)]
                    else:
                        route += [(index(g, a), index(g + 1, a)) for a in idle]
        return lax.ppermute(block, AXES, route)

    def swap(block):
        return move(block, [])

    def move_only(block, chains_of):
        pairs = [(chain[i], chain[i + 1]) for chain in chains_of for i in range(len(chain) - 1)]
        route = [(index(g, a), index(g, b)) for g in range(groups) for a, b in pairs]
        return lax.ppermute(block, AXES, route)

    down_lane = [1 if z == 1 else 0 for z in range(chains)]
    up_lane = [1 - c for c in down_lane]
    up = [(z, 0, up_lane[z]) for z in range(chains)] + [(last, 1, up_lane[last])]
    down = [(z, 0, down_lane[z]) for z in reversed(range(chains))] + [(0, 1, down_lane[0])]
    first = [
        up[:last] + down + [(0, 1, up_lane[0])],
        [up[last], up[-1], (last, 1, down_lane[last])],
    ]
    second = [up, down]

    def received(hops):
        planes, senders = [], []
        for z in range(chains):
            below = z - hops if z >= hops else -1
            above = z + hops if z + hops < chains else -1
            if hops == 2:
                below, above = last if z == 0 else below, 0 if z == last else above
            row = [above, below] if down_lane[z] == 0 else [below, above]
            lane_of = [down_lane, up_lane] if down_lane[z] == 0 else [up_lane, down_lane]
            planes.append(row)
            senders.append([lanes_of[plane] for plane, lanes_of in zip(row, lane_of)])
        return planes, senders

    near, far = received(1), received(2)
    hop1 = [rows[:last] + [rows[last][::-1]] for rows in near]
    tables = hop1, near, far

    table = slot_table(columns, lanes * width)
    r1 = move(x_blocks, first)
    own_swap = swap(x_blocks)
    r2 = move_only(own_swap, [up, down])
    r1, table = lax.optimization_barrier((r1, table))
    r3 = move(r1, second)
    t1 = swap(r1)
    r4a, r4b = move(r2[:1], second), move(r2[1:], second)
    t2 = swap(r2)

    order, own = rows * edge, slab * edge
    table = pltpu.with_memory_space_constraint(table, pltpu.SMEM)
    smem = pl.BlockSpec(memory_space=pltpu.SMEM)
    vmem = pl.BlockSpec(memory_space=pltpu.VMEM)
    params = pltpu.CompilerParams(vmem_limit_bytes=24 * 2**20)
    def held(*arrays):
        return [pltpu.with_memory_space_constraint(a, pltpu.VMEM) for a in arrays]

    high, low, left, part, notes = pl.pallas_call(
        functools.partial(early_kernel, tables),
        out_shape=[
            jax.ShapeDtypeStruct((order, order), jnp.bfloat16),
            jax.ShapeDtypeStruct((order, order), jnp.bfloat16),
            jax.ShapeDtypeStruct((2 * own, order), jnp.bfloat16),
            jax.ShapeDtypeStruct((own, order), jnp.float32),
            jax.ShapeDtypeStruct((8, 128), jnp.int32),
        ],
        in_specs=[smem] + [pl.BlockSpec(memory_space=pltpu.HBM)] + [vmem] * 6,
        out_specs=[vmem] * 5,
        scratch_shapes=[pltpu.VMEM(x_blocks.shape, jnp.float32), pltpu.SemaphoreType.DMA],
        compiler_params=params,
        name="early",
    )(table, pltpu.with_memory_space_constraint(x_blocks, pltpu.HBM), own_swap, r1, r2, t1, t2, r3)
    t3 = swap(r3)
    r4a, part = lax.optimization_barrier((r4a, part))
    t4a = swap(r4a)
    dense = [jax.ShapeDtypeStruct(a.shape, a.dtype) for a in (high, low, part)]

    def add_to_square(kernel, name, *pieces):
        at = 1 + len(pieces)
        return pl.pallas_call(
            functools.partial(kernel, tables),
            out_shape=dense,
            in_specs=[vmem] * (at + 4),
            out_specs=[vmem] * 3,
            input_output_aliases={at: 0, at + 1: 1, at + 3: 2},
            compiler_params=params,
            name=name,
        )(notes, *pieces, *held(high, low, left, part))

    high, low, part = add_to_square(waiting_kernel, "waiting", r4a)
    r4b, t4a, part = lax.optimization_barrier((r4b, t4a, part))
    t4b = swap(r4b)
    high, low, part = add_to_square(middle_kernel, "middle", r4b, t3, t4a)
    out, _, _, _ = pl.pallas_call(
        functools.partial(late_kernel, tables),
        out_shape=[jax.ShapeDtypeStruct(x_blocks.shape, jnp.float32)] + dense,
        in_specs=[vmem] * 6,
        out_specs=[pl.BlockSpec(memory_space=pltpu.HBM)] + [vmem] * 3,
        input_output_aliases={2: 1, 3: 2, 5: 3},
        scratch_shapes=[
            pltpu.VMEM((2 * own, order), jnp.bfloat16),
            pltpu.VMEM(x_blocks.shape, jnp.float32),
            pltpu.SemaphoreType.DMA((slab,)),
        ],
        compiler_params=params,
        name="late",
    )(notes, t4b, *held(high, low, left, part))
    return out


def local(x_blocks, columns):
    slab, width, edge, _ = x_blocks.shape
    rows, slots = columns.shape
    _, chains, panels, lanes = (lax.axis_size(axis) for axis in AXES)
    full = rows <= slots and rows == lanes * width and width in (2, 4)
    if full and rows <= 8 and slab == 2 and edge == 128 and panels >= 2 and lanes == 2 and chains == 4:
        return gather_local(x_blocks, columns)
    return ring_local(x_blocks, columns)


def solution(mesh):
    placed = (P(("groups", "blk"), ("panel", "depth"), None, None), P("groups", None))
    return jax.shard_map(
        local,
        mesh=mesh,
        in_specs=placed,
        out_specs=P(("groups", "blk"), ("panel", "depth"), None, None),
        check_vma=False,
    )
```

```python
import functools

import jax
import jax.numpy as jnp
from jax import lax
from jax.experimental import pallas as pl
from jax.experimental.pallas import tpu as pltpu
from jax.sharding import PartitionSpec as P

precise = lax.Precision.HIGHEST
AXES = ("groups", "blk", "panel", "depth")


def shifted(block, axis, distance):
    devices = range(lax.axis_size(axis))
    route = [((i - distance) % len(devices), i) for i in devices]
    return lax.ppermute(block, axis, route)


def slot_gather(blocks):
    return lax.all_gather(blocks, ("panel", "depth"), axis=1, tiled=True)


def slot_reduce(partial_value):
    return lax.psum_scatter(partial_value, ("panel", "depth"), scatter_dimension=1, tiled=True)


def rotate_one(incoming):
    return shifted(incoming, "blk", 1)


def ring_local(x_blocks, columns):
    slab_rows = x_blocks.shape[0]
    width_slots = x_blocks.shape[1]
    edge = x_blocks.shape[2]
    order_rows = columns.shape[0]
    all_slots = columns.shape[1]
    cycle_size = lax.axis_size("blk")
    cycle_place = lax.axis_index("blk")
    anchor = jnp.int32(0)
    first_own = cycle_place * slab_rows
    slot_first = lax.axis_index(("panel", "depth")) * width_slots
    my_cols = lax.dynamic_slice(columns, (first_own, anchor), (slab_rows, all_slots))
    own_cols = lax.dynamic_slice(my_cols, (anchor, slot_first), (slab_rows, width_slots))
    x_own = jnp.where((own_cols < order_rows)[:, :, None, None], x_blocks, jnp.float32(0.0))
    out_present = my_cols < order_rows
    empty = jnp.zeros((slab_rows, all_slots, edge, edge), jnp.float32)

    def contribute(partial_value, left_rows, incoming, source):
        group = incoming.shape[0]
        first_row = source * group
        their_cols = lax.dynamic_slice(columns, (first_row, slot_first), (group, width_slots))
        row_ids = first_row + jnp.arange(group, dtype=jnp.int32)
        selector = (my_cols[:, None, :] == row_ids[None, :, None]).astype(jnp.float32)
        picked = jnp.einsum("irs,isab->irab", selector, left_rows, precision=precise)
        products = jnp.einsum("irab,rubc->iruac", picked, incoming, precision=precise)
        targets = (their_cols[None, None, :, :] == my_cols[:, :, None, None]) & out_present[
            :, :, None, None
        ]
        placed = jnp.einsum(
            "isru,iruac->isac", targets.astype(jnp.float32), products, precision=precise
        )
        return partial_value + placed

    def one_way(left_rows, stored):

        def advance(offset, state):
            partial_value, incoming, stored = state
            source = (cycle_place - offset) % cycle_size
            partial_value = contribute(partial_value, left_rows, incoming, source)
            return (partial_value, rotate_one(incoming), stored)

        partial_value, incoming, stored = lax.fori_loop(
            0, cycle_size - 1, advance, (empty, x_own, stored)
        )
        source = (cycle_place + 1) % cycle_size
        return (contribute(partial_value, left_rows, incoming, source), stored)

    stored = jnp.zeros((1,), jnp.float32)
    left_first = slot_gather(x_own)
    partial_value, stored = one_way(left_first, stored)
    squared = slot_reduce(partial_value)
    left_second = slot_gather(squared)
    partial_value, stored = one_way(left_second, stored)
    cubed = slot_reduce(partial_value)
    return 3.0 * squared - 2.0 * cubed


def split(value):
    high = value.astype(jnp.bfloat16)
    low = (value - high.astype(jnp.float32)).astype(jnp.bfloat16)
    return high, low


def dot(left, right):
    return jnp.dot(left, right, preferred_element_type=jnp.float32)


def stacked_dot(left, high, low):
    half = left.shape[0] // 2
    both = dot(left, high)
    return both[:half] + (both[half:] + dot(left[:half], low))


def lookup(table, place, lane):
    found = jnp.int32(-1)
    for z, entries in enumerate(table):
        for c, entry in enumerate(entries):
            found = jnp.where((place == z) & (lane == c), entry, found)
    return found


def store_piece(piece, plane, code_of, high, low, own=None, slab=2, first=0):
    count, width, edge, _ = piece.shape
    act = 2 * width

    @pl.when(plane >= 0)
    def _():
        for r in range(count):
            row = plane * slab + first + r
            for w in range(width):
                code = code_of(first + r, w)
                col = pl.ds(pl.multiple_of((code & (act - 1)) * edge, edge), edge)
                block = jnp.where(code < act, piece[r, w], 0.0)
                block_high, block_low = split(block)
                at = pl.ds(pl.multiple_of(row * edge, edge), edge)
                high[at, col] = block_high
                low[at, col] = block_low
                if own is not None:
                    own[pl.ds(r * edge, edge), col] = block_high
                    own[pl.ds((slab + r) * edge, edge), col] = block_low


def table_codes(table_ref, plane, group, slab, width):
    row = jnp.maximum(plane, 0) * slab
    return lambda r, w: table_ref[row + r, group * width + w]


T3, R4, T4, OWN, KEPT = 0, 1, 2, 3, 4


def packed(values, bits):
    return functools.reduce(jnp.bitwise_or, [v << (bits * k) for k, v in enumerate(values)])


def noted_codes(notes, kind, width):
    codes = notes[0, kind]
    return lambda r, w: (codes >> (4 * (r * width + w))) & 15


def add_plane(plane, left, high, low, part_ref):
    depth, tile = part_ref.shape[0], 512

    @pl.when(plane >= 0)
    def _():
        rows = pl.ds(pl.multiple_of(plane * depth, depth), depth)
        for n in range(part_ref.shape[1] // tile):
            cols = pl.ds(n * tile, tile)
            part_ref[:, cols] += stacked_dot(left[:, rows], high[rows, cols], low[rows, cols])


def clear_row(plane, r, code_of, width, high, low):
    edge = high.shape[0] // (2 * width)

    @pl.when(plane >= 0)
    def _():
        at = pl.ds(pl.multiple_of((plane * 2 + r) * edge, edge), edge)
        for w in range(width):
            col = pl.ds(pl.multiple_of((code_of(r, w) & (2 * width - 1)) * edge, edge), edge)
            high[at, col] = jnp.zeros((edge, edge), jnp.bfloat16)
            low[at, col] = jnp.zeros((edge, edge), jnp.bfloat16)


def last_row_blocks(piece, plane, r, code_of, left, high, low):
    _, width, edge, _ = piece.shape
    act = 2 * width
    valid = plane >= 0
    at = pl.ds(pl.multiple_of((jnp.maximum(plane, 0) * 2 + r) * edge, edge), edge)
    codes = [code_of(r, w) for w in range(width)]
    cols = [pl.ds(pl.multiple_of((code & (act - 1)) * edge, edge), edge) for code in codes]
    blocks = [
        jnp.where(valid & (code < act), piece[0, w], 0.0) for w, code in enumerate(codes)
    ]
    block_high, block_low = split(jnp.concatenate(blocks, axis=1))
    more = stacked_dot(left[:, at], block_high, block_low)
    for w, col in enumerate(cols):
        part = slice(w * edge, (w + 1) * edge)
        high[at, col] = jnp.where(valid, block_high[:, part], high[at, col])
        low[at, col] = jnp.where(valid, block_low[:, part], low[at, col])
    return codes, cols, more


def early_kernel(
    tables, table_ref, own_hbm, own_swap, r1, r2, t1, t2, r3,
    high, low, left, part_ref, notes_ref, own_ref, own_sem,
):
    place, lane = lax.axis_index("blk"), lax.axis_index("depth")
    (hop1, hop1_senders), (near, near_senders), (far, far_senders) = tables
    slab, width = own_swap.shape[:2]
    act = 2 * width
    own_copy = pltpu.make_async_copy(own_hbm, own_ref, own_sem)
    own_copy.start()
    here, there = lookup(near, place, lane), lookup(near, place, 1 - lane)
    far_here, far_there = lookup(far, place, lane), lookup(far, place, 1 - lane)
    first_here, first_there = [lookup(hop1, place, c) for c in (lane, 1 - lane)]
    first_sender, first_other = [lookup(hop1_senders, place, c) for c in (lane, 1 - lane)]
    sender, other_sender = [lookup(near_senders, place, c) for c in (lane, 1 - lane)]
    far_sender, far_other = [lookup(far_senders, place, c) for c in (lane, 1 - lane)]
    part_ref[...] = jnp.zeros_like(part_ref)

    def codes(plane, group):
        return table_codes(table_ref, plane, group, slab, width)

    kinds = (
        (far_there, far_other),
        (far_here, 1 - far_sender),
        (far_there, 1 - far_other),
        (place, lane),
    )
    values = [
        packed([codes(plane, group)(r, w) for r in range(slab) for w in range(width)], 4)
        for plane, group in kinds
    ]
    values.append(packed([table_ref[place * slab + r, act] for r in range(slab)], act))
    notes = jnp.zeros(notes_ref.shape, jnp.int32)
    index = lax.broadcasted_iota(jnp.int32, notes.shape, 1)
    for at, value in enumerate(values):
        notes = jnp.where(index == at, value, notes)
    notes_ref[...] = notes

    store_piece(own_swap, place, codes(place, 1 - lane), high, low, left)
    store_piece(r1, first_here, codes(first_here, first_sender), high, low)
    store_piece(r2, here, codes(here, 1 - sender), high, low)
    store_piece(t1, first_there, codes(first_there, first_other), high, low)
    store_piece(t2, there, codes(there, 1 - other_sender), high, low)
    store_piece(r3, far_here, codes(far_here, far_sender), high, low)
    own_copy.wait()
    store_piece(own_ref, place, codes(place, lane), high, low, left)
    for plane in (place, here, there):
        add_plane(plane, left, high, low, part_ref)


def waiting_kernel(tables, notes_ref, r4a, high_in, low_in, left, part_in, high, low, part_ref):
    place, lane = lax.axis_index("blk"), lax.axis_index("depth")
    here = lookup(tables[-1][0], place, lane)
    width = r4a.shape[1]
    codes = noted_codes(notes_ref[...], R4, width)
    store_piece(r4a, here, codes, high, low)
    clear_row(here, 1, codes, width, high, low)
    add_plane(here, left, high, low, part_ref)


def middle_kernel(
    tables, notes_ref, r4b, t3, t4a, high_in, low_in, left, part_in, high, low, part_ref
):
    place, lane = lax.axis_index("blk"), lax.axis_index("depth")
    here, there = [lookup(tables[-1][0], place, c) for c in (lane, 1 - lane)]
    slab, width = t3.shape[:2]
    notes = notes_ref[...]
    codes = noted_codes(notes, T4, width)
    store_piece(t3, there, noted_codes(notes, T3, width), high, low)
    store_piece(t4a, there, codes, high, low)
    clear_row(there, 1, codes, width, high, low)
    edge, depth, tile = high.shape[0] // (2 * width), part_ref.shape[0], 512
    _, cols, more = last_row_blocks(
        r4b, here, 1, noted_codes(notes, R4, width), left, high, low
    )
    rows = pl.ds(pl.multiple_of(jnp.maximum(there, 0) * depth, depth), depth)
    for n in range(part_ref.shape[1] // tile):
        wide = pl.ds(n * tile, tile)
        plane = stacked_dot(left[:, rows], high[rows, wide], low[rows, wide])
        part_ref[:, wide] += jnp.where(there >= 0, plane, 0.0)
    for w, col in enumerate(cols):
        part_ref[:, col] += more[:, w * edge : (w + 1) * edge]


def late_kernel(
    tables, notes_ref, t4b, high_in, low_in, left, part_in,
    out_hbm, high, low, square, square_parts, out_ref, out_sem,
):
    place, lane = lax.axis_index("blk"), lax.axis_index("depth")
    there = lookup(tables[-1][0], place, 1 - lane)
    slab, width, edge, _ = out_ref.shape
    act = 2 * width
    holds = lax.axis_index("panel") == 0
    notes = notes_ref[...]
    own_codes = noted_codes(notes, OWN, width)
    codes, changed, more = last_row_blocks(
        t4b, there, 1, noted_codes(notes, T4, width), left, high, low
    )
    flags = notes[0, KEPT]

    def keep(r, c, col, block):
        kept = (flags >> (r * act + c)) & 1 > 0
        block_high, block_low = split(jnp.where(kept, block, 0.0))
        square_parts[pl.ds(2 * r * edge, edge), col] = block_high
        square_parts[pl.ds((2 * r + 1) * edge, edge), col] = block_low

    for r in range(slab):
        for c in range(square.shape[1] // edge):
            col = pl.ds(c * edge, edge)
            keep(r, c, col, square[pl.ds(r * edge, edge), col])
    sums = [square[:, col] + more[:, w * edge : (w + 1) * edge] for w, col in enumerate(changed)]
    for code, col, total in zip(codes, changed, sums):
        square[:, col] = total
        for r in range(slab):
            keep(r, code & (act - 1), col, total[r * edge : (r + 1) * edge])
    copies = []
    for r in range(slab):
        left_parts = square_parts[pl.ds(2 * r * edge, 2 * edge), :]
        codes = [own_codes(r, w) for w in range(width)]
        cols = [pl.ds(pl.multiple_of((code & (act - 1)) * edge, edge), edge) for code in codes]
        cube = stacked_dot(
            left_parts,
            jnp.concatenate([high[:, col] for col in cols], axis=1),
            jnp.concatenate([low[:, col] for col in cols], axis=1),
        )
        for w in range(width):
            value = 3.0 * square[pl.ds(r * edge, edge), cols[w]]
            value = value - 2.0 * cube[:, w * edge : (w + 1) * edge]
            out_ref[r, w] = jnp.where(holds & (codes[w] < act), value, 0.0)
        copies.append(pltpu.make_async_copy(out_ref.at[r], out_hbm.at[r], out_sem.at[r]))
        copies[-1].start()
    for copy in copies:
        copy.wait()


def slot_table(columns, act):
    rows = columns.shape[0]
    slots = columns[:, :act]
    here = slots < rows
    ids = jnp.arange(rows, dtype=jnp.int32)
    taken = jnp.any(slots[:, :, None] == ids, axis=1)
    count = jnp.sum(here.astype(jnp.int32), axis=1, keepdims=True)
    before = jnp.sum(
        (~taken[:, None, :] & (ids[None, :] < ids[:, None])[None]).astype(jnp.int32), axis=2
    )
    at = jnp.where(taken, -1, count + before)
    filled = jnp.sum(
        jnp.where(at[:, None, :] == jnp.arange(act, dtype=jnp.int32)[None, :, None], ids, 0), axis=2
    )
    codes = jnp.where(here, slots, filled + act)
    kept = jnp.sum(jnp.where(taken, 1 << ids, 0), axis=1, keepdims=True)
    return jnp.concatenate([codes, kept], axis=1).astype(jnp.int32)


def gather_local(x_blocks, columns):
    slab, width, edge, _ = x_blocks.shape
    rows = columns.shape[0]
    groups, chains, panels, lanes = (lax.axis_size(axis) for axis in AXES)
    last = chains - 1

    def index(g, place):
        z, x, c = place
        return (((g % groups) * chains + z) * panels + x) * lanes + c

    def move(block, cycles):
        pairs = [(cycle[i - 1], cycle[i]) for cycle in cycles for i in range(len(cycle))]
        busy = {a for a, _ in pairs}
        route = [(index(g, a), index(g, b)) for g in range(groups) for a, b in pairs]
        for z in range(chains):
            for x in range(panels):
                idle = [(z, x, c) for c in range(lanes) if (z, x, c) not in busy]
                for g in range(groups):
                    if len(idle) == lanes:
                        route += [(index(g, idle[c - 1]), index(g, idle[c])) for c in range(lanes)]
                    else:
                        route += [(index(g, a), index(g + 1, a)) for a in idle]
        return lax.ppermute(block, AXES, route)

    def swap(block):
        return move(block, [])

    def move_only(block, chains_of):
        pairs = [(chain[i], chain[i + 1]) for chain in chains_of for i in range(len(chain) - 1)]
        route = [(index(g, a), index(g, b)) for g in range(groups) for a, b in pairs]
        return lax.ppermute(block, AXES, route)

    down_lane = [1 if z == 1 else 0 for z in range(chains)]
    up_lane = [1 - c for c in down_lane]
    up = [(z, 0, up_lane[z]) for z in range(chains)] + [(last, 1, up_lane[last])]
    down = [(z, 0, down_lane[z]) for z in reversed(range(chains))] + [(0, 1, down_lane[0])]
    first = [
        up[:last] + down + [(0, 1, up_lane[0])],
        [up[last], up[-1], (last, 1, down_lane[last])],
    ]
    second = [up, down]

    def received(hops):
        planes, senders = [], []
        for z in range(chains):
            below = z - hops if z >= hops else -1
            above = z + hops if z + hops < chains else -1
            if hops == 2:
                below, above = last if z == 0 else below, 0 if z == last else above
            row = [above, below] if down_lane[z] == 0 else [below, above]
            lane_of = [down_lane, up_lane] if down_lane[z] == 0 else [up_lane, down_lane]
            planes.append(row)
            senders.append([lanes_of[plane] for plane, lanes_of in zip(row, lane_of)])
        return planes, senders

    near, far = received(1), received(2)
    hop1 = [rows[:last] + [rows[last][::-1]] for rows in near]
    tables = hop1, near, far

    table = slot_table(columns, lanes * width)
    r1 = move(x_blocks, first)
    own_swap = swap(x_blocks)
    r2 = move_only(own_swap, [up, down])
    r1, table = lax.optimization_barrier((r1, table))
    r3 = move(r1, second)
    t1 = swap(r1)
    r4a, r4b = move(r2[:1], second), move(r2[1:], second)
    t2 = swap(r2)

    order, own = rows * edge, slab * edge
    table = pltpu.with_memory_space_constraint(table, pltpu.SMEM)
    smem = pl.BlockSpec(memory_space=pltpu.SMEM)
    vmem = pl.BlockSpec(memory_space=pltpu.VMEM)
    params = pltpu.CompilerParams(vmem_limit_bytes=24 * 2**20)
    def held(*arrays):
        return [pltpu.with_memory_space_constraint(a, pltpu.VMEM) for a in arrays]

    high, low, left, part, notes = pl.pallas_call(
        functools.partial(early_kernel, tables),
        out_shape=[
            jax.ShapeDtypeStruct((order, order), jnp.bfloat16),
            jax.ShapeDtypeStruct((order, order), jnp.bfloat16),
            jax.ShapeDtypeStruct((2 * own, order), jnp.bfloat16),
            jax.ShapeDtypeStruct((own, order), jnp.float32),
            jax.ShapeDtypeStruct((8, 128), jnp.int32),
        ],
        in_specs=[smem] + [pl.BlockSpec(memory_space=pltpu.HBM)] + [vmem] * 6,
        out_specs=[vmem] * 5,
        scratch_shapes=[pltpu.VMEM(x_blocks.shape, jnp.float32), pltpu.SemaphoreType.DMA],
        compiler_params=params,
        name="early",
    )(table, pltpu.with_memory_space_constraint(x_blocks, pltpu.HBM), own_swap, r1, r2, t1, t2, r3)
    t3 = swap(r3)
    r4a, part = lax.optimization_barrier((r4a, part))
    t4a = swap(r4a)
    dense = [jax.ShapeDtypeStruct(a.shape, a.dtype) for a in (high, low, part)]

    def add_to_square(kernel, name, *pieces):
        at = 1 + len(pieces)
        return pl.pallas_call(
            functools.partial(kernel, tables),
            out_shape=dense,
            in_specs=[vmem] * (at + 4),
            out_specs=[vmem] * 3,
            input_output_aliases={at: 0, at + 1: 1, at + 3: 2},
            compiler_params=params,
            name=name,
        )(notes, *pieces, *held(high, low, left, part))

    high, low, part = add_to_square(waiting_kernel, "waiting", r4a)
    r4b, t4a, part = lax.optimization_barrier((r4b, t4a, part))
    t4b = swap(r4b)
    high, low, part = add_to_square(middle_kernel, "middle", r4b, t3, t4a)
    out, _, _, _ = pl.pallas_call(
        functools.partial(late_kernel, tables),
        out_shape=[jax.ShapeDtypeStruct(x_blocks.shape, jnp.float32)] + dense,
        in_specs=[vmem] * 6,
        out_specs=[pl.BlockSpec(memory_space=pltpu.HBM)] + [vmem] * 3,
        input_output_aliases={2: 1, 3: 2, 5: 3},
        scratch_shapes=[
            pltpu.VMEM((2 * own, order), jnp.bfloat16),
            pltpu.VMEM(x_blocks.shape, jnp.float32),
            pltpu.SemaphoreType.DMA((slab,)),
        ],
        compiler_params=params,
        name="late",
    )(notes, t4b, *held(high, low, left, part))
    return out


def local(x_blocks, columns):
    slab, width, edge, _ = x_blocks.shape
    rows, slots = columns.shape
    _, chains, panels, lanes = (lax.axis_size(axis) for axis in AXES)
    full = rows <= slots and rows == lanes * width and width in (2, 4)
    if full and rows <= 8 and slab == 2 and edge == 128 and panels >= 2 and lanes == 2 and chains == 4:
        return gather_local(x_blocks, columns)
    return ring_local(x_blocks, columns)


def solution(mesh):
    placed = (P(("groups", "blk"), ("panel", "depth"), None, None), P("groups", None))
    return jax.shard_map(
        local,
        mesh=mesh,
        in_specs=placed,
        out_specs=P(("groups", "blk"), ("panel", "depth"), None, None),
        check_vma=False,
    )
```

```python
import functools

import jax
import jax.numpy as jnp
from jax import lax
from jax.experimental import pallas as pl
from jax.experimental.pallas import tpu as pltpu
from jax.sharding import PartitionSpec as P

precise = lax.Precision.HIGHEST
AXES = ("groups", "blk", "panel", "depth")


def shifted(block, axis, distance):
    devices = range(lax.axis_size(axis))
    route = [((i - distance) % len(devices), i) for i in devices]
    return lax.ppermute(block, axis, route)


def slot_gather(blocks):
    return lax.all_gather(blocks, ("panel", "depth"), axis=1, tiled=True)


def slot_reduce(partial_value):
    return lax.psum_scatter(partial_value, ("panel", "depth"), scatter_dimension=1, tiled=True)


def rotate_one(incoming):
    return shifted(incoming, "blk", 1)


def ring_local(x_blocks, columns):
    slab_rows = x_blocks.shape[0]
    width_slots = x_blocks.shape[1]
    edge = x_blocks.shape[2]
    order_rows = columns.shape[0]
    all_slots = columns.shape[1]
    cycle_size = lax.axis_size("blk")
    cycle_place = lax.axis_index("blk")
    anchor = jnp.int32(0)
    first_own = cycle_place * slab_rows
    slot_first = lax.axis_index(("panel", "depth")) * width_slots
    my_cols = lax.dynamic_slice(columns, (first_own, anchor), (slab_rows, all_slots))
    own_cols = lax.dynamic_slice(my_cols, (anchor, slot_first), (slab_rows, width_slots))
    x_own = jnp.where((own_cols < order_rows)[:, :, None, None], x_blocks, jnp.float32(0.0))
    out_present = my_cols < order_rows
    empty = jnp.zeros((slab_rows, all_slots, edge, edge), jnp.float32)

    def contribute(partial_value, left_rows, incoming, source):
        group = incoming.shape[0]
        first_row = source * group
        their_cols = lax.dynamic_slice(columns, (first_row, slot_first), (group, width_slots))
        row_ids = first_row + jnp.arange(group, dtype=jnp.int32)
        selector = (my_cols[:, None, :] == row_ids[None, :, None]).astype(jnp.float32)
        picked = jnp.einsum("irs,isab->irab", selector, left_rows, precision=precise)
        products = jnp.einsum("irab,rubc->iruac", picked, incoming, precision=precise)
        targets = (their_cols[None, None, :, :] == my_cols[:, :, None, None]) & out_present[
            :, :, None, None
        ]
        placed = jnp.einsum(
            "isru,iruac->isac", targets.astype(jnp.float32), products, precision=precise
        )
        return partial_value + placed

    def one_way(left_rows, stored):

        def advance(offset, state):
            partial_value, incoming, stored = state
            source = (cycle_place - offset) % cycle_size
            partial_value = contribute(partial_value, left_rows, incoming, source)
            return (partial_value, rotate_one(incoming), stored)

        partial_value, incoming, stored = lax.fori_loop(
            0, cycle_size - 1, advance, (empty, x_own, stored)
        )
        source = (cycle_place + 1) % cycle_size
        return (contribute(partial_value, left_rows, incoming, source), stored)

    stored = jnp.zeros((1,), jnp.float32)
    left_first = slot_gather(x_own)
    partial_value, stored = one_way(left_first, stored)
    squared = slot_reduce(partial_value)
    left_second = slot_gather(squared)
    partial_value, stored = one_way(left_second, stored)
    cubed = slot_reduce(partial_value)
    return 3.0 * squared - 2.0 * cubed


def split(value):
    high = value.astype(jnp.bfloat16)
    low = (value - high.astype(jnp.float32)).astype(jnp.bfloat16)
    return high, low


def dot(left, right):
    return jnp.dot(left, right, preferred_element_type=jnp.float32)


def stacked_dot(left, high, low):
    half = left.shape[0] // 2
    both = dot(left, high)
    return both[:half] + (both[half:] + dot(left[:half], low))


def lookup(table, place, lane):
    found = jnp.int32(-1)
    for z, entries in enumerate(table):
        for c, entry in enumerate(entries):
            found = jnp.where((place == z) & (lane == c), entry, found)
    return found


def store_piece(piece, plane, code_of, high, low, own=None, slab=2, first=0):
    count, width, edge, _ = piece.shape
    act = 2 * width

    @pl.when(plane >= 0)
    def _():
        for r in range(count):
            row = plane * slab + first + r
            for w in range(width):
                code = code_of(first + r, w)
                col = pl.ds(pl.multiple_of((code & (act - 1)) * edge, edge), edge)
                block = jnp.where(code < act, piece[r, w], 0.0)
                block_high, block_low = split(block)
                at = pl.ds(pl.multiple_of(row * edge, edge), edge)
                high[at, col] = block_high
                low[at, col] = block_low
                if own is not None:
                    own[pl.ds(r * edge, edge), col] = block_high
                    own[pl.ds((slab + r) * edge, edge), col] = block_low


def table_codes(table_ref, plane, group, slab, width):
    row = jnp.maximum(plane, 0) * slab
    return lambda r, w: table_ref[row + r, group * width + w]


T3, R4, T4, OWN, KEPT = 0, 1, 2, 3, 4


def packed(values, bits):
    return functools.reduce(jnp.bitwise_or, [v << (bits * k) for k, v in enumerate(values)])


def noted_codes(notes, kind, width):
    codes = notes[0, kind]
    return lambda r, w: (codes >> (4 * (r * width + w))) & 15


def add_plane(plane, left, high, low, part_ref):
    depth, tile = part_ref.shape[0], 512

    @pl.when(plane >= 0)
    def _():
        rows = pl.ds(pl.multiple_of(plane * depth, depth), depth)
        for n in range(part_ref.shape[1] // tile):
            cols = pl.ds(n * tile, tile)
            part_ref[:, cols] += stacked_dot(left[:, rows], high[rows, cols], low[rows, cols])


def clear_row(plane, r, code_of, width, high, low):
    edge = high.shape[0] // (2 * width)

    @pl.when(plane >= 0)
    def _():
        at = pl.ds(pl.multiple_of((plane * 2 + r) * edge, edge), edge)
        for w in range(width):
            col = pl.ds(pl.multiple_of((code_of(r, w) & (2 * width - 1)) * edge, edge), edge)
            high[at, col] = jnp.zeros((edge, edge), jnp.bfloat16)
            low[at, col] = jnp.zeros((edge, edge), jnp.bfloat16)


def add_row_blocks(piece, plane, r, code_of, left, high, low, part_ref):
    _, width, edge, _ = piece.shape
    act = 2 * width

    @pl.when(plane >= 0)
    def _():
        at = pl.ds(pl.multiple_of((plane * 2 + r) * edge, edge), edge)
        codes = [code_of(r, w) for w in range(width)]
        cols = [pl.ds(pl.multiple_of((code & (act - 1)) * edge, edge), edge) for code in codes]
        blocks = [jnp.where(code < act, piece[0, w], 0.0) for w, code in enumerate(codes)]
        block_high, block_low = split(jnp.concatenate(blocks, axis=1))
        more = stacked_dot(left[:, at], block_high, block_low)
        sums = [part_ref[:, col] + more[:, w * edge : (w + 1) * edge] for w, col in enumerate(cols)]
        for w, col in enumerate(cols):
            part_ref[:, col] = sums[w]
            high[at, col] = block_high[:, w * edge : (w + 1) * edge]
            low[at, col] = block_low[:, w * edge : (w + 1) * edge]


def early_kernel(
    tables, table_ref, own_hbm, own_swap, r1, r2, t1, t2, r3,
    high, low, left, part_ref, notes_ref, own_ref, own_sem,
):
    place, lane = lax.axis_index("blk"), lax.axis_index("depth")
    (hop1, hop1_senders), (near, near_senders), (far, far_senders) = tables
    slab, width = own_swap.shape[:2]
    act = 2 * width
    own_copy = pltpu.make_async_copy(own_hbm, own_ref, own_sem)
    own_copy.start()
    here, there = lookup(near, place, lane), lookup(near, place, 1 - lane)
    far_here, far_there = lookup(far, place, lane), lookup(far, place, 1 - lane)
    first_here, first_there = [lookup(hop1, place, c) for c in (lane, 1 - lane)]
    first_sender, first_other = [lookup(hop1_senders, place, c) for c in (lane, 1 - lane)]
    sender, other_sender = [lookup(near_senders, place, c) for c in (lane, 1 - lane)]
    far_sender, far_other = [lookup(far_senders, place, c) for c in (lane, 1 - lane)]
    part_ref[...] = jnp.zeros_like(part_ref)

    def codes(plane, group):
        return table_codes(table_ref, plane, group, slab, width)

    kinds = (
        (far_there, far_other),
        (far_here, 1 - far_sender),
        (far_there, 1 - far_other),
        (place, lane),
    )
    values = [
        packed([codes(plane, group)(r, w) for r in range(slab) for w in range(width)], 4)
        for plane, group in kinds
    ]
    values.append(packed([table_ref[place * slab + r, act] for r in range(slab)], act))
    notes = jnp.zeros(notes_ref.shape, jnp.int32)
    index = lax.broadcasted_iota(jnp.int32, notes.shape, 1)
    for at, value in enumerate(values):
        notes = jnp.where(index == at, value, notes)
    notes_ref[...] = notes

    store_piece(own_swap, place, codes(place, 1 - lane), high, low, left)
    store_piece(r1, first_here, codes(first_here, first_sender), high, low)
    store_piece(r2, here, codes(here, 1 - sender), high, low)
    store_piece(t1, first_there, codes(first_there, first_other), high, low)
    store_piece(t2, there, codes(there, 1 - other_sender), high, low)
    store_piece(r3, far_here, codes(far_here, far_sender), high, low)
    own_copy.wait()
    store_piece(own_ref, place, codes(place, lane), high, low, left)
    for plane in (place, here, there):
        add_plane(plane, left, high, low, part_ref)


def waiting_kernel(tables, notes_ref, r4a, high_in, low_in, left, part_in, high, low, part_ref):
    place, lane = lax.axis_index("blk"), lax.axis_index("depth")
    here = lookup(tables[-1][0], place, lane)
    width = r4a.shape[1]
    codes = noted_codes(notes_ref[...], R4, width)
    store_piece(r4a, here, codes, high, low)
    clear_row(here, 1, codes, width, high, low)
    add_plane(here, left, high, low, part_ref)


def middle_kernel(
    tables, notes_ref, r4b, t3, t4a, high_in, low_in, left, part_in, high, low, part_ref
):
    place, lane = lax.axis_index("blk"), lax.axis_index("depth")
    here, there = [lookup(tables[-1][0], place, c) for c in (lane, 1 - lane)]
    slab, width = t3.shape[:2]
    notes = notes_ref[...]
    codes = noted_codes(notes, T4, width)
    store_piece(t3, there, noted_codes(notes, T3, width), high, low)
    store_piece(t4a, there, codes, high, low)
    clear_row(there, 1, codes, width, high, low)
    add_plane(there, left, high, low, part_ref)
    add_row_blocks(
        r4b, here, 1, noted_codes(notes, R4, width), left, high, low, part_ref
    )


def late_kernel(
    tables, notes_ref, t4b, high_in, low_in, left, part_in,
    out_hbm, high, low, square, square_parts, out_ref, out_sem,
):
    place, lane = lax.axis_index("blk"), lax.axis_index("depth")
    there = lookup(tables[-1][0], place, 1 - lane)
    slab, width, edge, _ = out_ref.shape
    act = 2 * width
    holds = lax.axis_index("panel") == 0
    notes = notes_ref[...]
    own_codes = noted_codes(notes, OWN, width)
    add_row_blocks(
        t4b, there, 1, noted_codes(notes, T4, width), left, high, low, square
    )
    flags = notes[0, KEPT]
    for r in range(slab):
        for c in range(square.shape[1] // edge):
            kept = (flags >> (r * act + c)) & 1 > 0
            col = pl.ds(c * edge, edge)
            block = jnp.where(kept, square[pl.ds(r * edge, edge), col], 0.0)
            block_high, block_low = split(block)
            square_parts[pl.ds(2 * r * edge, edge), col] = block_high
            square_parts[pl.ds((2 * r + 1) * edge, edge), col] = block_low
    copies = []
    for r in range(slab):
        left_parts = square_parts[pl.ds(2 * r * edge, 2 * edge), :]
        for first in range(0, width, 2):
            codes = [own_codes(r, first + k) for k in range(2)]
            cols = [pl.ds(pl.multiple_of((code & (act - 1)) * edge, edge), edge) for code in codes]
            cube = stacked_dot(
                left_parts,
                jnp.concatenate([high[:, col] for col in cols], axis=1),
                jnp.concatenate([low[:, col] for col in cols], axis=1),
            )
            for k in range(2):
                w = first + k
                value = 3.0 * square[pl.ds(r * edge, edge), cols[k]]
                value = value - 2.0 * cube[:, k * edge : (k + 1) * edge]
                out_ref[r, w] = jnp.where(holds & (codes[k] < act), value, 0.0)
                copies.append(
                    pltpu.make_async_copy(
                        out_ref.at[r, w], out_hbm.at[r, w], out_sem.at[len(copies)]
                    )
                )
                copies[-1].start()
    for copy in copies:
        copy.wait()


def slot_table(columns, act):
    rows = columns.shape[0]
    slots = columns[:, :act]
    here = slots < rows
    ids = jnp.arange(rows, dtype=jnp.int32)
    taken = jnp.any(slots[:, :, None] == ids, axis=1)
    count = jnp.sum(here.astype(jnp.int32), axis=1, keepdims=True)
    before = jnp.sum(
        (~taken[:, None, :] & (ids[None, :] < ids[:, None])[None]).astype(jnp.int32), axis=2
    )
    at = jnp.where(taken, -1, count + before)
    filled = jnp.sum(
        jnp.where(at[:, None, :] == jnp.arange(act, dtype=jnp.int32)[None, :, None], ids, 0), axis=2
    )
    codes = jnp.where(here, slots, filled + act)
    kept = jnp.sum(jnp.where(taken, 1 << ids, 0), axis=1, keepdims=True)
    return jnp.concatenate([codes, kept], axis=1).astype(jnp.int32)


def gather_local(x_blocks, columns):
    slab, width, edge, _ = x_blocks.shape
    rows = columns.shape[0]
    groups, chains, panels, lanes = (lax.axis_size(axis) for axis in AXES)
    last = chains - 1

    def index(g, place):
        z, x, c = place
        return (((g % groups) * chains + z) * panels + x) * lanes + c

    def move(block, cycles):
        pairs = [(cycle[i - 1], cycle[i]) for cycle in cycles for i in range(len(cycle))]
        busy = {a for a, _ in pairs}
        route = [(index(g, a), index(g, b)) for g in range(groups) for a, b in pairs]
        for z in range(chains):
            for x in range(panels):
                idle = [(z, x, c) for c in range(lanes) if (z, x, c) not in busy]
                for g in range(groups):
                    if len(idle) == lanes:
                        route += [(index(g, idle[c - 1]), index(g, idle[c])) for c in range(lanes)]
                    else:
                        route += [(index(g, a), index(g + 1, a)) for a in idle]
        return lax.ppermute(block, AXES, route)

    def swap(block):
        return move(block, [])

    def move_only(block, chains_of):
        pairs = [(chain[i], chain[i + 1]) for chain in chains_of for i in range(len(chain) - 1)]
        route = [(index(g, a), index(g, b)) for g in range(groups) for a, b in pairs]
        return lax.ppermute(block, AXES, route)

    down_lane = [1 if z == 1 else 0 for z in range(chains)]
    up_lane = [1 - c for c in down_lane]
    up = [(z, 0, up_lane[z]) for z in range(chains)] + [(last, 1, up_lane[last])]
    down = [(z, 0, down_lane[z]) for z in reversed(range(chains))] + [(0, 1, down_lane[0])]
    first = [
        up[:last] + down + [(0, 1, up_lane[0])],
        [up[last], up[-1], (last, 1, down_lane[last])],
    ]
    second = [up, down]

    def received(hops):
        planes, senders = [], []
        for z in range(chains):
            below = z - hops if z >= hops else -1
            above = z + hops if z + hops < chains else -1
            if hops == 2:
                below, above = last if z == 0 else below, 0 if z == last else above
            row = [above, below] if down_lane[z] == 0 else [below, above]
            lane_of = [down_lane, up_lane] if down_lane[z] == 0 else [up_lane, down_lane]
            planes.append(row)
            senders.append([lanes_of[plane] for plane, lanes_of in zip(row, lane_of)])
        return planes, senders

    near, far = received(1), received(2)
    hop1 = [rows[:last] + [rows[last][::-1]] for rows in near]
    tables = hop1, near, far

    table = slot_table(columns, lanes * width)
    r1 = move(x_blocks, first)
    own_swap = swap(x_blocks)
    r2 = move_only(own_swap, [up, down])
    r1, table = lax.optimization_barrier((r1, table))
    r3 = move(r1, second)
    t1 = swap(r1)
    r4a, r4b = move(r2[:1], second), move(r2[1:], second)
    t2 = swap(r2)

    order, own = rows * edge, slab * edge
    table = pltpu.with_memory_space_constraint(table, pltpu.SMEM)
    smem = pl.BlockSpec(memory_space=pltpu.SMEM)
    vmem = pl.BlockSpec(memory_space=pltpu.VMEM)
    params = pltpu.CompilerParams(vmem_limit_bytes=24 * 2**20)
    def held(*arrays):
        return [pltpu.with_memory_space_constraint(a, pltpu.VMEM) for a in arrays]

    high, low, left, part, notes = pl.pallas_call(
        functools.partial(early_kernel, tables),
        out_shape=[
            jax.ShapeDtypeStruct((order, order), jnp.bfloat16),
            jax.ShapeDtypeStruct((order, order), jnp.bfloat16),
            jax.ShapeDtypeStruct((2 * own, order), jnp.bfloat16),
            jax.ShapeDtypeStruct((own, order), jnp.float32),
            jax.ShapeDtypeStruct((8, 128), jnp.int32),
        ],
        in_specs=[smem] + [pl.BlockSpec(memory_space=pltpu.HBM)] + [vmem] * 6,
        out_specs=[vmem] * 5,
        scratch_shapes=[pltpu.VMEM(x_blocks.shape, jnp.float32), pltpu.SemaphoreType.DMA],
        compiler_params=params,
        name="early",
    )(table, pltpu.with_memory_space_constraint(x_blocks, pltpu.HBM), own_swap, r1, r2, t1, t2, r3)
    t3 = swap(r3)
    r4a, part = lax.optimization_barrier((r4a, part))
    t4a = swap(r4a)
    dense = [jax.ShapeDtypeStruct(a.shape, a.dtype) for a in (high, low, part)]

    def add_to_square(kernel, name, *pieces):
        at = 1 + len(pieces)
        return pl.pallas_call(
            functools.partial(kernel, tables),
            out_shape=dense,
            in_specs=[vmem] * (at + 4),
            out_specs=[vmem] * 3,
            input_output_aliases={at: 0, at + 1: 1, at + 3: 2},
            compiler_params=params,
            name=name,
        )(notes, *pieces, *held(high, low, left, part))

    high, low, part = add_to_square(waiting_kernel, "waiting", r4a)
    r4b, t4a, part = lax.optimization_barrier((r4b, t4a, part))
    t4b = swap(r4b)
    high, low, part = add_to_square(middle_kernel, "middle", r4b, t3, t4a)
    out, _, _, _ = pl.pallas_call(
        functools.partial(late_kernel, tables),
        out_shape=[jax.ShapeDtypeStruct(x_blocks.shape, jnp.float32)] + dense,
        in_specs=[vmem] * 6,
        out_specs=[pl.BlockSpec(memory_space=pltpu.HBM)] + [vmem] * 3,
        input_output_aliases={2: 1, 3: 2, 5: 3},
        scratch_shapes=[
            pltpu.VMEM((2 * own, order), jnp.bfloat16),
            pltpu.VMEM(x_blocks.shape, jnp.float32),
            pltpu.SemaphoreType.DMA((slab * width,)),
        ],
        compiler_params=params,
        name="late",
    )(notes, t4b, *held(high, low, left, part))
    return out


def local(x_blocks, columns):
    slab, width, edge, _ = x_blocks.shape
    rows, slots = columns.shape
    _, chains, panels, lanes = (lax.axis_size(axis) for axis in AXES)
    full = rows <= slots and rows == lanes * width and width in (2, 4)
    if full and rows <= 8 and slab == 2 and edge == 128 and panels >= 2 and lanes == 2 and chains == 4:
        return gather_local(x_blocks, columns)
    return ring_local(x_blocks, columns)


def solution(mesh):
    placed = (P(("groups", "blk"), ("panel", "depth"), None, None), P("groups", None))
    return jax.shard_map(
        local,
        mesh=mesh,
        in_specs=placed,
        out_specs=P(("groups", "blk"), ("panel", "depth"), None, None),
        check_vma=False,
    )
```

```python
import functools

import jax
import jax.numpy as jnp
from jax import lax
from jax.experimental import pallas as pl
from jax.experimental.pallas import tpu as pltpu
from jax.sharding import PartitionSpec as P

precise = lax.Precision.HIGHEST
AXES = ("groups", "blk", "panel", "depth")


def shifted(block, axis, distance):
    devices = range(lax.axis_size(axis))
    route = [((i - distance) % len(devices), i) for i in devices]
    return lax.ppermute(block, axis, route)


def slot_gather(blocks):
    return lax.all_gather(blocks, ("panel", "depth"), axis=1, tiled=True)


def slot_reduce(partial_value):
    return lax.psum_scatter(partial_value, ("panel", "depth"), scatter_dimension=1, tiled=True)


def rotate_one(incoming):
    return shifted(incoming, "blk", 1)


def ring_local(x_blocks, columns):
    slab_rows = x_blocks.shape[0]
    width_slots = x_blocks.shape[1]
    edge = x_blocks.shape[2]
    order_rows = columns.shape[0]
    all_slots = columns.shape[1]
    cycle_size = lax.axis_size("blk")
    cycle_place = lax.axis_index("blk")
    anchor = jnp.int32(0)
    first_own = cycle_place * slab_rows
    slot_first = lax.axis_index(("panel", "depth")) * width_slots
    my_cols = lax.dynamic_slice(columns, (first_own, anchor), (slab_rows, all_slots))
    own_cols = lax.dynamic_slice(my_cols, (anchor, slot_first), (slab_rows, width_slots))
    x_own = jnp.where((own_cols < order_rows)[:, :, None, None], x_blocks, jnp.float32(0.0))
    out_present = my_cols < order_rows
    empty = jnp.zeros((slab_rows, all_slots, edge, edge), jnp.float32)

    def contribute(partial_value, left_rows, incoming, source):
        group = incoming.shape[0]
        first_row = source * group
        their_cols = lax.dynamic_slice(columns, (first_row, slot_first), (group, width_slots))
        row_ids = first_row + jnp.arange(group, dtype=jnp.int32)
        selector = (my_cols[:, None, :] == row_ids[None, :, None]).astype(jnp.float32)
        picked = jnp.einsum("irs,isab->irab", selector, left_rows, precision=precise)
        products = jnp.einsum("irab,rubc->iruac", picked, incoming, precision=precise)
        targets = (their_cols[None, None, :, :] == my_cols[:, :, None, None]) & out_present[
            :, :, None, None
        ]
        placed = jnp.einsum(
            "isru,iruac->isac", targets.astype(jnp.float32), products, precision=precise
        )
        return partial_value + placed

    def one_way(left_rows, stored):

        def advance(offset, state):
            partial_value, incoming, stored = state
            source = (cycle_place - offset) % cycle_size
            partial_value = contribute(partial_value, left_rows, incoming, source)
            return (partial_value, rotate_one(incoming), stored)

        partial_value, incoming, stored = lax.fori_loop(
            0, cycle_size - 1, advance, (empty, x_own, stored)
        )
        source = (cycle_place + 1) % cycle_size
        return (contribute(partial_value, left_rows, incoming, source), stored)

    stored = jnp.zeros((1,), jnp.float32)
    left_first = slot_gather(x_own)
    partial_value, stored = one_way(left_first, stored)
    squared = slot_reduce(partial_value)
    left_second = slot_gather(squared)
    partial_value, stored = one_way(left_second, stored)
    cubed = slot_reduce(partial_value)
    return 3.0 * squared - 2.0 * cubed


def split(value):
    high = value.astype(jnp.bfloat16)
    low = (value - high.astype(jnp.float32)).astype(jnp.bfloat16)
    return high, low


def dot(left, right):
    return jnp.dot(left, right, preferred_element_type=jnp.float32)


def stacked_dot(left, high, low):
    half = left.shape[0] // 2
    both = dot(left, high)
    return both[:half] + (both[half:] + dot(left[:half], low))


def lookup(table, place, lane):
    found = jnp.int32(-1)
    for z, entries in enumerate(table):
        for c, entry in enumerate(entries):
            found = jnp.where((place == z) & (lane == c), entry, found)
    return found


def store_piece(piece, plane, code_of, high, low, own=None, slab=2, first=0):
    count, width, edge, _ = piece.shape
    act = 2 * width

    @pl.when(plane >= 0)
    def _():
        for r in range(count):
            row = plane * slab + first + r
            for w in range(width):
                code = code_of(first + r, w)
                col = pl.ds(pl.multiple_of((code & (act - 1)) * edge, edge), edge)
                block = jnp.where(code < act, piece[r, w], 0.0)
                block_high, block_low = split(block)
                at = pl.ds(pl.multiple_of(row * edge, edge), edge)
                high[at, col] = block_high
                low[at, col] = block_low
                if own is not None:
                    own[pl.ds(r * edge, edge), col] = block_high
                    own[pl.ds((slab + r) * edge, edge), col] = block_low


def table_codes(table_ref, plane, group, slab, width):
    row = jnp.maximum(plane, 0) * slab
    return lambda r, w: table_ref[row + r, group * width + w]


T3, R4, T4, OWN, KEPT = 0, 1, 2, 3, 4


def packed(values, bits):
    return functools.reduce(jnp.bitwise_or, [v << (bits * k) for k, v in enumerate(values)])


def noted_codes(notes, kind, width):
    codes = notes[0, kind]
    return lambda r, w: (codes >> (4 * (r * width + w))) & 15


def add_plane(plane, left, high, low, part_ref):
    depth, tile = part_ref.shape[0], 512

    @pl.when(plane >= 0)
    def _():
        rows = pl.ds(pl.multiple_of(plane * depth, depth), depth)
        for n in range(part_ref.shape[1] // tile):
            cols = pl.ds(n * tile, tile)
            part_ref[:, cols] += stacked_dot(left[:, rows], high[rows, cols], low[rows, cols])


def clear_row(plane, r, code_of, width, high, low):
    edge = high.shape[0] // (2 * width)

    @pl.when(plane >= 0)
    def _():
        at = pl.ds(pl.multiple_of((plane * 2 + r) * edge, edge), edge)
        for w in range(width):
            col = pl.ds(pl.multiple_of((code_of(r, w) & (2 * width - 1)) * edge, edge), edge)
            high[at, col] = jnp.zeros((edge, edge), jnp.bfloat16)
            low[at, col] = jnp.zeros((edge, edge), jnp.bfloat16)


def last_row_blocks(piece, plane, r, code_of, left, high, low):
    _, width, edge, _ = piece.shape
    act = 2 * width
    valid = plane >= 0
    at = pl.ds(pl.multiple_of((jnp.maximum(plane, 0) * 2 + r) * edge, edge), edge)
    codes = [code_of(r, w) for w in range(width)]
    cols = [pl.ds(pl.multiple_of((code & (act - 1)) * edge, edge), edge) for code in codes]
    blocks = [
        jnp.where(valid & (code < act), piece[0, w], 0.0) for w, code in enumerate(codes)
    ]
    block_high, block_low = split(jnp.concatenate(blocks, axis=1))
    more = stacked_dot(left[:, at], block_high, block_low)
    for w, col in enumerate(cols):
        part = slice(w * edge, (w + 1) * edge)
        high[at, col] = jnp.where(valid, block_high[:, part], high[at, col])
        low[at, col] = jnp.where(valid, block_low[:, part], low[at, col])
    return codes, cols, more


def early_kernel(
    tables, table_ref, own_hbm, own_swap, r1, r2, t1, t2, r3,
    high, low, left, part_ref, notes_ref, own_ref, own_sem,
):
    place, lane = lax.axis_index("blk"), lax.axis_index("depth")
    (hop1, hop1_senders), (near, near_senders), (far, far_senders) = tables
    slab, width = own_swap.shape[:2]
    act = 2 * width
    own_copy = pltpu.make_async_copy(own_hbm, own_ref, own_sem)
    own_copy.start()
    here, there = lookup(near, place, lane), lookup(near, place, 1 - lane)
    far_here, far_there = lookup(far, place, lane), lookup(far, place, 1 - lane)
    first_here, first_there = [lookup(hop1, place, c) for c in (lane, 1 - lane)]
    first_sender, first_other = [lookup(hop1_senders, place, c) for c in (lane, 1 - lane)]
    sender, other_sender = [lookup(near_senders, place, c) for c in (lane, 1 - lane)]
    far_sender, far_other = [lookup(far_senders, place, c) for c in (lane, 1 - lane)]
    part_ref[...] = jnp.zeros_like(part_ref)

    def codes(plane, group):
        return table_codes(table_ref, plane, group, slab, width)

    kinds = (
        (far_there, far_other),
        (far_here, 1 - far_sender),
        (far_there, 1 - far_other),
        (place, lane),
    )
    values = [
        packed([codes(plane, group)(r, w) for r in range(slab) for w in range(width)], 4)
        for plane, group in kinds
    ]
    values.append(packed([table_ref[place * slab + r, act] for r in range(slab)], act))
    notes = jnp.zeros(notes_ref.shape, jnp.int32)
    index = lax.broadcasted_iota(jnp.int32, notes.shape, 1)
    for at, value in enumerate(values):
        notes = jnp.where(index == at, value, notes)
    notes_ref[...] = notes

    store_piece(own_swap, place, codes(place, 1 - lane), high, low, left)
    store_piece(r1, first_here, codes(first_here, first_sender), high, low)
    store_piece(r2, here, codes(here, 1 - sender), high, low)
    store_piece(t1, first_there, codes(first_there, first_other), high, low)
    store_piece(t2, there, codes(there, 1 - other_sender), high, low)
    store_piece(r3, far_here, codes(far_here, far_sender), high, low)
    own_copy.wait()
    store_piece(own_ref, place, codes(place, lane), high, low, left)
    for plane in (place, here, there):
        add_plane(plane, left, high, low, part_ref)


def waiting_kernel(tables, notes_ref, r4a, high_in, low_in, left, part_in, high, low, part_ref):
    place, lane = lax.axis_index("blk"), lax.axis_index("depth")
    here = lookup(tables[-1][0], place, lane)
    width = r4a.shape[1]
    codes = noted_codes(notes_ref[...], R4, width)
    store_piece(r4a, here, codes, high, low)
    clear_row(here, 1, codes, width, high, low)
    add_plane(here, left, high, low, part_ref)


def middle_kernel(
    tables, notes_ref, r4b, t3, t4a, high_in, low_in, left, part_in, high, low, part_ref
):
    place, lane = lax.axis_index("blk"), lax.axis_index("depth")
    here, there = [lookup(tables[-1][0], place, c) for c in (lane, 1 - lane)]
    slab, width = t3.shape[:2]
    notes = notes_ref[...]
    codes = noted_codes(notes, T4, width)
    store_piece(t3, there, noted_codes(notes, T3, width), high, low)
    store_piece(t4a, there, codes, high, low)
    clear_row(there, 1, codes, width, high, low)
    edge, depth, tile = high.shape[0] // (2 * width), part_ref.shape[0], 512
    _, cols, more = last_row_blocks(
        r4b, here, 1, noted_codes(notes, R4, width), left, high, low
    )
    rows = pl.ds(pl.multiple_of(jnp.maximum(there, 0) * depth, depth), depth)
    for n in range(part_ref.shape[1] // tile):
        wide = pl.ds(n * tile, tile)
        plane = stacked_dot(left[:, rows], high[rows, wide], low[rows, wide])
        part_ref[:, wide] += jnp.where(there >= 0, plane, 0.0)
    for w, col in enumerate(cols):
        part_ref[:, col] += more[:, w * edge : (w + 1) * edge]


def late_kernel(
    tables, notes_ref, t4b, high_in, low_in, left, part_in,
    out_hbm, high, low, square, parts_0, parts_1, out_ref, out_sem,
):
    place, lane = lax.axis_index("blk"), lax.axis_index("depth")
    there = lookup(tables[-1][0], place, 1 - lane)
    slab, width, edge, _ = out_ref.shape
    act = 2 * width
    holds = lax.axis_index("panel") == 0
    notes = notes_ref[...]
    own_codes = noted_codes(notes, OWN, width)
    codes, changed, more = last_row_blocks(
        t4b, there, 1, noted_codes(notes, T4, width), left, high, low
    )
    flags = notes[0, KEPT]

    def keep(parts, r, c, col, block):
        kept = (flags >> (r * act + c)) & 1 > 0
        block_high, block_low = split(jnp.where(kept, block, 0.0))
        parts[pl.ds(0, edge), col] = block_high
        parts[pl.ds(edge, edge), col] = block_low

    before = [square[:, c * edge : (c + 1) * edge] for c in range(square.shape[1] // edge)]
    sums = [square[:, col] + more[:, w * edge : (w + 1) * edge] for w, col in enumerate(changed)]
    for col, total in zip(changed, sums):
        square[:, col] = total
    copies = []
    for r, parts in enumerate((parts_0, parts_1)):
        mine = slice(r * edge, (r + 1) * edge)
        for c, block in enumerate(before):
            keep(parts, r, c, pl.ds(c * edge, edge), block[mine])
        for code, col, total in zip(codes, changed, sums):
            keep(parts, r, code & (act - 1), col, total[mine])
        own = [own_codes(r, w) for w in range(width)]
        cols = [pl.ds(pl.multiple_of((code & (act - 1)) * edge, edge), edge) for code in own]
        cube = stacked_dot(
            parts[...],
            jnp.concatenate([high[:, col] for col in cols], axis=1),
            jnp.concatenate([low[:, col] for col in cols], axis=1),
        )
        for w in range(width):
            value = 3.0 * square[mine, cols[w]]
            value = value - 2.0 * cube[:, w * edge : (w + 1) * edge]
            out_ref[r, w] = jnp.where(holds & (own[w] < act), value, 0.0)
        copies.append(pltpu.make_async_copy(out_ref.at[r], out_hbm.at[r], out_sem.at[r]))
        copies[-1].start()
    for copy in copies:
        copy.wait()


def slot_table(columns, act):
    rows = columns.shape[0]
    slots = columns[:, :act]
    here = slots < rows
    ids = jnp.arange(rows, dtype=jnp.int32)
    taken = jnp.any(slots[:, :, None] == ids, axis=1)
    count = jnp.sum(here.astype(jnp.int32), axis=1, keepdims=True)
    before = jnp.sum(
        (~taken[:, None, :] & (ids[None, :] < ids[:, None])[None]).astype(jnp.int32), axis=2
    )
    at = jnp.where(taken, -1, count + before)
    filled = jnp.sum(
        jnp.where(at[:, None, :] == jnp.arange(act, dtype=jnp.int32)[None, :, None], ids, 0), axis=2
    )
    codes = jnp.where(here, slots, filled + act)
    kept = jnp.sum(jnp.where(taken, 1 << ids, 0), axis=1, keepdims=True)
    return jnp.concatenate([codes, kept], axis=1).astype(jnp.int32)


def gather_local(x_blocks, columns):
    slab, width, edge, _ = x_blocks.shape
    rows = columns.shape[0]
    groups, chains, panels, lanes = (lax.axis_size(axis) for axis in AXES)
    last = chains - 1

    def index(g, place):
        z, x, c = place
        return (((g % groups) * chains + z) * panels + x) * lanes + c

    def move(block, cycles):
        pairs = [(cycle[i - 1], cycle[i]) for cycle in cycles for i in range(len(cycle))]
        busy = {a for a, _ in pairs}
        route = [(index(g, a), index(g, b)) for g in range(groups) for a, b in pairs]
        for z in range(chains):
            for x in range(panels):
                idle = [(z, x, c) for c in range(lanes) if (z, x, c) not in busy]
                for g in range(groups):
                    if len(idle) == lanes:
                        route += [(index(g, idle[c - 1]), index(g, idle[c])) for c in range(lanes)]
                    else:
                        route += [(index(g, a), index(g + 1, a)) for a in idle]
        return lax.ppermute(block, AXES, route)

    def swap(block):
        return move(block, [])

    def move_only(block, chains_of):
        pairs = [(chain[i], chain[i + 1]) for chain in chains_of for i in range(len(chain) - 1)]
        route = [(index(g, a), index(g, b)) for g in range(groups) for a, b in pairs]
        return lax.ppermute(block, AXES, route)

    down_lane = [1 if z == 1 else 0 for z in range(chains)]
    up_lane = [1 - c for c in down_lane]
    up = [(z, 0, up_lane[z]) for z in range(chains)] + [(last, 1, up_lane[last])]
    down = [(z, 0, down_lane[z]) for z in reversed(range(chains))] + [(0, 1, down_lane[0])]
    first = [
        up[:last] + down + [(0, 1, up_lane[0])],
        [up[last], up[-1], (last, 1, down_lane[last])],
    ]
    second = [up, down]

    def received(hops):
        planes, senders = [], []
        for z in range(chains):
            below = z - hops if z >= hops else -1
            above = z + hops if z + hops < chains else -1
            if hops == 2:
                below, above = last if z == 0 else below, 0 if z == last else above
            row = [above, below] if down_lane[z] == 0 else [below, above]
            lane_of = [down_lane, up_lane] if down_lane[z] == 0 else [up_lane, down_lane]
            planes.append(row)
            senders.append([lanes_of[plane] for plane, lanes_of in zip(row, lane_of)])
        return planes, senders

    near, far = received(1), received(2)
    hop1 = [rows[:last] + [rows[last][::-1]] for rows in near]
    tables = hop1, near, far

    table = slot_table(columns, lanes * width)
    r1 = move(x_blocks, first)
    own_swap = swap(x_blocks)
    r2 = move_only(own_swap, [up, down])
    r1, table = lax.optimization_barrier((r1, table))
    r3 = move(r1, second)
    t1 = swap(r1)
    r4a, r4b = move(r2[:1], second), move(r2[1:], second)
    t2 = swap(r2)

    order, own = rows * edge, slab * edge
    table = pltpu.with_memory_space_constraint(table, pltpu.SMEM)
    smem = pl.BlockSpec(memory_space=pltpu.SMEM)
    vmem = pl.BlockSpec(memory_space=pltpu.VMEM)
    params = pltpu.CompilerParams(vmem_limit_bytes=24 * 2**20)
    def held(*arrays):
        return [pltpu.with_memory_space_constraint(a, pltpu.VMEM) for a in arrays]

    high, low, left, part, notes = pl.pallas_call(
        functools.partial(early_kernel, tables),
        out_shape=[
            jax.ShapeDtypeStruct((order, order), jnp.bfloat16),
            jax.ShapeDtypeStruct((order, order), jnp.bfloat16),
            jax.ShapeDtypeStruct((2 * own, order), jnp.bfloat16),
            jax.ShapeDtypeStruct((own, order), jnp.float32),
            jax.ShapeDtypeStruct((8, 128), jnp.int32),
        ],
        in_specs=[smem] + [pl.BlockSpec(memory_space=pltpu.HBM)] + [vmem] * 6,
        out_specs=[vmem] * 5,
        scratch_shapes=[pltpu.VMEM(x_blocks.shape, jnp.float32), pltpu.SemaphoreType.DMA],
        compiler_params=params,
        name="early",
    )(table, pltpu.with_memory_space_constraint(x_blocks, pltpu.HBM), own_swap, r1, r2, t1, t2, r3)
    t3 = swap(r3)
    r4a, part = lax.optimization_barrier((r4a, part))
    t4a = swap(r4a)
    dense = [jax.ShapeDtypeStruct(a.shape, a.dtype) for a in (high, low, part)]

    def add_to_square(kernel, name, *pieces):
        at = 1 + len(pieces)
        return pl.pallas_call(
            functools.partial(kernel, tables),
            out_shape=dense,
            in_specs=[vmem] * (at + 4),
            out_specs=[vmem] * 3,
            input_output_aliases={at: 0, at + 1: 1, at + 3: 2},
            compiler_params=params,
            name=name,
        )(notes, *pieces, *held(high, low, left, part))

    high, low, part = add_to_square(waiting_kernel, "waiting", r4a)
    r4b, t4a, part = lax.optimization_barrier((r4b, t4a, part))
    t4b = swap(r4b)
    high, low, part = add_to_square(middle_kernel, "middle", r4b, t3, t4a)
    out, _, _, _ = pl.pallas_call(
        functools.partial(late_kernel, tables),
        out_shape=[jax.ShapeDtypeStruct(x_blocks.shape, jnp.float32)] + dense,
        in_specs=[vmem] * 6,
        out_specs=[pl.BlockSpec(memory_space=pltpu.HBM)] + [vmem] * 3,
        input_output_aliases={2: 1, 3: 2, 5: 3},
        scratch_shapes=[
            pltpu.VMEM((2 * edge, order), jnp.bfloat16),
            pltpu.VMEM((2 * edge, order), jnp.bfloat16),
            pltpu.VMEM(x_blocks.shape, jnp.float32),
            pltpu.SemaphoreType.DMA((slab,)),
        ],
        compiler_params=params,
        name="late",
    )(notes, t4b, *held(high, low, left, part))
    return out


def local(x_blocks, columns):
    slab, width, edge, _ = x_blocks.shape
    rows, slots = columns.shape
    _, chains, panels, lanes = (lax.axis_size(axis) for axis in AXES)
    full = rows <= slots and rows == lanes * width and width in (2, 4)
    if full and rows <= 8 and slab == 2 and edge == 128 and panels >= 2 and lanes == 2 and chains == 4:
        return gather_local(x_blocks, columns)
    return ring_local(x_blocks, columns)


def solution(mesh):
    placed = (P(("groups", "blk"), ("panel", "depth"), None, None), P("groups", None))
    return jax.shard_map(
        local,
        mesh=mesh,
        in_specs=placed,
        out_specs=P(("groups", "blk"), ("panel", "depth"), None, None),
        check_vma=False,
    )
```

```python
import functools

import jax
import jax.numpy as jnp
from jax import lax
from jax.experimental import pallas as pl
from jax.experimental.pallas import tpu as pltpu
from jax.sharding import PartitionSpec as P

precise = lax.Precision.HIGHEST
AXES = ("groups", "blk", "panel", "depth")


def shifted(block, axis, distance):
    devices = range(lax.axis_size(axis))
    route = [((i - distance) % len(devices), i) for i in devices]
    return lax.ppermute(block, axis, route)


def slot_gather(blocks):
    return lax.all_gather(blocks, ("panel", "depth"), axis=1, tiled=True)


def slot_reduce(partial_value):
    return lax.psum_scatter(partial_value, ("panel", "depth"), scatter_dimension=1, tiled=True)


def rotate_one(incoming):
    return shifted(incoming, "blk", 1)


def ring_local(x_blocks, columns):
    slab_rows = x_blocks.shape[0]
    width_slots = x_blocks.shape[1]
    edge = x_blocks.shape[2]
    order_rows = columns.shape[0]
    all_slots = columns.shape[1]
    cycle_size = lax.axis_size("blk")
    cycle_place = lax.axis_index("blk")
    anchor = jnp.int32(0)
    first_own = cycle_place * slab_rows
    slot_first = lax.axis_index(("panel", "depth")) * width_slots
    my_cols = lax.dynamic_slice(columns, (first_own, anchor), (slab_rows, all_slots))
    own_cols = lax.dynamic_slice(my_cols, (anchor, slot_first), (slab_rows, width_slots))
    x_own = jnp.where((own_cols < order_rows)[:, :, None, None], x_blocks, jnp.float32(0.0))
    out_present = my_cols < order_rows
    empty = jnp.zeros((slab_rows, all_slots, edge, edge), jnp.float32)

    def contribute(partial_value, left_rows, incoming, source):
        group = incoming.shape[0]
        first_row = source * group
        their_cols = lax.dynamic_slice(columns, (first_row, slot_first), (group, width_slots))
        row_ids = first_row + jnp.arange(group, dtype=jnp.int32)
        selector = (my_cols[:, None, :] == row_ids[None, :, None]).astype(jnp.float32)
        picked = jnp.einsum("irs,isab->irab", selector, left_rows, precision=precise)
        products = jnp.einsum("irab,rubc->iruac", picked, incoming, precision=precise)
        targets = (their_cols[None, None, :, :] == my_cols[:, :, None, None]) & out_present[
            :, :, None, None
        ]
        placed = jnp.einsum(
            "isru,iruac->isac", targets.astype(jnp.float32), products, precision=precise
        )
        return partial_value + placed

    def one_way(left_rows, stored):

        def advance(offset, state):
            partial_value, incoming, stored = state
            source = (cycle_place - offset) % cycle_size
            partial_value = contribute(partial_value, left_rows, incoming, source)
            return (partial_value, rotate_one(incoming), stored)

        partial_value, incoming, stored = lax.fori_loop(
            0, cycle_size - 1, advance, (empty, x_own, stored)
        )
        source = (cycle_place + 1) % cycle_size
        return (contribute(partial_value, left_rows, incoming, source), stored)

    stored = jnp.zeros((1,), jnp.float32)
    left_first = slot_gather(x_own)
    partial_value, stored = one_way(left_first, stored)
    squared = slot_reduce(partial_value)
    left_second = slot_gather(squared)
    partial_value, stored = one_way(left_second, stored)
    cubed = slot_reduce(partial_value)
    return 3.0 * squared - 2.0 * cubed


def split(value):
    high = value.astype(jnp.bfloat16)
    low = (value - high.astype(jnp.float32)).astype(jnp.bfloat16)
    return high, low


def dot(left, right):
    return jnp.dot(left, right, preferred_element_type=jnp.float32)


def stacked_dot(left, high, low):
    half = left.shape[0] // 2
    both = dot(left, high)
    return both[:half] + (both[half:] + dot(left[:half], low))


def lookup(table, place, lane):
    found = jnp.int32(-1)
    for z, entries in enumerate(table):
        for c, entry in enumerate(entries):
            found = jnp.where((place == z) & (lane == c), entry, found)
    return found


def store_piece(piece, plane, code_of, high, low, own=None, slab=2, first=0):
    count, width, edge, _ = piece.shape
    act = 2 * width

    @pl.when(plane >= 0)
    def _():
        for r in range(count):
            row = plane * slab + first + r
            for w in range(width):
                code = code_of(first + r, w)
                col = pl.ds(pl.multiple_of((code & (act - 1)) * edge, edge), edge)
                block = jnp.where(code < act, piece[r, w], 0.0)
                block_high, block_low = split(block)
                at = pl.ds(pl.multiple_of(row * edge, edge), edge)
                high[at, col] = block_high
                low[at, col] = block_low
                if own is not None:
                    own[pl.ds(r * edge, edge), col] = block_high
                    own[pl.ds((slab + r) * edge, edge), col] = block_low


def table_codes(table_ref, plane, group, slab, width):
    row = jnp.maximum(plane, 0) * slab
    return lambda r, w: table_ref[row + r, group * width + w]


T3, R4, T4, OWN, KEPT = 0, 1, 2, 3, 4


def packed(values, bits):
    return functools.reduce(jnp.bitwise_or, [v << (bits * k) for k, v in enumerate(values)])


def noted_codes(notes, kind, width):
    codes = notes[0, kind]
    return lambda r, w: (codes >> (4 * (r * width + w))) & 15


def add_plane(plane, left, high, low, part_ref):
    depth, tile = part_ref.shape[0], 512

    @pl.when(plane >= 0)
    def _():
        rows = pl.ds(pl.multiple_of(plane * depth, depth), depth)
        for n in range(part_ref.shape[1] // tile):
            cols = pl.ds(n * tile, tile)
            part_ref[:, cols] += stacked_dot(left[:, rows], high[rows, cols], low[rows, cols])


def clear_row(plane, r, code_of, width, high, low):
    edge = high.shape[0] // (2 * width)

    @pl.when(plane >= 0)
    def _():
        at = pl.ds(pl.multiple_of((plane * 2 + r) * edge, edge), edge)
        for w in range(width):
            col = pl.ds(pl.multiple_of((code_of(r, w) & (2 * width - 1)) * edge, edge), edge)
            high[at, col] = jnp.zeros((edge, edge), jnp.bfloat16)
            low[at, col] = jnp.zeros((edge, edge), jnp.bfloat16)


def last_row_blocks(piece, plane, r, code_of, left, high, low):
    _, width, edge, _ = piece.shape
    act = 2 * width
    valid = plane >= 0
    at = pl.ds(pl.multiple_of((jnp.maximum(plane, 0) * 2 + r) * edge, edge), edge)
    codes = [code_of(r, w) for w in range(width)]
    cols = [pl.ds(pl.multiple_of((code & (act - 1)) * edge, edge), edge) for code in codes]
    blocks = [
        jnp.where(valid & (code < act), piece[0, w], 0.0) for w, code in enumerate(codes)
    ]
    block_high, block_low = split(jnp.concatenate(blocks, axis=1))
    more = stacked_dot(left[:, at], block_high, block_low)
    for w, col in enumerate(cols):
        part = slice(w * edge, (w + 1) * edge)
        high[at, col] = jnp.where(valid, block_high[:, part], high[at, col])
        low[at, col] = jnp.where(valid, block_low[:, part], low[at, col])
    return codes, cols, more


def early_kernel(
    tables, table_ref, own_hbm, own_swap, r1, r2, t1, t2, r3,
    high, low, left, part_ref, notes_ref, own_ref, own_sem,
):
    place, lane = lax.axis_index("blk"), lax.axis_index("depth")
    (hop1, hop1_senders), (near, near_senders), (far, far_senders) = tables
    slab, width = own_swap.shape[:2]
    act = 2 * width
    own_copy = pltpu.make_async_copy(own_hbm, own_ref, own_sem)
    own_copy.start()
    here, there = lookup(near, place, lane), lookup(near, place, 1 - lane)
    far_here, far_there = lookup(far, place, lane), lookup(far, place, 1 - lane)
    first_here, first_there = [lookup(hop1, place, c) for c in (lane, 1 - lane)]
    first_sender, first_other = [lookup(hop1_senders, place, c) for c in (lane, 1 - lane)]
    sender, other_sender = [lookup(near_senders, place, c) for c in (lane, 1 - lane)]
    far_sender, far_other = [lookup(far_senders, place, c) for c in (lane, 1 - lane)]
    part_ref[...] = jnp.zeros_like(part_ref)

    def codes(plane, group):
        return table_codes(table_ref, plane, group, slab, width)

    kinds = (
        (far_there, far_other),
        (far_here, 1 - far_sender),
        (far_there, 1 - far_other),
        (place, lane),
    )
    values = [
        packed([codes(plane, group)(r, w) for r in range(slab) for w in range(width)], 4)
        for plane, group in kinds
    ]
    values.append(packed([table_ref[place * slab + r, act] for r in range(slab)], act))
    notes = jnp.zeros(notes_ref.shape, jnp.int32)
    index = lax.broadcasted_iota(jnp.int32, notes.shape, 1)
    for at, value in enumerate(values):
        notes = jnp.where(index == at, value, notes)
    notes_ref[...] = notes

    store_piece(own_swap, place, codes(place, 1 - lane), high, low, left)
    store_piece(r1, first_here, codes(first_here, first_sender), high, low)
    store_piece(r2, here, codes(here, 1 - sender), high, low)
    store_piece(t1, first_there, codes(first_there, first_other), high, low)
    store_piece(t2, there, codes(there, 1 - other_sender), high, low)
    store_piece(r3, far_here, codes(far_here, far_sender), high, low)
    own_copy.wait()
    store_piece(own_ref, place, codes(place, lane), high, low, left)
    for plane in (place, here, there):
        add_plane(plane, left, high, low, part_ref)


def waiting_kernel(tables, notes_ref, r4a, high_in, low_in, left, part_in, high, low, part_ref):
    place, lane = lax.axis_index("blk"), lax.axis_index("depth")
    here = lookup(tables[-1][0], place, lane)
    width = r4a.shape[1]
    codes = noted_codes(notes_ref[...], R4, width)
    store_piece(r4a, here, codes, high, low)
    clear_row(here, 1, codes, width, high, low)
    add_plane(here, left, high, low, part_ref)


def middle_kernel(
    tables, notes_ref, r4b, t3, t4a, high_in, low_in, left, part_in, high, low, part_ref
):
    place, lane = lax.axis_index("blk"), lax.axis_index("depth")
    here, there = [lookup(tables[-1][0], place, c) for c in (lane, 1 - lane)]
    slab, width = t3.shape[:2]
    notes = notes_ref[...]
    codes = noted_codes(notes, T4, width)
    store_piece(t3, there, noted_codes(notes, T3, width), high, low)
    store_piece(t4a, there, codes, high, low)
    clear_row(there, 1, codes, width, high, low)
    edge, depth, tile = high.shape[0] // (2 * width), part_ref.shape[0], 512
    _, cols, more = last_row_blocks(
        r4b, here, 1, noted_codes(notes, R4, width), left, high, low
    )
    rows = pl.ds(pl.multiple_of(jnp.maximum(there, 0) * depth, depth), depth)
    for n in range(part_ref.shape[1] // tile):
        wide = pl.ds(n * tile, tile)
        plane = stacked_dot(left[:, rows], high[rows, wide], low[rows, wide])
        part_ref[:, wide] += jnp.where(there >= 0, plane, 0.0)
    for w, col in enumerate(cols):
        part_ref[:, col] += more[:, w * edge : (w + 1) * edge]


def late_kernel(
    tables, notes_ref, t4b, high_in, low_in, left, part_in,
    out_hbm, high, low, square, square_parts, out_ref, out_sem,
):
    place, lane = lax.axis_index("blk"), lax.axis_index("depth")
    there = lookup(tables[-1][0], place, 1 - lane)
    slab, width, edge, _ = out_ref.shape
    act = 2 * width
    holds = lax.axis_index("panel") == 0
    notes = notes_ref[...]
    own_codes = noted_codes(notes, OWN, width)
    codes, changed, more = last_row_blocks(
        t4b, there, 1, noted_codes(notes, T4, width), left, high, low
    )
    flags = notes[0, KEPT]

    def keep(r, c, col, block):
        kept = (flags >> (r * act + c)) & 1 > 0
        block_high, block_low = split(jnp.where(kept, block, 0.0))
        square_parts[pl.ds(2 * r * edge, edge), col] = block_high
        square_parts[pl.ds((2 * r + 1) * edge, edge), col] = block_low

    for r in range(slab):
        for c in range(square.shape[1] // edge):
            col = pl.ds(c * edge, edge)
            keep(r, c, col, square[pl.ds(r * edge, edge), col])
    sums = [square[:, col] + more[:, w * edge : (w + 1) * edge] for w, col in enumerate(changed)]
    for code, col, total in zip(codes, changed, sums):
        square[:, col] = total
        for r in range(slab):
            keep(r, code & (act - 1), col, total[r * edge : (r + 1) * edge])
    copies = []
    for r in range(slab):
        left_parts = square_parts[pl.ds(2 * r * edge, 2 * edge), :]
        codes = [own_codes(r, w) for w in range(width)]
        cols = [pl.ds(pl.multiple_of((code & (act - 1)) * edge, edge), edge) for code in codes]
        cube = stacked_dot(
            left_parts,
            jnp.concatenate([high[:, col] for col in cols], axis=1),
            jnp.concatenate([low[:, col] for col in cols], axis=1),
        )
        for w in range(width):
            value = 3.0 * square[pl.ds(r * edge, edge), cols[w]]
            value = value - 2.0 * cube[:, w * edge : (w + 1) * edge]
            out_ref[r, w] = jnp.where(holds & (codes[w] < act), value, 0.0)
        copies.append(pltpu.make_async_copy(out_ref.at[r], out_hbm.at[r], out_sem.at[r]))
        copies[-1].start()
    for copy in copies:
        copy.wait()


def slot_table(columns, act):
    rows = columns.shape[0]
    slots = columns[:, :act]
    here = slots < rows
    ids = jnp.arange(rows, dtype=jnp.int32)
    taken = jnp.any(slots[:, :, None] == ids, axis=1)
    count = jnp.sum(here.astype(jnp.int32), axis=1, keepdims=True)
    before = jnp.sum(
        (~taken[:, None, :] & (ids[None, :] < ids[:, None])[None]).astype(jnp.int32), axis=2
    )
    at = jnp.where(taken, -1, count + before)
    filled = jnp.sum(
        jnp.where(at[:, None, :] == jnp.arange(act, dtype=jnp.int32)[None, :, None], ids, 0), axis=2
    )
    codes = jnp.where(here, slots, filled + act)
    kept = jnp.sum(jnp.where(taken, 1 << ids, 0), axis=1, keepdims=True)
    return jnp.concatenate([codes, kept], axis=1).astype(jnp.int32)


def gather_local(x_blocks, columns):
    slab, width, edge, _ = x_blocks.shape
    rows = columns.shape[0]
    groups, chains, panels, lanes = (lax.axis_size(axis) for axis in AXES)
    last = chains - 1

    def index(g, place):
        z, x, c = place
        return (((g % groups) * chains + z) * panels + x) * lanes + c

    def move(block, cycles):
        pairs = [(cycle[i - 1], cycle[i]) for cycle in cycles for i in range(len(cycle))]
        busy = {a for a, _ in pairs}
        route = [(index(g, a), index(g, b)) for g in range(groups) for a, b in pairs]
        for z in range(chains):
            for x in range(panels):
                idle = [(z, x, c) for c in range(lanes) if (z, x, c) not in busy]
                for g in range(groups):
                    if len(idle) == lanes:
                        route += [(index(g, idle[c - 1]), index(g, idle[c])) for c in range(lanes)]
                    else:
                        route += [(index(g, a), index(g + 1, a)) for a in idle]
        return lax.ppermute(block, AXES, route)

    def swap(block):
        return move(block, [])

    def move_only(block, chains_of):
        pairs = [(chain[i], chain[i + 1]) for chain in chains_of for i in range(len(chain) - 1)]
        route = [(index(g, a), index(g, b)) for g in range(groups) for a, b in pairs]
        return lax.ppermute(block, AXES, route)

    down_lane = [1 if z == 1 else 0 for z in range(chains)]
    up_lane = [1 - c for c in down_lane]
    up = [(z, 0, up_lane[z]) for z in range(chains)] + [(last, 1, up_lane[last])]
    down = [(z, 0, down_lane[z]) for z in reversed(range(chains))] + [(0, 1, down_lane[0])]
    first = [
        up[:last] + down + [(0, 1, up_lane[0])],
        [up[last], up[-1], (last, 1, down_lane[last])],
    ]
    second = [
        up[:-1] + [(last, 1, down_lane[last]), up[-1]],
        down[:-1] + [(0, 1, up_lane[0]), down[-1]],
    ]

    def received(hops):
        planes, senders = [], []
        for z in range(chains):
            below = z - hops if z >= hops else -1
            above = z + hops if z + hops < chains else -1
            if hops == 2:
                below, above = last if z == 0 else below, 0 if z == last else above
            row = [above, below] if down_lane[z] == 0 else [below, above]
            lane_of = [down_lane, up_lane] if down_lane[z] == 0 else [up_lane, down_lane]
            planes.append(row)
            senders.append([lanes_of[plane] for plane, lanes_of in zip(row, lane_of)])
        return planes, senders

    near, far = received(1), received(2)
    hop1 = [rows[:last] + [rows[last][::-1]] for rows in near]
    tables = hop1, near, far

    table = slot_table(columns, lanes * width)
    r1 = move(x_blocks, first)
    own_swap = swap(x_blocks)
    r2 = move_only(own_swap, [up, down])
    r1, table = lax.optimization_barrier((r1, table))
    r3 = move(r1, second)
    t1 = swap(r1)
    r4a, r4b = move(r2[:1], second), move(r2[1:], second)
    t2 = swap(r2)

    order, own = rows * edge, slab * edge
    table = pltpu.with_memory_space_constraint(table, pltpu.SMEM)
    smem = pl.BlockSpec(memory_space=pltpu.SMEM)
    vmem = pl.BlockSpec(memory_space=pltpu.VMEM)
    params = pltpu.CompilerParams(vmem_limit_bytes=24 * 2**20)
    def held(*arrays):
        return [pltpu.with_memory_space_constraint(a, pltpu.VMEM) for a in arrays]

    high, low, left, part, notes = pl.pallas_call(
        functools.partial(early_kernel, tables),
        out_shape=[
            jax.ShapeDtypeStruct((order, order), jnp.bfloat16),
            jax.ShapeDtypeStruct((order, order), jnp.bfloat16),
            jax.ShapeDtypeStruct((2 * own, order), jnp.bfloat16),
            jax.ShapeDtypeStruct((own, order), jnp.float32),
            jax.ShapeDtypeStruct((8, 128), jnp.int32),
        ],
        in_specs=[smem] + [pl.BlockSpec(memory_space=pltpu.HBM)] + [vmem] * 6,
        out_specs=[vmem] * 5,
        scratch_shapes=[pltpu.VMEM(x_blocks.shape, jnp.float32), pltpu.SemaphoreType.DMA],
        compiler_params=params,
        name="early",
    )(table, pltpu.with_memory_space_constraint(x_blocks, pltpu.HBM), own_swap, r1, r2, t1, t2, r3)
    t3 = swap(r3)
    r4a, part = lax.optimization_barrier((r4a, part))
    t4a = swap(r4a)
    dense = [jax.ShapeDtypeStruct(a.shape, a.dtype) for a in (high, low, part)]

    def add_to_square(kernel, name, *pieces):
        at = 1 + len(pieces)
        return pl.pallas_call(
            functools.partial(kernel, tables),
            out_shape=dense,
            in_specs=[vmem] * (at + 4),
            out_specs=[vmem] * 3,
            input_output_aliases={at: 0, at + 1: 1, at + 3: 2},
            compiler_params=params,
            name=name,
        )(notes, *pieces, *held(high, low, left, part))

    high, low, part = add_to_square(waiting_kernel, "waiting", r4a)
    r4b, t4a, part = lax.optimization_barrier((r4b, t4a, part))
    t4b = swap(r4b)
    high, low, part = add_to_square(middle_kernel, "middle", r4b, t3, t4a)
    out, _, _, _ = pl.pallas_call(
        functools.partial(late_kernel, tables),
        out_shape=[jax.ShapeDtypeStruct(x_blocks.shape, jnp.float32)] + dense,
        in_specs=[vmem] * 6,
        out_specs=[pl.BlockSpec(memory_space=pltpu.HBM)] + [vmem] * 3,
        input_output_aliases={2: 1, 3: 2, 5: 3},
        scratch_shapes=[
            pltpu.VMEM((2 * own, order), jnp.bfloat16),
            pltpu.VMEM(x_blocks.shape, jnp.float32),
            pltpu.SemaphoreType.DMA((slab,)),
        ],
        compiler_params=params,
        name="late",
    )(notes, t4b, *held(high, low, left, part))
    return out


def local(x_blocks, columns):
    slab, width, edge, _ = x_blocks.shape
    rows, slots = columns.shape
    _, chains, panels, lanes = (lax.axis_size(axis) for axis in AXES)
    full = rows <= slots and rows == lanes * width and width in (2, 4)
    if full and rows <= 8 and slab == 2 and edge == 128 and panels >= 2 and lanes == 2 and chains == 4:
        return gather_local(x_blocks, columns)
    return ring_local(x_blocks, columns)


def solution(mesh):
    placed = (P(("groups", "blk"), ("panel", "depth"), None, None), P("groups", None))
    return jax.shard_map(
        local,
        mesh=mesh,
        in_specs=placed,
        out_specs=P(("groups", "blk"), ("panel", "depth"), None, None),
        check_vma=False,
    )
```

```python
import functools

import jax
import jax.numpy as jnp
from jax import lax
from jax.experimental import pallas as pl
from jax.experimental.pallas import tpu as pltpu
from jax.sharding import PartitionSpec as P

precise = lax.Precision.HIGHEST
AXES = ("groups", "blk", "panel", "depth")


def shifted(block, axis, distance):
    devices = range(lax.axis_size(axis))
    route = [((i - distance) % len(devices), i) for i in devices]
    return lax.ppermute(block, axis, route)


def slot_gather(blocks):
    return lax.all_gather(blocks, ("panel", "depth"), axis=1, tiled=True)


def slot_reduce(partial_value):
    return lax.psum_scatter(partial_value, ("panel", "depth"), scatter_dimension=1, tiled=True)


def rotate_one(incoming):
    return shifted(incoming, "blk", 1)


def ring_local(x_blocks, columns):
    slab_rows = x_blocks.shape[0]
    width_slots = x_blocks.shape[1]
    edge = x_blocks.shape[2]
    order_rows = columns.shape[0]
    all_slots = columns.shape[1]
    cycle_size = lax.axis_size("blk")
    cycle_place = lax.axis_index("blk")
    anchor = jnp.int32(0)
    first_own = cycle_place * slab_rows
    slot_first = lax.axis_index(("panel", "depth")) * width_slots
    my_cols = lax.dynamic_slice(columns, (first_own, anchor), (slab_rows, all_slots))
    own_cols = lax.dynamic_slice(my_cols, (anchor, slot_first), (slab_rows, width_slots))
    x_own = jnp.where((own_cols < order_rows)[:, :, None, None], x_blocks, jnp.float32(0.0))
    out_present = my_cols < order_rows
    empty = jnp.zeros((slab_rows, all_slots, edge, edge), jnp.float32)

    def contribute(partial_value, left_rows, incoming, source):
        group = incoming.shape[0]
        first_row = source * group
        their_cols = lax.dynamic_slice(columns, (first_row, slot_first), (group, width_slots))
        row_ids = first_row + jnp.arange(group, dtype=jnp.int32)
        selector = (my_cols[:, None, :] == row_ids[None, :, None]).astype(jnp.float32)
        picked = jnp.einsum("irs,isab->irab", selector, left_rows, precision=precise)
        products = jnp.einsum("irab,rubc->iruac", picked, incoming, precision=precise)
        targets = (their_cols[None, None, :, :] == my_cols[:, :, None, None]) & out_present[
            :, :, None, None
        ]
        placed = jnp.einsum(
            "isru,iruac->isac", targets.astype(jnp.float32), products, precision=precise
        )
        return partial_value + placed

    def one_way(left_rows, stored):

        def advance(offset, state):
            partial_value, incoming, stored = state
            source = (cycle_place - offset) % cycle_size
            partial_value = contribute(partial_value, left_rows, incoming, source)
            return (partial_value, rotate_one(incoming), stored)

        partial_value, incoming, stored = lax.fori_loop(
            0, cycle_size - 1, advance, (empty, x_own, stored)
        )
        source = (cycle_place + 1) % cycle_size
        return (contribute(partial_value, left_rows, incoming, source), stored)

    stored = jnp.zeros((1,), jnp.float32)
    left_first = slot_gather(x_own)
    partial_value, stored = one_way(left_first, stored)
    squared = slot_reduce(partial_value)
    left_second = slot_gather(squared)
    partial_value, stored = one_way(left_second, stored)
    cubed = slot_reduce(partial_value)
    return 3.0 * squared - 2.0 * cubed


def split(value):
    high = value.astype(jnp.bfloat16)
    low = (value - high.astype(jnp.float32)).astype(jnp.bfloat16)
    return high, low


def dot(left, right):
    return jnp.dot(left, right, preferred_element_type=jnp.float32)


def stacked_dot(left, high, low):
    half = left.shape[0] // 2
    both = dot(left, high)
    return both[:half] + (both[half:] + dot(left[:half], low))


def lookup(table, place, lane):
    found = jnp.int32(-1)
    for z, entries in enumerate(table):
        for c, entry in enumerate(entries):
            found = jnp.where((place == z) & (lane == c), entry, found)
    return found


def store_piece(piece, plane, code_of, high, low, own=None, slab=2, first=0):
    count, width, edge, _ = piece.shape
    act = 2 * width

    @pl.when(plane >= 0)
    def _():
        for r in range(count):
            row = plane * slab + first + r
            for w in range(width):
                code = code_of(first + r, w)
                col = pl.ds(pl.multiple_of((code & (act - 1)) * edge, edge), edge)
                block = jnp.where(code < act, piece[r, w], 0.0)
                block_high, block_low = split(block)
                at = pl.ds(pl.multiple_of(row * edge, edge), edge)
                high[at, col] = block_high
                low[at, col] = block_low
                if own is not None:
                    own[pl.ds(r * edge, edge), col] = block_high
                    own[pl.ds((slab + r) * edge, edge), col] = block_low


def table_codes(table_ref, plane, group, slab, width):
    row = jnp.maximum(plane, 0) * slab
    return lambda r, w: table_ref[row + r, group * width + w]


T3, R4, T4, OWN, KEPT = 0, 1, 2, 3, 4


def packed(values, bits):
    return functools.reduce(jnp.bitwise_or, [v << (bits * k) for k, v in enumerate(values)])


def noted_codes(notes, kind, width):
    codes = notes[0, kind]
    return lambda r, w: (codes >> (4 * (r * width + w))) & 15


def add_plane(plane, left, high, low, part_ref):
    depth, tile = part_ref.shape[0], 512

    @pl.when(plane >= 0)
    def _():
        rows = pl.ds(pl.multiple_of(plane * depth, depth), depth)
        for n in range(part_ref.shape[1] // tile):
            cols = pl.ds(n * tile, tile)
            part_ref[:, cols] += stacked_dot(left[:, rows], high[rows, cols], low[rows, cols])


def clear_row(plane, r, code_of, width, high, low):
    edge = high.shape[0] // (2 * width)

    @pl.when(plane >= 0)
    def _():
        at = pl.ds(pl.multiple_of((plane * 2 + r) * edge, edge), edge)
        for w in range(width):
            col = pl.ds(pl.multiple_of((code_of(r, w) & (2 * width - 1)) * edge, edge), edge)
            high[at, col] = jnp.zeros((edge, edge), jnp.bfloat16)
            low[at, col] = jnp.zeros((edge, edge), jnp.bfloat16)


def last_row_blocks(piece, plane, r, code_of, left, high, low):
    _, width, edge, _ = piece.shape
    act = 2 * width
    valid = plane >= 0
    at = pl.ds(pl.multiple_of((jnp.maximum(plane, 0) * 2 + r) * edge, edge), edge)
    codes = [code_of(r, w) for w in range(width)]
    cols = [pl.ds(pl.multiple_of((code & (act - 1)) * edge, edge), edge) for code in codes]
    blocks = [
        jnp.where(valid & (code < act), piece[0, w], 0.0) for w, code in enumerate(codes)
    ]
    block_high, block_low = split(jnp.concatenate(blocks, axis=1))
    more = stacked_dot(left[:, at], block_high, block_low)
    for w, col in enumerate(cols):
        part = slice(w * edge, (w + 1) * edge)
        high[at, col] = jnp.where(valid, block_high[:, part], high[at, col])
        low[at, col] = jnp.where(valid, block_low[:, part], low[at, col])
    return codes, cols, more


def early_kernel(
    tables, table_ref, own_hbm, own_swap, r1, r2, t1, t2, r3,
    high, low, left, part_ref, notes_ref, own_ref, own_sem,
):
    place, lane = lax.axis_index("blk"), lax.axis_index("depth")
    (hop1, hop1_senders), (near, near_senders), (far, far_senders) = tables
    slab, width = own_swap.shape[:2]
    act = 2 * width
    own_copy = pltpu.make_async_copy(own_hbm, own_ref, own_sem)
    own_copy.start()
    here, there = lookup(near, place, lane), lookup(near, place, 1 - lane)
    far_here, far_there = lookup(far, place, lane), lookup(far, place, 1 - lane)
    first_here, first_there = [lookup(hop1, place, c) for c in (lane, 1 - lane)]
    first_sender, first_other = [lookup(hop1_senders, place, c) for c in (lane, 1 - lane)]
    sender, other_sender = [lookup(near_senders, place, c) for c in (lane, 1 - lane)]
    far_sender, far_other = [lookup(far_senders, place, c) for c in (lane, 1 - lane)]
    part_ref[...] = jnp.zeros_like(part_ref)

    def codes(plane, group):
        return table_codes(table_ref, plane, group, slab, width)

    kinds = (
        (far_there, far_other),
        (far_here, 1 - far_sender),
        (far_there, 1 - far_other),
        (place, lane),
    )
    values = [
        packed([codes(plane, group)(r, w) for r in range(slab) for w in range(width)], 4)
        for plane, group in kinds
    ]
    values.append(packed([table_ref[place * slab + r, act] for r in range(slab)], act))
    notes = jnp.zeros(notes_ref.shape, jnp.int32)
    index = lax.broadcasted_iota(jnp.int32, notes.shape, 1)
    for at, value in enumerate(values):
        notes = jnp.where(index == at, value, notes)
    notes_ref[...] = notes

    store_piece(own_swap, place, codes(place, 1 - lane), high, low, left)
    store_piece(r1, first_here, codes(first_here, first_sender), high, low)
    store_piece(r2, here, codes(here, 1 - sender), high, low)
    store_piece(t1, first_there, codes(first_there, first_other), high, low)
    store_piece(t2, there, codes(there, 1 - other_sender), high, low)
    store_piece(r3, far_here, codes(far_here, far_sender), high, low)
    own_copy.wait()
    store_piece(own_ref, place, codes(place, lane), high, low, left)
    for plane in (place, here, there):
        add_plane(plane, left, high, low, part_ref)


def waiting_kernel(tables, notes_ref, r4a, high_in, low_in, left, part_in, high, low, part_ref):
    place, lane = lax.axis_index("blk"), lax.axis_index("depth")
    here = lookup(tables[-1][0], place, lane)
    width = r4a.shape[1]
    codes = noted_codes(notes_ref[...], R4, width)
    store_piece(r4a, here, codes, high, low)
    clear_row(here, 1, codes, width, high, low)
    add_plane(here, left, high, low, part_ref)


def middle_kernel(
    tables, notes_ref, r4b, t3, t4a, high_in, low_in, left, part_in, high, low, part_ref
):
    place, lane = lax.axis_index("blk"), lax.axis_index("depth")
    here, there = [lookup(tables[-1][0], place, c) for c in (lane, 1 - lane)]
    slab, width = t3.shape[:2]
    notes = notes_ref[...]
    codes = noted_codes(notes, T4, width)
    store_piece(t3, there, noted_codes(notes, T3, width), high, low)
    store_piece(t4a, there, codes, high, low)
    clear_row(there, 1, codes, width, high, low)
    edge, depth, tile = high.shape[0] // (2 * width), part_ref.shape[0], 512
    _, cols, more = last_row_blocks(
        r4b, here, 1, noted_codes(notes, R4, width), left, high, low
    )
    rows = pl.ds(pl.multiple_of(jnp.maximum(there, 0) * depth, depth), depth)
    for n in range(part_ref.shape[1] // tile):
        wide = pl.ds(n * tile, tile)
        plane = stacked_dot(left[:, rows], high[rows, wide], low[rows, wide])
        part_ref[:, wide] += jnp.where(there >= 0, plane, 0.0)
    for w, col in enumerate(cols):
        part_ref[:, col] += more[:, w * edge : (w + 1) * edge]


def late_kernel(
    tables, notes_ref, t4b, high_in, low_in, left, part_in,
    out_hbm, high, low, square, square_parts, out_ref, out_sem,
):
    place, lane = lax.axis_index("blk"), lax.axis_index("depth")
    there = lookup(tables[-1][0], place, 1 - lane)
    slab, width, edge, _ = out_ref.shape
    act = 2 * width
    holds = lax.axis_index("panel") == 0
    notes = notes_ref[...]
    own_codes = noted_codes(notes, OWN, width)
    codes, changed, more = last_row_blocks(
        t4b, there, 1, noted_codes(notes, T4, width), left, high, low
    )
    flags = notes[0, KEPT]

    def keep(r, c, col, block):
        kept = (flags >> (r * act + c)) & 1 > 0
        block_high, block_low = split(jnp.where(kept, block, 0.0))
        square_parts[pl.ds(2 * r * edge, edge), col] = block_high
        square_parts[pl.ds((2 * r + 1) * edge, edge), col] = block_low

    for r in range(slab):
        for c in range(square.shape[1] // edge):
            col = pl.ds(c * edge, edge)
            keep(r, c, col, square[pl.ds(r * edge, edge), col])
    sums = [square[:, col] + more[:, w * edge : (w + 1) * edge] for w, col in enumerate(changed)]
    for code, col, total in zip(codes, changed, sums):
        square[:, col] = total
        for r in range(slab):
            keep(r, code & (act - 1), col, total[r * edge : (r + 1) * edge])
    copies = []
    for r in range(slab):
        left_parts = square_parts[pl.ds(2 * r * edge, 2 * edge), :]
        codes = [own_codes(r, w) for w in range(width)]
        cols = [pl.ds(pl.multiple_of((code & (act - 1)) * edge, edge), edge) for code in codes]
        cube = stacked_dot(
            left_parts,
            jnp.concatenate([high[:, col] for col in cols], axis=1),
            jnp.concatenate([low[:, col] for col in cols], axis=1),
        )
        for w in range(width):
            value = 3.0 * square[pl.ds(r * edge, edge), cols[w]]
            value = value - 2.0 * cube[:, w * edge : (w + 1) * edge]
            out_ref[r, w] = jnp.where(holds & (codes[w] < act), value, 0.0)
        copies.append(pltpu.make_async_copy(out_ref.at[r], out_hbm.at[r], out_sem.at[r]))
        copies[-1].start()
    for copy in copies:
        copy.wait()


def slot_table(columns, act):
    rows = columns.shape[0]
    slots = columns[:, :act]
    here = slots < rows
    ids = jnp.arange(rows, dtype=jnp.int32)
    taken = jnp.any(slots[:, :, None] == ids, axis=1)
    count = jnp.sum(here.astype(jnp.int32), axis=1, keepdims=True)
    before = jnp.sum(
        (~taken[:, None, :] & (ids[None, :] < ids[:, None])[None]).astype(jnp.int32), axis=2
    )
    at = jnp.where(taken, -1, count + before)
    filled = jnp.sum(
        jnp.where(at[:, None, :] == jnp.arange(act, dtype=jnp.int32)[None, :, None], ids, 0), axis=2
    )
    codes = jnp.where(here, slots, filled + act)
    kept = jnp.sum(jnp.where(taken, 1 << ids, 0), axis=1, keepdims=True)
    return jnp.concatenate([codes, kept], axis=1).astype(jnp.int32)


def gather_local(x_blocks, columns):
    slab, width, edge, _ = x_blocks.shape
    rows = columns.shape[0]
    groups, chains, panels, lanes = (lax.axis_size(axis) for axis in AXES)
    last = chains - 1

    def index(g, place):
        z, x, c = place
        return (((g % groups) * chains + z) * panels + x) * lanes + c

    def move(block, cycles):
        pairs = [(cycle[i - 1], cycle[i]) for cycle in cycles for i in range(len(cycle))]
        busy = {a for a, _ in pairs}
        route = [(index(g, a), index(g, b)) for g in range(groups) for a, b in pairs]
        for z in range(chains):
            for x in range(panels):
                idle = [(z, x, c) for c in range(lanes) if (z, x, c) not in busy]
                for g in range(groups):
                    if len(idle) == lanes:
                        route += [(index(g, idle[c - 1]), index(g, idle[c])) for c in range(lanes)]
                    else:
                        route += [(index(g, a), index(g + 1, a)) for a in idle]
        return lax.ppermute(block, AXES, route)

    def swap(block):
        return move(block, [])

    def move_only(block, chains_of):
        pairs = [(chain[i], chain[i + 1]) for chain in chains_of for i in range(len(chain) - 1)]
        route = [(index(g, a), index(g, b)) for g in range(groups) for a, b in pairs]
        return lax.ppermute(block, AXES, route)

    down_lane = [1 if z in (1, 2) else 0 for z in range(chains)]
    up_lane = [1 - c for c in down_lane]
    up = [(z, 0, up_lane[z]) for z in range(chains)] + [(last, 1, up_lane[last])]
    down = [(z, 0, down_lane[z]) for z in reversed(range(chains))] + [(0, 1, down_lane[0])]
    first = [
        up[:last] + down + [(0, 1, up_lane[0])],
        [up[last], up[-1], (last, 1, down_lane[last])],
    ]
    second = [up, down]

    def received(hops):
        planes, senders = [], []
        for z in range(chains):
            below = z - hops if z >= hops else -1
            above = z + hops if z + hops < chains else -1
            if hops == 2:
                below, above = last if z == 0 else below, 0 if z == last else above
            row = [above, below] if down_lane[z] == 0 else [below, above]
            lane_of = [down_lane, up_lane] if down_lane[z] == 0 else [up_lane, down_lane]
            planes.append(row)
            senders.append([lanes_of[plane] for plane, lanes_of in zip(row, lane_of)])
        return planes, senders

    near, far = received(1), received(2)
    hop1 = [rows[:last] + [rows[last][::-1]] for rows in near]
    tables = hop1, near, far

    table = slot_table(columns, lanes * width)
    r1 = move(x_blocks, first)
    own_swap = swap(x_blocks)
    r2 = move_only(own_swap, [up, down])
    r1, table = lax.optimization_barrier((r1, table))
    r3 = move(r1, second)
    t1 = swap(r1)
    r4a, r4b = move(r2[:1], second), move(r2[1:], second)
    t2 = swap(r2)

    order, own = rows * edge, slab * edge
    table = pltpu.with_memory_space_constraint(table, pltpu.SMEM)
    smem = pl.BlockSpec(memory_space=pltpu.SMEM)
    vmem = pl.BlockSpec(memory_space=pltpu.VMEM)
    params = pltpu.CompilerParams(vmem_limit_bytes=24 * 2**20)
    def held(*arrays):
        return [pltpu.with_memory_space_constraint(a, pltpu.VMEM) for a in arrays]

    high, low, left, part, notes = pl.pallas_call(
        functools.partial(early_kernel, tables),
        out_shape=[
            jax.ShapeDtypeStruct((order, order), jnp.bfloat16),
            jax.ShapeDtypeStruct((order, order), jnp.bfloat16),
            jax.ShapeDtypeStruct((2 * own, order), jnp.bfloat16),
            jax.ShapeDtypeStruct((own, order), jnp.float32),
            jax.ShapeDtypeStruct((8, 128), jnp.int32),
        ],
        in_specs=[smem] + [pl.BlockSpec(memory_space=pltpu.HBM)] + [vmem] * 6,
        out_specs=[vmem] * 5,
        scratch_shapes=[pltpu.VMEM(x_blocks.shape, jnp.float32), pltpu.SemaphoreType.DMA],
        compiler_params=params,
        name="early",
    )(table, pltpu.with_memory_space_constraint(x_blocks, pltpu.HBM), own_swap, r1, r2, t1, t2, r3)
    t3 = swap(r3)
    r4a, part = lax.optimization_barrier((r4a, part))
    t4a = swap(r4a)
    dense = [jax.ShapeDtypeStruct(a.shape, a.dtype) for a in (high, low, part)]

    def add_to_square(kernel, name, *pieces):
        at = 1 + len(pieces)
        return pl.pallas_call(
            functools.partial(kernel, tables),
            out_shape=dense,
            in_specs=[vmem] * (at + 4),
            out_specs=[vmem] * 3,
            input_output_aliases={at: 0, at + 1: 1, at + 3: 2},
            compiler_params=params,
            name=name,
        )(notes, *pieces, *held(high, low, left, part))

    high, low, part = add_to_square(waiting_kernel, "waiting", r4a)
    r4b, t4a, part = lax.optimization_barrier((r4b, t4a, part))
    t4b = swap(r4b)
    high, low, part = add_to_square(middle_kernel, "middle", r4b, t3, t4a)
    out, _, _, _ = pl.pallas_call(
        functools.partial(late_kernel, tables),
        out_shape=[jax.ShapeDtypeStruct(x_blocks.shape, jnp.float32)] + dense,
        in_specs=[vmem] * 6,
        out_specs=[pl.BlockSpec(memory_space=pltpu.HBM)] + [vmem] * 3,
        input_output_aliases={2: 1, 3: 2, 5: 3},
        scratch_shapes=[
            pltpu.VMEM((2 * own, order), jnp.bfloat16),
            pltpu.VMEM(x_blocks.shape, jnp.float32),
            pltpu.SemaphoreType.DMA((slab,)),
        ],
        compiler_params=params,
        name="late",
    )(notes, t4b, *held(high, low, left, part))
    return out


def local(x_blocks, columns):
    slab, width, edge, _ = x_blocks.shape
    rows, slots = columns.shape
    _, chains, panels, lanes = (lax.axis_size(axis) for axis in AXES)
    full = rows <= slots and rows == lanes * width and width in (2, 4)
    if full and rows <= 8 and slab == 2 and edge == 128 and panels >= 2 and lanes == 2 and chains == 4:
        return gather_local(x_blocks, columns)
    return ring_local(x_blocks, columns)


def solution(mesh):
    placed = (P(("groups", "blk"), ("panel", "depth"), None, None), P("groups", None))
    return jax.shard_map(
        local,
        mesh=mesh,
        in_specs=placed,
        out_specs=P(("groups", "blk"), ("panel", "depth"), None, None),
        check_vma=False,
    )
```

```python
import functools

import jax
import jax.numpy as jnp
from jax import lax
from jax.experimental import pallas as pl
from jax.experimental.pallas import tpu as pltpu
from jax.sharding import PartitionSpec as P

precise = lax.Precision.HIGHEST
AXES = ("groups", "blk", "panel", "depth")


def shifted(block, axis, distance):
    devices = range(lax.axis_size(axis))
    route = [((i - distance) % len(devices), i) for i in devices]
    return lax.ppermute(block, axis, route)


def slot_gather(blocks):
    return lax.all_gather(blocks, ("panel", "depth"), axis=1, tiled=True)


def slot_reduce(partial_value):
    return lax.psum_scatter(partial_value, ("panel", "depth"), scatter_dimension=1, tiled=True)


def rotate_one(incoming):
    return shifted(incoming, "blk", 1)


def ring_local(x_blocks, columns):
    slab_rows = x_blocks.shape[0]
    width_slots = x_blocks.shape[1]
    edge = x_blocks.shape[2]
    order_rows = columns.shape[0]
    all_slots = columns.shape[1]
    cycle_size = lax.axis_size("blk")
    cycle_place = lax.axis_index("blk")
    anchor = jnp.int32(0)
    first_own = cycle_place * slab_rows
    slot_first = lax.axis_index(("panel", "depth")) * width_slots
    my_cols = lax.dynamic_slice(columns, (first_own, anchor), (slab_rows, all_slots))
    own_cols = lax.dynamic_slice(my_cols, (anchor, slot_first), (slab_rows, width_slots))
    x_own = jnp.where((own_cols < order_rows)[:, :, None, None], x_blocks, jnp.float32(0.0))
    out_present = my_cols < order_rows
    empty = jnp.zeros((slab_rows, all_slots, edge, edge), jnp.float32)

    def contribute(partial_value, left_rows, incoming, source):
        group = incoming.shape[0]
        first_row = source * group
        their_cols = lax.dynamic_slice(columns, (first_row, slot_first), (group, width_slots))
        row_ids = first_row + jnp.arange(group, dtype=jnp.int32)
        selector = (my_cols[:, None, :] == row_ids[None, :, None]).astype(jnp.float32)
        picked = jnp.einsum("irs,isab->irab", selector, left_rows, precision=precise)
        products = jnp.einsum("irab,rubc->iruac", picked, incoming, precision=precise)
        targets = (their_cols[None, None, :, :] == my_cols[:, :, None, None]) & out_present[
            :, :, None, None
        ]
        placed = jnp.einsum(
            "isru,iruac->isac", targets.astype(jnp.float32), products, precision=precise
        )
        return partial_value + placed

    def one_way(left_rows, stored):

        def advance(offset, state):
            partial_value, incoming, stored = state
            source = (cycle_place - offset) % cycle_size
            partial_value = contribute(partial_value, left_rows, incoming, source)
            return (partial_value, rotate_one(incoming), stored)

        partial_value, incoming, stored = lax.fori_loop(
            0, cycle_size - 1, advance, (empty, x_own, stored)
        )
        source = (cycle_place + 1) % cycle_size
        return (contribute(partial_value, left_rows, incoming, source), stored)

    stored = jnp.zeros((1,), jnp.float32)
    left_first = slot_gather(x_own)
    partial_value, stored = one_way(left_first, stored)
    squared = slot_reduce(partial_value)
    left_second = slot_gather(squared)
    partial_value, stored = one_way(left_second, stored)
    cubed = slot_reduce(partial_value)
    return 3.0 * squared - 2.0 * cubed


def split(value):
    high = value.astype(jnp.bfloat16)
    low = (value - high.astype(jnp.float32)).astype(jnp.bfloat16)
    return high, low


def dot(left, right):
    return jnp.dot(left, right, preferred_element_type=jnp.float32)


def stacked_dot(left, high, low):
    half = left.shape[0] // 2
    both = dot(left, high)
    return both[:half] + (both[half:] + dot(left[:half], low))


def lookup(table, place, lane):
    found = jnp.int32(-1)
    for z, entries in enumerate(table):
        for c, entry in enumerate(entries):
            found = jnp.where((place == z) & (lane == c), entry, found)
    return found


def store_piece(piece, plane, code_of, high, low, own=None, slab=2, first=0):
    count, width, edge, _ = piece.shape
    act = 2 * width

    @pl.when(plane >= 0)
    def _():
        for r in range(count):
            row = plane * slab + first + r
            for w in range(width):
                code = code_of(first + r, w)
                col = pl.ds(pl.multiple_of((code & (act - 1)) * edge, edge), edge)
                block = jnp.where(code < act, piece[r, w], 0.0)
                block_high, block_low = split(block)
                at = pl.ds(pl.multiple_of(row * edge, edge), edge)
                high[at, col] = block_high
                low[at, col] = block_low
                if own is not None:
                    own[pl.ds(r * edge, edge), col] = block_high
                    own[pl.ds((slab + r) * edge, edge), col] = block_low


def table_codes(table_ref, plane, group, slab, width):
    row = jnp.maximum(plane, 0) * slab
    return lambda r, w: table_ref[row + r, group * width + w]


T3, R4, T4, OWN, KEPT = 0, 1, 2, 3, 4


def packed(values, bits):
    return functools.reduce(jnp.bitwise_or, [v << (bits * k) for k, v in enumerate(values)])


def noted_codes(notes, kind, width):
    codes = notes[0, kind]
    return lambda r, w: (codes >> (4 * (r * width + w))) & 15


def add_plane(plane, left, high, low, part_ref):
    depth, tile = part_ref.shape[0], 512

    @pl.when(plane >= 0)
    def _():
        rows = pl.ds(pl.multiple_of(plane * depth, depth), depth)
        for n in range(part_ref.shape[1] // tile):
            cols = pl.ds(n * tile, tile)
            part_ref[:, cols] += stacked_dot(left[:, rows], high[rows, cols], low[rows, cols])


def clear_row(plane, r, code_of, width, high, low):
    edge = high.shape[0] // (2 * width)

    @pl.when(plane >= 0)
    def _():
        at = pl.ds(pl.multiple_of((plane * 2 + r) * edge, edge), edge)
        for w in range(width):
            col = pl.ds(pl.multiple_of((code_of(r, w) & (2 * width - 1)) * edge, edge), edge)
            high[at, col] = jnp.zeros((edge, edge), jnp.bfloat16)
            low[at, col] = jnp.zeros((edge, edge), jnp.bfloat16)


def add_row_blocks(piece, plane, r, code_of, left, high, low, part_ref):
    _, width, edge, _ = piece.shape
    act = 2 * width

    @pl.when(plane >= 0)
    def _():
        at = pl.ds(pl.multiple_of((plane * 2 + r) * edge, edge), edge)
        codes = [code_of(r, w) for w in range(width)]
        cols = [pl.ds(pl.multiple_of((code & (act - 1)) * edge, edge), edge) for code in codes]
        blocks = [jnp.where(code < act, piece[0, w], 0.0) for w, code in enumerate(codes)]
        block_high, block_low = split(jnp.concatenate(blocks, axis=1))
        more = stacked_dot(left[:, at], block_high, block_low)
        sums = [part_ref[:, col] + more[:, w * edge : (w + 1) * edge] for w, col in enumerate(cols)]
        for w, col in enumerate(cols):
            part_ref[:, col] = sums[w]
            high[at, col] = block_high[:, w * edge : (w + 1) * edge]
            low[at, col] = block_low[:, w * edge : (w + 1) * edge]


def last_row_blocks(piece, plane, r, code_of, left, high, low):
    _, width, edge, _ = piece.shape
    act = 2 * width
    valid = plane >= 0
    at = pl.ds(pl.multiple_of((jnp.maximum(plane, 0) * 2 + r) * edge, edge), edge)
    codes = [code_of(r, w) for w in range(width)]
    cols = [pl.ds(pl.multiple_of((code & (act - 1)) * edge, edge), edge) for code in codes]
    blocks = [
        jnp.where(valid & (code < act), piece[0, w], 0.0) for w, code in enumerate(codes)
    ]
    block_high, block_low = split(jnp.concatenate(blocks, axis=1))
    more = stacked_dot(left[:, at], block_high, block_low)
    for w, col in enumerate(cols):
        part = slice(w * edge, (w + 1) * edge)
        high[at, col] = jnp.where(valid, block_high[:, part], high[at, col])
        low[at, col] = jnp.where(valid, block_low[:, part], low[at, col])
    return codes, cols, more


def early_kernel(
    tables, table_ref, own_hbm, own_swap, r1, r2, t1, t2, r3,
    high, low, left, part_ref, notes_ref, own_ref, own_sem,
):
    place, lane = lax.axis_index("blk"), lax.axis_index("depth")
    (hop1, hop1_senders), (near, near_senders), (far, far_senders) = tables
    slab, width = own_swap.shape[:2]
    act = 2 * width
    own_copy = pltpu.make_async_copy(own_hbm, own_ref, own_sem)
    own_copy.start()
    here, there = lookup(near, place, lane), lookup(near, place, 1 - lane)
    far_here, far_there = lookup(far, place, lane), lookup(far, place, 1 - lane)
    first_here, first_there = [lookup(hop1, place, c) for c in (lane, 1 - lane)]
    first_sender, first_other = [lookup(hop1_senders, place, c) for c in (lane, 1 - lane)]
    sender, other_sender = [lookup(near_senders, place, c) for c in (lane, 1 - lane)]
    far_sender, far_other = [lookup(far_senders, place, c) for c in (lane, 1 - lane)]
    part_ref[...] = jnp.zeros_like(part_ref)

    def codes(plane, group):
        return table_codes(table_ref, plane, group, slab, width)

    kinds = (
        (far_there, far_other),
        (far_here, 1 - far_sender),
        (far_there, 1 - far_other),
        (place, lane),
    )
    values = [
        packed([codes(plane, group)(r, w) for r in range(slab) for w in range(width)], 4)
        for plane, group in kinds
    ]
    values.append(packed([table_ref[place * slab + r, act] for r in range(slab)], act))
    notes = jnp.zeros(notes_ref.shape, jnp.int32)
    index = lax.broadcasted_iota(jnp.int32, notes.shape, 1)
    for at, value in enumerate(values):
        notes = jnp.where(index == at, value, notes)
    notes_ref[...] = notes

    store_piece(own_swap, place, codes(place, 1 - lane), high, low, left)
    store_piece(r1, first_here, codes(first_here, first_sender), high, low)
    store_piece(r2, here, codes(here, 1 - sender), high, low)
    store_piece(t1, first_there, codes(first_there, first_other), high, low)
    store_piece(t2, there, codes(there, 1 - other_sender), high, low)
    store_piece(r3, far_here, codes(far_here, far_sender), high, low)
    own_copy.wait()
    store_piece(own_ref, place, codes(place, lane), high, low, left)
    for plane in (place, here, there):
        add_plane(plane, left, high, low, part_ref)


def waiting_kernel(tables, notes_ref, r4a, high_in, low_in, left, part_in, high, low, part_ref):
    place, lane = lax.axis_index("blk"), lax.axis_index("depth")
    here = lookup(tables[-1][0], place, lane)
    width = r4a.shape[1]
    codes = noted_codes(notes_ref[...], R4, width)
    store_piece(r4a, here, codes, high, low)
    clear_row(here, 1, codes, width, high, low)
    add_plane(here, left, high, low, part_ref)


def middle_kernel(
    tables, notes_ref, r4b, t3, t4a, high_in, low_in, left, part_in, high, low, part_ref
):
    place, lane = lax.axis_index("blk"), lax.axis_index("depth")
    here, there = [lookup(tables[-1][0], place, c) for c in (lane, 1 - lane)]
    slab, width = t3.shape[:2]
    notes = notes_ref[...]
    codes = noted_codes(notes, T4, width)
    store_piece(t3, there, noted_codes(notes, T3, width), high, low)
    store_piece(t4a, there, codes, high, low)
    clear_row(there, 1, codes, width, high, low)
    add_plane(there, left, high, low, part_ref)
    add_row_blocks(
        r4b, here, 1, noted_codes(notes, R4, width), left, high, low, part_ref
    )


def late_kernel(
    tables, notes_ref, t4b, high_in, low_in, left, part_in,
    out_hbm, high, low, square, square_parts, out_ref, out_sem,
):
    place, lane = lax.axis_index("blk"), lax.axis_index("depth")
    there = lookup(tables[-1][0], place, 1 - lane)
    slab, width, edge, _ = out_ref.shape
    act = 2 * width
    holds = lax.axis_index("panel") == 0
    notes = notes_ref[...]
    own_codes = noted_codes(notes, OWN, width)
    codes, changed, more = last_row_blocks(
        t4b, there, 1, noted_codes(notes, T4, width), left, high, low
    )
    flags = notes[0, KEPT]

    def keep(r, c, col, block):
        kept = (flags >> (r * act + c)) & 1 > 0
        block_high, block_low = split(jnp.where(kept, block, 0.0))
        square_parts[pl.ds(2 * r * edge, edge), col] = block_high
        square_parts[pl.ds((2 * r + 1) * edge, edge), col] = block_low

    for r in range(slab):
        for c in range(square.shape[1] // edge):
            col = pl.ds(c * edge, edge)
            keep(r, c, col, square[pl.ds(r * edge, edge), col])
    sums = [square[:, col] + more[:, w * edge : (w + 1) * edge] for w, col in enumerate(changed)]
    for code, col, total in zip(codes, changed, sums):
        square[:, col] = total
        for r in range(slab):
            keep(r, code & (act - 1), col, total[r * edge : (r + 1) * edge])
    copies = []
    for r in range(slab):
        left_parts = square_parts[pl.ds(2 * r * edge, 2 * edge), :]
        codes = [own_codes(r, w) for w in range(width)]
        cols = [pl.ds(pl.multiple_of((code & (act - 1)) * edge, edge), edge) for code in codes]
        cube = stacked_dot(
            left_parts,
            jnp.concatenate([high[:, col] for col in cols], axis=1),
            jnp.concatenate([low[:, col] for col in cols], axis=1),
        )
        for w in range(width):
            value = 3.0 * square[pl.ds(r * edge, edge), cols[w]]
            value = value - 2.0 * cube[:, w * edge : (w + 1) * edge]
            out_ref[r, w] = jnp.where(holds & (codes[w] < act), value, 0.0)
        copies.append(pltpu.make_async_copy(out_ref.at[r], out_hbm.at[r], out_sem.at[r]))
        copies[-1].start()
    for copy in copies:
        copy.wait()


def slot_table(columns, act):
    rows = columns.shape[0]
    slots = columns[:, :act]
    here = slots < rows
    ids = jnp.arange(rows, dtype=jnp.int32)
    taken = jnp.any(slots[:, :, None] == ids, axis=1)
    count = jnp.sum(here.astype(jnp.int32), axis=1, keepdims=True)
    before = jnp.sum(
        (~taken[:, None, :] & (ids[None, :] < ids[:, None])[None]).astype(jnp.int32), axis=2
    )
    at = jnp.where(taken, -1, count + before)
    filled = jnp.sum(
        jnp.where(at[:, None, :] == jnp.arange(act, dtype=jnp.int32)[None, :, None], ids, 0), axis=2
    )
    codes = jnp.where(here, slots, filled + act)
    kept = jnp.sum(jnp.where(taken, 1 << ids, 0), axis=1, keepdims=True)
    return jnp.concatenate([codes, kept], axis=1).astype(jnp.int32)


def gather_local(x_blocks, columns):
    slab, width, edge, _ = x_blocks.shape
    rows = columns.shape[0]
    groups, chains, panels, lanes = (lax.axis_size(axis) for axis in AXES)
    last = chains - 1

    def index(g, place):
        z, x, c = place
        return (((g % groups) * chains + z) * panels + x) * lanes + c

    def move(block, cycles):
        pairs = [(cycle[i - 1], cycle[i]) for cycle in cycles for i in range(len(cycle))]
        busy = {a for a, _ in pairs}
        route = [(index(g, a), index(g, b)) for g in range(groups) for a, b in pairs]
        for z in range(chains):
            for x in range(panels):
                idle = [(z, x, c) for c in range(lanes) if (z, x, c) not in busy]
                for g in range(groups):
                    if len(idle) == lanes:
                        route += [(index(g, idle[c - 1]), index(g, idle[c])) for c in range(lanes)]
                    else:
                        route += [(index(g, a), index(g + 1, a)) for a in idle]
        return lax.ppermute(block, AXES, route)

    def swap(block):
        return move(block, [])

    def move_only(block, chains_of):
        pairs = [(chain[i], chain[i + 1]) for chain in chains_of for i in range(len(chain) - 1)]
        route = [(index(g, a), index(g, b)) for g in range(groups) for a, b in pairs]
        return lax.ppermute(block, AXES, route)

    down_lane = [1 if z == 1 else 0 for z in range(chains)]
    up_lane = [1 - c for c in down_lane]
    up = [(z, 0, up_lane[z]) for z in range(chains)] + [(last, 1, up_lane[last])]
    down = [(z, 0, down_lane[z]) for z in reversed(range(chains))] + [(0, 1, down_lane[0])]
    first = [
        up[:last] + down + [(0, 1, up_lane[0])],
        [up[last], up[-1], (last, 1, down_lane[last])],
    ]
    second = [up, down]

    def received(hops):
        planes, senders = [], []
        for z in range(chains):
            below = z - hops if z >= hops else -1
            above = z + hops if z + hops < chains else -1
            if hops == 2:
                below, above = last if z == 0 else below, 0 if z == last else above
            row = [above, below] if down_lane[z] == 0 else [below, above]
            lane_of = [down_lane, up_lane] if down_lane[z] == 0 else [up_lane, down_lane]
            planes.append(row)
            senders.append([lanes_of[plane] for plane, lanes_of in zip(row, lane_of)])
        return planes, senders

    near, far = received(1), received(2)
    hop1 = [rows[:last] + [rows[last][::-1]] for rows in near]
    tables = hop1, near, far

    table = slot_table(columns, lanes * width)
    r1 = move(x_blocks, first)
    own_swap = swap(x_blocks)
    r2 = move_only(own_swap, [up, down])
    r1, table = lax.optimization_barrier((r1, table))
    r3 = move(r1, second)
    t1 = swap(r1)
    r4a, r4b = move(r2[:1], second), move(r2[1:], second)
    t2 = swap(r2)

    order, own = rows * edge, slab * edge
    table = pltpu.with_memory_space_constraint(table, pltpu.SMEM)
    smem = pl.BlockSpec(memory_space=pltpu.SMEM)
    vmem = pl.BlockSpec(memory_space=pltpu.VMEM)
    params = pltpu.CompilerParams(vmem_limit_bytes=24 * 2**20)
    def held(*arrays):
        return [pltpu.with_memory_space_constraint(a, pltpu.VMEM) for a in arrays]

    high, low, left, part, notes = pl.pallas_call(
        functools.partial(early_kernel, tables),
        out_shape=[
            jax.ShapeDtypeStruct((order, order), jnp.bfloat16),
            jax.ShapeDtypeStruct((order, order), jnp.bfloat16),
            jax.ShapeDtypeStruct((2 * own, order), jnp.bfloat16),
            jax.ShapeDtypeStruct((own, order), jnp.float32),
            jax.ShapeDtypeStruct((8, 128), jnp.int32),
        ],
        in_specs=[smem] + [pl.BlockSpec(memory_space=pltpu.HBM)] + [vmem] * 6,
        out_specs=[vmem] * 5,
        scratch_shapes=[pltpu.VMEM(x_blocks.shape, jnp.float32), pltpu.SemaphoreType.DMA],
        compiler_params=params,
        name="early",
    )(table, pltpu.with_memory_space_constraint(x_blocks, pltpu.HBM), own_swap, r1, r2, t1, t2, r3)
    t3 = swap(r3)
    r4a, part = lax.optimization_barrier((r4a, part))
    t4a = swap(r4a)
    dense = [jax.ShapeDtypeStruct(a.shape, a.dtype) for a in (high, low, part)]

    def add_to_square(kernel, name, *pieces):
        at = 1 + len(pieces)
        return pl.pallas_call(
            functools.partial(kernel, tables),
            out_shape=dense,
            in_specs=[vmem] * (at + 4),
            out_specs=[vmem] * 3,
            input_output_aliases={at: 0, at + 1: 1, at + 3: 2},
            compiler_params=params,
            name=name,
        )(notes, *pieces, *held(high, low, left, part))

    high, low, part = add_to_square(waiting_kernel, "waiting", r4a)
    r4b, t4a, part = lax.optimization_barrier((r4b, t4a, part))
    t4b = swap(r4b)
    high, low, part = add_to_square(middle_kernel, "middle", r4b, t3, t4a)
    out, _, _, _ = pl.pallas_call(
        functools.partial(late_kernel, tables),
        out_shape=[jax.ShapeDtypeStruct(x_blocks.shape, jnp.float32)] + dense,
        in_specs=[vmem] * 6,
        out_specs=[pl.BlockSpec(memory_space=pltpu.HBM)] + [vmem] * 3,
        input_output_aliases={2: 1, 3: 2, 5: 3},
        scratch_shapes=[
            pltpu.VMEM((2 * own, order), jnp.bfloat16),
            pltpu.VMEM(x_blocks.shape, jnp.float32),
            pltpu.SemaphoreType.DMA((slab,)),
        ],
        compiler_params=params,
        name="late",
    )(notes, t4b, *held(high, low, left, part))
    return out


def local(x_blocks, columns):
    slab, width, edge, _ = x_blocks.shape
    rows, slots = columns.shape
    _, chains, panels, lanes = (lax.axis_size(axis) for axis in AXES)
    full = rows <= slots and rows == lanes * width and width in (2, 4)
    if full and rows <= 8 and slab == 2 and edge == 128 and panels >= 2 and lanes == 2 and chains == 4:
        return gather_local(x_blocks, columns)
    return ring_local(x_blocks, columns)


def solution(mesh):
    placed = (P(("groups", "blk"), ("panel", "depth"), None, None), P("groups", None))
    return jax.shard_map(
        local,
        mesh=mesh,
        in_specs=placed,
        out_specs=P(("groups", "blk"), ("panel", "depth"), None, None),
        check_vma=False,
    )
```
